32 devices in a mesh: rows: 8 (over y, x, core), cols: 4 (over z).
Axes of the slice: x: 2, y: 2, z: 4, core: 2. Of those that a mesh axis runs over, the one named last changes fastest.
Arguments:
- tokens: bfloat16 [104, 2048], P(None, 'rows'), may hold values from -24 to 24
- arrival: int32 [104], replicated, may hold values from 0 to 103, each once
- cache_lengths: int32 [104], replicated, may hold values from 1 to 1023, as said below
- move_slot: int32 [8, 4], replicated, may hold values from 0 to 12, as said below
- move_target: int32 [8, 4], replicated, may hold values from 0 to 7, as said below
- page_table: int32 [8, 4, 13, 8], P('rows', 'cols'), may hold values from 0 to 103, as said below
- kv_pool: bfloat16 [832, 4, 32, 512], P('rows', 'cols'), may hold values from -400 to 400
- ssm_state: bfloat16 [104, 32, 64, 256], P('rows', 'cols'), may hold values from -1.5 to 1.5
- conv_x: bfloat16 [104, 3, 2048], P('rows', None, 'cols'), may hold values from -6 to 6
- conv_bc: bfloat16 [104, 3, 512], P('rows'), may hold values from -6 to 6
- norm_gain: bfloat16 [2048], P('rows'), may hold values from 0.099609375 to 1.8984375
- weight_z: bfloat16 [2048, 2048], P('rows', 'cols'), may hold values from -0.125 to 0.125
- weight_x: bfloat16 [2048, 2048], P('rows', 'cols'), may hold values from -0.125 to 0.125
- weight_dt: bfloat16 [2048, 32], P('rows', 'cols'), may hold values from -0.125 to 0.125
- weight_bc: bfloat16 [2048, 512], P('rows'), may hold values from -0.125 to 0.125
- weight_qkv: bfloat16 [2048, 1536], P('rows'), may hold values from -0.125 to 0.125
- conv_weight_x: bfloat16 [4, 2048], P(None, 'cols'), may hold values from -3 to 3
- conv_weight_bc: bfloat16 [4, 512], replicated, may hold values from -3 to 3
- dt_bias: float32 [32], P('cols'), may hold values from -4 to -1
- a_log: float32 [32], P('cols'), may hold values from 0 to 2.5
- d_skip: float32 [32], P('cols'), may hold values from 0.5 to 1.5
- weight_ssm_out: bfloat16 [2048, 2048], P('cols'), may hold values from -0.125 to 0.125
- weight_attn_out: bfloat16 [1024, 2048], P('cols'), may hold values from -0.1875 to 0.1875
Outputs:
- mixed: bfloat16 [104, 2048], P('rows', 'cols')
- ssm_next: bfloat16 [104, 32, 64, 256], P('rows', 'cols')
- conv_x_next: bfloat16 [104, 3, 2048], P('rows', None, 'cols')
- conv_bc_next: bfloat16 [104, 3, 512], P('rows')
- kv_next: bfloat16 [832, 4, 32, 512], P('rows', 'cols')
The draws below stay inside these ranges and needn't reach their ends.
Inputs may be any that keep to these rules, and one draw needn't show every extreme that they name: `cache_lengths`: some request has 1023 cached tokens. `move_slot`: each row lists 4 distinct slots. `move_target`: each row lists 4 distinct row indices other than its own; every row index is named exactly 4 times, by distinct sources. `page_table`: the 13 x 8 entries of one device are each of 0 to 103 once.
All inputs are finite; a program needn't handle non-finite values.
Results may differ from the reference program's by a relative error of at most 0.011.
Values may be sent and summed in bfloat16 or wider, within the bound.
No kernel may reach another device: no remote copies, remote signals or barrier semaphores. Data moves between devices by JAX's collectives and lax.ppermute only.
A program may use at most 64 MiB of HBM per device.

```python
import jax
import jax.numpy as jnp
from jax import lax

D = 2048
NH = 32
HP = 64
NS = 256
KW = 4
QH = 8
KVH = 2
HD = 128
CTX = 1024
PAGE = 32
SLOTS = 13
DI = 2048
QKV = 1536
REQUESTS = 104
MIG = 4
PPD = 8
POOL = 104
N_ROWS = 8
N_COLS = 4


def draw_tokens(key, part):
    features = jnp.arange(D, dtype=jnp.float32) / D
    feature_scale = 0.5 + features
    values = jax.random.normal(key, (REQUESTS, D), jnp.float32) * feature_scale[None, :]
    return jnp.clip(values, -24.0, 24.0).astype(jnp.bfloat16)


def draw_cache_lengths(key, part):
    first_key, second_key, third_key = jax.random.split(jax.random.fold_in(key, 3), 3)
    first_draw = jax.random.randint(first_key, (REQUESTS,), 1, CTX)
    second_draw = jax.random.randint(second_key, (REQUESTS,), 1, CTX)
    shorter = jnp.minimum(first_draw, second_draw)
    longest = jax.random.randint(third_key, (), 0, REQUESTS)
    return jnp.where(jnp.arange(REQUESTS) == longest, CTX - 1, shorter).astype(jnp.int32)


def move_tables(key):
    base_key = jax.random.fold_in(key, 7)
    first_key, second_key, third_key = jax.random.split(base_key, 3)
    device_order = jax.random.permutation(first_key, N_ROWS)
    position = jnp.zeros((N_ROWS,), jnp.int32).at[device_order].set(jnp.arange(N_ROWS, dtype=jnp.int32))
    offsets = 1 + jax.random.permutation(second_key, N_ROWS - 1)[:MIG]
    targets = device_order[(position[:, None] + offsets[None, :]) % N_ROWS]
    scores = jax.random.randint(third_key, (N_ROWS, SLOTS), 0, 1 << 20) * SLOTS + jnp.arange(SLOTS)[None, :]
    leaving = jnp.argsort(scores, axis=1)[:, :MIG]
    return (leaving.astype(jnp.int32), targets.astype(jnp.int32))


def draw_move_slot(key, part):
    return move_tables(key)[0]


def draw_move_target(key, part):
    return move_tables(key)[1]


def draw_page_table(key, part):
    scores = jax.random.randint(jax.random.fold_in(key, 11), (N_ROWS, N_COLS, POOL), 0, 1 << 20) * POOL + jnp.arange(POOL)[None, None, :]
    ordering = jnp.argsort(scores, axis=2)
    return ordering.reshape(N_ROWS, N_COLS, SLOTS, PPD).astype(jnp.int32)


def draw_kv_pool(key, part):
    shape = (N_ROWS * POOL, N_COLS, PAGE, 2 * KVH * HD)
    first_key = jax.random.fold_in(jax.random.fold_in(key, 13), 0)
    noise = jax.random.normal(first_key, shape, jnp.float32)
    return jnp.clip(noise, -400.0, 400.0).astype(jnp.bfloat16)


def steps_of(stream_key, extent, cuts, low, top_value):
    def one(dim, shards_of):
        steps = jax.random.uniform(jax.random.fold_in(jax.random.fold_in(stream_key, 6), dim), (shards_of,), jnp.float32, low / len(cuts), top_value / len(cuts))
        return jnp.repeat(jnp.exp(steps), extent[dim] // shards_of).reshape((-1,) + (1,) * (len(extent) - dim - 1))

    loudness = one(*cuts[0])
    for cut in cuts[1:]:
        loudness = loudness * one(*cut)
    return loudness


def scatter_about(key, dims, spread, most, shards=(), kind=jnp.bfloat16):
    gain = steps_of(key, dims, shards, -0.22, 0.18) if shards else 1.0
    result = jax.random.normal(key, dims, jnp.float32) * spread * gain
    return jnp.minimum(jnp.maximum(result, -most), most).astype(kind)


def setup_inputs(seed: int = 0) -> dict:
    key_of = jax.random.split(jax.random.key(seed), 24)
    tokens = draw_tokens(jax.random.fold_in(key_of[23], 71), 0)
    arrival = jax.random.permutation(key_of[1], REQUESTS).astype(jnp.int32)
    cache_lengths = draw_cache_lengths(jax.random.fold_in(key_of[23], 71), 0)
    move_slot = draw_move_slot(jax.random.fold_in(key_of[23], 71), 0)
    move_target = draw_move_target(jax.random.fold_in(key_of[23], 71), 0)
    page_table = draw_page_table(jax.random.fold_in(key_of[23], 71), 0)
    kv_pool = draw_kv_pool(jax.random.fold_in(key_of[23], 71), 0)
    ssm_state = scatter_about(key_of[7], (REQUESTS, NH, HP, NS), 0.25, 1.5, ((0, 8), (1, 4)))
    conv_x = scatter_about(key_of[8], (REQUESTS, KW - 1, DI), 1.0, 6.0, ((0, 8), (2, 4)))
    conv_bc = scatter_about(key_of[9], (REQUESTS, KW - 1, 2 * NS), 1.0, 6.0, ((0, 8),))
    norm_gain = jnp.clip(1.0 + 0.18 * jax.random.normal(key_of[10], (D,), jnp.float32), 0.099609375, 1.8984375).astype(jnp.bfloat16)
    weight_z = scatter_about(key_of[11], (D, DI), D ** -0.5, 0.125, ((0, 8), (1, 4)))
    weight_x = scatter_about(key_of[12], (D, DI), D ** -0.5, 0.125, ((0, 8), (1, 4)))
    weight_dt = scatter_about(key_of[13], (D, NH), D ** -0.5, 0.125, ((0, 8), (1, 4)))
    weight_bc = scatter_about(key_of[14], (D, 2 * NS), D ** -0.5, 0.125, ((0, 8),))
    weight_qkv = scatter_about(key_of[15], (D, QKV), D ** -0.5, 0.125, ((0, 8),))
    conv_weight_x = scatter_about(key_of[16], (KW, DI), KW ** -0.5, 3.0, ((1, 4),))
    conv_weight_bc = scatter_about(key_of[17], (KW, 2 * NS), KW ** -0.5, 3.0)
    dt_bias = jnp.clip(-4.0 + 3.0 * jax.random.uniform(key_of[18], (NH,), jnp.float32) ** steps_of(key_of[18], (NH,), ((0, 4),), -0.2, 0.2), -4.0, -1.0)
    a_log = jnp.clip(2.5 * jax.random.uniform(key_of[19], (NH,), jnp.float32) ** steps_of(key_of[19], (NH,), ((0, 4),), -0.2, 0.2), 0.0, 2.5)
    d_skip = jnp.clip(0.5 + 1.0 * jax.random.uniform(key_of[20], (NH,), jnp.float32) ** steps_of(key_of[20], (NH,), ((0, 4),), -0.2, 0.2), 0.5, 1.5)
    weight_ssm_out = scatter_about(key_of[21], (DI, D), DI ** -0.5, 0.125, ((0, 4),))
    weight_attn_out = scatter_about(key_of[22], (QH * HD, D), (QH * HD) ** -0.5, 0.1875, ((0, 4),))
    return {"tokens": tokens, "arrival": arrival, "cache_lengths": cache_lengths, "move_slot": move_slot, "move_target": move_target, "page_table": page_table, "kv_pool": kv_pool, "ssm_state": ssm_state, "conv_x": conv_x, "conv_bc": conv_bc, "norm_gain": norm_gain, "weight_z": weight_z, "weight_x": weight_x, "weight_dt": weight_dt, "weight_bc": weight_bc, "weight_qkv": weight_qkv, "conv_weight_x": conv_weight_x, "conv_weight_bc": conv_weight_bc, "dt_bias": dt_bias, "a_log": a_log, "d_skip": d_skip, "weight_ssm_out": weight_ssm_out, "weight_attn_out": weight_attn_out}


EPSILON = 1e-05
FLOOR_SCORE = -1e+30
PRECISE = lax.Precision.HIGHEST

def residents(move_slot, move_target, row_count, slot_count):
    move_count = move_slot.shape[1]
    devices = jnp.arange(row_count, dtype=jnp.int32)
    matches = move_target[:, None, :] == devices[None, :, None]
    sending = jnp.any(matches, axis=2)
    slot_from = lax.optimization_barrier(jnp.sum(jnp.where(matches, move_slot[:, None, :], 0), axis=2))
    ranking = jnp.cumsum(sending.astype(jnp.int32), axis=0) - 1
    leaving = devices[:, None] * slot_count + slot_from
    turn_order = jnp.arange(move_count, dtype=jnp.int32)
    chosen = sending[:, :, None] & (ranking[:, :, None] == turn_order[None, None, :])
    incoming = lax.optimization_barrier(jnp.sum(jnp.where(chosen, leaving[:, :, None], 0), axis=0))
    places = jnp.arange(slot_count, dtype=jnp.int32)
    vacant = move_slot[:, :, None] == places[None, None, :]
    filled = lax.optimization_barrier(jnp.sum(jnp.where(vacant, incoming[:, :, None], 0), axis=1))
    staying = devices[:, None] * slot_count + places[None, :]
    return jnp.where(jnp.any(vacant, axis=1), filled, staying).astype(jnp.int32)

def reference(tokens, arrival, cache_lengths, move_slot, move_target, page_table, kv_pool, ssm_state, conv_x, conv_bc, norm_gain, weight_z, weight_x, weight_dt, weight_bc, weight_qkv, conv_weight_x, conv_weight_bc, dt_bias, a_log, d_skip, weight_ssm_out, weight_attn_out):
    layout = residents(move_slot, move_target, N_ROWS, SLOTS).reshape(-1)
    inverse = jnp.zeros((REQUESTS,), jnp.int32).at[arrival].set(jnp.arange(REQUESTS, dtype=jnp.int32))
    picked = jnp.take(tokens, inverse[layout], axis=0)
    widened = picked.astype(jnp.float32)
    square_sum = lax.optimization_barrier(jnp.sum(jnp.square(widened), axis=1))
    scaled = (widened * norm_gain.astype(jnp.float32)[None, :]).astype(jnp.bfloat16)
    root_mean = jnp.sqrt(square_sum / D + EPSILON)[:, None]

    def project(weight):
        return (jnp.dot(scaled, weight, preferred_element_type=jnp.float32) / root_mean).astype(jnp.bfloat16)
    gate_in = project(weight_z)
    value_in = project(weight_x)
    step_in = project(weight_dt)
    bc_in = project(weight_bc)
    qkv_in = project(weight_qkv)
    window_x = jnp.concatenate([jnp.take(conv_x, layout, axis=0), value_in[:, None, :]], axis=1)
    window_bc = jnp.concatenate([jnp.take(conv_bc, layout, axis=0), bc_in[:, None, :]], axis=1)
    conv_x_next = window_x[:, 1:]
    conv_bc_next = window_bc[:, 1:]
    value_act = jax.nn.silu(lax.optimization_barrier(jnp.sum(window_x.astype(jnp.float32) * conv_weight_x.astype(jnp.float32)[None], axis=1)))
    bc_act = jax.nn.silu(lax.optimization_barrier(jnp.sum(window_bc.astype(jnp.float32) * conv_weight_bc.astype(jnp.float32)[None], axis=1))).astype(jnp.bfloat16)
    b_in = bc_act[:, :NS].astype(jnp.float32)
    c_out = bc_act[:, NS:].astype(jnp.float32)
    step_size = jax.nn.softplus(step_in.astype(jnp.float32) + dt_bias.astype(jnp.float32)[None, :])
    decay_rate = jnp.exp(-jnp.exp(a_log.astype(jnp.float32))[None, :] * step_size)
    skip_wide = d_skip.astype(jnp.float32)

    def ssm_row(index):
        request = layout[index]
        prior = lax.dynamic_index_in_dim(ssm_state, request, 0, keepdims=False).astype(jnp.float32)
        value_heads = value_act[index].reshape(NH, HP)
        state_new = decay_rate[index][:, None, None] * prior + (step_size[index][:, None] * value_heads)[:, :, None] * b_in[index][None, None, :]
        readout = jnp.einsum('hpn,n->hp', state_new, c_out[index], precision=PRECISE) + skip_wide[:, None] * value_heads
        return (state_new.astype(jnp.bfloat16), readout.reshape(DI))
    ssm_next, readout = lax.map(ssm_row, jnp.arange(REQUESTS, dtype=jnp.int32))
    gated = (readout * jax.nn.silu(gate_in.astype(jnp.float32))).astype(jnp.bfloat16)
    group_size = QH // KVH
    queries = qkv_in[:, :QH * HD].reshape(REQUESTS, KVH, group_size, HD).astype(jnp.float32)
    key_new = qkv_in[:, QH * HD:(QH + KVH) * HD].reshape(REQUESTS, KVH, HD)
    value_new = qkv_in[:, (QH + KVH) * HD:].reshape(REQUESTS, KVH, HD)
    page_total = CTX // PAGE
    logical = jnp.arange(page_total, dtype=jnp.int32)
    page_col = logical % N_COLS
    page_local = logical // N_COLS
    score_scale = HD ** (-0.5)

    def attend(index):
        request = layout[index]
        home_row = request // SLOTS
        home_slot = request % SLOTS
        source_pages = home_row * POOL + page_table[home_row, page_col, home_slot, page_local]
        page_rows = kv_pool[source_pages, page_col].reshape(CTX, 2 * KVH * HD).astype(jnp.float32)
        cached_keys = page_rows[:, :KVH * HD].reshape(CTX, KVH, HD)
        cached_values = page_rows[:, KVH * HD:].reshape(CTX, KVH, HD)
        query_row = queries[index]
        scores = jnp.einsum('kgd,tkd->kgt', query_row, cached_keys, precision=PRECISE) * score_scale
        live_mask = (jnp.arange(CTX) < cache_lengths[request])[None, None, :]
        own_score = jnp.einsum('kgd,kd->kg', query_row, key_new[index].astype(jnp.float32), precision=PRECISE) * score_scale
        row_peak = jnp.maximum(lax.optimization_barrier(jnp.max(jnp.where(live_mask, scores, FLOOR_SCORE), axis=2)), own_score)
        weights = jnp.where(live_mask, jnp.exp(scores - row_peak[:, :, None]), 0.0)
        own_weight = jnp.exp(own_score - row_peak)
        row_total = lax.optimization_barrier(jnp.sum(weights, axis=2)) + own_weight
        weighted = jnp.einsum('kgt,tkd->kgd', weights, cached_values, precision=PRECISE) + own_weight[:, :, None] * value_new[index].astype(jnp.float32)[:, None, :]
        return (weighted / row_total[:, :, None]).reshape(QH * HD).astype(jnp.bfloat16)
    attended = lax.map(attend, jnp.arange(REQUESTS, dtype=jnp.int32))
    mixed = (jnp.dot(gated, weight_ssm_out, preferred_element_type=jnp.float32) + jnp.dot(attended, weight_attn_out, preferred_element_type=jnp.float32)).astype(jnp.bfloat16)
    flat_table = page_table.reshape(N_ROWS, N_COLS, POOL)
    row_ids = jnp.arange(N_ROWS, dtype=jnp.int32)[:, None, None]
    col_ids = jnp.arange(N_COLS, dtype=jnp.int32)[None, :, None]
    owner = jnp.zeros((N_ROWS, N_COLS, POOL), jnp.int32).at[row_ids, col_ids, flat_table].set(jnp.broadcast_to(jnp.arange(POOL, dtype=jnp.int32)[None, None, :], flat_table.shape))
    owner_slot = owner // PPD
    owner_page = owner % PPD
    owner_request = jnp.take(layout, row_ids * SLOTS + owner_slot)
    anchor_row = owner_request // SLOTS
    anchor_slot = owner_request % SLOTS
    source = anchor_row * POOL + page_table[anchor_row, col_ids, anchor_slot, owner_page]
    source = jnp.transpose(source, (0, 2, 1)).reshape(N_ROWS * POOL, N_COLS)
    moved = kv_pool[source, jnp.arange(N_COLS, dtype=jnp.int32)[None, :]]
    served = jnp.arange(REQUESTS, dtype=jnp.int32)
    lengths_now = jnp.take(cache_lengths, layout)
    logical_page = lengths_now // PAGE
    block_col = logical_page % N_COLS
    block_page = logical_page // N_COLS
    offset_in = lengths_now % PAGE
    target_row = served // SLOTS
    target_slot = served % SLOTS
    target_page = target_row * POOL + page_table[target_row, block_col, target_slot, block_page]
    fresh_rows = jnp.concatenate([key_new.reshape(REQUESTS, KVH * HD), value_new.reshape(REQUESTS, KVH * HD)], axis=1)
    kv_next = moved.at[target_page, block_col, offset_in].set(fresh_rows)
    return (mixed, ssm_next, conv_x_next, conv_bc_next, kv_next)
```

```python
import functools

import jax
import jax.numpy as jnp
from jax import lax
from jax.experimental import pallas as pl
from jax.experimental.pallas import tpu as pltpu
from jax.sharding import PartitionSpec as P

HP = 64
NS = 256
KW = 4
QH = 8
KVH = 2
HD = 128
PAGE = 32
LANES = 128
BLOCK = 16

EPSILON = 1e-05
FLOOR_SCORE = -1e30
VMEM_LIMIT = 32 * 1024 * 1024

F32 = jnp.float32
BF16 = jnp.bfloat16
I32 = jnp.int32

SMEM_SPEC = pl.BlockSpec(memory_space=pltpu.SMEM)
VMEM_SPEC = pl.BlockSpec(memory_space=pltpu.VMEM)
ANY_SPEC = pl.BlockSpec(memory_space=pl.ANY)


def silu(v):
    return v / (1.0 + jnp.exp(-v))


def dot(a, b):
    return jnp.dot(a, b, preferred_element_type=F32)


def dot_t(a, b):
    return lax.dot_general(a, b, (((1,), (1,)), ((), ())), preferred_element_type=F32)


def row_iota(shape):
    return lax.broadcasted_iota(I32, shape, 0)


def lane_iota(shape):
    return lax.broadcasted_iota(I32, shape, 1)


class Columns:
    def __init__(self, inner):
        self.z = 0
        self.x = inner
        self.bc = 2 * inner
        self.q = self.bc + 2 * NS
        self.kv = self.q + QH * HD
        self.tail = self.kv + 2 * KVH * HD
        self.width = self.tail + 2 * LANES


class Plan:
    def __init__(self, slots, moves):
        self.source = 0
        self.moved = slots
        self.length = 2 * slots
        self.arrive_slot = 3 * slots
        self.arrive_source = self.arrive_slot + moves
        self.stay_slot = self.arrive_source + moves
        self.size = self.stay_slot + slots - moves


def project_kernel(
    row_ref, arrival, lengths, move_slot, move_target, page_table,
    tokens, gain, conv_x, conv_bc, w_z, w_x, w_dt, w_bc, w_qkv, pool, state,
    out, pages_send, state_send, plan,
    layout, inverse, count, wide, picked, acc_x, acc_bc, tail, sems,
):
    row_count, moves = move_slot.shape
    slots, inner = conv_x.shape[0], conv_x.shape[2]
    pages_here = page_table.shape[1]
    heads = w_dt.shape[1]
    cols, at = Columns(inner), Plan(slots, moves)
    me = row_ref[0]

    copies = []
    for m in range(moves):
        slot, target = move_slot[me, m], move_target[me, m]
        copies.append(pltpu.make_async_copy(state.at[slot], state_send.at[target], sems.at[m, pages_here]))
        for page in range(pages_here):
            copies.append(
                pltpu.make_async_copy(
                    pool.at[page_table[slot, page]], pages_send.at[target, page], sems.at[m, page]
                )
            )
    for copy in copies:
        copy.start()

    wide[...] = tokens[...].astype(F32)
    picked[...] = jnp.zeros_like(picked)

    def begin(t, carry):
        count[t] = 0
        for s in range(slots):
            q = t * slots + s
            layout[q] = q
            inverse[arrival[q]] = q
        return carry

    lax.fori_loop(0, row_count, begin, 0)

    def place(i, carry):
        for m in range(moves):
            target = move_target[i, m]
            turn = count[target]
            count[target] = turn + 1
            layout[target * slots + move_slot[target, turn]] = i * slots + move_slot[i, m]
        return carry

    lax.fori_loop(0, row_count, place, 0)

    def pick(t, carry):
        for s in range(slots):
            source = inverse[layout[t * slots + s]]
            picked[pl.ds(t * BLOCK + s, 1), :] = wide[pl.ds(source, 1), :]
        return carry

    lax.fori_loop(0, row_count, pick, 0)

    rows = picked[...]
    squares = jnp.sum(rows * rows, axis=1, keepdims=True)
    scaled = (rows * gain[...].astype(F32)).astype(BF16)

    acc_x[...] = dot(scaled, w_z[...]).reshape(acc_x.shape)
    acc_bc[...] = dot(scaled, w_bc[...]).reshape(acc_bc.shape)
    for m in range(moves):
        slot, target = move_slot[me, m], move_target[me, m]
        acc_x[target, slots : slots + KW - 1, :] = conv_x[slot].astype(F32)
        acc_bc[target, slots : slots + KW - 1, :] = conv_bc[slot].astype(F32)
    total = row_count * BLOCK
    out[:, cols.z : cols.x] = acc_x[...].reshape(total, inner).astype(BF16)
    out[:, cols.bc : cols.q] = acc_bc[...].reshape(total, 2 * NS).astype(BF16)
    out[:, cols.x : cols.bc] = dot(scaled, w_x[...]).astype(BF16)
    out[:, cols.q : cols.tail] = dot(scaled, w_qkv[...]).astype(BF16)
    tail[...] = jnp.zeros_like(tail)
    tail[:, :heads] = dot(scaled, w_dt[...])
    tail[:, heads : heads + 1] = squares
    high = tail[...].astype(BF16)
    out[:, cols.tail : cols.tail + LANES] = high
    out[:, cols.tail + LANES :] = (tail[...] - high.astype(F32)).astype(BF16)

    stays = 0
    for s in range(slots):
        request = layout[me * slots + s]
        source = lax.div(request, I32(slots))
        moved = jnp.where(source == me, 0, 1)
        plan[at.source + s] = source
        plan[at.moved + s] = moved
        plan[at.length + s] = lengths[request]

        @pl.when(moved == 0)
        def _(s=s, stays=stays):
            plan[at.stay_slot + stays] = s

        stays = stays + 1 - moved
    for m in range(moves):
        slot = move_slot[me, m]
        plan[at.arrive_slot + m] = slot
        plan[at.arrive_source + m] = lax.div(layout[me * slots + slot], I32(slots))

    for copy in copies:
        copy.wait()


def widen(per_head, inner):
    rows = per_head.shape[0]
    first = lane_iota((rows, 2 * HP)) < HP
    pieces = []
    for h in range(0, inner // HP, 2):
        pieces.append(jnp.where(first, per_head[:, h : h + 1], per_head[:, h + 1 : h + 2]))
    return pieces[0] if len(pieces) == 1 else jnp.concatenate(pieces, axis=1)


def advance_state(slot, prior, c_out, b_twice, drive, decay, readout, result):
    heads = prior.shape[0]
    flat = prior[...].reshape(heads * HP, NS)
    read = dot_t(c_out[...], flat)
    here = row_iota(read.shape) == slot
    readout[...] = jnp.where(here, read, readout[...])
    twice = b_twice[...]
    row = row_iota(twice.shape)
    selected = jnp.where((row == slot) | (row == slot + BLOCK), twice, 0.0).astype(BF16)
    outer = dot(drive[...], selected).reshape(heads, HP, NS)
    for h in range(heads):
        rate = decay[pl.ds(slot, 1), h : h + 1]
        result[h] = (rate * prior[h].astype(F32) + outer[h]).astype(BF16)


def mix_kernel(
    plan, received, conv_x, conv_bc, cw_x, cw_bc, dt_bias, a_log, d_skip, state,
    conv_x_next, conv_bc_next, state_next, queries, kv_new, drive, decay, b_twice, c_out,
    readout, scale, base,
    window_x, window_bc, held, made, in_sems, out_sems,
    *, row_count, moves, width,
):
    slots, inner = conv_x.shape[0], conv_x.shape[2]
    heads = dt_bias.shape[1]
    cols, at = Columns(inner), Plan(slots, moves)
    stays = slots - moves
    loads = []
    for j in range(stays):
        loads.append(pltpu.make_async_copy(state.at[plan[at.stay_slot + j]], held.at[j], in_sems.at[j]))
        loads[-1].start()

    def summed(start, stop):
        total = received[0:BLOCK, start:stop].astype(F32)
        for i in range(1, row_count):
            total = total + received[i * BLOCK : (i + 1) * BLOCK, start:stop].astype(F32)
        return total

    tail = summed(cols.tail, cols.tail + LANES) + summed(cols.tail + LANES, cols.width)
    root = jnp.sqrt(tail[:, heads : heads + 1] / width + EPSILON)

    def projected(start, stop):
        return (summed(start, stop) / root).astype(BF16).astype(F32)

    value_in = projected(cols.x, cols.bc)
    bc_in = projected(cols.bc, cols.q)
    step_in = (tail[:, :heads] / root).astype(BF16).astype(F32)

    for s in range(slots):
        start = pl.multiple_of(plan[at.source + s] * BLOCK, BLOCK)
        moved = plan[at.moved + s] == 1
        for own, fresh, begin, end, window, following in (
            (conv_x, value_in, cols.z, cols.x, window_x, conv_x_next),
            (conv_bc, bc_in, cols.bc, cols.q, window_bc, conv_bc_next),
        ):
            arrived = received[pl.ds(start, BLOCK), begin:end].astype(F32)[slots : slots + KW - 1]
            past = jnp.where(moved, arrived, own[s].astype(F32))
            for k in range(KW - 1):
                window[k, s : s + 1, :] = past[k : k + 1]
            following[s] = jnp.concatenate([past[1:], fresh[s : s + 1]], axis=0).astype(BF16)

    def convolved(window, taps, fresh):
        total = fresh * taps[KW - 1 : KW, :].astype(F32)
        for k in range(KW - 1):
            total = total + window[k] * taps[k : k + 1, :].astype(F32)
        return silu(total)

    window_x[:, slots:, :] = jnp.zeros((KW - 1, BLOCK - slots, inner), F32)
    window_bc[:, slots:, :] = jnp.zeros((KW - 1, BLOCK - slots, 2 * NS), F32)
    value_act = convolved(window_x, cw_x, value_in)
    bc_act = convolved(window_bc, cw_bc, bc_in).astype(BF16).astype(F32)
    b_in, c_val = bc_act[:, :NS], bc_act[:, NS:]
    b_twice[...] = jnp.concatenate([b_in, b_in], axis=0)
    c_out[...] = c_val.astype(BF16)

    shifted = step_in + dt_bias[...]
    step_size = jnp.maximum(shifted, 0.0) + jnp.log(1.0 + jnp.exp(-jnp.abs(shifted)))
    rate = jnp.exp(-jnp.exp(a_log[...]) * step_size)
    decay[...] = rate
    driven = widen(step_size, inner) * value_act
    high = driven.astype(BF16).astype(F32)
    drive[...] = jnp.transpose(jnp.concatenate([high, driven - high], axis=0)).astype(BF16)
    gate = silu(projected(cols.z, cols.x))
    b_dot_c = jnp.sum(b_in * c_val, axis=1, keepdims=True)
    skip = widen(jnp.broadcast_to(d_skip[...], (BLOCK, heads)), inner)
    base[...] = (driven * b_dot_c + skip * value_act) * gate
    scale[...] = widen(rate, inner) * gate

    q_in = projected(cols.q, cols.kv)
    for h in range(QH):
        queries[pl.ds(h, BLOCK, stride=QH), :] = q_in[:, h * HD : (h + 1) * HD]
    kv_new[...] = projected(cols.kv, cols.tail)

    readout[...] = jnp.zeros_like(readout)
    stores = []
    for j in range(stays):
        slot = plan[at.stay_slot + j]
        loads[j].wait()
        advance_state(slot, held.at[j], c_out, b_twice, drive, decay, readout, made.at[j])
        stores.append(pltpu.make_async_copy(made.at[j], state_next.at[slot], out_sems.at[j]))
        stores[-1].start()
    for store in stores:
        store.wait()


def attend_kernel(
    col_ref, plan, page_table, queries, kv_new, pool, arrived,
    pool_next, send,
    pages, scores, weighted, peaks, totals, in_sems, out_sems,
    *, moves, col_count,
):
    slots, pages_here = page_table.shape
    at = Plan(slots, moves)
    col = col_ref[0]
    tokens_here = pages_here * PAGE
    kv_width = KVH * HD
    for s in range(slots):
        moved = plan[at.moved + s] == 1

        @pl.when(moved)
        def _(s=s):
            pltpu.make_async_copy(arrived.at[plan[at.source + s]], pages.at[s], in_sems.at[s]).start()

        @pl.when(jnp.logical_not(moved))
        def _(s=s):
            for page in range(pages_here):
                pltpu.make_async_copy(
                    pool.at[page_table[s, page]], pages.at[s, page], in_sems.at[s]
                ).start()

    first_group = row_iota((QH, HD)) < QH // KVH
    lane = lane_iota((QH, tokens_here))
    position = (lax.shift_right_logical(lane, 5) * col_count + col) * PAGE + lax.bitwise_and(lane, PAGE - 1)
    stores = []
    for s in range(slots):
        pltpu.make_async_copy(arrived.at[0], pages.at[s], in_sems.at[s]).wait()
        length = plan[at.length + s]
        logical = lax.div(length, I32(PAGE))

        @pl.when(lax.rem(logical, I32(col_count)) == col)
        def _(s=s, length=length, logical=logical):
            local_page = lax.div(logical, I32(col_count))
            old = pages[s, local_page].astype(F32)
            here = row_iota(old.shape) == lax.rem(length, I32(PAGE))
            pages[s, local_page] = jnp.where(here, kv_new[s : s + 1, :], old).astype(BF16)

        for page in range(pages_here):
            stores.append(
                pltpu.make_async_copy(
                    pages.at[s, page], pool_next.at[page_table[s, page]], out_sems.at[s, page]
                )
            )
            stores[-1].start()
        keys = pages[s, :, :, :kv_width].reshape(tokens_here, kv_width)
        query = queries[s * QH : (s + 1) * QH, :]
        query = jnp.concatenate(
            [jnp.where(first_group, query, 0.0), jnp.where(first_group, 0.0, query)], axis=1
        ).astype(BF16)
        score = dot_t(query, keys) * (HD ** -0.5)
        scores[s * QH : (s + 1) * QH, :] = jnp.where(position <= length, score, FLOOR_SCORE)

    live_rows = slots * QH
    everything = scores[0:live_rows, :]
    peak = jnp.max(everything, axis=1, keepdims=True)
    weights = jnp.where(everything > 0.5 * FLOOR_SCORE, jnp.exp(everything - peak), 0.0)
    total = jnp.sum(weights, axis=1, keepdims=True)
    scores[0:live_rows, :] = weights
    for ref, value in ((weighted, None), (peaks, peak), (totals, total)):
        ref[live_rows:, :] = jnp.zeros((BLOCK * QH - live_rows, HD), F32)
        if value is not None:
            ref[0:live_rows, :] = jnp.broadcast_to(value, (live_rows, HD))
    for s in range(slots):
        values = pages[s, :, :, kv_width:].reshape(tokens_here, kv_width)
        weight = scores[s * QH : (s + 1) * QH, :]
        high = weight.astype(BF16).astype(F32)
        both = dot(jnp.concatenate([high, weight - high], axis=0).astype(BF16), values)
        joined = both[:QH] + both[QH:]
        weighted[s * QH : (s + 1) * QH, :] = jnp.where(first_group, joined[:, :HD], joined[:, HD:])

    share = QH * HD // col_count
    part = min(share, HD)
    lanes = lane_iota((BLOCK, LANES))
    for c in range(col_count):
        stats = jnp.zeros((BLOCK, LANES), F32)
        for j in range(share // part):
            head = (c * share + j * part) // HD
            begin = (c * share + j * part) % HD
            rows = pl.ds(head, BLOCK, stride=QH)
            send[c * BLOCK : (c + 1) * BLOCK, j * part : (j + 1) * part] = weighted[rows, :][
                :, begin : begin + part
            ]
            stats = jnp.where(lanes == 2 * j, peaks[rows, :], stats)
            stats = jnp.where(lanes == 2 * j + 1, totals[rows, :], stats)
        send[c * BLOCK : (c + 1) * BLOCK, share:] = stats
    for store in stores:
        store.wait()


def output_kernel(
    plan, arrived, state_in, drive, decay, b_twice, c_out, readout_in, scale, base, partials, w_ssm, w_attn,
    state_next, send,
    readout, held, made, in_sems, out_sems,
    *, slots, moves, col_count,
):
    del state_in
    at = Plan(slots, moves)
    loads = []
    for m in range(moves):
        loads.append(
            pltpu.make_async_copy(arrived.at[plan[at.arrive_source + m]], held.at[m], in_sems.at[m])
        )
        loads[-1].start()

    share = w_attn.shape[0]
    part = min(share, HD)
    pieces = []
    for j in range(share // part):
        block = [partials[c * BLOCK : (c + 1) * BLOCK, :] for c in range(col_count)]
        peaks = [b[:, share + 2 * j : share + 2 * j + 1] for b in block]
        joint = functools.reduce(jnp.maximum, peaks)
        factors = [jnp.exp(p - joint) for p in peaks]
        total = sum(f * b[:, share + 2 * j + 1 : share + 2 * j + 2] for f, b in zip(factors, block))
        value = sum(f * b[:, j * part : (j + 1) * part] for f, b in zip(factors, block))
        pieces.append(value / total)
    attended = pieces[0] if len(pieces) == 1 else jnp.concatenate(pieces, axis=1)
    attended = jnp.where(row_iota(attended.shape) < slots, attended, 0.0).astype(BF16)

    readout[...] = readout_in[...]
    stores = []
    for m in range(moves):
        slot = plan[at.arrive_slot + m]
        loads[m].wait()
        advance_state(slot, held.at[m], c_out, b_twice, drive, decay, readout, made.at[m])
        stores.append(pltpu.make_async_copy(made.at[m], state_next.at[slot], out_sems.at[m]))
        stores[-1].start()
    gated = (readout[...] * scale[...] + base[...]).astype(BF16)
    columns = w_ssm.shape[1] // col_count
    for c in range(col_count):
        span = slice(c * columns, (c + 1) * columns)
        send[c * BLOCK : (c + 1) * BLOCK, :] = dot(gated, w_ssm[:, span]) + dot(attended, w_attn[:, span])
    for store in stores:
        store.wait()


def sum_kernel(received, out, *, col_count):
    total = received[0:BLOCK, :]
    for c in range(1, col_count):
        total = total + received[c * BLOCK : (c + 1) * BLOCK, :]
    out[...] = total[: out.shape[0]].astype(BF16)


def shape(dims, dtype):
    return jax.ShapeDtypeStruct(tuple(dims), dtype)


def params():
    return pltpu.CompilerParams(vmem_limit_bytes=VMEM_LIMIT)


def cost(flops, moved):
    return pl.CostEstimate(flops=int(flops), bytes_accessed=int(moved), transcendentals=0)


def exchange(value, axis):
    return lax.all_to_all(value, axis, split_axis=0, concat_axis=0, tiled=True)


def local(
    tokens, arrival, cache_lengths, move_slot, move_target, page_table, kv_pool, ssm_state,
    conv_x, conv_bc, norm_gain, weight_z, weight_x, weight_dt, weight_bc, weight_qkv,
    conv_weight_x, conv_weight_bc, dt_bias, a_log, d_skip, weight_ssm_out, weight_attn_out,
):
    row_count = lax.axis_size("rows")
    col_count = lax.axis_size("cols")
    row_index = lax.axis_index("rows").astype(I32).reshape(1)
    col_index = lax.axis_index("cols").astype(I32).reshape(1)
    slots, heads = ssm_state.shape[0], ssm_state.shape[1]
    total, depth = tokens.shape
    moves = move_slot.shape[1]
    pages_here, width = page_table.shape[3], kv_pool.shape[3]
    inner = heads * HP
    stays = slots - moves
    cols, at = Columns(inner), Plan(slots, moves)
    table = page_table[0, 0]
    pool = kv_pool[:, 0]
    rows = row_count * BLOCK
    state_bytes = 2 * inner * NS
    page_bytes = 2 * pages_here * PAGE * width

    partial_sums, pages_send, state_send, plan = pl.pallas_call(
        project_kernel,
        out_shape=(
            shape((rows, cols.width), BF16),
            shape((row_count, pages_here, PAGE, width), BF16),
            shape((row_count, heads, HP, NS), BF16),
            shape((at.size,), I32),
        ),
        in_specs=[SMEM_SPEC] * 6 + [VMEM_SPEC] * 9 + [ANY_SPEC] * 2,
        out_specs=(VMEM_SPEC, ANY_SPEC, ANY_SPEC, SMEM_SPEC),
        scratch_shapes=[
            pltpu.SMEM((total,), I32),
            pltpu.SMEM((total,), I32),
            pltpu.SMEM((row_count,), I32),
            pltpu.VMEM((total, depth), F32),
            pltpu.VMEM((rows, depth), F32),
            pltpu.VMEM((row_count, BLOCK, inner), F32),
            pltpu.VMEM((row_count, BLOCK, 2 * NS), F32),
            pltpu.VMEM((rows, LANES), F32),
            pltpu.SemaphoreType.DMA((moves, pages_here + 1)),
        ],
        compiler_params=params(),
        cost_estimate=cost(2 * rows * depth * cols.width, 8e6),
        name="project",
    )(
        row_index, arrival, cache_lengths, move_slot, move_target, table,
        tokens, norm_gain.reshape(1, -1), conv_x, conv_bc,
        weight_z, weight_x, weight_dt, weight_bc, weight_qkv, pool, ssm_state,
    )
    received = exchange(partial_sums, "rows")
    pages_arrived = exchange(pages_send, "rows")
    state_arrived = exchange(state_send, "rows")

    (
        conv_x_next, conv_bc_next, state_partly, queries, kv_new, drive, decay, b_twice, c_out,
        readout, scale, base,
    ) = pl.pallas_call(
        functools.partial(mix_kernel, row_count=row_count, moves=moves, width=depth * row_count),
        out_shape=(
            shape(conv_x.shape, BF16),
            shape(conv_bc.shape, BF16),
            shape(ssm_state.shape, BF16),
            shape((BLOCK * QH, HD), F32),
            shape((BLOCK, 2 * KVH * HD), F32),
            shape((inner, 2 * BLOCK), BF16),
            shape((BLOCK, heads), F32),
            shape((2 * BLOCK, NS), F32),
            shape((BLOCK, NS), BF16),
            shape((BLOCK, inner), F32),
            shape((BLOCK, inner), F32),
            shape((BLOCK, inner), F32),
        ),
        in_specs=[SMEM_SPEC] + [VMEM_SPEC] * 8 + [ANY_SPEC],
        out_specs=(VMEM_SPEC, VMEM_SPEC, ANY_SPEC) + (VMEM_SPEC,) * 9,
        scratch_shapes=[
            pltpu.VMEM((KW - 1, BLOCK, inner), F32),
            pltpu.VMEM((KW - 1, BLOCK, 2 * NS), F32),
            pltpu.VMEM((stays, heads, HP, NS), BF16),
            pltpu.VMEM((stays, heads, HP, NS), BF16),
            pltpu.SemaphoreType.DMA((stays,)),
            pltpu.SemaphoreType.DMA((stays,)),
        ],
        compiler_params=params(),
        cost_estimate=cost(4 * stays * inner * NS * 32, 4 * stays * state_bytes),
        name="mix",
    )(
        plan, received, conv_x, conv_bc, conv_weight_x, conv_weight_bc,
        dt_bias.reshape(1, -1), a_log.reshape(1, -1), d_skip.reshape(1, -1), ssm_state,
    )

    share = QH * HD // col_count
    pool_next, partials_send = pl.pallas_call(
        functools.partial(attend_kernel, moves=moves, col_count=col_count),
        out_shape=(shape(pool.shape, BF16), shape((col_count * BLOCK, share + LANES), F32)),
        in_specs=[SMEM_SPEC] * 3 + [VMEM_SPEC] * 2 + [ANY_SPEC] * 2,
        out_specs=(ANY_SPEC, VMEM_SPEC),
        scratch_shapes=[
            pltpu.VMEM((slots, pages_here, PAGE, width), BF16),
            pltpu.VMEM((BLOCK * QH, pages_here * PAGE), F32),
            pltpu.VMEM((BLOCK * QH, HD), F32),
            pltpu.VMEM((BLOCK * QH, HD), F32),
            pltpu.VMEM((BLOCK * QH, HD), F32),
            pltpu.SemaphoreType.DMA((slots,)),
            pltpu.SemaphoreType.DMA((slots, pages_here)),
        ],
        compiler_params=params(),
        cost_estimate=cost(4 * slots * 16 * pages_here * PAGE * 256, 4 * slots * page_bytes),
        name="attend",
    )(col_index, plan, table, queries, kv_new, pool, pages_arrived)
    partials = exchange(partials_send, "cols")

    state_next, mixed_send = pl.pallas_call(
        functools.partial(output_kernel, slots=slots, moves=moves, col_count=col_count),
        out_shape=(
            shape(ssm_state.shape, BF16),
            shape((col_count * BLOCK, weight_ssm_out.shape[1] // col_count), F32),
        ),
        in_specs=[SMEM_SPEC] + [ANY_SPEC] * 2 + [VMEM_SPEC] * 10,
        out_specs=(ANY_SPEC, VMEM_SPEC),
        scratch_shapes=[
            pltpu.VMEM((BLOCK, inner), F32),
            pltpu.VMEM((moves, heads, HP, NS), BF16),
            pltpu.VMEM((moves, heads, HP, NS), BF16),
            pltpu.SemaphoreType.DMA((moves,)),
            pltpu.SemaphoreType.DMA((moves,)),
        ],
        input_output_aliases={2: 0},
        compiler_params=params(),
        cost_estimate=cost(2 * BLOCK * 768 * 2048, 4 * moves * state_bytes),
        name="output",
    )(
        plan, state_arrived, state_partly, drive, decay, b_twice, c_out, readout, scale, base,
        partials, weight_ssm_out, weight_attn_out,
    )
    mixed = pl.pallas_call(
        functools.partial(sum_kernel, col_count=col_count),
        out_shape=shape((slots, mixed_send.shape[1]), BF16),
        in_specs=[VMEM_SPEC],
        out_specs=VMEM_SPEC,
        name="total",
    )(exchange(mixed_send, "cols"))
    return (mixed, state_next, conv_x_next, conv_bc_next, pool_next[:, None])


def solution(mesh):
    in_specs = (
        P(None, "rows"),
        P(),
        P(),
        P(),
        P(),
        P("rows", "cols", None, None),
        P("rows", "cols", None, None),
        P("rows", "cols", None, None),
        P("rows", None, "cols"),
        P("rows", None, None),
        P("rows"),
        P("rows", "cols"),
        P("rows", "cols"),
        P("rows", "cols"),
        P("rows", None),
        P("rows", None),
        P(None, "cols"),
        P(),
        P("cols"),
        P("cols"),
        P("cols"),
        P("cols", None),
        P("cols", None),
    )
    out_specs = (
        P("rows", "cols"),
        P("rows", "cols", None, None),
        P("rows", None, "cols"),
        P("rows", None, None),
        P("rows", "cols", None, None),
    )
    return jax.shard_map(local, mesh=mesh, in_specs=in_specs, out_specs=out_specs, check_vma=False)
```

```python
import functools

import jax
import jax.numpy as jnp
from jax import lax
from jax.experimental import pallas as pl
from jax.experimental.pallas import tpu as pltpu
from jax.sharding import PartitionSpec as P

HP = 64
NS = 256
KW = 4
QH = 8
KVH = 2
HD = 128
PAGE = 32
LANES = 128
BLOCK = 16

EPSILON = 1e-05
FLOOR_SCORE = -1e30
VMEM_LIMIT = 60 * 1024 * 1024

F32 = jnp.float32
BF16 = jnp.bfloat16
I32 = jnp.int32

SMEM_SPEC = pl.BlockSpec(memory_space=pltpu.SMEM)
VMEM_SPEC = pl.BlockSpec(memory_space=pltpu.VMEM)
ANY_SPEC = pl.BlockSpec(memory_space=pl.ANY)


def silu(v):
    return v / (1.0 + jnp.exp(-v))


def dot(a, b):
    return jnp.dot(a, b, preferred_element_type=F32)


def dot_t(a, b):
    return lax.dot_general(a, b, (((1,), (1,)), ((), ())), preferred_element_type=F32)


def row_iota(shape):
    return lax.broadcasted_iota(I32, shape, 0)


def lane_iota(shape):
    return lax.broadcasted_iota(I32, shape, 1)


class Columns:
    def __init__(self, inner):
        self.z = 0
        self.x = inner
        self.bc = 2 * inner
        self.q = self.bc + 2 * NS
        self.kv = self.q + QH * HD
        self.tail = self.kv + 2 * KVH * HD
        self.width = self.tail + 2 * LANES


class Plan:
    def __init__(self, slots, moves):
        self.length = 0
        self.slot = slots
        self.target = self.slot + moves
        self.source = self.target + moves
        self.arrived_length = self.source + moves
        self.stay = self.arrived_length + moves
        self.size = self.stay + slots - moves


class Note:
    gated, key_value, drive, drive_low, mixing, conv_x, conv_bc, attended = 0, 1, 2, 3, 4, 5, 8, 11
    decay, decay_low = NS, NS + LANES


def project_kernel(
    row_ref, arrival, lengths, move_slot, move_target, table,
    tokens, gain, w_z, w_x, w_dt, w_bc, w_qkv, pool, state,
    out, plan, *rest,
    slots,
):
    moves, row_count = move_slot.shape
    pages_here = table.shape[0]
    heads, depth = w_dt.shape
    inner = heads * HP
    cols, at = Columns(inner), Plan(slots, moves)
    parcels = rest[: row_count - 1]
    inverse, wide, picked, tail, packed, in_sems, out_sems = rest[row_count - 1 :]
    me = row_ref[0]

    loads = []
    for m in range(moves):
        slot = move_slot[m, me]
        for page in range(pages_here):
            loads.append(
                pltpu.make_async_copy(pool.at[table[page, slot]], packed.at[m, page], in_sems.at[m, page])
            )
        for half in range(2):
            loads.append(
                pltpu.make_async_copy(
                    state.at[slot, :, half * PAGE : (half + 1) * PAGE, :],
                    packed.at[m, pages_here:, :, half * NS : (half + 1) * NS],
                    in_sems.at[m, pages_here + half],
                )
            )
    for load in loads:
        load.start()

    wide[...] = tokens[...].astype(F32)
    picked[...] = jnp.zeros_like(picked)

    def invert(t, carry):
        for s in range(slots):
            inverse[arrival[t * slots + s]] = t * slots + s
        return carry

    lax.fori_loop(0, row_count, invert, 0)

    def pick(t, carry):
        for s in range(slots):
            picked[pl.ds(t * BLOCK + s, 1), :] = wide[pl.ds(inverse[t * slots + s], 1), :]
        return carry

    lax.fori_loop(0, row_count, pick, 0)

    for load in loads:
        load.wait()
    for m in range(moves):
        away = lax.bitwise_xor(move_target[m, me], me)
        for d in range(1, row_count):

            @pl.when(away == d)
            def _(m=m, d=d):
                pltpu.make_async_copy(packed.at[m], parcels[d - 1], out_sems.at[m]).start()

    rows = picked[...]
    squares = jnp.sum(rows * rows, axis=1, keepdims=True)
    scaled = (rows * gain[...].astype(F32).reshape(1, depth)).astype(BF16)
    out[:, cols.z : cols.x] = dot(scaled, w_z[...]).astype(BF16)
    out[:, cols.x : cols.bc] = dot(scaled, w_x[...]).astype(BF16)
    out[:, cols.bc : cols.q] = dot(scaled, w_bc[...]).astype(BF16)
    out[:, cols.q : cols.tail] = dot(scaled, w_qkv[...]).astype(BF16)
    tail[...] = jnp.zeros_like(tail)
    tail[:, :heads] = dot_t(scaled, w_dt[...])
    tail[:, heads : heads + 1] = squares
    high = tail[...].astype(BF16)
    out[:, cols.tail : cols.tail + LANES] = high
    out[:, cols.tail + LANES :] = (tail[...] - high.astype(F32)).astype(BF16)

    stays = 0
    for s in range(slots):
        plan[at.length + s] = lengths[me * slots + s]
        leaves = move_slot[0, me] == s
        for m in range(1, moves):
            leaves = jnp.logical_or(leaves, move_slot[m, me] == s)

        @pl.when(jnp.logical_not(leaves))
        def _(s=s, stays=stays):
            plan[at.stay + stays] = s

        stays = stays + jnp.where(leaves, 0, 1)
    for m in range(moves):
        plan[at.slot + m] = move_slot[m, me]
        plan[at.target + m] = move_target[m, me]

    def seek(i, turn):
        for m in range(moves):
            comes = move_target[m, i] == me

            @pl.when(comes)
            def _(m=m, turn=turn):
                plan[at.source + turn] = i
                plan[at.arrived_length + turn] = lengths[i * slots + move_slot[m, i]]

            turn = turn + jnp.where(comes, 1, 0)
        return turn

    lax.fori_loop(0, row_count, seek, I32(0))
    for m in range(moves):
        pltpu.make_async_copy(packed.at[m], parcels[0], out_sems.at[m]).wait()


def widen(per_head, inner):
    rows = per_head.shape[0]
    first = lane_iota((rows, 2 * HP)) < HP
    pieces = []
    for h in range(0, inner // HP, 2):
        pieces.append(jnp.where(first, per_head[:, h : h + 1], per_head[:, h + 1 : h + 2]))
    return pieces[0] if len(pieces) == 1 else jnp.concatenate(pieces, axis=1)


class Sums:
    def __init__(self, received, heads, row_count, width):
        self.received, self.row_count = received, row_count
        cols = Columns(heads * HP)
        tail = self.total(cols.tail, cols.tail + LANES) + self.total(cols.tail + LANES, cols.width)
        self.root = jnp.sqrt(tail[:, heads : heads + 1] / width + EPSILON)
        self.step_in = (tail[:, :heads] / self.root).astype(BF16).astype(F32)

    def total(self, start, stop):
        result = self.received[0:BLOCK, start:stop].astype(F32)
        for i in range(1, self.row_count):
            result = result + self.received[i * BLOCK : (i + 1) * BLOCK, start:stop].astype(F32)
        return result

    def projected(self, start, stop):
        return (self.total(start, stop) / self.root).astype(BF16).astype(F32)


def insert_row(page, row, offset):
    old = page[...].astype(F32)
    page[...] = jnp.where(row_iota(old.shape) == offset, row, old).astype(BF16)


def place_of(length, col_count):
    logical = lax.div(length, I32(PAGE))
    return lax.rem(logical, I32(col_count)), lax.div(logical, I32(col_count)), lax.rem(length, I32(PAGE))


def attend_kernel(
    col_ref, plan, table, received, pool,
    pool_next, send, kv_new,
    pages, queries, scores, weighted, peaks, totals, in_sems, out_sems,
    *, moves, heads, row_count, col_count, width,
):
    pages_here, slots = table.shape
    cols, at = Columns(heads * HP), Plan(slots, moves)
    col = col_ref[0]
    tokens_here = pages_here * PAGE
    kv_width = KVH * HD
    loads = []
    for s in range(slots):
        for page in range(pages_here):
            loads.append(
                pltpu.make_async_copy(pool.at[table[page, s]], pages.at[s, page], in_sems.at[s, page])
            )
            loads[-1].start()

    sums = Sums(received, heads, row_count, width)
    kv_new[...] = sums.projected(cols.kv, cols.tail)
    q_in = sums.projected(cols.q, cols.kv)
    for h in range(QH):
        queries[pl.ds(h, BLOCK, stride=QH), :] = q_in[:, h * HD : (h + 1) * HD]

    first_group = row_iota((QH, HD)) < QH // KVH
    lane = lane_iota((QH, tokens_here))
    position = (lax.shift_right_logical(lane, 5) * col_count + col) * PAGE + lax.bitwise_and(lane, PAGE - 1)
    for s in range(slots):
        for load in loads[s * pages_here : (s + 1) * pages_here]:
            load.wait()
        length = plan[at.length + s]
        owner, local_page, offset = place_of(length, col_count)

        @pl.when(owner == col)
        def _(s=s, local_page=local_page, offset=offset):
            insert_row(pages.at[s, local_page], kv_new[s : s + 1, :], offset)

        keys = pages[s, :, :, :kv_width].reshape(tokens_here, kv_width)
        query = queries[s * QH : (s + 1) * QH, :]
        query = jnp.concatenate(
            [jnp.where(first_group, query, 0.0), jnp.where(first_group, 0.0, query)], axis=1
        ).astype(BF16)
        score = dot_t(query, keys) * (HD ** -0.5)
        scores[s * QH : (s + 1) * QH, :] = jnp.where(position <= length, score, FLOOR_SCORE)

    stores = []
    for j in range(slots - moves):
        slot = plan[at.stay + j]
        for page in range(pages_here):
            stores.append(
                pltpu.make_async_copy(
                    pages.at[slot, page], pool_next.at[table[page, slot]], out_sems.at[j, page]
                )
            )
            stores[-1].start()

    live_rows = slots * QH
    everything = scores[0:live_rows, :]
    peak = jnp.max(everything, axis=1, keepdims=True)
    weights = jnp.where(everything > 0.5 * FLOOR_SCORE, jnp.exp(everything - peak), 0.0)
    total = jnp.sum(weights, axis=1, keepdims=True)
    scores[0:live_rows, :] = weights
    for ref, value in ((weighted, None), (peaks, peak), (totals, total)):
        ref[live_rows:, :] = jnp.zeros((BLOCK * QH - live_rows, HD), F32)
        if value is not None:
            ref[0:live_rows, :] = jnp.broadcast_to(value, (live_rows, HD))
    for s in range(slots):
        values = pages[s, :, :, kv_width:].reshape(tokens_here, kv_width)
        weight = scores[s * QH : (s + 1) * QH, :]
        high = weight.astype(BF16).astype(F32)
        both = dot(jnp.concatenate([high, weight - high], axis=0).astype(BF16), values)
        joined = both[:QH] + both[QH:]
        weighted[s * QH : (s + 1) * QH, :] = jnp.where(first_group, joined[:, :HD], joined[:, HD:])

    share = QH * HD // col_count
    part = min(share, HD)
    lanes = lane_iota((BLOCK, LANES))
    for c in range(col_count):
        stats = jnp.zeros((BLOCK, LANES), F32)
        for j in range(share // part):
            head = (c * share + j * part) // HD
            begin = (c * share + j * part) % HD
            rows = pl.ds(head, BLOCK, stride=QH)
            send[c * BLOCK : (c + 1) * BLOCK, j * part : (j + 1) * part] = weighted[rows, :][
                :, begin : begin + part
            ]
            stats = jnp.where(lanes == 2 * j, peaks[rows, :], stats)
            stats = jnp.where(lanes == 2 * j + 1, totals[rows, :], stats)
        send[c * BLOCK : (c + 1) * BLOCK, share:] = stats
    for store in stores:
        store.wait()


def mix_kernel(
    plan, received, conv_x, conv_bc, cw_x, cw_bc, dt_bias, a_log, d_skip, state,
    conv_x_next, conv_bc_next, state_next, gated, driven_out, decay, b_out,
    readout, held, made, drive, b_twice, in_sems, out_sems,
    *, moves, row_count, width,
):
    slots, inner = conv_x.shape[1], conv_x.shape[2]
    heads = dt_bias.shape[0]
    cols, at = Columns(inner), Plan(slots, moves)
    loads = []
    for s in range(slots):
        loads.append(pltpu.make_async_copy(state.at[s], held.at[s], in_sems.at[s]))
        loads[-1].start()

    sums = Sums(received, heads, row_count, width)

    def convolved(past, taps, fresh, following):
        past_rows = [past[k].astype(F32) for k in range(KW - 1)]
        total = fresh[:slots] * taps[KW - 1 : KW, :].astype(F32)
        for k in range(KW - 1):
            total = total + past_rows[k] * taps[k : k + 1, :].astype(F32)
            following[k] = past_rows[k + 1] if k < KW - 2 else fresh[:slots]
        return jnp.concatenate([silu(total), jnp.zeros((BLOCK - slots, total.shape[1]), F32)], axis=0)

    value_act = convolved(conv_x, cw_x, sums.projected(cols.x, cols.bc), conv_x_next)
    bc_act = convolved(conv_bc, cw_bc, sums.projected(cols.bc, cols.q), conv_bc_next)
    bc_act = bc_act.astype(BF16).astype(F32)
    b_in, c_val = bc_act[:, :NS], bc_act[:, NS:]
    b_out[...] = b_in
    b_twice[...] = jnp.concatenate([b_in, b_in], axis=0)
    c_out = c_val.astype(BF16)

    shifted = sums.step_in + dt_bias[...].reshape(1, heads)
    step_size = jnp.maximum(shifted, 0.0) + jnp.log(1.0 + jnp.exp(-jnp.abs(shifted)))
    rate = jnp.exp(-jnp.exp(a_log[...].reshape(1, heads)) * step_size)
    decay[...] = rate
    driven = widen(step_size, inner) * value_act
    driven_out[...] = driven
    high = driven.astype(BF16).astype(F32)
    drive[...] = jnp.transpose(jnp.concatenate([high, driven - high], axis=0)).astype(BF16)

    readout[...] = jnp.zeros_like(readout)

    def read(s, carry):
        pltpu.make_async_copy(state.at[s], held.at[s], in_sems.at[s]).wait()
        value = dot_t(c_out, held[s].reshape(inner, NS))
        readout[...] = jnp.where(row_iota(value.shape) == s, value, readout[...])
        return carry

    for s in range(slots):
        read(s, 0)

    stores = []
    for j in range(slots - moves):
        slot = plan[at.stay + j]
        advance_state(slot, held.at[slot], b_twice, drive, decay, made.at[j])
        stores.append(pltpu.make_async_copy(made.at[j], state_next.at[slot], out_sems.at[j]))
        stores[-1].start()

    gate = silu(sums.projected(cols.z, cols.x))
    b_dot_c = jnp.sum(b_in * c_val, axis=1, keepdims=True)
    skip = widen(jnp.broadcast_to(d_skip[...].reshape(1, heads), (BLOCK, heads)), inner)
    total = widen(rate, inner) * readout[...] + driven * b_dot_c + skip * value_act
    gated[...] = (total * gate).astype(BF16).astype(F32)
    for store in stores:
        store.wait()


def advance_state(slot, prior, b_twice, drive, decay, result):
    heads = result.shape[0]
    twice = b_twice[...]
    half = twice.shape[0] // 2
    row = row_iota(twice.shape)
    selected = jnp.where((row == slot) | (row == slot + half), twice, 0.0).astype(BF16)
    outer = dot(drive[...], selected).reshape(heads, HP, NS)
    for h in range(heads):
        rate = decay[pl.ds(slot, 1), h : h + 1]
        result[h] = (rate * prior[h].astype(F32) + outer[h]).astype(BF16)


def merge_kernel(
    plan, partials, gated, kv_new, driven, decay, b_in, conv_x, conv_bc,
    attended, send,
    block, attended_wide,
    *, moves, row_count, col_count,
):
    slots, inner = conv_x.shape[1], conv_x.shape[2]
    heads, share = decay.shape[1], attended.shape[1]
    at = Plan(slots, moves)
    part = min(share, HD)
    pieces = []
    for j in range(share // part):
        blocks = [partials[c * BLOCK : (c + 1) * BLOCK, :] for c in range(col_count)]
        peaks = [b[:, share + 2 * j : share + 2 * j + 1] for b in blocks]
        joint = functools.reduce(jnp.maximum, peaks)
        factors = [jnp.exp(p - joint) for p in peaks]
        total = sum(f * b[:, share + 2 * j + 1 : share + 2 * j + 2] for f, b in zip(factors, blocks))
        value = sum(f * b[:, j * part : (j + 1) * part] for f, b in zip(factors, blocks))
        pieces.append(value / total)
    joined = pieces[0] if len(pieces) == 1 else jnp.concatenate(pieces, axis=1)
    joined = jnp.where(row_iota(joined.shape) < slots, joined, 0.0).astype(BF16)
    attended[...] = joined.astype(F32)

    block[...] = jnp.zeros_like(block)
    for m in range(moves):
        slot = plan[at.slot + m]
        row = pl.ds(slot, 1)

        def put(index, value, start=0):
            block[index : index + 1, start : start + value.shape[1]] = value

        put(Note.gated, gated[row, :])
        put(Note.key_value, kv_new[row, :])
        for index, value, start, low_index, low_start in (
            (Note.drive, driven[row, :], 0, Note.drive_low, 0),
            (Note.mixing, decay[row, :], Note.decay, Note.mixing, Note.decay_low),
        ):
            high = value.astype(BF16).astype(F32)
            put(index, high, start)
            put(low_index, value - high, low_start)
        put(Note.mixing, b_in[row, :])
        for k in range(KW - 1):
            put(Note.conv_x + k, conv_x[k, row, :])
            put(Note.conv_bc + k, conv_bc[k, row, :])
        put(Note.attended, attended[row, :])
        start = pl.multiple_of(plan[at.target + m] * BLOCK, BLOCK)
        send[pl.ds(start, BLOCK), :] = block[...].astype(BF16)


def output_kernel(plan, gated, attended, notes, w_ssm, w_attn, send, gated_here, attended_here, *, slots, moves, col_count):
    at = Plan(slots, moves)
    inner, share = gated.shape[1], attended.shape[1]
    gated_here[...] = gated[...]
    attended_here[...] = attended[...]
    for m in range(moves):
        start = pl.multiple_of(plan[at.source + m] * BLOCK, BLOCK)
        note = notes[pl.ds(start, BLOCK), :].astype(F32)
        row = pl.ds(plan[at.slot + m], 1)
        gated_here[row, :] = note[Note.gated : Note.gated + 1, :inner]
        attended_here[row, :] = note[Note.attended : Note.attended + 1, :share]
    columns = w_ssm.shape[1] // col_count
    left, right = gated_here[...].astype(BF16), attended_here[...].astype(BF16)
    for c in range(col_count):
        span = slice(c * columns, (c + 1) * columns)
        send[c * BLOCK : (c + 1) * BLOCK, :] = dot(left, w_ssm[:, span]) + dot(right, w_attn[:, span])


def sum_kernel(received, out, *, col_count):
    total = received[0:BLOCK, :]
    for c in range(1, col_count):
        total = total + received[c * BLOCK : (c + 1) * BLOCK, :]
    out[...] = total[: out.shape[0]].astype(BF16)


def arrive_kernel(
    row_ref, col_ref, plan, table, notes, conv_x, conv_bc, state_in, pool_in, *rest, moves, row_count, col_count
):
    del state_in, pool_in
    pages_here, slots = table.shape
    inner = conv_x.shape[2]
    heads = inner // HP
    at = Plan(slots, moves)
    parcels = rest[: row_count - 1]
    conv_x_next, conv_bc_next, state_next, pool_next = rest[row_count - 1 : row_count + 3]
    packed, made, drive, decay, b_twice, window_x, window_bc, in_sems, out_sems = rest[row_count + 3 :]
    me, col = row_ref[0], col_ref[0]
    for m in range(moves):
        away = lax.bitwise_xor(plan[at.source + m], me)
        for d in range(1, row_count):

            @pl.when(away == d)
            def _(m=m, d=d):
                pltpu.make_async_copy(parcels[d - 1], packed.at[m], in_sems.at[m]).start()

    for k in range(KW - 1):
        window_x[k] = conv_x[k]
        window_bc[k] = conv_bc[k]
    rows = []
    b_twice[...] = jnp.zeros_like(b_twice)
    half = b_twice.shape[0] // 2
    for m in range(moves):
        start = pl.multiple_of(plan[at.source + m] * BLOCK, BLOCK)
        note = notes[pl.ds(start, BLOCK), :].astype(F32)
        rows.append(note)
        row = pl.ds(plan[at.slot + m], 1)
        for k in range(KW - 1):
            window_x[k, row, :] = note[Note.conv_x + k : Note.conv_x + k + 1, :inner]
            window_bc[k, row, :] = note[Note.conv_bc + k : Note.conv_bc + k + 1, : 2 * NS]
        mixing = note[Note.mixing : Note.mixing + 1, :]
        b_twice[m : m + 1, :] = mixing[:, :NS]
        b_twice[half + m : half + m + 1, :] = mixing[:, :NS]
        decay[m : m + 1, :] = (
            mixing[:, Note.decay : Note.decay + heads] + mixing[:, Note.decay_low : Note.decay_low + heads]
        )
    padding = [jnp.zeros((half - moves, inner), F32)]
    stacked = [note[Note.drive : Note.drive + 1, :inner] for note in rows] + padding
    stacked += [note[Note.drive_low : Note.drive_low + 1, :inner] for note in rows] + padding
    drive[...] = jnp.transpose(jnp.concatenate(stacked, axis=0)).astype(BF16)
    for k in range(KW - 1):
        conv_x_next[k] = window_x[k].astype(BF16)
        conv_bc_next[k] = window_bc[k].astype(BF16)

    stores = []
    for m in range(moves):
        slot = plan[at.slot + m]
        pltpu.make_async_copy(parcels[0], packed.at[m], in_sems.at[m]).wait()
        owner, local_page, offset = place_of(plan[at.arrived_length + m], col_count)
        key_value = rows[m][Note.key_value : Note.key_value + 1, : 2 * KVH * HD]

        @pl.when(owner == col)
        def _(m=m, local_page=local_page, offset=offset, key_value=key_value):
            insert_row(packed.at[m, local_page], key_value, offset)

        for page in range(pages_here):
            stores.append(
                pltpu.make_async_copy(
                    packed.at[m, page], pool_next.at[table[page, slot]], out_sems.at[m, page]
                )
            )
            stores[-1].start()
        prior = [
            jnp.concatenate([packed[m, pages_here + h, :, :NS], packed[m, pages_here + h, :, NS:]], axis=0)
            for h in range(heads)
        ]
        advance_state(m, prior, b_twice, drive, decay, made.at[m])
        stores.append(pltpu.make_async_copy(made.at[m], state_next.at[slot], out_sems.at[m, pages_here]))
        stores[-1].start()
    for store in stores:
        store.wait()


def shape(dims, dtype):
    return jax.ShapeDtypeStruct(tuple(dims), dtype)


def params():
    return pltpu.CompilerParams(vmem_limit_bytes=VMEM_LIMIT)


def cost(flops, moved):
    return pl.CostEstimate(flops=int(flops), bytes_accessed=int(moved), transcendentals=0)


def exchange(value, axis):
    return lax.all_to_all(value, axis, split_axis=0, concat_axis=0, tiled=True)


def local(
    tokens, arrival, cache_lengths, move_slot, move_target, page_table, kv_pool, ssm_state,
    conv_x, conv_bc, norm_gain, weight_z, weight_x, weight_dt, weight_bc, weight_qkv,
    conv_weight_x, conv_weight_bc, dt_bias, a_log, d_skip, weight_ssm_out, weight_attn_out,
):
    row_count = lax.axis_size("rows")
    col_count = lax.axis_size("cols")
    row_index = lax.axis_index("rows").astype(I32).reshape(1)
    col_index = lax.axis_index("cols").astype(I32).reshape(1)
    slots, heads = ssm_state.shape[0], ssm_state.shape[1]
    total, depth = tokens.shape
    moves = move_slot.shape[1]
    pages_here, width = page_table.shape[3], kv_pool.shape[3]
    inner = heads * HP
    stays = slots - moves
    cols, at = Columns(inner), Plan(slots, moves)
    table = page_table[0, 0].T
    pool = kv_pool[:, 0]
    past_x, past_bc = conv_x.transpose(1, 0, 2), conv_bc.transpose(1, 0, 2)
    rows = row_count * BLOCK
    model = depth * row_count
    share = QH * HD // col_count
    state_bytes = 2 * inner * NS
    page_bytes = 2 * pages_here * PAGE * width
    parcel = shape((pages_here + heads, PAGE, width), BF16)
    parcels_here = pltpu.VMEM((moves,) + parcel.shape, BF16)

    partial_sums, plan, *parcels = pl.pallas_call(
        functools.partial(project_kernel, slots=slots),
        out_shape=[shape((rows, cols.width), BF16), shape((at.size,), I32)] + [parcel] * (row_count - 1),
        in_specs=[SMEM_SPEC] * 6 + [VMEM_SPEC] * 7 + [ANY_SPEC] * 2,
        out_specs=[VMEM_SPEC, SMEM_SPEC] + [ANY_SPEC] * (row_count - 1),
        scratch_shapes=[
            pltpu.SMEM((total,), I32),
            pltpu.VMEM((total, depth), F32),
            pltpu.VMEM((rows, depth), F32),
            pltpu.VMEM((rows, LANES), F32),
            parcels_here,
            pltpu.SemaphoreType.DMA((moves, pages_here + 2)),
            pltpu.SemaphoreType.DMA((moves,)),
        ],
        compiler_params=params(),
        cost_estimate=cost(2 * rows * depth * cols.width, 8e6),
        name="project",
    )(
        row_index, arrival, cache_lengths, move_slot.T, move_target.T, table,
        tokens, norm_gain, weight_z, weight_x, weight_dt.T, weight_bc, weight_qkv, pool, ssm_state,
    )
    received = exchange(partial_sums, "rows")
    parcels = [
        lax.ppermute(sent, "rows", [(i, i ^ (d + 1)) for i in range(row_count)])
        for d, sent in enumerate(parcels)
    ]

    pool_next, partials_send, kv_new = pl.pallas_call(
        functools.partial(
            attend_kernel, moves=moves, heads=heads, row_count=row_count, col_count=col_count, width=model
        ),
        out_shape=(
            shape(pool.shape, BF16),
            shape((col_count * BLOCK, share + LANES), F32),
            shape((BLOCK, 2 * KVH * HD), F32),
        ),
        in_specs=[SMEM_SPEC] * 3 + [VMEM_SPEC, ANY_SPEC],
        out_specs=(ANY_SPEC, VMEM_SPEC, VMEM_SPEC),
        scratch_shapes=[
            pltpu.VMEM((slots, pages_here, PAGE, width), BF16),
            pltpu.VMEM((BLOCK * QH, HD), F32),
            pltpu.VMEM((BLOCK * QH, pages_here * PAGE), F32),
            pltpu.VMEM((BLOCK * QH, HD), F32),
            pltpu.VMEM((BLOCK * QH, HD), F32),
            pltpu.VMEM((BLOCK * QH, HD), F32),
            pltpu.SemaphoreType.DMA((slots, pages_here)),
            pltpu.SemaphoreType.DMA((stays, pages_here)),
        ],
        compiler_params=params(),
        cost_estimate=cost(4 * slots * 16 * pages_here * PAGE * 256, 4 * slots * page_bytes),
        name="attend",
    )(col_index, plan, table, received, pool)
    partials = exchange(partials_send, "cols")

    next_x, next_bc, state_next, gated, driven, decay, b_in = pl.pallas_call(
        functools.partial(mix_kernel, moves=moves, row_count=row_count, width=model),
        out_shape=(
            shape(past_x.shape, F32),
            shape(past_bc.shape, F32),
            shape(ssm_state.shape, BF16),
            shape((BLOCK, inner), F32),
            shape((BLOCK, inner), F32),
            shape((BLOCK, heads), F32),
            shape((BLOCK, NS), F32),
        ),
        in_specs=[SMEM_SPEC] + [VMEM_SPEC] * 8 + [ANY_SPEC],
        out_specs=(VMEM_SPEC, VMEM_SPEC, ANY_SPEC) + (VMEM_SPEC,) * 4,
        scratch_shapes=[
            pltpu.VMEM((BLOCK, inner), F32),
            pltpu.VMEM((slots, heads, HP, NS), BF16),
            pltpu.VMEM((stays, heads, HP, NS), BF16),
            pltpu.VMEM((inner, 2 * BLOCK), BF16),
            pltpu.VMEM((2 * BLOCK, NS), F32),
            pltpu.SemaphoreType.DMA((slots,)),
            pltpu.SemaphoreType.DMA((stays,)),
        ],
        compiler_params=params(),
        cost_estimate=cost(4 * slots * inner * NS * 32, 4 * slots * state_bytes),
        name="mix",
    )(plan, received, past_x, past_bc, conv_weight_x, conv_weight_bc, dt_bias, a_log, d_skip, ssm_state)

    note_width = max(inner, 2 * NS, 2 * KVH * HD, share)
    attended, notes_send = pl.pallas_call(
        functools.partial(merge_kernel, moves=moves, row_count=row_count, col_count=col_count),
        out_shape=(shape((BLOCK, share), F32), shape((rows, note_width), BF16)),
        in_specs=[SMEM_SPEC] + [VMEM_SPEC] * 8,
        out_specs=(VMEM_SPEC, VMEM_SPEC),
        scratch_shapes=[pltpu.VMEM((BLOCK, note_width), F32), pltpu.VMEM((BLOCK, share), F32)],
        compiler_params=params(),
        cost_estimate=cost(1e6, 1e6),
        name="merge",
    )(plan, partials, gated, kv_new, driven, decay, b_in, next_x, next_bc)
    notes = exchange(notes_send, "rows")

    mixed_send = pl.pallas_call(
        functools.partial(output_kernel, slots=slots, moves=moves, col_count=col_count),
        out_shape=shape((col_count * BLOCK, weight_ssm_out.shape[1] // col_count), F32),
        in_specs=[SMEM_SPEC] + [VMEM_SPEC] * 5,
        out_specs=VMEM_SPEC,
        scratch_shapes=[pltpu.VMEM((BLOCK, inner), F32), pltpu.VMEM((BLOCK, share), F32)],
        compiler_params=params(),
        cost_estimate=cost(2 * BLOCK * (inner + share) * weight_ssm_out.shape[1], 4e6),
        name="output",
    )(plan, gated, attended, notes, weight_ssm_out, weight_attn_out)
    mixed_parts = exchange(mixed_send, "cols")

    conv_x_next, conv_bc_next, state_next, pool_next = pl.pallas_call(
        functools.partial(arrive_kernel, moves=moves, row_count=row_count, col_count=col_count),
        out_shape=(
            shape(past_x.shape, BF16),
            shape(past_bc.shape, BF16),
            shape(ssm_state.shape, BF16),
            shape(pool.shape, BF16),
        ),
        in_specs=[SMEM_SPEC] * 4 + [VMEM_SPEC] * 3 + [ANY_SPEC] * (row_count + 1),
        out_specs=(VMEM_SPEC, VMEM_SPEC, ANY_SPEC, ANY_SPEC),
        scratch_shapes=[
            parcels_here,
            pltpu.VMEM((moves, heads, HP, NS), BF16),
            pltpu.VMEM((inner, 2 * BLOCK), BF16),
            pltpu.VMEM((BLOCK, heads), F32),
            pltpu.VMEM((2 * BLOCK, NS), F32),
            pltpu.VMEM((KW - 1, slots, inner), F32),
            pltpu.VMEM((KW - 1, slots, 2 * NS), F32),
            pltpu.SemaphoreType.DMA((moves,)),
            pltpu.SemaphoreType.DMA((moves, pages_here + 1)),
        ],
        input_output_aliases={7: 2, 8: 3},
        compiler_params=params(),
        cost_estimate=cost(1e6, 4 * moves * (state_bytes + page_bytes)),
        name="arrive",
    )(row_index, col_index, plan, table, notes, next_x, next_bc, state_next, pool_next, *parcels)

    mixed = pl.pallas_call(
        functools.partial(sum_kernel, col_count=col_count),
        out_shape=shape((slots, mixed_send.shape[1]), BF16),
        in_specs=[VMEM_SPEC],
        out_specs=VMEM_SPEC,
        compiler_params=params(),
        name="total",
    )(mixed_parts)
    return (
        mixed, state_next, conv_x_next.transpose(1, 0, 2), conv_bc_next.transpose(1, 0, 2), pool_next[:, None]
    )


def solution(mesh):
    in_specs = (
        P(None, "rows"),
        P(),
        P(),
        P(),
        P(),
        P("rows", "cols", None, None),
        P("rows", "cols", None, None),
        P("rows", "cols", None, None),
        P("rows", None, "cols"),
        P("rows", None, None),
        P("rows"),
        P("rows", "cols"),
        P("rows", "cols"),
        P("rows", "cols"),
        P("rows", None),
        P("rows", None),
        P(None, "cols"),
        P(),
        P("cols"),
        P("cols"),
        P("cols"),
        P("cols", None),
        P("cols", None),
    )
    out_specs = (
        P("rows", "cols"),
        P("rows", "cols", None, None),
        P("rows", None, "cols"),
        P("rows", None, None),
        P("rows", "cols", None, None),
    )
    return jax.shard_map(local, mesh=mesh, in_specs=in_specs, out_specs=out_specs, check_vma=False)
```

```python
import functools

import jax
import jax.numpy as jnp
from jax import lax
from jax.experimental import pallas as pl
from jax.experimental.pallas import tpu as pltpu
from jax.sharding import PartitionSpec as P

HP = 64
NS = 256
KW = 4
QH = 8
KVH = 2
HD = 128
PAGE = 32
LANES = 128
BLOCK = 16

EPSILON = 1e-05
FLOOR_SCORE = -1e30
VMEM_LIMIT = 60 * 1024 * 1024

F32 = jnp.float32
BF16 = jnp.bfloat16
I32 = jnp.int32

SMEM_SPEC = pl.BlockSpec(memory_space=pltpu.SMEM)
VMEM_SPEC = pl.BlockSpec(memory_space=pltpu.VMEM)
ANY_SPEC = pl.BlockSpec(memory_space=pl.ANY)


def silu(v):
    return v / (1.0 + jnp.exp(-v))


def dot(a, b):
    return jnp.dot(a, b, preferred_element_type=F32)


def dot_t(a, b):
    return lax.dot_general(a, b, (((1,), (1,)), ((), ())), preferred_element_type=F32)


def row_iota(shape):
    return lax.broadcasted_iota(I32, shape, 0)


def lane_iota(shape):
    return lax.broadcasted_iota(I32, shape, 1)


class Columns:
    def __init__(self, inner):
        self.z = 0
        self.x = inner
        self.bc = 2 * inner
        self.q = self.bc + 2 * NS
        self.kv = self.q + QH * HD
        self.tail = self.kv + 2 * KVH * HD
        self.width = self.tail + 2 * LANES


class Plan:
    def __init__(self, slots, moves):
        self.length = 0
        self.slot = slots
        self.away = self.slot + moves
        self.source = self.away + moves
        self.from_away = self.source + moves
        self.arrived_length = self.from_away + moves
        self.stay = self.arrived_length + moves
        self.size = self.stay + slots - moves


class Note:
    gated, key_value, drive, drive_low, mixing, conv_x, conv_bc, attended = 0, 1, 2, 3, 4, 5, 8, 11
    decay, decay_low = NS, NS + LANES


def project_kernel(
    row_ref, arrival, lengths, move_slot, move_target, table,
    tokens, gain, w_z, w_x, w_dt, w_bc, w_qkv, pool, state,
    parcels, plan, *rest,
    slots,
):
    moves, row_count = move_slot.shape
    pages_here = table.shape[0]
    heads, depth = w_dt.shape
    inner = heads * HP
    cols, at = Columns(inner), Plan(slots, moves)
    outs = rest[:row_count]
    inverse, wide, picked, tail, packed, in_sems, out_sems = rest[row_count:]
    me = row_ref[0]

    loads = []
    for m in range(moves):
        slot = move_slot[m, me]
        for page in range(pages_here):
            loads.append(
                pltpu.make_async_copy(pool.at[table[page, slot]], packed.at[m, page], in_sems.at[m, page])
            )
        for half in range(2):
            loads.append(
                pltpu.make_async_copy(
                    state.at[slot, :, half * PAGE : (half + 1) * PAGE, :],
                    packed.at[m, pages_here:, :, half * NS : (half + 1) * NS],
                    in_sems.at[m, pages_here + half],
                )
            )
    for load in loads:
        load.start()

    wide[...] = tokens[...].astype(F32)
    picked[...] = jnp.zeros_like(picked)

    def invert(t, carry):
        for s in range(slots):
            inverse[arrival[t * slots + s]] = t * slots + s
        return carry

    lax.fori_loop(0, row_count, invert, 0)

    def pick(d, carry):
        first = lax.bitwise_xor(me, d) * slots
        for s in range(slots):
            picked[pl.ds(d * BLOCK + s, 1), :] = wide[pl.ds(inverse[first + s], 1), :]
        return carry

    lax.fori_loop(0, row_count, pick, 0)

    for load in loads:
        load.wait()
    stores = [
        pltpu.make_async_copy(packed.at[m], parcels.at[move_target[m, me]], out_sems.at[m])
        for m in range(moves)
    ]
    for store in stores:
        store.start()

    rows = picked[...]
    squares = jnp.sum(rows * rows, axis=1, keepdims=True)
    scaled = (rows * gain[...].astype(F32).reshape(1, depth)).astype(BF16)

    def put(start, value):
        value = value.astype(BF16)
        for d, out in enumerate(outs):
            out[:, start : start + value.shape[1]] = value[d * BLOCK : (d + 1) * BLOCK]

    put(cols.z, dot(scaled, w_z[...]))
    put(cols.x, dot(scaled, w_x[...]))
    put(cols.bc, dot(scaled, w_bc[...]))
    put(cols.q, dot(scaled, w_qkv[...]))
    tail[...] = jnp.zeros_like(tail)
    tail[:, :heads] = dot_t(scaled, w_dt[...])
    tail[:, heads : heads + 1] = squares
    high = tail[...].astype(BF16)
    put(cols.tail, high)
    put(cols.tail + LANES, tail[...] - high.astype(F32))

    stays = 0
    for s in range(slots):
        plan[at.length + s] = lengths[me * slots + s]
        leaves = move_slot[0, me] == s
        for m in range(1, moves):
            leaves = jnp.logical_or(leaves, move_slot[m, me] == s)

        @pl.when(jnp.logical_not(leaves))
        def _(s=s, stays=stays):
            plan[at.stay + stays] = s

        stays = stays + jnp.where(leaves, 0, 1)
    for m in range(moves):
        plan[at.slot + m] = move_slot[m, me]
        plan[at.away + m] = lax.bitwise_xor(move_target[m, me], me)

    def seek(i, turn):
        for m in range(moves):
            comes = move_target[m, i] == me

            @pl.when(comes)
            def _(m=m, turn=turn):
                plan[at.source + turn] = i
                plan[at.from_away + turn] = lax.bitwise_xor(i, me)
                plan[at.arrived_length + turn] = lengths[i * slots + move_slot[m, i]]

            turn = turn + jnp.where(comes, 1, 0)
        return turn

    lax.fori_loop(0, row_count, seek, I32(0))
    for store in stores:
        store.wait()


def widen(per_head, inner):
    rows = per_head.shape[0]
    first = lane_iota((rows, 2 * HP)) < HP
    pieces = []
    for h in range(0, inner // HP, 2):
        pieces.append(jnp.where(first, per_head[:, h : h + 1], per_head[:, h + 1 : h + 2]))
    return pieces[0] if len(pieces) == 1 else jnp.concatenate(pieces, axis=1)


class Sums:
    def __init__(self, received, heads, width):
        self.received = received
        cols = Columns(heads * HP)
        tail = self.total(cols.tail, cols.tail + LANES) + self.total(cols.tail + LANES, cols.width)
        self.root = jnp.sqrt(tail[:, heads : heads + 1] / width + EPSILON)
        self.step_in = (tail[:, :heads] / self.root).astype(BF16).astype(F32)

    def total(self, start, stop):
        return sum(part[:, start:stop].astype(F32) for part in self.received)

    def projected(self, start, stop):
        return (self.total(start, stop) / self.root).astype(BF16).astype(F32)


def insert_row(page, row, offset):
    old = page[...].astype(F32)
    page[...] = jnp.where(row_iota(old.shape) == offset, row, old).astype(BF16)


def place_of(length, col_count):
    logical = lax.div(length, I32(PAGE))
    return lax.rem(logical, I32(col_count)), lax.div(logical, I32(col_count)), lax.rem(length, I32(PAGE))


def attend_kernel(
    col_ref, plan, table, pool, *rest, moves, heads, row_count, col_count, width
):
    received = rest[:row_count]
    pool_next, kv_new = rest[row_count : row_count + 2]
    sends = rest[row_count + 2 : row_count + 2 + col_count]
    pages, queries, scores, weighted, peaks, totals, in_sems, out_sems = rest[row_count + 2 + col_count :]
    pages_here, slots = table.shape
    cols, at = Columns(heads * HP), Plan(slots, moves)
    col = col_ref[0]
    tokens_here = pages_here * PAGE
    kv_width = KVH * HD
    loads = []
    for s in range(slots):
        for page in range(pages_here):
            loads.append(
                pltpu.make_async_copy(pool.at[table[page, s]], pages.at[s, page], in_sems.at[s, page])
            )
            loads[-1].start()

    sums = Sums(received, heads, width)
    kv_new[...] = sums.projected(cols.kv, cols.tail)
    q_in = sums.projected(cols.q, cols.kv)
    for h in range(QH):
        queries[pl.ds(h, BLOCK, stride=QH), :] = q_in[:, h * HD : (h + 1) * HD]

    first_group = row_iota((QH, HD)) < QH // KVH
    lane = lane_iota((QH, tokens_here))
    position = (lax.shift_right_logical(lane, 5) * col_count + col) * PAGE + lax.bitwise_and(lane, PAGE - 1)
    for s in range(slots):
        for load in loads[s * pages_here : (s + 1) * pages_here]:
            load.wait()
        length = plan[at.length + s]
        owner, local_page, offset = place_of(length, col_count)

        @pl.when(owner == col)
        def _(s=s, local_page=local_page, offset=offset):
            insert_row(pages.at[s, local_page], kv_new[s : s + 1, :], offset)

        keys = pages[s, :, :, :kv_width].reshape(tokens_here, kv_width)
        query = queries[s * QH : (s + 1) * QH, :]
        query = jnp.concatenate(
            [jnp.where(first_group, query, 0.0), jnp.where(first_group, 0.0, query)], axis=1
        ).astype(BF16)
        score = dot_t(query, keys) * (HD ** -0.5)
        scores[s * QH : (s + 1) * QH, :] = jnp.where(position <= length, score, FLOOR_SCORE)

    stores = []
    for j in range(slots - moves):
        slot = plan[at.stay + j]
        for page in range(pages_here):
            stores.append(
                pltpu.make_async_copy(
                    pages.at[slot, page], pool_next.at[table[page, slot]], out_sems.at[j, page]
                )
            )
            stores[-1].start()

    live_rows = slots * QH
    everything = scores[0:live_rows, :]
    peak = jnp.max(everything, axis=1, keepdims=True)
    weights = jnp.where(everything > 0.5 * FLOOR_SCORE, jnp.exp(everything - peak), 0.0)
    total = jnp.sum(weights, axis=1, keepdims=True)
    scores[0:live_rows, :] = weights
    for ref, value in ((weighted, None), (peaks, peak), (totals, total)):
        ref[live_rows:, :] = jnp.zeros((BLOCK * QH - live_rows, HD), F32)
        if value is not None:
            ref[0:live_rows, :] = jnp.broadcast_to(value, (live_rows, HD))
    for s in range(slots):
        values = pages[s, :, :, kv_width:].reshape(tokens_here, kv_width)
        weight = scores[s * QH : (s + 1) * QH, :]
        high = weight.astype(BF16).astype(F32)
        both = dot(jnp.concatenate([high, weight - high], axis=0).astype(BF16), values)
        joined = both[:QH] + both[QH:]
        weighted[s * QH : (s + 1) * QH, :] = jnp.where(first_group, joined[:, :HD], joined[:, HD:])

    share = QH * HD // col_count
    part = min(share, HD)
    lanes = lane_iota((BLOCK, LANES))
    for d, send in enumerate(sends):
        first = lax.bitwise_xor(col, d) * share
        stats = jnp.zeros((BLOCK, LANES), F32)
        for j in range(share // part):
            rows = pl.ds(lax.div(first + j * part, I32(HD)), BLOCK, stride=QH)
            whole = weighted[rows, :]
            piece = whole[:, :part]
            for begin in range(part, HD, part):
                piece = jnp.where(lax.rem(first, I32(HD)) == begin, whole[:, begin : begin + part], piece)
            send[:, j * part : (j + 1) * part] = piece
            stats = jnp.where(lanes == 2 * j, peaks[rows, :], stats)
            stats = jnp.where(lanes == 2 * j + 1, totals[rows, :], stats)
        send[:, share:] = stats
    for store in stores:
        store.wait()


def mix_kernel(
    plan, conv_x, conv_bc, cw_x, cw_bc, dt_bias, a_log, d_skip, state, *rest, moves, row_count, width
):
    received = rest[:row_count]
    conv_x_next, conv_bc_next, state_next, gated, driven_out, decay, b_out = rest[row_count : row_count + 7]
    readout, held, made, drive, b_twice, in_sems, out_sems = rest[row_count + 7 :]
    slots, inner = conv_x.shape[1], conv_x.shape[2]
    heads = dt_bias.shape[0]
    cols, at = Columns(inner), Plan(slots, moves)
    loads = []
    for s in range(slots):
        loads.append(pltpu.make_async_copy(state.at[s], held.at[s], in_sems.at[s]))
        loads[-1].start()

    sums = Sums(received, heads, width)

    def convolved(past, taps, fresh, following):
        past_rows = [past[k].astype(F32) for k in range(KW - 1)]
        total = fresh[:slots] * taps[KW - 1 : KW, :].astype(F32)
        for k in range(KW - 1):
            total = total + past_rows[k] * taps[k : k + 1, :].astype(F32)
            following[k] = past_rows[k + 1] if k < KW - 2 else fresh[:slots]
        return jnp.concatenate([silu(total), jnp.zeros((BLOCK - slots, total.shape[1]), F32)], axis=0)

    value_act = convolved(conv_x, cw_x, sums.projected(cols.x, cols.bc), conv_x_next)
    bc_act = convolved(conv_bc, cw_bc, sums.projected(cols.bc, cols.q), conv_bc_next)
    bc_act = bc_act.astype(BF16).astype(F32)
    b_in, c_val = bc_act[:, :NS], bc_act[:, NS:]
    b_out[...] = b_in
    b_twice[...] = jnp.concatenate([b_in, b_in], axis=0)
    c_out = c_val.astype(BF16)

    shifted = sums.step_in + dt_bias[...].reshape(1, heads)
    step_size = jnp.maximum(shifted, 0.0) + jnp.log(1.0 + jnp.exp(-jnp.abs(shifted)))
    rate = jnp.exp(-jnp.exp(a_log[...].reshape(1, heads)) * step_size)
    decay[...] = rate
    driven = widen(step_size, inner) * value_act
    driven_out[...] = driven
    high = driven.astype(BF16).astype(F32)
    drive[...] = jnp.transpose(jnp.concatenate([high, driven - high], axis=0)).astype(BF16)

    readout[...] = jnp.zeros_like(readout)

    for s in range(slots):
        loads[s].wait()
        value = dot_t(c_out, held[s].reshape(inner, NS))
        readout[s : s + 1, :] = value[s : s + 1]

    stores = []
    for j in range(slots - moves):
        slot = plan[at.stay + j]
        advance_state(slot, held.at[slot], b_twice, drive, decay, made.at[j])
        stores.append(pltpu.make_async_copy(made.at[j], state_next.at[slot], out_sems.at[j]))
        stores[-1].start()

    gate = silu(sums.projected(cols.z, cols.x))
    b_dot_c = jnp.sum(b_in * c_val, axis=1, keepdims=True)
    skip = widen(jnp.broadcast_to(d_skip[...].reshape(1, heads), (BLOCK, heads)), inner)
    total = widen(rate, inner) * readout[...] + driven * b_dot_c + skip * value_act
    gated[...] = (total * gate).astype(BF16).astype(F32)
    for store in stores:
        store.wait()


def advance_state(slot, prior, b_twice, drive, decay, result):
    heads = result.shape[0]
    twice = b_twice[...]
    half = twice.shape[0] // 2
    row = row_iota(twice.shape)
    selected = jnp.where((row == slot) | (row == slot + half), twice, 0.0).astype(BF16)
    outer = dot(drive[...], selected).reshape(heads, HP, NS)
    for h in range(heads):
        rate = decay[pl.ds(slot, 1), h : h + 1]
        result[h] = (rate * prior[h].astype(F32) + outer[h]).astype(BF16)


def merge_kernel(
    plan, gated, kv_new, driven, decay, b_in, conv_x, conv_bc, *rest, moves, row_count, col_count
):
    partials, attended = rest[:col_count], rest[col_count]
    sends, block = rest[col_count + 1 : -1], rest[-1]
    slots, inner = conv_x.shape[1], conv_x.shape[2]
    heads, share = decay.shape[1], attended.shape[1]
    at = Plan(slots, moves)
    part = min(share, HD)
    pieces = []
    for j in range(share // part):
        blocks = [partial[...] for partial in partials]
        peaks = [b[:, share + 2 * j : share + 2 * j + 1] for b in blocks]
        joint = functools.reduce(jnp.maximum, peaks)
        factors = [jnp.exp(p - joint) for p in peaks]
        total = sum(f * b[:, share + 2 * j + 1 : share + 2 * j + 2] for f, b in zip(factors, blocks))
        value = sum(f * b[:, j * part : (j + 1) * part] for f, b in zip(factors, blocks))
        pieces.append(value / total)
    joined = pieces[0] if len(pieces) == 1 else jnp.concatenate(pieces, axis=1)
    joined = jnp.where(row_iota(joined.shape) < slots, joined, 0.0).astype(BF16)
    attended[...] = joined.astype(F32)

    block[...] = jnp.zeros_like(block)
    for m in range(moves):
        slot = plan[at.slot + m]
        row = pl.ds(slot, 1)

        def put(index, value, start=0):
            block[index : index + 1, start : start + value.shape[1]] = value

        put(Note.gated, gated[row, :])
        put(Note.key_value, kv_new[row, :])
        for index, value, start, low_index, low_start in (
            (Note.drive, driven[row, :], 0, Note.drive_low, 0),
            (Note.mixing, decay[row, :], Note.decay, Note.mixing, Note.decay_low),
        ):
            high = value.astype(BF16).astype(F32)
            put(index, high, start)
            put(low_index, value - high, low_start)
        put(Note.mixing, b_in[row, :])
        for k in range(KW - 1):
            put(Note.conv_x + k, conv_x[k, row, :])
            put(Note.conv_bc + k, conv_bc[k, row, :])
        put(Note.attended, attended[row, :])
        for d, send in enumerate(sends, 1):

            @pl.when(plan[at.away + m] == d)
            def _(send=send):
                send[...] = block[...].astype(BF16)


def pick_note(plan, at, m, notes, note):
    for d, sent in enumerate(notes, 1):

        @pl.when(plan[at.from_away + m] == d)
        def _(sent=sent):
            note[...] = sent[...].astype(F32)


def output_kernel(col_ref, plan, gated, attended, w_ssm, w_attn, *rest, slots, moves, row_count, col_count):
    notes, sends = rest[: row_count - 1], rest[row_count - 1 : row_count - 1 + col_count]
    gated_here, attended_here, note = rest[row_count - 1 + col_count :]
    at = Plan(slots, moves)
    inner, share = gated.shape[1], attended.shape[1]
    gated_here[...] = gated[...]
    attended_here[...] = attended[...]
    for m in range(moves):
        pick_note(plan, at, m, notes, note)
        row = pl.ds(plan[at.slot + m], 1)
        gated_here[row, :] = note[Note.gated : Note.gated + 1, :inner]
        attended_here[row, :] = note[Note.attended : Note.attended + 1, :share]
    columns = w_ssm.shape[1] // col_count
    left, right = gated_here[...].astype(BF16), attended_here[...].astype(BF16)
    for d, send in enumerate(sends):
        first = pl.multiple_of(lax.bitwise_xor(col_ref[0], d) * columns, columns)
        span = pl.ds(first, columns)
        send[...] = dot(left, w_ssm[:, span]) + dot(right, w_attn[:, span])


def sum_kernel(*refs):
    parts, out = refs[:-1], refs[-1]
    out[...] = sum(part[...] for part in parts)[: out.shape[0]].astype(BF16)


def arrive_kernel(
    col_ref, plan, table, conv_x, conv_bc, state_in, pool_in, parcels, *rest, moves, row_count, col_count
):
    del state_in, pool_in
    notes, rest = rest[: row_count - 1], rest[row_count - 1 :]
    pages_here, slots = table.shape
    inner = conv_x.shape[2]
    heads = inner // HP
    at = Plan(slots, moves)
    conv_x_next, conv_bc_next, state_next, pool_next = rest[:4]
    packed, made, drive, decay, b_twice, window_x, window_bc, picked, in_sems, out_sems = rest[4:]
    col = col_ref[0]
    loads = []
    for m in range(moves):
        loads.append(pltpu.make_async_copy(parcels.at[plan[at.source + m]], packed.at[m], in_sems.at[m]))
        loads[-1].start()

    for k in range(KW - 1):
        window_x[k] = conv_x[k]
        window_bc[k] = conv_bc[k]
    rows = []
    b_twice[...] = jnp.zeros_like(b_twice)
    half = b_twice.shape[0] // 2
    for m in range(moves):
        pick_note(plan, at, m, notes, picked)
        note = picked[...]
        rows.append(note)
        row = pl.ds(plan[at.slot + m], 1)
        for k in range(KW - 1):
            window_x[k, row, :] = note[Note.conv_x + k : Note.conv_x + k + 1, :inner]
            window_bc[k, row, :] = note[Note.conv_bc + k : Note.conv_bc + k + 1, : 2 * NS]
        mixing = note[Note.mixing : Note.mixing + 1, :]
        b_twice[m : m + 1, :] = mixing[:, :NS]
        b_twice[half + m : half + m + 1, :] = mixing[:, :NS]
        decay[m : m + 1, :] = (
            mixing[:, Note.decay : Note.decay + heads] + mixing[:, Note.decay_low : Note.decay_low + heads]
        )
    padding = [jnp.zeros((half - moves, inner), F32)]
    stacked = [note[Note.drive : Note.drive + 1, :inner] for note in rows] + padding
    stacked += [note[Note.drive_low : Note.drive_low + 1, :inner] for note in rows] + padding
    drive[...] = jnp.transpose(jnp.concatenate(stacked, axis=0)).astype(BF16)
    for k in range(KW - 1):
        conv_x_next[k] = window_x[k].astype(BF16)
        conv_bc_next[k] = window_bc[k].astype(BF16)

    stores = []
    for m in range(moves):
        slot = plan[at.slot + m]
        loads[m].wait()
        owner, local_page, offset = place_of(plan[at.arrived_length + m], col_count)
        key_value = rows[m][Note.key_value : Note.key_value + 1, : 2 * KVH * HD]

        @pl.when(owner == col)
        def _(m=m, local_page=local_page, offset=offset, key_value=key_value):
            insert_row(packed.at[m, local_page], key_value, offset)

        for page in range(pages_here):
            stores.append(
                pltpu.make_async_copy(
                    packed.at[m, page], pool_next.at[table[page, slot]], out_sems.at[m, page]
                )
            )
            stores[-1].start()
        prior = [
            jnp.concatenate([packed[m, pages_here + h, :, :NS], packed[m, pages_here + h, :, NS:]], axis=0)
            for h in range(heads)
        ]
        advance_state(m, prior, b_twice, drive, decay, made.at[m])
        stores.append(pltpu.make_async_copy(made.at[m], state_next.at[slot], out_sems.at[m, pages_here]))
        stores[-1].start()
    for store in stores:
        store.wait()


def shape(dims, dtype):
    return jax.ShapeDtypeStruct(tuple(dims), dtype)


def params(limit=VMEM_LIMIT):
    return pltpu.CompilerParams(vmem_limit_bytes=limit)


def cost(flops, moved):
    return pl.CostEstimate(flops=int(flops), bytes_accessed=int(moved), transcendentals=0)


def exchange(value, axis):
    return lax.all_to_all(value, axis, split_axis=0, concat_axis=0, tiled=True)


def trade(blocks, axis, first=0):
    count = lax.axis_size(axis)
    return [
        block if d == 0 else lax.ppermute(block, axis, [(i, i ^ d) for i in range(count)])
        for d, block in enumerate(blocks, first)
    ]


def local(
    tokens, arrival, cache_lengths, move_slot, move_target, page_table, kv_pool, ssm_state,
    conv_x, conv_bc, norm_gain, weight_z, weight_x, weight_dt, weight_bc, weight_qkv,
    conv_weight_x, conv_weight_bc, dt_bias, a_log, d_skip, weight_ssm_out, weight_attn_out,
):
    row_count = lax.axis_size("rows")
    col_count = lax.axis_size("cols")
    row_index = lax.axis_index("rows").astype(I32).reshape(1)
    col_index = lax.axis_index("cols").astype(I32).reshape(1)
    slots, heads = ssm_state.shape[0], ssm_state.shape[1]
    total, depth = tokens.shape
    moves = move_slot.shape[1]
    pages_here, width = page_table.shape[3], kv_pool.shape[3]
    inner = heads * HP
    stays = slots - moves
    cols, at = Columns(inner), Plan(slots, moves)
    table = page_table[0, 0].T
    pool = kv_pool[:, 0]
    past_x, past_bc = conv_x.transpose(1, 0, 2), conv_bc.transpose(1, 0, 2)
    rows = row_count * BLOCK
    model = depth * row_count
    share = QH * HD // col_count
    state_bytes = 2 * inner * NS
    page_bytes = 2 * pages_here * PAGE * width
    parcel = (pages_here + heads, PAGE, width)
    parcels_here = pltpu.VMEM((moves,) + parcel, BF16)

    parcels, plan, *partial_sums = pl.pallas_call(
        functools.partial(project_kernel, slots=slots),
        out_shape=[shape((row_count,) + parcel, BF16), shape((at.size,), I32)]
        + [shape((BLOCK, cols.width), BF16)] * row_count,
        in_specs=[SMEM_SPEC] * 6 + [VMEM_SPEC] * 7 + [ANY_SPEC] * 2,
        out_specs=[ANY_SPEC, SMEM_SPEC] + [VMEM_SPEC] * row_count,
        scratch_shapes=[
            pltpu.SMEM((total,), I32),
            pltpu.VMEM((total, depth), F32),
            pltpu.VMEM((rows, depth), F32),
            pltpu.VMEM((rows, LANES), F32),
            parcels_here,
            pltpu.SemaphoreType.DMA((moves, pages_here + 2)),
            pltpu.SemaphoreType.DMA((moves,)),
        ],
        compiler_params=params(),
        cost_estimate=cost(2 * rows * depth * cols.width, 8e6),
        name="project",
    )(
        row_index, arrival, cache_lengths, move_slot.T, move_target.T, table,
        tokens, norm_gain, weight_z, weight_x, weight_dt.T, weight_bc, weight_qkv, pool, ssm_state,
    )
    received = trade(partial_sums, "rows")
    parcels = exchange(parcels, "rows")

    pool_next, kv_new, *partials = pl.pallas_call(
        functools.partial(
            attend_kernel, moves=moves, heads=heads, row_count=row_count, col_count=col_count, width=model
        ),
        out_shape=[shape(pool.shape, BF16), shape((BLOCK, 2 * KVH * HD), F32)]
        + [shape((BLOCK, share + LANES), F32)] * col_count,
        in_specs=[SMEM_SPEC] * 3 + [ANY_SPEC] + [VMEM_SPEC] * row_count,
        out_specs=[ANY_SPEC] + [VMEM_SPEC] * (1 + col_count),
        scratch_shapes=[
            pltpu.VMEM((slots, pages_here, PAGE, width), BF16),
            pltpu.VMEM((BLOCK * QH, HD), F32),
            pltpu.VMEM((BLOCK * QH, pages_here * PAGE), F32),
            pltpu.VMEM((BLOCK * QH, HD), F32),
            pltpu.VMEM((BLOCK * QH, HD), F32),
            pltpu.VMEM((BLOCK * QH, HD), F32),
            pltpu.SemaphoreType.DMA((slots, pages_here)),
            pltpu.SemaphoreType.DMA((stays, pages_here)),
        ],
        compiler_params=params(),
        cost_estimate=cost(4 * slots * 16 * pages_here * PAGE * 256, 4 * slots * page_bytes),
        name="attend",
    )(col_index, plan, table, pool, *received)
    partials = trade(partials, "cols")

    next_x, next_bc, state_next, gated, driven, decay, b_in = pl.pallas_call(
        functools.partial(mix_kernel, moves=moves, row_count=row_count, width=model),
        out_shape=(
            shape(past_x.shape, F32),
            shape(past_bc.shape, F32),
            shape(ssm_state.shape, BF16),
            shape((BLOCK, inner), F32),
            shape((BLOCK, inner), F32),
            shape((BLOCK, heads), F32),
            shape((BLOCK, NS), F32),
        ),
        in_specs=[SMEM_SPEC] + [VMEM_SPEC] * 7 + [ANY_SPEC] + [VMEM_SPEC] * row_count,
        out_specs=(VMEM_SPEC, VMEM_SPEC, ANY_SPEC) + (VMEM_SPEC,) * 4,
        scratch_shapes=[
            pltpu.VMEM((BLOCK, inner), F32),
            pltpu.VMEM((slots, heads, HP, NS), BF16),
            pltpu.VMEM((stays, heads, HP, NS), BF16),
            pltpu.VMEM((inner, 2 * BLOCK), BF16),
            pltpu.VMEM((2 * BLOCK, NS), F32),
            pltpu.SemaphoreType.DMA((slots,)),
            pltpu.SemaphoreType.DMA((stays,)),
        ],
        compiler_params=params(),
        cost_estimate=cost(4 * slots * inner * NS * 32, 4 * slots * state_bytes),
        name="mix",
    )(plan, past_x, past_bc, conv_weight_x, conv_weight_bc, dt_bias, a_log, d_skip, ssm_state, *received)

    note = (BLOCK, max(inner, 2 * NS, 2 * KVH * HD, share))
    attended, *notes = pl.pallas_call(
        functools.partial(merge_kernel, moves=moves, row_count=row_count, col_count=col_count),
        out_shape=[shape((BLOCK, share), F32)] + [shape(note, BF16)] * (row_count - 1),
        in_specs=[SMEM_SPEC] + [VMEM_SPEC] * (7 + col_count),
        out_specs=[VMEM_SPEC] * row_count,
        scratch_shapes=[pltpu.VMEM(note, F32)],
        compiler_params=params(),
        cost_estimate=cost(1e6, 1e6),
        name="merge",
    )(plan, gated, kv_new, driven, decay, b_in, next_x, next_bc, *partials)
    notes = trade(notes, "rows", 1)

    columns = weight_ssm_out.shape[1] // col_count
    terms = pl.pallas_call(
        functools.partial(
            output_kernel, slots=slots, moves=moves, row_count=row_count, col_count=col_count
        ),
        out_shape=[shape((BLOCK, columns), F32)] * col_count,
        in_specs=[SMEM_SPEC] * 2 + [VMEM_SPEC] * (4 + row_count - 1),
        out_specs=[VMEM_SPEC] * col_count,
        scratch_shapes=[
            pltpu.VMEM((BLOCK, inner), F32), pltpu.VMEM((BLOCK, share), F32), pltpu.VMEM(note, F32)
        ],
        compiler_params=params(),
        cost_estimate=cost(2 * BLOCK * (inner + share) * weight_ssm_out.shape[1], 4e6),
        name="output",
    )(col_index, plan, gated, attended, weight_ssm_out, weight_attn_out, *notes)
    terms = trade(terms, "cols")

    conv_x_next, conv_bc_next, state_next, pool_next = pl.pallas_call(
        functools.partial(arrive_kernel, moves=moves, row_count=row_count, col_count=col_count),
        out_shape=(
            shape(past_x.shape, BF16),
            shape(past_bc.shape, BF16),
            shape(ssm_state.shape, BF16),
            shape(pool.shape, BF16),
        ),
        in_specs=[SMEM_SPEC] * 3 + [VMEM_SPEC] * 2 + [ANY_SPEC] * 3 + [VMEM_SPEC] * (row_count - 1),
        out_specs=(VMEM_SPEC, VMEM_SPEC, ANY_SPEC, ANY_SPEC),
        scratch_shapes=[
            parcels_here,
            pltpu.VMEM((moves, heads, HP, NS), BF16),
            pltpu.VMEM((inner, 2 * BLOCK), BF16),
            pltpu.VMEM((BLOCK, heads), F32),
            pltpu.VMEM((2 * BLOCK, NS), F32),
            pltpu.VMEM((KW - 1, slots, inner), F32),
            pltpu.VMEM((KW - 1, slots, 2 * NS), F32),
            pltpu.VMEM(note, F32),
            pltpu.SemaphoreType.DMA((moves,)),
            pltpu.SemaphoreType.DMA((moves, pages_here + 1)),
        ],
        input_output_aliases={5: 2, 6: 3},
        compiler_params=params(),
        cost_estimate=cost(1e6, 4 * moves * (state_bytes + page_bytes)),
        name="arrive",
    )(col_index, plan, table, next_x, next_bc, state_next, pool_next, parcels, *notes)

    mixed = pl.pallas_call(
        sum_kernel,
        out_shape=shape((slots, columns), BF16),
        in_specs=[VMEM_SPEC] * col_count,
        out_specs=VMEM_SPEC,
        compiler_params=params(),
        name="total",
    )(*terms)
    return (
        mixed, state_next, conv_x_next.transpose(1, 0, 2), conv_bc_next.transpose(1, 0, 2), pool_next[:, None]
    )


def solution(mesh):
    in_specs = (
        P(None, "rows"),
        P(),
        P(),
        P(),
        P(),
        P("rows", "cols", None, None),
        P("rows", "cols", None, None),
        P("rows", "cols", None, None),
        P("rows", None, "cols"),
        P("rows", None, None),
        P("rows"),
        P("rows", "cols"),
        P("rows", "cols"),
        P("rows", "cols"),
        P("rows", None),
        P("rows", None),
        P(None, "cols"),
        P(),
        P("cols"),
        P("cols"),
        P("cols"),
        P("cols", None),
        P("cols", None),
    )
    out_specs = (
        P("rows", "cols"),
        P("rows", "cols", None, None),
        P("rows", None, "cols"),
        P("rows", None, None),
        P("rows", "cols", None, None),
    )
    return jax.shard_map(local, mesh=mesh, in_specs=in_specs, out_specs=out_specs, check_vma=False)
```

```python
import functools

import jax
import jax.numpy as jnp
from jax import lax
from jax.experimental import pallas as pl
from jax.experimental.pallas import tpu as pltpu
from jax.sharding import PartitionSpec as P

HP = 64
NS = 256
KW = 4
QH = 8
KVH = 2
HD = 128
PAGE = 32
LANES = 128
BLOCK = 16

EPSILON = 1e-05
FLOOR_SCORE = -1e30
FIRST_LIMIT = 60 * 1024 * 1024
VMEM_LIMIT = 57 * 1024 * 1024

F32 = jnp.float32
BF16 = jnp.bfloat16
I32 = jnp.int32

SMEM_SPEC = pl.BlockSpec(memory_space=pltpu.SMEM)
VMEM_SPEC = pl.BlockSpec(memory_space=pltpu.VMEM)
ANY_SPEC = pl.BlockSpec(memory_space=pl.ANY)


def silu(v):
    return v / (1.0 + jnp.exp(-v))


def dot(a, b):
    return jnp.dot(a, b, preferred_element_type=F32)


def dot_t(a, b):
    return lax.dot_general(a, b, (((1,), (1,)), ((), ())), preferred_element_type=F32)


def row_iota(shape):
    return lax.broadcasted_iota(I32, shape, 0)


def lane_iota(shape):
    return lax.broadcasted_iota(I32, shape, 1)


class Columns:
    def __init__(self, inner):
        self.z = 0
        self.x = inner
        self.bc = 2 * inner
        self.q = self.bc + 2 * NS
        self.kv = self.q + QH * HD
        self.tail = self.kv + 2 * KVH * HD
        self.width = self.tail + 2 * LANES


class Plan:
    def __init__(self, slots, moves):
        self.length = 0
        self.slot = slots
        self.away = self.slot + moves
        self.source = self.away + moves
        self.from_away = self.source + moves
        self.arrived_length = self.from_away + moves
        self.stay = self.arrived_length + moves
        self.size = self.stay + slots - moves


class Note:
    mixed, key_value, drive, drive_low, mixing, conv_x, conv_bc = 0, 1, 2, 3, 4, 5, 8
    decay, decay_low = NS, NS + LANES


def project_kernel(
    row_ref, arrival, lengths, move_slot, move_target, table,
    tokens, gain, w_z, w_x, w_dt, w_bc, w_qkv, pool, state,
    parcels, plan, *rest,
    slots,
):
    moves, row_count = move_slot.shape
    pages_here = table.shape[0]
    heads, depth = w_dt.shape
    inner = heads * HP
    cols, at = Columns(inner), Plan(slots, moves)
    outs = rest[:row_count]
    inverse, wide, picked, tail, packed, in_sems, out_sems = rest[row_count:]
    me = row_ref[0]

    loads = []
    for m in range(moves):
        slot = move_slot[m, me]
        for page in range(pages_here):
            loads.append(
                pltpu.make_async_copy(pool.at[table[page, slot]], packed.at[m, page], in_sems.at[m, page])
            )
        for half in range(2):
            loads.append(
                pltpu.make_async_copy(
                    state.at[slot, :, half * PAGE : (half + 1) * PAGE, :],
                    packed.at[m, pages_here:, :, half * NS : (half + 1) * NS],
                    in_sems.at[m, pages_here + half],
                )
            )
    for load in loads:
        load.start()

    wide[...] = tokens[...].astype(F32)
    picked[...] = jnp.zeros_like(picked)

    def invert(t, carry):
        for s in range(slots):
            inverse[arrival[t * slots + s]] = t * slots + s
        return carry

    lax.fori_loop(0, row_count, invert, 0)

    def pick(d, carry):
        first = lax.bitwise_xor(me, d) * slots
        for s in range(slots):
            picked[pl.ds(d * BLOCK + s, 1), :] = wide[pl.ds(inverse[first + s], 1), :]
        return carry

    lax.fori_loop(0, row_count, pick, 0)

    for load in loads:
        load.wait()
    stores = [
        pltpu.make_async_copy(packed.at[m], parcels.at[move_target[m, me]], out_sems.at[m])
        for m in range(moves)
    ]
    for store in stores:
        store.start()

    rows = picked[...]
    squares = jnp.sum(rows * rows, axis=1, keepdims=True)
    scaled = (rows * gain[...].astype(F32).reshape(1, depth)).astype(BF16)

    def put(start, value):
        value = value.astype(BF16)
        for d, out in enumerate(outs):
            out[:, start : start + value.shape[1]] = value[d * BLOCK : (d + 1) * BLOCK]

    put(cols.z, dot(scaled, w_z[...]))
    put(cols.x, dot(scaled, w_x[...]))
    put(cols.bc, dot(scaled, w_bc[...]))
    put(cols.q, dot(scaled, w_qkv[...]))
    tail[...] = jnp.zeros_like(tail)
    tail[:, :heads] = dot_t(scaled, w_dt[...])
    tail[:, heads : heads + 1] = squares
    high = tail[...].astype(BF16)
    put(cols.tail, high)
    put(cols.tail + LANES, tail[...] - high.astype(F32))

    stays = 0
    for s in range(slots):
        plan[at.length + s] = lengths[me * slots + s]
        leaves = move_slot[0, me] == s
        for m in range(1, moves):
            leaves = jnp.logical_or(leaves, move_slot[m, me] == s)

        @pl.when(jnp.logical_not(leaves))
        def _(s=s, stays=stays):
            plan[at.stay + stays] = s

        stays = stays + jnp.where(leaves, 0, 1)
    for m in range(moves):
        plan[at.slot + m] = move_slot[m, me]
        plan[at.away + m] = lax.bitwise_xor(move_target[m, me], me)

    def seek(i, turn):
        for m in range(moves):
            comes = move_target[m, i] == me

            @pl.when(comes)
            def _(m=m, turn=turn):
                plan[at.source + turn] = i
                plan[at.from_away + turn] = lax.bitwise_xor(i, me)
                plan[at.arrived_length + turn] = lengths[i * slots + move_slot[m, i]]

            turn = turn + jnp.where(comes, 1, 0)
        return turn

    lax.fori_loop(0, row_count, seek, I32(0))
    for store in stores:
        store.wait()


def widen(per_head, inner):
    rows = per_head.shape[0]
    first = lane_iota((rows, 2 * HP)) < HP
    pieces = []
    for h in range(0, inner // HP, 2):
        pieces.append(jnp.where(first, per_head[:, h : h + 1], per_head[:, h + 1 : h + 2]))
    return pieces[0] if len(pieces) == 1 else jnp.concatenate(pieces, axis=1)


class Sums:
    def __init__(self, received, heads, width):
        self.received = received
        cols = Columns(heads * HP)
        tail = self.total(cols.tail, cols.tail + LANES) + self.total(cols.tail + LANES, cols.width)
        self.root = jnp.sqrt(tail[:, heads : heads + 1] / width + EPSILON)
        self.step_in = (tail[:, :heads] / self.root).astype(BF16).astype(F32)

    def total(self, start, stop):
        return sum(part[:, start:stop].astype(F32) for part in self.received)

    def projected(self, start, stop):
        return (self.total(start, stop) / self.root).astype(BF16).astype(F32)


def insert_row(page, row, offset):
    old = page[...].astype(F32)
    page[...] = jnp.where(row_iota(old.shape) == offset, row, old).astype(BF16)


def place_of(length, col_count):
    logical = lax.div(length, I32(PAGE))
    return lax.rem(logical, I32(col_count)), lax.div(logical, I32(col_count)), lax.rem(length, I32(PAGE))


def attend_kernel(
    col_ref, plan, table, pool, *rest, moves, heads, row_count, col_count, width
):
    received = rest[:row_count]
    pool_next, kv_new = rest[row_count : row_count + 2]
    sends = rest[row_count + 2 : row_count + 2 + col_count]
    pages, queries, scores, weighted, peaks, totals, in_sems, out_sems = rest[row_count + 2 + col_count :]
    pages_here, slots = table.shape
    cols, at = Columns(heads * HP), Plan(slots, moves)
    col = col_ref[0]
    tokens_here = pages_here * PAGE
    kv_width = KVH * HD
    loads = []
    for s in range(slots):
        for page in range(pages_here):
            loads.append(
                pltpu.make_async_copy(pool.at[table[page, s]], pages.at[s, page], in_sems.at[s, page])
            )
            loads[-1].start()

    sums = Sums(received, heads, width)
    kv_new[...] = sums.projected(cols.kv, cols.tail)
    q_in = sums.projected(cols.q, cols.kv)
    for h in range(QH):
        queries[pl.ds(h, BLOCK, stride=QH), :] = q_in[:, h * HD : (h + 1) * HD]

    first_group = row_iota((QH, HD)) < QH // KVH
    lane = lane_iota((QH, tokens_here))
    position = (lax.shift_right_logical(lane, 5) * col_count + col) * PAGE + lax.bitwise_and(lane, PAGE - 1)
    for s in range(slots):
        for load in loads[s * pages_here : (s + 1) * pages_here]:
            load.wait()
        length = plan[at.length + s]
        owner, local_page, offset = place_of(length, col_count)

        @pl.when(owner == col)
        def _(s=s, local_page=local_page, offset=offset):
            insert_row(pages.at[s, local_page], kv_new[s : s + 1, :], offset)

        keys = pages[s, :, :, :kv_width].reshape(tokens_here, kv_width)
        query = queries[s * QH : (s + 1) * QH, :]
        query = jnp.concatenate(
            [jnp.where(first_group, query, 0.0), jnp.where(first_group, 0.0, query)], axis=1
        ).astype(BF16)
        score = dot_t(query, keys) * (HD ** -0.5)
        scores[s * QH : (s + 1) * QH, :] = jnp.where(position <= length, score, FLOOR_SCORE)

    stores = []
    for j in range(slots - moves):
        slot = plan[at.stay + j]
        for page in range(pages_here):
            stores.append(
                pltpu.make_async_copy(
                    pages.at[slot, page], pool_next.at[table[page, slot]], out_sems.at[j, page]
                )
            )
            stores[-1].start()

    live_rows = slots * QH
    everything = scores[0:live_rows, :]
    peak = jnp.max(everything, axis=1, keepdims=True)
    weights = jnp.where(everything > 0.5 * FLOOR_SCORE, jnp.exp(everything - peak), 0.0)
    total = jnp.sum(weights, axis=1, keepdims=True)
    scores[0:live_rows, :] = weights
    for ref, value in ((weighted, None), (peaks, peak), (totals, total)):
        ref[live_rows:, :] = jnp.zeros((BLOCK * QH - live_rows, HD), F32)
        if value is not None:
            ref[0:live_rows, :] = jnp.broadcast_to(value, (live_rows, HD))
    for s in range(slots):
        values = pages[s, :, :, kv_width:].reshape(tokens_here, kv_width)
        weight = scores[s * QH : (s + 1) * QH, :]
        high = weight.astype(BF16).astype(F32)
        both = dot(jnp.concatenate([high, weight - high], axis=0).astype(BF16), values)
        joined = both[:QH] + both[QH:]
        weighted[s * QH : (s + 1) * QH, :] = jnp.where(first_group, joined[:, :HD], joined[:, HD:])

    share = QH * HD // col_count
    part = min(share, HD)
    lanes = lane_iota((BLOCK, LANES))
    for d, send in enumerate(sends):
        first = lax.bitwise_xor(col, d) * share
        stats = jnp.zeros((BLOCK, LANES), F32)
        for j in range(share // part):
            rows = pl.ds(lax.div(first + j * part, I32(HD)), BLOCK, stride=QH)
            whole = weighted[rows, :]
            piece = whole[:, :part]
            for begin in range(part, HD, part):
                piece = jnp.where(lax.rem(first, I32(HD)) == begin, whole[:, begin : begin + part], piece)
            send[:, j * part : (j + 1) * part] = piece
            stats = jnp.where(lanes == 2 * j, peaks[rows, :], stats)
            stats = jnp.where(lanes == 2 * j + 1, totals[rows, :], stats)
        send[:, share:] = stats
    for store in stores:
        store.wait()


def mix_kernel(
    plan, conv_x, conv_bc, cw_x, cw_bc, dt_bias, a_log, d_skip, state, *rest, moves, row_count, width
):
    received = rest[:row_count]
    conv_x_next, conv_bc_next, state_next, gated, driven_out, decay, b_out = rest[row_count : row_count + 7]
    readout, held, made, drive, b_twice, in_sems, out_sems = rest[row_count + 7 :]
    slots, inner = conv_x.shape[1], conv_x.shape[2]
    heads = dt_bias.shape[0]
    cols, at = Columns(inner), Plan(slots, moves)
    loads = []
    for s in range(slots):
        loads.append(pltpu.make_async_copy(state.at[s], held.at[s], in_sems.at[s]))
        loads[-1].start()

    sums = Sums(received, heads, width)

    def convolved(past, taps, fresh, following):
        past_rows = [past[k].astype(F32) for k in range(KW - 1)]
        total = fresh[:slots] * taps[KW - 1 : KW, :].astype(F32)
        for k in range(KW - 1):
            total = total + past_rows[k] * taps[k : k + 1, :].astype(F32)
            following[k] = past_rows[k + 1] if k < KW - 2 else fresh[:slots]
        return jnp.concatenate([silu(total), jnp.zeros((BLOCK - slots, total.shape[1]), F32)], axis=0)

    value_act = convolved(conv_x, cw_x, sums.projected(cols.x, cols.bc), conv_x_next)
    bc_act = convolved(conv_bc, cw_bc, sums.projected(cols.bc, cols.q), conv_bc_next)
    bc_act = bc_act.astype(BF16).astype(F32)
    b_in, c_val = bc_act[:, :NS], bc_act[:, NS:]
    b_out[...] = b_in
    b_twice[...] = jnp.concatenate([b_in, b_in], axis=0)
    c_out = c_val.astype(BF16)

    shifted = sums.step_in + dt_bias[...].reshape(1, heads)
    step_size = jnp.maximum(shifted, 0.0) + jnp.log(1.0 + jnp.exp(-jnp.abs(shifted)))
    rate = jnp.exp(-jnp.exp(a_log[...].reshape(1, heads)) * step_size)
    decay[...] = rate
    driven = widen(step_size, inner) * value_act
    driven_out[...] = driven
    high = driven.astype(BF16).astype(F32)
    drive[...] = jnp.transpose(jnp.concatenate([high, driven - high], axis=0)).astype(BF16)

    readout[...] = jnp.zeros_like(readout)

    for s in range(slots):
        loads[s].wait()
        value = dot_t(c_out, held[s].reshape(inner, NS))
        readout[s : s + 1, :] = value[s : s + 1]

    stores = []
    for j in range(slots - moves):
        slot = plan[at.stay + j]
        advance_state(slot, held.at[slot], b_twice, drive, decay, made.at[j])
        stores.append(pltpu.make_async_copy(made.at[j], state_next.at[slot], out_sems.at[j]))
        stores[-1].start()

    gate = silu(sums.projected(cols.z, cols.x))
    b_dot_c = jnp.sum(b_in * c_val, axis=1, keepdims=True)
    skip = widen(jnp.broadcast_to(d_skip[...].reshape(1, heads), (BLOCK, heads)), inner)
    total = widen(rate, inner) * readout[...] + driven * b_dot_c + skip * value_act
    gated[...] = (total * gate).astype(BF16).astype(F32)
    for store in stores:
        store.wait()


def advance_state(slot, prior, b_twice, drive, decay, result):
    heads = result.shape[0]
    twice = b_twice[...]
    half = twice.shape[0] // 2
    row = row_iota(twice.shape)
    selected = jnp.where((row == slot) | (row == slot + half), twice, 0.0).astype(BF16)
    outer = dot(drive[...], selected).reshape(heads, HP, NS)
    for h in range(heads):
        rate = decay[pl.ds(slot, 1), h : h + 1]
        result[h] = (rate * prior[h].astype(F32) + outer[h]).astype(BF16)


def output_kernel(col_ref, gated, w_ssm, w_attn, *rest, slots, col_count):
    partials, sends = rest[:col_count], rest[col_count:]
    share = w_attn.shape[0]
    part = min(share, HD)
    blocks = [partial[...] for partial in partials]
    pieces = []
    for j in range(share // part):
        peaks = [b[:, share + 2 * j : share + 2 * j + 1] for b in blocks]
        joint = functools.reduce(jnp.maximum, peaks)
        factors = [jnp.exp(p - joint) for p in peaks]
        total = sum(f * b[:, share + 2 * j + 1 : share + 2 * j + 2] for f, b in zip(factors, blocks))
        value = sum(f * b[:, j * part : (j + 1) * part] for f, b in zip(factors, blocks))
        pieces.append(value / total)
    joined = pieces[0] if len(pieces) == 1 else jnp.concatenate(pieces, axis=1)
    right = jnp.where(row_iota(joined.shape) < slots, joined, 0.0).astype(BF16)
    left = gated[...].astype(BF16)
    columns = w_ssm.shape[1] // col_count
    for d, send in enumerate(sends):
        first = pl.multiple_of(lax.bitwise_xor(col_ref[0], d) * columns, columns)
        span = pl.ds(first, columns)
        send[...] = dot(left, w_ssm[:, span]) + dot(right, w_attn[:, span])


def total_kernel(
    plan, kv_new, driven, decay, b_in, conv_x, conv_bc, *rest, moves, row_count, col_count
):
    terms, mixed = rest[:col_count], rest[col_count]
    sends, block = rest[col_count + 1 : -1], rest[-1]
    at = Plan(conv_x.shape[1], moves)
    mixed[...] = sum(term[...] for term in terms).astype(BF16).astype(F32)

    block[...] = jnp.zeros_like(block)
    for m in range(moves):
        row = pl.ds(plan[at.slot + m], 1)

        def put(index, value, start=0):
            block[index : index + 1, start : start + value.shape[1]] = value

        put(Note.mixed, mixed[row, :])
        put(Note.key_value, kv_new[row, :])
        for index, value, start, low_index, low_start in (
            (Note.drive, driven[row, :], 0, Note.drive_low, 0),
            (Note.mixing, decay[row, :], Note.decay, Note.mixing, Note.decay_low),
        ):
            high = value.astype(BF16).astype(F32)
            put(index, high, start)
            put(low_index, value - high, low_start)
        put(Note.mixing, b_in[row, :])
        for k in range(KW - 1):
            put(Note.conv_x + k, conv_x[k, row, :])
            put(Note.conv_bc + k, conv_bc[k, row, :])
        for d, send in enumerate(sends, 1):

            @pl.when(plan[at.away + m] == d)
            def _(send=send):
                send[...] = block[...].astype(BF16)


def pick_note(plan, at, m, notes, note):
    for d, sent in enumerate(notes, 1):

        @pl.when(plan[at.from_away + m] == d)
        def _(sent=sent):
            note[...] = sent[...].astype(F32)


def arrive_kernel(
    col_ref, plan, table, mixed_home, conv_x, conv_bc, state_in, pool_in, parcels, *rest,
    moves, row_count, col_count,
):
    del state_in, pool_in
    notes, rest = rest[: row_count - 1], rest[row_count - 1 :]
    pages_here, slots = table.shape
    inner = conv_x.shape[2]
    heads = inner // HP
    at = Plan(slots, moves)
    mixed, conv_x_next, conv_bc_next, state_next, pool_next = rest[:5]
    packed, made, drive, decay, b_twice, window_x, window_bc, window_mixed, picked, in_sems, out_sems = rest[5:]
    col = col_ref[0]
    loads = []
    for m in range(moves):
        loads.append(pltpu.make_async_copy(parcels.at[plan[at.source + m]], packed.at[m], in_sems.at[m]))
        loads[-1].start()

    for k in range(KW - 1):
        window_x[k] = conv_x[k]
        window_bc[k] = conv_bc[k]
    window_mixed[...] = mixed_home[...]
    rows = []
    b_twice[...] = jnp.zeros_like(b_twice)
    half = b_twice.shape[0] // 2
    for m in range(moves):
        pick_note(plan, at, m, notes, picked)
        note = picked[...]
        rows.append(note)
        row = pl.ds(plan[at.slot + m], 1)
        window_mixed[row, :] = note[Note.mixed : Note.mixed + 1, : window_mixed.shape[1]]
        for k in range(KW - 1):
            window_x[k, row, :] = note[Note.conv_x + k : Note.conv_x + k + 1, :inner]
            window_bc[k, row, :] = note[Note.conv_bc + k : Note.conv_bc + k + 1, : 2 * NS]
        mixing = note[Note.mixing : Note.mixing + 1, :]
        b_twice[m : m + 1, :] = mixing[:, :NS]
        b_twice[half + m : half + m + 1, :] = mixing[:, :NS]
        decay[m : m + 1, :] = (
            mixing[:, Note.decay : Note.decay + heads] + mixing[:, Note.decay_low : Note.decay_low + heads]
        )
    padding = [jnp.zeros((half - moves, inner), F32)]
    stacked = [note[Note.drive : Note.drive + 1, :inner] for note in rows] + padding
    stacked += [note[Note.drive_low : Note.drive_low + 1, :inner] for note in rows] + padding
    drive[...] = jnp.transpose(jnp.concatenate(stacked, axis=0)).astype(BF16)
    mixed[...] = window_mixed[0:slots, :].astype(BF16)
    for k in range(KW - 1):
        conv_x_next[k] = window_x[k].astype(BF16)
        conv_bc_next[k] = window_bc[k].astype(BF16)

    stores = []
    for m in range(moves):
        slot = plan[at.slot + m]
        loads[m].wait()
        owner, local_page, offset = place_of(plan[at.arrived_length + m], col_count)
        key_value = rows[m][Note.key_value : Note.key_value + 1, : 2 * KVH * HD]

        @pl.when(owner == col)
        def _(m=m, local_page=local_page, offset=offset, key_value=key_value):
            insert_row(packed.at[m, local_page], key_value, offset)

        for page in range(pages_here):
            stores.append(
                pltpu.make_async_copy(
                    packed.at[m, page], pool_next.at[table[page, slot]], out_sems.at[m, page]
                )
            )
            stores[-1].start()
        prior = [
            jnp.concatenate([packed[m, pages_here + h, :, :NS], packed[m, pages_here + h, :, NS:]], axis=0)
            for h in range(heads)
        ]
        advance_state(m, prior, b_twice, drive, decay, made.at[m])
        stores.append(pltpu.make_async_copy(made.at[m], state_next.at[slot], out_sems.at[m, pages_here]))
        stores[-1].start()
    for store in stores:
        store.wait()


def shape(dims, dtype):
    return jax.ShapeDtypeStruct(tuple(dims), dtype)


def params(limit=VMEM_LIMIT):
    return pltpu.CompilerParams(vmem_limit_bytes=limit)


def cost(flops, moved):
    return pl.CostEstimate(flops=int(flops), bytes_accessed=int(moved), transcendentals=0)


def exchange(value, axis):
    return lax.all_to_all(value, axis, split_axis=0, concat_axis=0, tiled=True)


def trade(blocks, axis, first=0):
    count = lax.axis_size(axis)
    return [
        block if d == 0 else lax.ppermute(block, axis, [(i, i ^ d) for i in range(count)])
        for d, block in enumerate(blocks, first)
    ]


def local(
    tokens, arrival, cache_lengths, move_slot, move_target, page_table, kv_pool, ssm_state,
    conv_x, conv_bc, norm_gain, weight_z, weight_x, weight_dt, weight_bc, weight_qkv,
    conv_weight_x, conv_weight_bc, dt_bias, a_log, d_skip, weight_ssm_out, weight_attn_out,
):
    row_count = lax.axis_size("rows")
    col_count = lax.axis_size("cols")
    row_index = lax.axis_index("rows").astype(I32).reshape(1)
    col_index = lax.axis_index("cols").astype(I32).reshape(1)
    slots, heads = ssm_state.shape[0], ssm_state.shape[1]
    total, depth = tokens.shape
    moves = move_slot.shape[1]
    pages_here, width = page_table.shape[3], kv_pool.shape[3]
    inner = heads * HP
    stays = slots - moves
    cols, at = Columns(inner), Plan(slots, moves)
    table = page_table[0, 0].T
    pool = kv_pool[:, 0]
    past_x, past_bc = conv_x.transpose(1, 0, 2), conv_bc.transpose(1, 0, 2)
    rows = row_count * BLOCK
    model = depth * row_count
    share = QH * HD // col_count
    state_bytes = 2 * inner * NS
    page_bytes = 2 * pages_here * PAGE * width
    parcel = (pages_here + heads, PAGE, width)
    parcels_here = pltpu.VMEM((moves,) + parcel, BF16)

    parcels, plan, *partial_sums = pl.pallas_call(
        functools.partial(project_kernel, slots=slots),
        out_shape=[shape((row_count,) + parcel, BF16), shape((at.size,), I32)]
        + [shape((BLOCK, cols.width), BF16)] * row_count,
        in_specs=[SMEM_SPEC] * 6 + [VMEM_SPEC] * 7 + [ANY_SPEC] * 2,
        out_specs=[ANY_SPEC, SMEM_SPEC] + [VMEM_SPEC] * row_count,
        scratch_shapes=[
            pltpu.SMEM((total,), I32),
            pltpu.VMEM((total, depth), F32),
            pltpu.VMEM((rows, depth), F32),
            pltpu.VMEM((rows, LANES), F32),
            parcels_here,
            pltpu.SemaphoreType.DMA((moves, pages_here + 2)),
            pltpu.SemaphoreType.DMA((moves,)),
        ],
        compiler_params=params(FIRST_LIMIT),
        cost_estimate=cost(2 * rows * depth * cols.width, 8e6),
        name="project",
    )(
        row_index, arrival, cache_lengths, move_slot.T, move_target.T, table,
        tokens, norm_gain, weight_z, weight_x, weight_dt.T, weight_bc, weight_qkv, pool, ssm_state,
    )
    received = trade(partial_sums, "rows")
    parcels, received = lax.optimization_barrier((parcels, received))
    parcels = exchange(parcels, "rows")

    pool_next, kv_new, *partials = pl.pallas_call(
        functools.partial(
            attend_kernel, moves=moves, heads=heads, row_count=row_count, col_count=col_count, width=model
        ),
        out_shape=[shape(pool.shape, BF16), shape((BLOCK, 2 * KVH * HD), F32)]
        + [shape((BLOCK, share + LANES), F32)] * col_count,
        in_specs=[SMEM_SPEC] * 3 + [ANY_SPEC] + [VMEM_SPEC] * row_count,
        out_specs=[ANY_SPEC] + [VMEM_SPEC] * (1 + col_count),
        scratch_shapes=[
            pltpu.VMEM((slots, pages_here, PAGE, width), BF16),
            pltpu.VMEM((BLOCK * QH, HD), F32),
            pltpu.VMEM((BLOCK * QH, pages_here * PAGE), F32),
            pltpu.VMEM((BLOCK * QH, HD), F32),
            pltpu.VMEM((BLOCK * QH, HD), F32),
            pltpu.VMEM((BLOCK * QH, HD), F32),
            pltpu.SemaphoreType.DMA((slots, pages_here)),
            pltpu.SemaphoreType.DMA((stays, pages_here)),
        ],
        compiler_params=params(),
        cost_estimate=cost(4 * slots * 16 * pages_here * PAGE * 256, 4 * slots * page_bytes),
        name="attend",
    )(col_index, plan, table, pool, *received)
    partials = trade(partials, "cols")

    next_x, next_bc, state_next, gated, driven, decay, b_in = pl.pallas_call(
        functools.partial(mix_kernel, moves=moves, row_count=row_count, width=model),
        out_shape=(
            shape(past_x.shape, F32),
            shape(past_bc.shape, F32),
            shape(ssm_state.shape, BF16),
            shape((BLOCK, inner), F32),
            shape((BLOCK, inner), F32),
            shape((BLOCK, heads), F32),
            shape((BLOCK, NS), F32),
        ),
        in_specs=[SMEM_SPEC] + [VMEM_SPEC] * 7 + [ANY_SPEC] + [VMEM_SPEC] * row_count,
        out_specs=(VMEM_SPEC, VMEM_SPEC, ANY_SPEC) + (VMEM_SPEC,) * 4,
        scratch_shapes=[
            pltpu.VMEM((BLOCK, inner), F32),
            pltpu.VMEM((slots, heads, HP, NS), BF16),
            pltpu.VMEM((stays, heads, HP, NS), BF16),
            pltpu.VMEM((inner, 2 * BLOCK), BF16),
            pltpu.VMEM((2 * BLOCK, NS), F32),
            pltpu.SemaphoreType.DMA((slots,)),
            pltpu.SemaphoreType.DMA((stays,)),
        ],
        compiler_params=params(),
        cost_estimate=cost(4 * slots * inner * NS * 32, 4 * slots * state_bytes),
        name="mix",
    )(plan, past_x, past_bc, conv_weight_x, conv_weight_bc, dt_bias, a_log, d_skip, ssm_state, *received)

    columns = weight_ssm_out.shape[1] // col_count
    terms = pl.pallas_call(
        functools.partial(output_kernel, slots=slots, col_count=col_count),
        out_shape=[shape((BLOCK, columns), F32)] * col_count,
        in_specs=[SMEM_SPEC] + [VMEM_SPEC] * (3 + col_count),
        out_specs=[VMEM_SPEC] * col_count,
        compiler_params=params(),
        cost_estimate=cost(2 * BLOCK * (inner + share) * weight_ssm_out.shape[1], 4e6),
        name="output",
    )(col_index, gated, weight_ssm_out, weight_attn_out, *partials)
    terms = trade(terms, "cols")

    note = (BLOCK, max(inner, 2 * NS, 2 * KVH * HD, columns))
    mixed_home, *notes = pl.pallas_call(
        functools.partial(total_kernel, moves=moves, row_count=row_count, col_count=col_count),
        out_shape=[shape((BLOCK, columns), F32)] + [shape(note, BF16)] * (row_count - 1),
        in_specs=[SMEM_SPEC] + [VMEM_SPEC] * (6 + col_count),
        out_specs=[VMEM_SPEC] * row_count,
        scratch_shapes=[pltpu.VMEM(note, F32)],
        compiler_params=params(),
        cost_estimate=cost(1e6, 1e6),
        name="total",
    )(plan, kv_new, driven, decay, b_in, next_x, next_bc, *terms)
    notes = trade(notes, "rows", 1)

    mixed, conv_x_next, conv_bc_next, state_next, pool_next = pl.pallas_call(
        functools.partial(arrive_kernel, moves=moves, row_count=row_count, col_count=col_count),
        out_shape=(
            shape((slots, columns), BF16),
            shape(past_x.shape, BF16),
            shape(past_bc.shape, BF16),
            shape(ssm_state.shape, BF16),
            shape(pool.shape, BF16),
        ),
        in_specs=[SMEM_SPEC] * 3 + [VMEM_SPEC] * 3 + [ANY_SPEC] * 3 + [VMEM_SPEC] * (row_count - 1),
        out_specs=[VMEM_SPEC] * 3 + [ANY_SPEC] * 2,
        scratch_shapes=[
            parcels_here,
            pltpu.VMEM((moves, heads, HP, NS), BF16),
            pltpu.VMEM((inner, 2 * BLOCK), BF16),
            pltpu.VMEM((BLOCK, heads), F32),
            pltpu.VMEM((2 * BLOCK, NS), F32),
            pltpu.VMEM((KW - 1, slots, inner), F32),
            pltpu.VMEM((KW - 1, slots, 2 * NS), F32),
            pltpu.VMEM((BLOCK, columns), F32),
            pltpu.VMEM(note, F32),
            pltpu.SemaphoreType.DMA((moves,)),
            pltpu.SemaphoreType.DMA((moves, pages_here + 1)),
        ],
        input_output_aliases={6: 3, 7: 4},
        compiler_params=params(),
        cost_estimate=cost(1e6, 4 * moves * (state_bytes + page_bytes)),
        name="arrive",
    )(col_index, plan, table, mixed_home, next_x, next_bc, state_next, pool_next, parcels, *notes)
    return (
        mixed, state_next, conv_x_next.transpose(1, 0, 2), conv_bc_next.transpose(1, 0, 2), pool_next[:, None]
    )


def solution(mesh):
    in_specs = (
        P(None, "rows"),
        P(),
        P(),
        P(),
        P(),
        P("rows", "cols", None, None),
        P("rows", "cols", None, None),
        P("rows", "cols", None, None),
        P("rows", None, "cols"),
        P("rows", None, None),
        P("rows"),
        P("rows", "cols"),
        P("rows", "cols"),
        P("rows", "cols"),
        P("rows", None),
        P("rows", None),
        P(None, "cols"),
        P(),
        P("cols"),
        P("cols"),
        P("cols"),
        P("cols", None),
        P("cols", None),
    )
    out_specs = (
        P("rows", "cols"),
        P("rows", "cols", None, None),
        P("rows", None, "cols"),
        P("rows", None, None),
        P("rows", "cols", None, None),
    )
    return jax.shard_map(local, mesh=mesh, in_specs=in_specs, out_specs=out_specs, check_vma=False)
```

```python
import functools

import jax
import jax.numpy as jnp
from jax import lax
from jax.experimental import pallas as pl
from jax.experimental.pallas import tpu as pltpu
from jax.sharding import PartitionSpec as P

HP = 64
NS = 256
KW = 4
QH = 8
KVH = 2
HD = 128
PAGE = 32
LANES = 128
BLOCK = 16

EPSILON = 1e-05
FLOOR_SCORE = -1e30
FIRST_LIMIT = 60 * 1024 * 1024
VMEM_LIMIT = 57 * 1024 * 1024

F32 = jnp.float32
BF16 = jnp.bfloat16
I32 = jnp.int32

SMEM_SPEC = pl.BlockSpec(memory_space=pltpu.SMEM)
BRIEF = pl.CostEstimate(flops=1, bytes_accessed=1, transcendentals=0)
VMEM_SPEC = pl.BlockSpec(memory_space=pltpu.VMEM)
ANY_SPEC = pl.BlockSpec(memory_space=pl.ANY)


def silu(v):
    return v / (1.0 + jnp.exp(-v))


def dot(a, b):
    return jnp.dot(a, b, preferred_element_type=F32)


def dot_t(a, b):
    return lax.dot_general(a, b, (((1,), (1,)), ((), ())), preferred_element_type=F32)


def row_iota(shape):
    return lax.broadcasted_iota(I32, shape, 0)


def lane_iota(shape):
    return lax.broadcasted_iota(I32, shape, 1)


class Columns:
    def __init__(self, inner):
        self.z = 0
        self.x = inner
        self.bc = 2 * inner
        self.q = self.bc + 2 * NS
        self.kv = self.q + QH * HD
        self.tail = self.kv + 2 * KVH * HD
        self.width = self.tail + 2 * LANES


class Plan:
    def __init__(self, slots, moves):
        self.length = 0
        self.slot = slots
        self.target = self.slot + moves
        self.away = self.target + moves
        self.source = self.away + moves
        self.from_away = self.source + moves
        self.arrived_length = self.from_away + moves
        self.stay = self.arrived_length + moves
        self.size = self.stay + slots - moves


class Note:
    mixed, key_value, drive, drive_low, mixing, conv_x, conv_bc = 0, 1, 2, 3, 4, 5, 8
    decay, decay_low = NS, NS + LANES


def project_kernel(
    row_ref, arrival, lengths, move_slot, move_target,
    tokens, gain, w_z, w_x, w_dt, w_bc, w_qkv,
    plan, mine, theirs,
    inverse, wide, picked, tail,
    *, slots,
):
    moves, row_count = move_slot.shape
    heads, depth = w_dt.shape
    inner = heads * HP
    cols, at = Columns(inner), Plan(slots, moves)
    me, half = row_ref[0], row_count // 2

    wide[...] = tokens[...].astype(F32)
    picked[...] = jnp.zeros_like(picked)

    def invert(t, carry):
        for s in range(slots):
            inverse[arrival[t * slots + s]] = t * slots + s
        return carry

    lax.fori_loop(0, row_count, invert, 0)

    def pick(b, carry):
        d = jnp.where(b < half, 2 * b, 2 * (b - half) + 1)
        first = lax.bitwise_xor(me, d) * slots
        for s in range(slots):
            picked[pl.ds(b * BLOCK + s, 1), :] = wide[pl.ds(inverse[first + s], 1), :]
        return carry

    lax.fori_loop(0, row_count, pick, 0)

    rows = picked[...]
    squares = jnp.sum(rows * rows, axis=1, keepdims=True)
    scaled = (rows * gain[...].astype(F32).reshape(1, depth)).astype(BF16)

    def put(start, value):
        span = slice(start, start + value.shape[1])
        mine[:, span] = value[: half * BLOCK].astype(F32)
        theirs[:, span] = value[half * BLOCK :].astype(BF16)

    put(cols.z, dot(scaled, w_z[...]))
    put(cols.x, dot(scaled, w_x[...]))
    put(cols.bc, dot(scaled, w_bc[...]))
    put(cols.q, dot(scaled, w_qkv[...]))
    tail[...] = jnp.zeros_like(tail)
    tail[:, :heads] = dot_t(scaled, w_dt[...])
    tail[:, heads : heads + 1] = squares
    high = tail[...].astype(BF16)
    put(cols.tail, high)
    put(cols.tail + LANES, tail[...] - high.astype(F32))

    stays = 0
    for s in range(slots):
        plan[at.length + s] = lengths[me * slots + s]
        leaves = move_slot[0, me] == s
        for m in range(1, moves):
            leaves = jnp.logical_or(leaves, move_slot[m, me] == s)

        @pl.when(jnp.logical_not(leaves))
        def _(s=s, stays=stays):
            plan[at.stay + stays] = s

        stays = stays + jnp.where(leaves, 0, 1)
    for m in range(moves):
        plan[at.slot + m] = move_slot[m, me]
        plan[at.target + m] = move_target[m, me]
        plan[at.away + m] = lax.bitwise_xor(move_target[m, me], me)

    def seek(i, turn):
        for m in range(moves):
            comes = move_target[m, i] == me

            @pl.when(comes)
            def _(m=m, turn=turn):
                plan[at.source + turn] = i
                plan[at.from_away + turn] = lax.bitwise_xor(i, me)
                plan[at.arrived_length + turn] = lengths[i * slots + move_slot[m, i]]

            turn = turn + jnp.where(comes, 1, 0)
        return turn

    lax.fori_loop(0, row_count, seek, I32(0))


def pack_kernel(plan, table, pool, state, *rest, moves, row_count):
    pages_here, slots = table.shape
    at = Plan(slots, moves)
    parcels = rest[: row_count - 1]
    packed, in_sems, out_sems = rest[row_count - 1 :]
    loads = []
    for m in range(moves):
        slot = plan[at.slot + m]
        loads.append([])
        for page in range(pages_here):
            loads[m].append(
                pltpu.make_async_copy(pool.at[table[page, slot]], packed.at[m, page], in_sems.at[m, page])
            )
        for part in range(2):
            loads[m].append(
                pltpu.make_async_copy(
                    state.at[slot, :, part * PAGE : (part + 1) * PAGE, :],
                    packed.at[m, pages_here:, :, part * NS : (part + 1) * NS],
                    in_sems.at[m, pages_here + part],
                )
            )
        for load in loads[m]:
            load.start()
    for m in range(moves):
        for load in loads[m]:
            load.wait()
        for d, parcel in enumerate(parcels, 1):

            @pl.when(plan[at.away + m] == d)
            def _(m=m, parcel=parcel):
                pltpu.make_async_copy(packed.at[m], parcel, out_sems.at[m]).start()

    for m in range(moves):
        pltpu.make_async_copy(packed.at[m], parcels[0], out_sems.at[m]).wait()


def pair_kernel(mine, theirs, own, *others):
    for j, out in enumerate((own,) + others):
        span = slice(j * BLOCK, (j + 1) * BLOCK)
        out[...] = (mine[span, :] + theirs[span, :].astype(F32)).astype(out.dtype)


def widen(per_head, inner):
    rows = per_head.shape[0]
    first = lane_iota((rows, 2 * HP)) < HP
    pieces = []
    for h in range(0, inner // HP, 2):
        pieces.append(jnp.where(first, per_head[:, h : h + 1], per_head[:, h + 1 : h + 2]))
    return pieces[0] if len(pieces) == 1 else jnp.concatenate(pieces, axis=1)


class Sums:
    def __init__(self, received, heads, width):
        self.received = received
        cols = Columns(heads * HP)
        tail = self.total(cols.tail, cols.tail + LANES) + self.total(cols.tail + LANES, cols.width)
        self.root = jnp.sqrt(tail[:, heads : heads + 1] / width + EPSILON)
        self.step_in = (tail[:, :heads] / self.root).astype(BF16).astype(F32)

    def total(self, start, stop):
        return sum(part[:, start:stop].astype(F32) for part in self.received)

    def projected(self, start, stop):
        return (self.total(start, stop) / self.root).astype(BF16).astype(F32)


def insert_row(page, row, offset):
    old = page[...].astype(F32)
    page[...] = jnp.where(row_iota(old.shape) == offset, row, old).astype(BF16)


def place_of(length, col_count):
    logical = lax.div(length, I32(PAGE))
    return lax.rem(logical, I32(col_count)), lax.div(logical, I32(col_count)), lax.rem(length, I32(PAGE))


def attend_kernel(
    col_ref, plan, table, pool, *rest, moves, heads, chip_count, col_count, width
):
    received, (pool_next, kv_new, send) = rest[:chip_count], rest[chip_count : chip_count + 3]
    pages, queries, scores, weighted, peaks, totals, in_sems, out_sems = rest[chip_count + 3 :]
    pages_here, slots = table.shape
    cols, at = Columns(heads * HP), Plan(slots, moves)
    col = col_ref[0]
    tokens_here = pages_here * PAGE
    kv_width = KVH * HD
    loads = []
    for s in range(slots):
        for page in range(pages_here):
            loads.append(
                pltpu.make_async_copy(pool.at[table[page, s]], pages.at[s, page], in_sems.at[s, page])
            )
            loads[-1].start()

    sums = Sums(received, heads, width)
    kv_new[...] = sums.projected(cols.kv, cols.tail)
    q_in = sums.projected(cols.q, cols.kv)
    for h in range(QH):
        queries[pl.ds(h, BLOCK, stride=QH), :] = q_in[:, h * HD : (h + 1) * HD]

    first_group = row_iota((QH, HD)) < QH // KVH
    lane = lane_iota((QH, tokens_here))
    position = (lax.shift_right_logical(lane, 5) * col_count + col) * PAGE + lax.bitwise_and(lane, PAGE - 1)
    for s in range(slots):
        for load in loads[s * pages_here : (s + 1) * pages_here]:
            load.wait()
        length = plan[at.length + s]
        owner, local_page, offset = place_of(length, col_count)

        @pl.when(owner == col)
        def _(s=s, local_page=local_page, offset=offset):
            insert_row(pages.at[s, local_page], kv_new[s : s + 1, :], offset)

        keys = pages[s, :, :, :kv_width].reshape(tokens_here, kv_width)
        query = queries[s * QH : (s + 1) * QH, :]
        query = jnp.concatenate(
            [jnp.where(first_group, query, 0.0), jnp.where(first_group, 0.0, query)], axis=1
        ).astype(BF16)
        score = dot_t(query, keys) * (HD ** -0.5)
        scores[s * QH : (s + 1) * QH, :] = jnp.where(position <= length, score, FLOOR_SCORE)

    stores = []
    for j in range(slots - moves):
        slot = plan[at.stay + j]
        for page in range(pages_here):
            stores.append(
                pltpu.make_async_copy(
                    pages.at[slot, page], pool_next.at[table[page, slot]], out_sems.at[j, page]
                )
            )
            stores[-1].start()

    live_rows = slots * QH
    everything = scores[0:live_rows, :]
    peak = jnp.max(everything, axis=1, keepdims=True)
    weights = jnp.where(everything > 0.5 * FLOOR_SCORE, jnp.exp(everything - peak), 0.0)
    total = jnp.sum(weights, axis=1, keepdims=True)
    scores[0:live_rows, :] = weights
    for ref, value in ((weighted, None), (peaks, peak), (totals, total)):
        ref[live_rows:, :] = jnp.zeros((BLOCK * QH - live_rows, HD), F32)
        if value is not None:
            ref[0:live_rows, :] = jnp.broadcast_to(value, (live_rows, HD))
    for s in range(slots):
        values = pages[s, :, :, kv_width:].reshape(tokens_here, kv_width)
        weight = scores[s * QH : (s + 1) * QH, :]
        high = weight.astype(BF16).astype(F32)
        both = dot(jnp.concatenate([high, weight - high], axis=0).astype(BF16), values)
        joined = both[:QH] + both[QH:]
        weighted[s * QH : (s + 1) * QH, :] = jnp.where(first_group, joined[:, :HD], joined[:, HD:])

    share = QH * HD // col_count
    part = min(share, HD)
    lanes = lane_iota((BLOCK, LANES))
    for c in range(col_count):
        block = slice(c * BLOCK, (c + 1) * BLOCK)
        stats = jnp.zeros((BLOCK, LANES), F32)
        for j in range(share // part):
            head, begin = divmod(c * share + j * part, HD)
            rows = pl.ds(head, BLOCK, stride=QH)
            send[block, j * part : (j + 1) * part] = weighted[rows, :][:, begin : begin + part]
            stats = jnp.where(lanes == 2 * j, peaks[rows, :], stats)
            stats = jnp.where(lanes == 2 * j + 1, totals[rows, :], stats)
        send[block, share:] = stats
    for store in stores:
        store.wait()


def mix_kernel(
    plan, conv_x, conv_bc, cw_x, cw_bc, dt_bias, a_log, d_skip, state, *rest, moves, chip_count, width
):
    received = rest[:chip_count]
    conv_x_next, conv_bc_next, state_next, gated, driven_out, decay, b_out = rest[chip_count : chip_count + 7]
    readout, held, made, drive, b_twice, in_sems, out_sems = rest[chip_count + 7 :]
    slots, inner = conv_x.shape[1], conv_x.shape[2]
    heads = dt_bias.shape[0]
    cols, at = Columns(inner), Plan(slots, moves)
    loads = []
    for s in range(slots):
        loads.append(pltpu.make_async_copy(state.at[s], held.at[s], in_sems.at[s]))
        loads[-1].start()

    sums = Sums(received, heads, width)

    def convolved(past, taps, fresh, following):
        past_rows = [past[k].astype(F32) for k in range(KW - 1)]
        total = fresh[:slots] * taps[KW - 1 : KW, :].astype(F32)
        for k in range(KW - 1):
            total = total + past_rows[k] * taps[k : k + 1, :].astype(F32)
            following[k] = past_rows[k + 1] if k < KW - 2 else fresh[:slots]
        return jnp.concatenate([silu(total), jnp.zeros((BLOCK - slots, total.shape[1]), F32)], axis=0)

    value_act = convolved(conv_x, cw_x, sums.projected(cols.x, cols.bc), conv_x_next)
    bc_act = convolved(conv_bc, cw_bc, sums.projected(cols.bc, cols.q), conv_bc_next)
    bc_act = bc_act.astype(BF16).astype(F32)
    b_in, c_val = bc_act[:, :NS], bc_act[:, NS:]
    b_out[...] = b_in
    b_twice[...] = jnp.concatenate([b_in, b_in], axis=0)
    c_out = c_val.astype(BF16)

    shifted = sums.step_in + dt_bias[...].reshape(1, heads)
    step_size = jnp.maximum(shifted, 0.0) + jnp.log(1.0 + jnp.exp(-jnp.abs(shifted)))
    rate = jnp.exp(-jnp.exp(a_log[...].reshape(1, heads)) * step_size)
    decay[...] = rate
    driven = widen(step_size, inner) * value_act
    driven_out[...] = driven
    high = driven.astype(BF16).astype(F32)
    drive[...] = jnp.transpose(jnp.concatenate([high, driven - high], axis=0)).astype(BF16)

    readout[...] = jnp.zeros_like(readout)

    for s in range(slots):
        loads[s].wait()
        value = dot_t(c_out, held[s].reshape(inner, NS))
        readout[s : s + 1, :] = value[s : s + 1]

    stores = []
    for j in range(slots - moves):
        slot = plan[at.stay + j]
        advance_state(slot, held.at[slot], b_twice, drive, decay, made.at[j])
        stores.append(pltpu.make_async_copy(made.at[j], state_next.at[slot], out_sems.at[j]))
        stores[-1].start()

    gate = silu(sums.projected(cols.z, cols.x))
    b_dot_c = jnp.sum(b_in * c_val, axis=1, keepdims=True)
    skip = widen(jnp.broadcast_to(d_skip[...].reshape(1, heads), (BLOCK, heads)), inner)
    total = widen(rate, inner) * readout[...] + driven * b_dot_c + skip * value_act
    gated[...] = (total * gate).astype(BF16).astype(F32)
    for store in stores:
        store.wait()


def advance_state(slot, prior, b_twice, drive, decay, result):
    heads = result.shape[0]
    twice = b_twice[...]
    half = twice.shape[0] // 2
    row = row_iota(twice.shape)
    selected = jnp.where((row == slot) | (row == slot + half), twice, 0.0).astype(BF16)
    outer = dot(drive[...], selected).reshape(heads, HP, NS)
    for h in range(heads):
        rate = decay[pl.ds(slot, 1), h : h + 1]
        result[h] = (rate * prior[h].astype(F32) + outer[h]).astype(BF16)


def output_kernel(gated, w_ssm, w_attn, partials, send, *, slots, col_count):
    share = w_attn.shape[0]
    part = min(share, HD)
    blocks = [partials[c * BLOCK : (c + 1) * BLOCK, :] for c in range(col_count)]
    pieces = []
    for j in range(share // part):
        peaks = [b[:, share + 2 * j : share + 2 * j + 1] for b in blocks]
        joint = functools.reduce(jnp.maximum, peaks)
        factors = [jnp.exp(p - joint) for p in peaks]
        total = sum(f * b[:, share + 2 * j + 1 : share + 2 * j + 2] for f, b in zip(factors, blocks))
        value = sum(f * b[:, j * part : (j + 1) * part] for f, b in zip(factors, blocks))
        pieces.append(value / total)
    joined = pieces[0] if len(pieces) == 1 else jnp.concatenate(pieces, axis=1)
    right = jnp.where(row_iota(joined.shape) < slots, joined, 0.0).astype(BF16)
    left = gated[...].astype(BF16)
    columns = w_ssm.shape[1] // col_count
    for c in range(col_count):
        span = slice(c * columns, (c + 1) * columns)
        send[c * BLOCK : (c + 1) * BLOCK, :] = dot(left, w_ssm[:, span]) + dot(right, w_attn[:, span])


def total_kernel(
    plan, kv_new, driven, decay, b_in, conv_x, conv_bc, terms, mixed, send, block, *, moves, col_count
):
    at = Plan(conv_x.shape[1], moves)
    total = sum(terms[c * BLOCK : (c + 1) * BLOCK, :] for c in range(col_count))
    mixed[...] = total.astype(BF16).astype(F32)

    block[...] = jnp.zeros_like(block)
    for m in range(moves):
        row = pl.ds(plan[at.slot + m], 1)

        def put(index, value, start=0):
            block[index : index + 1, start : start + value.shape[1]] = value

        put(Note.mixed, mixed[row, :])
        put(Note.key_value, kv_new[row, :])
        for index, value, start, low_index, low_start in (
            (Note.drive, driven[row, :], 0, Note.drive_low, 0),
            (Note.mixing, decay[row, :], Note.decay, Note.mixing, Note.decay_low),
        ):
            high = value.astype(BF16).astype(F32)
            put(index, high, start)
            put(low_index, value - high, low_start)
        put(Note.mixing, b_in[row, :])
        for k in range(KW - 1):
            put(Note.conv_x + k, conv_x[k, row, :])
            put(Note.conv_bc + k, conv_bc[k, row, :])
        start = pl.multiple_of(plan[at.target + m] * BLOCK, BLOCK)
        send[pl.ds(start, BLOCK), :] = block[...].astype(BF16)


def arrive_kernel(
    col_ref, plan, table, mixed_home, conv_x, conv_bc, state_in, pool_in, notes, *rest,
    moves, row_count, col_count,
):
    del state_in, pool_in
    parcels, rest = rest[: row_count - 1], rest[row_count - 1 :]
    pages_here, slots = table.shape
    inner = conv_x.shape[2]
    heads = inner // HP
    at = Plan(slots, moves)
    mixed, conv_x_next, conv_bc_next, state_next, pool_next = rest[:5]
    packed, made, drive, decay, b_twice, window_x, window_bc, window_mixed, in_sems, out_sems = rest[5:]
    col = col_ref[0]
    for m in range(moves):
        for d, parcel in enumerate(parcels, 1):

            @pl.when(plan[at.from_away + m] == d)
            def _(m=m, parcel=parcel):
                pltpu.make_async_copy(parcel, packed.at[m], in_sems.at[m]).start()


    for k in range(KW - 1):
        window_x[k] = conv_x[k]
        window_bc[k] = conv_bc[k]
    window_mixed[...] = mixed_home[...]
    rows = []
    b_twice[...] = jnp.zeros_like(b_twice)
    half = b_twice.shape[0] // 2
    for m in range(moves):
        start = pl.multiple_of(plan[at.source + m] * BLOCK, BLOCK)
        note = notes[pl.ds(start, BLOCK), :].astype(F32)
        rows.append(note)
        row = pl.ds(plan[at.slot + m], 1)
        window_mixed[row, :] = note[Note.mixed : Note.mixed + 1, : window_mixed.shape[1]]
        for k in range(KW - 1):
            window_x[k, row, :] = note[Note.conv_x + k : Note.conv_x + k + 1, :inner]
            window_bc[k, row, :] = note[Note.conv_bc + k : Note.conv_bc + k + 1, : 2 * NS]
        mixing = note[Note.mixing : Note.mixing + 1, :]
        b_twice[m : m + 1, :] = mixing[:, :NS]
        b_twice[half + m : half + m + 1, :] = mixing[:, :NS]
        decay[m : m + 1, :] = (
            mixing[:, Note.decay : Note.decay + heads] + mixing[:, Note.decay_low : Note.decay_low + heads]
        )
    padding = [jnp.zeros((half - moves, inner), F32)]
    stacked = [note[Note.drive : Note.drive + 1, :inner] for note in rows] + padding
    stacked += [note[Note.drive_low : Note.drive_low + 1, :inner] for note in rows] + padding
    drive[...] = jnp.transpose(jnp.concatenate(stacked, axis=0)).astype(BF16)
    mixed[...] = window_mixed[0:slots, :].astype(BF16)
    for k in range(KW - 1):
        conv_x_next[k] = window_x[k].astype(BF16)
        conv_bc_next[k] = window_bc[k].astype(BF16)

    stores = []
    for m in range(moves):
        slot = plan[at.slot + m]
        pltpu.make_async_copy(parcels[0], packed.at[m], in_sems.at[m]).wait()
        owner, local_page, offset = place_of(plan[at.arrived_length + m], col_count)
        key_value = rows[m][Note.key_value : Note.key_value + 1, : 2 * KVH * HD]

        @pl.when(owner == col)
        def _(m=m, local_page=local_page, offset=offset, key_value=key_value):
            insert_row(packed.at[m, local_page], key_value, offset)

        for page in range(pages_here):
            stores.append(
                pltpu.make_async_copy(
                    packed.at[m, page], pool_next.at[table[page, slot]], out_sems.at[m, page]
                )
            )
            stores[-1].start()
        prior = [
            jnp.concatenate([packed[m, pages_here + h, :, :NS], packed[m, pages_here + h, :, NS:]], axis=0)
            for h in range(heads)
        ]
        advance_state(m, prior, b_twice, drive, decay, made.at[m])
        stores.append(pltpu.make_async_copy(made.at[m], state_next.at[slot], out_sems.at[m, pages_here]))
        stores[-1].start()
    for store in stores:
        store.wait()


def shape(dims, dtype):
    return jax.ShapeDtypeStruct(tuple(dims), dtype)


def params(limit=VMEM_LIMIT):
    return pltpu.CompilerParams(vmem_limit_bytes=limit)


def exchange(value, axis):
    return lax.all_to_all(value, axis, split_axis=0, concat_axis=0, tiled=True)


def trade(block, axis, d):
    return lax.ppermute(block, axis, [(i, i ^ d) for i in range(lax.axis_size(axis))])


def ordered(value, first):
    return lax.optimization_barrier((value, first))[0]


def local(
    tokens, arrival, cache_lengths, move_slot, move_target, page_table, kv_pool, ssm_state,
    conv_x, conv_bc, norm_gain, weight_z, weight_x, weight_dt, weight_bc, weight_qkv,
    conv_weight_x, conv_weight_bc, dt_bias, a_log, d_skip, weight_ssm_out, weight_attn_out,
):
    row_count = lax.axis_size("rows")
    col_count = lax.axis_size("cols")
    row_index = lax.axis_index("rows").astype(I32).reshape(1)
    col_index = lax.axis_index("cols").astype(I32).reshape(1)
    slots, heads = ssm_state.shape[0], ssm_state.shape[1]
    total, depth = tokens.shape
    moves = move_slot.shape[1]
    pages_here, width = page_table.shape[3], kv_pool.shape[3]
    inner = heads * HP
    stays = slots - moves
    cols, at = Columns(inner), Plan(slots, moves)
    table = page_table[0, 0].T
    pool = kv_pool[:, 0]
    past_x, past_bc = conv_x.transpose(1, 0, 2), conv_bc.transpose(1, 0, 2)
    rows = row_count * BLOCK
    model = depth * row_count
    share = QH * HD // col_count
    parcel = (pages_here + heads, PAGE, width)
    parcels_here = pltpu.VMEM((moves,) + parcel, BF16)

    chip_count = row_count // 2
    plan, mine, theirs = pl.pallas_call(
        functools.partial(project_kernel, slots=slots),
        out_shape=[
            shape((at.size,), I32),
            shape((chip_count * BLOCK, cols.width), F32),
            shape((chip_count * BLOCK, cols.width), BF16),
        ],
        in_specs=[SMEM_SPEC] * 5 + [VMEM_SPEC] * 7,
        out_specs=[SMEM_SPEC] + [VMEM_SPEC] * 2,
        scratch_shapes=[
            pltpu.SMEM((total,), I32),
            pltpu.VMEM((total, depth), F32),
            pltpu.VMEM((rows, depth), F32),
            pltpu.VMEM((rows, LANES), F32),
        ],
        compiler_params=params(FIRST_LIMIT),
        cost_estimate=BRIEF,
        name="project",
    )(
        row_index, arrival, cache_lengths, move_slot.T, move_target.T,
        tokens, norm_gain, weight_z, weight_x, weight_dt.T, weight_bc, weight_qkv,
    )
    parcels = pl.pallas_call(
        functools.partial(pack_kernel, moves=moves, row_count=row_count),
        out_shape=[shape(parcel, BF16)] * (row_count - 1),
        in_specs=[SMEM_SPEC] * 2 + [ANY_SPEC] * 2,
        out_specs=[ANY_SPEC] * (row_count - 1),
        scratch_shapes=[
            parcels_here,
            pltpu.SemaphoreType.DMA((moves, pages_here + 2)),
            pltpu.SemaphoreType.DMA((moves,)),
        ],
        compiler_params=params(FIRST_LIMIT),
        cost_estimate=BRIEF,
        name="pack",
    )(plan, table, pool, ssm_state)

    sums = pl.pallas_call(
        pair_kernel,
        out_shape=[shape((BLOCK, cols.width), F32)] + [shape((BLOCK, cols.width), BF16)] * (chip_count - 1),
        in_specs=[VMEM_SPEC] * 2,
        out_specs=[VMEM_SPEC] * chip_count,
        compiler_params=params(FIRST_LIMIT),
        cost_estimate=BRIEF,
        name="pair",
    )(mine, trade(theirs, "rows", 1))
    received = [sums[0]] + [trade(block, "rows", 2 * j) for j, block in enumerate(sums[1:], 1)]

    order = [d for j in range(2) for d in range(2 + j, row_count, 2)] + [1]
    early = order[:-2]
    moving = {d: parcels[d - 1] for d in order}
    for d in early:
        moving[d] = ordered(moving[d], received)

    pool_next, kv_new, partials = pl.pallas_call(
        functools.partial(
            attend_kernel, moves=moves, heads=heads, chip_count=chip_count, col_count=col_count, width=model
        ),
        out_shape=[
            shape(pool.shape, BF16),
            shape((BLOCK, 2 * KVH * HD), F32),
            shape((col_count * BLOCK, share + LANES), F32),
        ],
        in_specs=[SMEM_SPEC] * 3 + [ANY_SPEC] + [VMEM_SPEC] * chip_count,
        out_specs=[ANY_SPEC] + [VMEM_SPEC] * 2,
        scratch_shapes=[
            pltpu.VMEM((slots, pages_here, PAGE, width), BF16),
            pltpu.VMEM((BLOCK * QH, HD), F32),
            pltpu.VMEM((BLOCK * QH, pages_here * PAGE), F32),
            pltpu.VMEM((BLOCK * QH, HD), F32),
            pltpu.VMEM((BLOCK * QH, HD), F32),
            pltpu.VMEM((BLOCK * QH, HD), F32),
            pltpu.SemaphoreType.DMA((slots, pages_here)),
            pltpu.SemaphoreType.DMA((stays, pages_here)),
        ],
        compiler_params=params(),
        cost_estimate=BRIEF,
        name="attend",
    )(col_index, plan, table, pool, *received)
    received = ordered(received, partials)
    partials = exchange(partials, "cols")

    next_x, next_bc, state_next, gated, driven, decay, b_in = pl.pallas_call(
        functools.partial(mix_kernel, moves=moves, chip_count=chip_count, width=model),
        out_shape=(
            shape(past_x.shape, F32),
            shape(past_bc.shape, F32),
            shape(ssm_state.shape, BF16),
            shape((BLOCK, inner), F32),
            shape((BLOCK, inner), F32),
            shape((BLOCK, heads), F32),
            shape((BLOCK, NS), F32),
        ),
        in_specs=[SMEM_SPEC] + [VMEM_SPEC] * 7 + [ANY_SPEC] + [VMEM_SPEC] * chip_count,
        out_specs=(VMEM_SPEC, VMEM_SPEC, ANY_SPEC) + (VMEM_SPEC,) * 4,
        scratch_shapes=[
            pltpu.VMEM((BLOCK, inner), F32),
            pltpu.VMEM((slots, heads, HP, NS), BF16),
            pltpu.VMEM((stays, heads, HP, NS), BF16),
            pltpu.VMEM((inner, 2 * BLOCK), BF16),
            pltpu.VMEM((2 * BLOCK, NS), F32),
            pltpu.SemaphoreType.DMA((slots,)),
            pltpu.SemaphoreType.DMA((stays,)),
        ],
        compiler_params=params(),
        cost_estimate=BRIEF,
        name="mix",
    )(plan, past_x, past_bc, conv_weight_x, conv_weight_bc, dt_bias, a_log, d_skip, ssm_state, *received)

    columns = weight_ssm_out.shape[1] // col_count
    terms = pl.pallas_call(
        functools.partial(output_kernel, slots=slots, col_count=col_count),
        out_shape=shape((col_count * BLOCK, columns), F32),
        in_specs=[VMEM_SPEC] * 4,
        out_specs=VMEM_SPEC,
        compiler_params=params(),
        cost_estimate=BRIEF,
        name="output",
    )(gated, weight_ssm_out, weight_attn_out, partials)
    for d in order[-2:]:
        moving[d] = ordered(moving[d], terms)
    parcels = [trade(moving[d], "rows", d) for d in range(1, row_count)]
    terms = exchange(terms, "cols")

    note = (BLOCK, max(inner, 2 * NS, 2 * KVH * HD, columns))
    mixed_home, notes = pl.pallas_call(
        functools.partial(total_kernel, moves=moves, col_count=col_count),
        out_shape=[shape((BLOCK, columns), F32), shape((rows, note[1]), BF16)],
        in_specs=[SMEM_SPEC] + [VMEM_SPEC] * 7,
        out_specs=[VMEM_SPEC] * 2,
        scratch_shapes=[pltpu.VMEM(note, F32)],
        compiler_params=params(),
        cost_estimate=BRIEF,
        name="total",
    )(plan, kv_new, driven, decay, b_in, next_x, next_bc, terms)
    notes = exchange(notes, "rows")

    mixed, conv_x_next, conv_bc_next, state_next, pool_next = pl.pallas_call(
        functools.partial(arrive_kernel, moves=moves, row_count=row_count, col_count=col_count),
        out_shape=(
            shape((slots, columns), BF16),
            shape(past_x.shape, BF16),
            shape(past_bc.shape, BF16),
            shape(ssm_state.shape, BF16),
            shape(pool.shape, BF16),
        ),
        in_specs=[SMEM_SPEC] * 3 + [VMEM_SPEC] * 3 + [ANY_SPEC] * 2 + [VMEM_SPEC] + [ANY_SPEC] * (row_count - 1),
        out_specs=[VMEM_SPEC] * 3 + [ANY_SPEC] * 2,
        scratch_shapes=[
            parcels_here,
            pltpu.VMEM((moves, heads, HP, NS), BF16),
            pltpu.VMEM((inner, 2 * BLOCK), BF16),
            pltpu.VMEM((BLOCK, heads), F32),
            pltpu.VMEM((2 * BLOCK, NS), F32),
            pltpu.VMEM((KW - 1, slots, inner), F32),
            pltpu.VMEM((KW - 1, slots, 2 * NS), F32),
            pltpu.VMEM((BLOCK, columns), F32),
            pltpu.SemaphoreType.DMA((moves,)),
            pltpu.SemaphoreType.DMA((moves, pages_here + 1)),
        ],
        input_output_aliases={6: 3, 7: 4},
        compiler_params=params(),
        cost_estimate=BRIEF,
        name="arrive",
    )(col_index, plan, table, mixed_home, next_x, next_bc, state_next, pool_next, notes, *parcels)
    return (
        mixed, state_next, conv_x_next.transpose(1, 0, 2), conv_bc_next.transpose(1, 0, 2), pool_next[:, None]
    )


def solution(mesh):
    in_specs = (
        P(None, "rows"),
        P(),
        P(),
        P(),
        P(),
        P("rows", "cols", None, None),
        P("rows", "cols", None, None),
        P("rows", "cols", None, None),
        P("rows", None, "cols"),
        P("rows", None, None),
        P("rows"),
        P("rows", "cols"),
        P("rows", "cols"),
        P("rows", "cols"),
        P("rows", None),
        P("rows", None),
        P(None, "cols"),
        P(),
        P("cols"),
        P("cols"),
        P("cols"),
        P("cols", None),
        P("cols", None),
    )
    out_specs = (
        P("rows", "cols"),
        P("rows", "cols", None, None),
        P("rows", None, "cols"),
        P("rows", None, None),
        P("rows", "cols", None, None),
    )
    return jax.shard_map(local, mesh=mesh, in_specs=in_specs, out_specs=out_specs, check_vma=False)
```

```python
import functools

import jax
import jax.numpy as jnp
from jax import lax
from jax.experimental import pallas as pl
from jax.experimental.pallas import tpu as pltpu
from jax.sharding import PartitionSpec as P

HP = 64
NS = 256
KW = 4
QH = 8
KVH = 2
HD = 128
PAGE = 32
LANES = 128
BLOCK = 16

EPSILON = 1e-05
FLOOR_SCORE = -1e30
FIRST_LIMIT = 60 * 1024 * 1024
VMEM_LIMIT = 57 * 1024 * 1024

F32 = jnp.float32
BF16 = jnp.bfloat16
I32 = jnp.int32

SMEM_SPEC = pl.BlockSpec(memory_space=pltpu.SMEM)
BRIEF = pl.CostEstimate(flops=1, bytes_accessed=1, transcendentals=0)
VMEM_SPEC = pl.BlockSpec(memory_space=pltpu.VMEM)
ANY_SPEC = pl.BlockSpec(memory_space=pl.ANY)


def silu(v):
    return v / (1.0 + jnp.exp(-v))


def dot(a, b):
    return jnp.dot(a, b, preferred_element_type=F32)


def dot_t(a, b):
    return lax.dot_general(a, b, (((1,), (1,)), ((), ())), preferred_element_type=F32)


def row_iota(shape):
    return lax.broadcasted_iota(I32, shape, 0)


def lane_iota(shape):
    return lax.broadcasted_iota(I32, shape, 1)


class Columns:
    def __init__(self, inner):
        self.z = 0
        self.x = inner
        self.bc = 2 * inner
        self.q = self.bc + 2 * NS
        self.kv = self.q + QH * HD
        self.tail = self.kv + 2 * KVH * HD
        self.width = self.tail + 2 * LANES


class Plan:
    def __init__(self, slots, moves):
        self.length = 0
        self.slot = slots
        self.target = self.slot + moves
        self.away = self.target + moves
        self.source = self.away + moves
        self.from_away = self.source + moves
        self.arrived_length = self.from_away + moves
        self.stay = self.arrived_length + moves
        self.size = self.stay + slots - moves


class Note:
    mixed, key_value, drive, drive_low, mixing, conv_x, conv_bc = 0, 1, 2, 3, 4, 5, 8
    decay, decay_low = NS, NS + LANES


def project_kernel(
    row_ref, arrival, lengths, move_slot, move_target,
    tokens, gain, w_z, w_x, w_dt, w_bc, w_qkv,
    plan, mine, theirs,
    inverse, wide, picked, tail,
    *, slots,
):
    moves, row_count = move_slot.shape
    heads, depth = w_dt.shape
    inner = heads * HP
    cols, at = Columns(inner), Plan(slots, moves)
    me, half = row_ref[0], row_count // 2

    wide[...] = tokens[...].astype(F32)
    picked[...] = jnp.zeros_like(picked)

    def invert(t, carry):
        for s in range(slots):
            inverse[arrival[t * slots + s]] = t * slots + s
        return carry

    lax.fori_loop(0, row_count, invert, 0)

    def pick(b, carry):
        d = jnp.where(b < half, 2 * b, 2 * (b - half) + 1)
        first = lax.bitwise_xor(me, d) * slots
        for s in range(slots):
            picked[pl.ds(b * BLOCK + s, 1), :] = wide[pl.ds(inverse[first + s], 1), :]
        return carry

    lax.fori_loop(0, row_count, pick, 0)

    rows = picked[...]
    squares = jnp.sum(rows * rows, axis=1, keepdims=True)
    scaled = (rows * gain[...].astype(F32).reshape(1, depth)).astype(BF16)

    def put(start, value):
        span = slice(start, start + value.shape[1])
        mine[:, span] = value[: half * BLOCK].astype(F32)
        theirs[:, span] = value[half * BLOCK :].astype(BF16)

    put(cols.z, dot(scaled, w_z[...]))
    put(cols.x, dot(scaled, w_x[...]))
    put(cols.bc, dot(scaled, w_bc[...]))
    put(cols.q, dot(scaled, w_qkv[...]))
    tail[...] = jnp.zeros_like(tail)
    tail[:, :heads] = dot_t(scaled, w_dt[...])
    tail[:, heads : heads + 1] = squares
    high = tail[...].astype(BF16)
    put(cols.tail, high)
    put(cols.tail + LANES, tail[...] - high.astype(F32))

    stays = 0
    for s in range(slots):
        plan[at.length + s] = lengths[me * slots + s]
        leaves = move_slot[0, me] == s
        for m in range(1, moves):
            leaves = jnp.logical_or(leaves, move_slot[m, me] == s)

        @pl.when(jnp.logical_not(leaves))
        def _(s=s, stays=stays):
            plan[at.stay + stays] = s

        stays = stays + jnp.where(leaves, 0, 1)
    for m in range(moves):
        plan[at.slot + m] = move_slot[m, me]
        plan[at.target + m] = move_target[m, me]
        plan[at.away + m] = lax.bitwise_xor(move_target[m, me], me)

    def seek(i, turn):
        for m in range(moves):
            comes = move_target[m, i] == me

            @pl.when(comes)
            def _(m=m, turn=turn):
                plan[at.source + turn] = i
                plan[at.from_away + turn] = lax.bitwise_xor(i, me)
                plan[at.arrived_length + turn] = lengths[i * slots + move_slot[m, i]]

            turn = turn + jnp.where(comes, 1, 0)
        return turn

    lax.fori_loop(0, row_count, seek, I32(0))


def pack_kernel(plan, table, pool, state, *rest, moves, row_count):
    pages_here, slots = table.shape
    at = Plan(slots, moves)
    parcels = rest[: row_count - 1]
    packed, in_sems, out_sems = rest[row_count - 1 :]
    loads = []
    for m in range(moves):
        slot = plan[at.slot + m]
        loads.append([])
        for page in range(pages_here):
            loads[m].append(
                pltpu.make_async_copy(pool.at[table[page, slot]], packed.at[m, page], in_sems.at[m, page])
            )
        for part in range(2):
            loads[m].append(
                pltpu.make_async_copy(
                    state.at[slot, :, part * PAGE : (part + 1) * PAGE, :],
                    packed.at[m, pages_here:, :, part * NS : (part + 1) * NS],
                    in_sems.at[m, pages_here + part],
                )
            )
        for load in loads[m]:
            load.start()
    for m in range(moves):
        for load in loads[m]:
            load.wait()
        for d, parcel in enumerate(parcels, 1):

            @pl.when(plan[at.away + m] == d)
            def _(m=m, parcel=parcel):
                pltpu.make_async_copy(packed.at[m], parcel, out_sems.at[m]).start()

    for m in range(moves):
        pltpu.make_async_copy(packed.at[m], parcels[0], out_sems.at[m]).wait()


def pair_kernel(mine, theirs, own, *others):
    for j, out in enumerate((own,) + others):
        span = slice(j * BLOCK, (j + 1) * BLOCK)
        out[...] = (mine[span, :] + theirs[span, :].astype(F32)).astype(out.dtype)


def widen(per_head, inner):
    rows = per_head.shape[0]
    first = lane_iota((rows, 2 * HP)) < HP
    pieces = []
    for h in range(0, inner // HP, 2):
        pieces.append(jnp.where(first, per_head[:, h : h + 1], per_head[:, h + 1 : h + 2]))
    return pieces[0] if len(pieces) == 1 else jnp.concatenate(pieces, axis=1)


class Sums:
    def __init__(self, received, heads, width):
        self.received = received
        cols = Columns(heads * HP)
        tail = self.total(cols.tail, cols.tail + LANES) + self.total(cols.tail + LANES, cols.width)
        self.root = jnp.sqrt(tail[:, heads : heads + 1] / width + EPSILON)
        self.step_in = (tail[:, :heads] / self.root).astype(BF16).astype(F32)

    def total(self, start, stop):
        return sum(part[:, start:stop].astype(F32) for part in self.received)

    def projected(self, start, stop):
        return (self.total(start, stop) / self.root).astype(BF16).astype(F32)


def inserted(page, row, offset):
    return jnp.where(row_iota(page.shape) == offset, row, page.astype(F32)).astype(BF16)


def place_of(length, col_count):
    logical = lax.div(length, I32(PAGE))
    return lax.rem(logical, I32(col_count)), lax.div(logical, I32(col_count)), lax.rem(length, I32(PAGE))


def attend_kernel(
    col_ref, plan, table, pool, *rest, moves, heads, chip_count, col_count, width
):
    received, (pool_next, kv_new, send) = rest[:chip_count], rest[chip_count : chip_count + 3]
    pages, queries, scores, weighted, peaks, totals, in_sems, out_sems = rest[chip_count + 3 :]
    pages_here, slots = table.shape
    cols, at = Columns(heads * HP), Plan(slots, moves)
    col = col_ref[0]
    tokens_here = pages_here * PAGE
    kv_width = KVH * HD
    chunks = in_sems.shape[0]
    step = pool.shape[0] // chunks
    spans = [pl.ds(k * step, step) for k in range(chunks)]
    loads = [pltpu.make_async_copy(pool.at[span], pages.at[span], in_sems.at[k]) for k, span in enumerate(spans)]
    for load in loads:
        load.start()

    sums = Sums(received, heads, width)
    kv_new[...] = sums.projected(cols.kv, cols.tail)
    q_in = sums.projected(cols.q, cols.kv)
    for h in range(QH):
        queries[pl.ds(h, BLOCK, stride=QH), :] = q_in[:, h * HD : (h + 1) * HD]

    first_group = row_iota((QH, HD)) < QH // KVH
    lane = lane_iota((QH, tokens_here))
    position = (lax.shift_right_logical(lane, 5) * col_count + col) * PAGE + lax.bitwise_and(lane, PAGE - 1)
    for load in loads:
        load.wait()
    for s in range(slots):
        owner, local_page, offset = place_of(plan[at.length + s], col_count)
        page = table[local_page, s]
        pages[page] = inserted(pages[page], kv_new[s : s + 1, :], jnp.where(owner == col, offset, -1))
    stores = [
        pltpu.make_async_copy(pages.at[span], pool_next.at[span], out_sems.at[k]) for k, span in enumerate(spans)
    ]
    for store in stores:
        store.start()

    def cached(s, start):
        parts = [pages[table[page, s], :, start : start + kv_width] for page in range(pages_here)]
        return jnp.concatenate(parts, axis=0)

    for s in range(slots):
        query = queries[s * QH : (s + 1) * QH, :]
        query = jnp.concatenate(
            [jnp.where(first_group, query, 0.0), jnp.where(first_group, 0.0, query)], axis=1
        ).astype(BF16)
        score = dot_t(query, cached(s, 0)) * (HD ** -0.5)
        scores[s * QH : (s + 1) * QH, :] = jnp.where(position <= plan[at.length + s], score, FLOOR_SCORE)

    live_rows = slots * QH
    everything = scores[0:live_rows, :]
    peak = jnp.max(everything, axis=1, keepdims=True)
    weights = jnp.where(everything > 0.5 * FLOOR_SCORE, jnp.exp(everything - peak), 0.0)
    total = jnp.sum(weights, axis=1, keepdims=True)
    scores[0:live_rows, :] = weights
    for ref, value in ((weighted, None), (peaks, peak), (totals, total)):
        ref[live_rows:, :] = jnp.zeros((BLOCK * QH - live_rows, HD), F32)
        if value is not None:
            ref[0:live_rows, :] = jnp.broadcast_to(value, (live_rows, HD))
    for s in range(slots):
        weight = scores[s * QH : (s + 1) * QH, :]
        high = weight.astype(BF16).astype(F32)
        both = dot(jnp.concatenate([high, weight - high], axis=0).astype(BF16), cached(s, kv_width))
        joined = both[:QH] + both[QH:]
        weighted[s * QH : (s + 1) * QH, :] = jnp.where(first_group, joined[:, :HD], joined[:, HD:])

    share = QH * HD // col_count
    part = min(share, HD)
    lanes = lane_iota((BLOCK, LANES))
    for c in range(col_count):
        block = slice(c * BLOCK, (c + 1) * BLOCK)
        stats = jnp.zeros((BLOCK, LANES), F32)
        for j in range(share // part):
            head, begin = divmod(c * share + j * part, HD)
            rows = pl.ds(head, BLOCK, stride=QH)
            send[block, j * part : (j + 1) * part] = weighted[rows, :][:, begin : begin + part]
            stats = jnp.where(lanes == 2 * j, peaks[rows, :], stats)
            stats = jnp.where(lanes == 2 * j + 1, totals[rows, :], stats)
        send[block, share:] = stats
    for store in stores:
        store.wait()


def mix_kernel(
    conv_x, conv_bc, cw_x, cw_bc, dt_bias, a_log, d_skip, state, *rest, chip_count, width
):
    received = rest[:chip_count]
    conv_x_next, conv_bc_next, gated, driven_out, decay, drive, b_twice = rest[chip_count : chip_count + 7]
    readout, held, in_sems = rest[chip_count + 7 :]
    slots, inner = conv_x.shape[1], conv_x.shape[2]
    heads = dt_bias.shape[0]
    cols = Columns(inner)
    loads = []
    for s in range(slots):
        loads.append(pltpu.make_async_copy(state.at[s], held.at[s], in_sems.at[s]))
        loads[-1].start()

    sums = Sums(received, heads, width)

    def convolved(past, taps, fresh, following):
        past_rows = [past[k].astype(F32) for k in range(KW - 1)]
        total = fresh[:slots] * taps[KW - 1 : KW, :].astype(F32)
        for k in range(KW - 1):
            total = total + past_rows[k] * taps[k : k + 1, :].astype(F32)
            following[k] = past_rows[k + 1] if k < KW - 2 else fresh[:slots]
        return jnp.concatenate([silu(total), jnp.zeros((BLOCK - slots, total.shape[1]), F32)], axis=0)

    value_act = convolved(conv_x, cw_x, sums.projected(cols.x, cols.bc), conv_x_next)
    bc_act = convolved(conv_bc, cw_bc, sums.projected(cols.bc, cols.q), conv_bc_next)
    bc_act = bc_act.astype(BF16).astype(F32)
    b_in, c_val = bc_act[:, :NS], bc_act[:, NS:]
    b_twice[...] = jnp.concatenate([b_in, b_in], axis=0)
    c_out = c_val.astype(BF16)

    shifted = sums.step_in + dt_bias[...].reshape(1, heads)
    step_size = jnp.maximum(shifted, 0.0) + jnp.log(1.0 + jnp.exp(-jnp.abs(shifted)))
    rate = jnp.exp(-jnp.exp(a_log[...].reshape(1, heads)) * step_size)
    decay[...] = rate
    driven = widen(step_size, inner) * value_act
    driven_out[...] = driven
    high = driven.astype(BF16).astype(F32)
    drive[...] = jnp.transpose(jnp.concatenate([high, driven - high], axis=0)).astype(BF16)

    readout[...] = jnp.zeros_like(readout)

    for s in range(slots):
        loads[s].wait()
        value = dot_t(c_out, held[s].reshape(inner, NS))
        readout[s : s + 1, :] = value[s : s + 1]

    gate = silu(sums.projected(cols.z, cols.x))
    b_dot_c = jnp.sum(b_in * c_val, axis=1, keepdims=True)
    skip = widen(jnp.broadcast_to(d_skip[...].reshape(1, heads), (BLOCK, heads)), inner)
    total = widen(rate, inner) * readout[...] + driven * b_dot_c + skip * value_act
    gated[...] = (total * gate).astype(BF16).astype(F32)


def stay_kernel(plan, drive, decay, b_twice, state, state_next, held, made, in_sems, out_sems, *, moves):
    stays = held.shape[0]
    at = Plan(state.shape[0], moves)
    loads = []
    for j in range(stays):
        loads.append(pltpu.make_async_copy(state.at[plan[at.stay + j]], held.at[j], in_sems.at[j]))
        loads[-1].start()
    stores = []
    for j in range(stays):
        slot = plan[at.stay + j]
        loads[j].wait()
        advance_state(slot, held.at[j], b_twice, drive, decay, made.at[j])
        stores.append(pltpu.make_async_copy(made.at[j], state_next.at[slot], out_sems.at[j]))
        stores[-1].start()
    for store in stores:
        store.wait()


def advance_state(slot, prior, b_twice, drive, decay, result):
    heads = result.shape[0]
    twice = b_twice[...]
    half = twice.shape[0] // 2
    row = row_iota(twice.shape)
    selected = jnp.where((row == slot) | (row == slot + half), twice, 0.0).astype(BF16)
    outer = dot(drive[...], selected).reshape(heads, HP, NS)
    for h in range(heads):
        rate = decay[pl.ds(slot, 1), h : h + 1]
        result[h] = (rate * prior[h].astype(F32) + outer[h]).astype(BF16)


def output_kernel(gated, w_ssm, w_attn, partials, send, *, slots, col_count):
    share = w_attn.shape[0]
    part = min(share, HD)
    blocks = [partials[c * BLOCK : (c + 1) * BLOCK, :] for c in range(col_count)]
    pieces = []
    for j in range(share // part):
        peaks = [b[:, share + 2 * j : share + 2 * j + 1] for b in blocks]
        joint = functools.reduce(jnp.maximum, peaks)
        factors = [jnp.exp(p - joint) for p in peaks]
        total = sum(f * b[:, share + 2 * j + 1 : share + 2 * j + 2] for f, b in zip(factors, blocks))
        value = sum(f * b[:, j * part : (j + 1) * part] for f, b in zip(factors, blocks))
        pieces.append(value / total)
    joined = pieces[0] if len(pieces) == 1 else jnp.concatenate(pieces, axis=1)
    right = jnp.where(row_iota(joined.shape) < slots, joined, 0.0).astype(BF16)
    left = gated[...].astype(BF16)
    columns = w_ssm.shape[1] // col_count
    for c in range(col_count):
        span = slice(c * columns, (c + 1) * columns)
        send[c * BLOCK : (c + 1) * BLOCK, :] = dot(left, w_ssm[:, span]) + dot(right, w_attn[:, span])


def total_kernel(
    plan, kv_new, driven, decay, b_twice, conv_x, conv_bc, terms, mixed, send, block, *, moves, col_count
):
    at = Plan(conv_x.shape[1], moves)
    total = sum(terms[c * BLOCK : (c + 1) * BLOCK, :] for c in range(col_count))
    mixed[...] = total.astype(BF16).astype(F32)

    block[...] = jnp.zeros_like(block)
    for m in range(moves):
        row = pl.ds(plan[at.slot + m], 1)

        def put(index, value, start=0):
            block[index : index + 1, start : start + value.shape[1]] = value

        put(Note.mixed, mixed[row, :])
        put(Note.key_value, kv_new[row, :])
        for index, value, start, low_index, low_start in (
            (Note.drive, driven[row, :], 0, Note.drive_low, 0),
            (Note.mixing, decay[row, :], Note.decay, Note.mixing, Note.decay_low),
        ):
            high = value.astype(BF16).astype(F32)
            put(index, high, start)
            put(low_index, value - high, low_start)
        put(Note.mixing, b_twice[row, :])
        for k in range(KW - 1):
            put(Note.conv_x + k, conv_x[k, row, :])
            put(Note.conv_bc + k, conv_bc[k, row, :])
        start = pl.multiple_of(plan[at.target + m] * BLOCK, BLOCK)
        send[pl.ds(start, BLOCK), :] = block[...].astype(BF16)


def place_kernel(plan, table, pool_in, *rest, moves, row_count, col_count):
    del pool_in
    pages_here, slots = table.shape
    at = Plan(slots, moves)
    parcels = rest[: row_count - 1]
    pool_next, states, last_pages, packed, in_sems, out_sems = rest[row_count - 1 :]
    for m in range(moves):
        for d, parcel in enumerate(parcels, 1):

            @pl.when(plan[at.from_away + m] == d)
            def _(m=m, parcel=parcel):
                pltpu.make_async_copy(parcel, packed.at[m], in_sems.at[m]).start()

    stores = []
    for m in range(moves):
        pltpu.make_async_copy(parcels[0], packed.at[m], in_sems.at[m]).wait()
        slot = plan[at.slot + m]
        for page in range(pages_here):
            stores.append(
                pltpu.make_async_copy(
                    packed.at[m, page], pool_next.at[table[page, slot]], out_sems.at[m, page]
                )
            )
            stores[-1].start()
        stores.append(
            pltpu.make_async_copy(packed.at[m, pages_here:], states.at[m], out_sems.at[m, pages_here])
        )
        stores[-1].start()
        local_page = place_of(plan[at.arrived_length + m], col_count)[1]
        last_pages[m] = packed[m, local_page]
    for store in stores:
        store.wait()


def arrive_kernel(
    col_ref, plan, table, mixed_home, conv_x, conv_bc, notes, states, last_pages, state_in, pool_in,
    mixed, conv_x_next, conv_bc_next, state_next, pool_next,
    made, drive, decay, b_twice, window_x, window_bc, window_mixed, filled, state_sems, page_sems,
    *, moves, col_count,
):
    del state_in, pool_in
    slots, inner = conv_x.shape[1], conv_x.shape[2]
    heads = inner // HP
    at = Plan(slots, moves)
    col = col_ref[0]

    stores, rows = [], []
    b_twice[...] = jnp.zeros_like(b_twice)
    half = b_twice.shape[0] // 2
    for m in range(moves):
        start = pl.multiple_of(plan[at.source + m] * BLOCK, BLOCK)
        note = notes[pl.ds(start, BLOCK), :].astype(F32)
        rows.append(note)
        slot = plan[at.slot + m]
        owner, local_page, offset = place_of(plan[at.arrived_length + m], col_count)
        key_value = note[Note.key_value : Note.key_value + 1, : 2 * KVH * HD]
        filled[m] = inserted(last_pages[m], key_value, jnp.where(owner == col, offset, -1))
        stores.append(
            pltpu.make_async_copy(filled.at[m], pool_next.at[table[local_page, slot]], page_sems.at[m])
        )
        stores[-1].start()
        mixing = note[Note.mixing : Note.mixing + 1, :]
        b_twice[m : m + 1, :] = mixing[:, :NS]
        b_twice[half + m : half + m + 1, :] = mixing[:, :NS]
        decay[m : m + 1, :] = (
            mixing[:, Note.decay : Note.decay + heads] + mixing[:, Note.decay_low : Note.decay_low + heads]
        )
    padding = [jnp.zeros((half - moves, inner), F32)]
    stacked = [note[Note.drive : Note.drive + 1, :inner] for note in rows] + padding
    stacked += [note[Note.drive_low : Note.drive_low + 1, :inner] for note in rows] + padding
    drive[...] = jnp.transpose(jnp.concatenate(stacked, axis=0)).astype(BF16)
    for m in range(moves):
        prior = [
            jnp.concatenate([states[m, h, :, :NS], states[m, h, :, NS:]], axis=0) for h in range(heads)
        ]
        advance_state(m, prior, b_twice, drive, decay, made.at[m])
        stores.append(pltpu.make_async_copy(made.at[m], state_next.at[plan[at.slot + m]], state_sems.at[m]))
        stores[-1].start()

    window_mixed[...] = mixed_home[...]
    for k in range(KW - 1):
        window_x[k] = conv_x[k]
        window_bc[k] = conv_bc[k]
    for m, note in enumerate(rows):
        row = pl.ds(plan[at.slot + m], 1)
        window_mixed[row, :] = note[Note.mixed : Note.mixed + 1, : window_mixed.shape[1]]
        for k in range(KW - 1):
            window_x[k, row, :] = note[Note.conv_x + k : Note.conv_x + k + 1, :inner]
            window_bc[k, row, :] = note[Note.conv_bc + k : Note.conv_bc + k + 1, : 2 * NS]
    mixed[...] = window_mixed[0:slots, :].astype(BF16)
    for k in range(KW - 1):
        conv_x_next[k] = window_x[k].astype(BF16)
        conv_bc_next[k] = window_bc[k].astype(BF16)
    for store in stores:
        store.wait()


def shape(dims, dtype):
    return jax.ShapeDtypeStruct(tuple(dims), dtype)


def params(limit=VMEM_LIMIT):
    return pltpu.CompilerParams(vmem_limit_bytes=limit)


def exchange(value, axis):
    return lax.all_to_all(value, axis, split_axis=0, concat_axis=0, tiled=True)


def trade(block, axis, d):
    return lax.ppermute(block, axis, [(i, i ^ d) for i in range(lax.axis_size(axis))])


def ordered(value, first):
    return lax.optimization_barrier((value, first))[0]


def local(
    tokens, arrival, cache_lengths, move_slot, move_target, page_table, kv_pool, ssm_state,
    conv_x, conv_bc, norm_gain, weight_z, weight_x, weight_dt, weight_bc, weight_qkv,
    conv_weight_x, conv_weight_bc, dt_bias, a_log, d_skip, weight_ssm_out, weight_attn_out,
):
    row_count = lax.axis_size("rows")
    col_count = lax.axis_size("cols")
    row_index = lax.axis_index("rows").astype(I32).reshape(1)
    col_index = lax.axis_index("cols").astype(I32).reshape(1)
    slots, heads = ssm_state.shape[0], ssm_state.shape[1]
    total, depth = tokens.shape
    moves = move_slot.shape[1]
    pages_here, width = page_table.shape[3], kv_pool.shape[3]
    inner = heads * HP
    stays = slots - moves
    cols, at = Columns(inner), Plan(slots, moves)
    table = page_table[0, 0].T
    pool = kv_pool[:, 0]
    past_x, past_bc = conv_x.transpose(1, 0, 2), conv_bc.transpose(1, 0, 2)
    rows = row_count * BLOCK
    model = depth * row_count
    share = QH * HD // col_count
    parcel = (pages_here + heads, PAGE, width)
    parcels_here = pltpu.VMEM((moves,) + parcel, BF16)

    chip_count = row_count // 2
    plan, mine, theirs = pl.pallas_call(
        functools.partial(project_kernel, slots=slots),
        out_shape=[
            shape((at.size,), I32),
            shape((chip_count * BLOCK, cols.width), F32),
            shape((chip_count * BLOCK, cols.width), BF16),
        ],
        in_specs=[SMEM_SPEC] * 5 + [VMEM_SPEC] * 7,
        out_specs=[SMEM_SPEC] + [VMEM_SPEC] * 2,
        scratch_shapes=[
            pltpu.SMEM((total,), I32),
            pltpu.VMEM((total, depth), F32),
            pltpu.VMEM((rows, depth), F32),
            pltpu.VMEM((rows, LANES), F32),
        ],
        compiler_params=params(FIRST_LIMIT),
        cost_estimate=BRIEF,
        name="project",
    )(
        row_index, arrival, cache_lengths, move_slot.T, move_target.T,
        tokens, norm_gain, weight_z, weight_x, weight_dt.T, weight_bc, weight_qkv,
    )
    parcels = pl.pallas_call(
        functools.partial(pack_kernel, moves=moves, row_count=row_count),
        out_shape=[shape(parcel, BF16)] * (row_count - 1),
        in_specs=[SMEM_SPEC] * 2 + [ANY_SPEC] * 2,
        out_specs=[ANY_SPEC] * (row_count - 1),
        scratch_shapes=[
            parcels_here,
            pltpu.SemaphoreType.DMA((moves, pages_here + 2)),
            pltpu.SemaphoreType.DMA((moves,)),
        ],
        compiler_params=params(FIRST_LIMIT),
        cost_estimate=BRIEF,
        name="pack",
    )(plan, table, pool, ssm_state)

    sums = pl.pallas_call(
        pair_kernel,
        out_shape=[shape((BLOCK, cols.width), F32)] + [shape((BLOCK, cols.width), BF16)] * (chip_count - 1),
        in_specs=[VMEM_SPEC] * 2,
        out_specs=[VMEM_SPEC] * chip_count,
        compiler_params=params(FIRST_LIMIT),
        cost_estimate=BRIEF,
        name="pair",
    )(mine, trade(theirs, "rows", 1))
    received = [sums[0]] + [trade(block, "rows", 2 * j) for j, block in enumerate(sums[1:], 1)]

    moving = [None] + list(parcels)

    def migrate(parts, after):
        for d in parts:
            moving[d] = trade(ordered(moving[d], after), "rows", d)
        return [moving[d] for d in parts]

    thirds = [range(2 + j, row_count, 2)[: chip_count // 2] for j in range(2)]
    first, second = (list(part) for part in thirds)
    third = [d for d in range(2, row_count) if d not in first + second]
    first_moved = migrate(first, received)
    second_moved = migrate(second, received)

    pool_next, kv_new, partials = pl.pallas_call(
        functools.partial(
            attend_kernel, moves=moves, heads=heads, chip_count=chip_count, col_count=col_count, width=model
        ),
        out_shape=[
            shape(pool.shape, BF16),
            shape((BLOCK, 2 * KVH * HD), F32),
            shape((col_count * BLOCK, share + LANES), F32),
        ],
        in_specs=[SMEM_SPEC] * 3 + [ANY_SPEC] + [VMEM_SPEC] * chip_count,
        out_specs=[ANY_SPEC] + [VMEM_SPEC] * 2,
        scratch_shapes=[
            pltpu.VMEM(pool.shape, BF16),
            pltpu.VMEM((BLOCK * QH, HD), F32),
            pltpu.VMEM((BLOCK * QH, pages_here * PAGE), F32),
            pltpu.VMEM((BLOCK * QH, HD), F32),
            pltpu.VMEM((BLOCK * QH, HD), F32),
            pltpu.VMEM((BLOCK * QH, HD), F32),
            pltpu.SemaphoreType.DMA((2 if pool.shape[0] % 4 else 4,)),
            pltpu.SemaphoreType.DMA((2 if pool.shape[0] % 4 else 4,)),
        ],
        compiler_params=params(),
        cost_estimate=BRIEF,
        name="attend",
    )(col_index, plan, table, pool, *received)
    received = ordered(received, (partials, first_moved))
    partials = exchange(partials, "cols")

    next_x, next_bc, gated, driven, decay, drive, b_twice = pl.pallas_call(
        functools.partial(mix_kernel, chip_count=chip_count, width=model),
        out_shape=(
            shape(past_x.shape, F32),
            shape(past_bc.shape, F32),
            shape((BLOCK, inner), F32),
            shape((BLOCK, inner), F32),
            shape((BLOCK, heads), F32),
            shape((inner, 2 * BLOCK), BF16),
            shape((2 * BLOCK, NS), F32),
        ),
        in_specs=[VMEM_SPEC] * 7 + [ANY_SPEC] + [VMEM_SPEC] * chip_count,
        out_specs=(VMEM_SPEC,) * 7,
        scratch_shapes=[
            pltpu.VMEM((BLOCK, inner), F32),
            pltpu.VMEM((slots, heads, HP, NS), BF16),
            pltpu.SemaphoreType.DMA((slots,)),
        ],
        compiler_params=params(),
        cost_estimate=BRIEF,
        name="mix",
    )(past_x, past_bc, conv_weight_x, conv_weight_bc, dt_bias, a_log, d_skip, ssm_state, *received)

    columns = weight_ssm_out.shape[1] // col_count
    migrate(third + [1], gated)
    terms = pl.pallas_call(
        functools.partial(output_kernel, slots=slots, col_count=col_count),
        out_shape=shape((col_count * BLOCK, columns), F32),
        in_specs=[VMEM_SPEC] * 4,
        out_specs=VMEM_SPEC,
        compiler_params=params(),
        cost_estimate=BRIEF,
        name="output",
    )(gated, weight_ssm_out, weight_attn_out, partials)
    drive = ordered(drive, terms)
    terms = exchange(terms, "cols")
    state_next = pl.pallas_call(
        functools.partial(stay_kernel, moves=moves),
        out_shape=shape(ssm_state.shape, BF16),
        in_specs=[SMEM_SPEC] + [VMEM_SPEC] * 3 + [ANY_SPEC],
        out_specs=ANY_SPEC,
        scratch_shapes=[
            pltpu.VMEM((stays, heads, HP, NS), BF16),
            pltpu.VMEM((stays, heads, HP, NS), BF16),
            pltpu.SemaphoreType.DMA((stays,)),
            pltpu.SemaphoreType.DMA((stays,)),
        ],
        compiler_params=params(),
        cost_estimate=BRIEF,
        name="stay",
    )(plan, drive, decay, b_twice, ssm_state)

    terms = ordered(terms, second_moved)
    note = (BLOCK, max(inner, 2 * NS, 2 * KVH * HD, columns))
    mixed_home, notes = pl.pallas_call(
        functools.partial(total_kernel, moves=moves, col_count=col_count),
        out_shape=[shape((BLOCK, columns), F32), shape((rows, note[1]), BF16)],
        in_specs=[SMEM_SPEC] + [VMEM_SPEC] * 7,
        out_specs=[VMEM_SPEC] * 2,
        scratch_shapes=[pltpu.VMEM(note, F32)],
        compiler_params=params(),
        cost_estimate=BRIEF,
        name="total",
    )(plan, kv_new, driven, decay, b_twice, next_x, next_bc, terms)
    pool_next = ordered(pool_next, notes)
    notes = exchange(notes, "rows")
    pool_next, states, last_pages = pl.pallas_call(
        functools.partial(place_kernel, moves=moves, row_count=row_count, col_count=col_count),
        out_shape=[
            shape(pool.shape, BF16),
            shape((moves, heads, PAGE, width), BF16),
            shape((moves, PAGE, width), BF16),
        ],
        in_specs=[SMEM_SPEC] * 2 + [ANY_SPEC] * row_count,
        out_specs=[ANY_SPEC] * 2 + [VMEM_SPEC],
        scratch_shapes=[
            parcels_here,
            pltpu.SemaphoreType.DMA((moves,)),
            pltpu.SemaphoreType.DMA((moves, pages_here + 1)),
        ],
        input_output_aliases={2: 0},
        compiler_params=params(),
        cost_estimate=BRIEF,
        name="place",
    )(plan, table, pool_next, *moving[1:])

    mixed, conv_x_next, conv_bc_next, state_next, pool_next = pl.pallas_call(
        functools.partial(arrive_kernel, moves=moves, col_count=col_count),
        out_shape=(
            shape((slots, columns), BF16),
            shape(past_x.shape, BF16),
            shape(past_bc.shape, BF16),
            shape(ssm_state.shape, BF16),
            shape(pool.shape, BF16),
        ),
        in_specs=[SMEM_SPEC] * 3 + [VMEM_SPEC] * 6 + [ANY_SPEC] * 2,
        out_specs=[VMEM_SPEC] * 3 + [ANY_SPEC] * 2,
        scratch_shapes=[
            pltpu.VMEM((moves, heads, HP, NS), BF16),
            pltpu.VMEM((inner, 2 * BLOCK), BF16),
            pltpu.VMEM((BLOCK, heads), F32),
            pltpu.VMEM((2 * BLOCK, NS), F32),
            pltpu.VMEM((KW - 1, slots, inner), F32),
            pltpu.VMEM((KW - 1, slots, 2 * NS), F32),
            pltpu.VMEM((BLOCK, columns), F32),
            pltpu.VMEM((moves, PAGE, width), BF16),
            pltpu.SemaphoreType.DMA((moves,)),
            pltpu.SemaphoreType.DMA((moves,)),
        ],
        input_output_aliases={9: 3, 10: 4},
        compiler_params=params(),
        cost_estimate=BRIEF,
        name="arrive",
    )(col_index, plan, table, mixed_home, next_x, next_bc, notes, states, last_pages, state_next, pool_next)
    return (
        mixed, state_next, conv_x_next.transpose(1, 0, 2), conv_bc_next.transpose(1, 0, 2), pool_next[:, None]
    )


def solution(mesh):
    in_specs = (
        P(None, "rows"),
        P(),
        P(),
        P(),
        P(),
        P("rows", "cols", None, None),
        P("rows", "cols", None, None),
        P("rows", "cols", None, None),
        P("rows", None, "cols"),
        P("rows", None, None),
        P("rows"),
        P("rows", "cols"),
        P("rows", "cols"),
        P("rows", "cols"),
        P("rows", None),
        P("rows", None),
        P(None, "cols"),
        P(),
        P("cols"),
        P("cols"),
        P("cols"),
        P("cols", None),
        P("cols", None),
    )
    out_specs = (
        P("rows", "cols"),
        P("rows", "cols", None, None),
        P("rows", None, "cols"),
        P("rows", None, None),
        P("rows", "cols", None, None),
    )
    return jax.shard_map(local, mesh=mesh, in_specs=in_specs, out_specs=out_specs, check_vma=False)
```

```python
import functools

import jax
import jax.numpy as jnp
from jax import lax
from jax.experimental import pallas as pl
from jax.experimental.pallas import tpu as pltpu
from jax.sharding import PartitionSpec as P

HP = 64
NS = 256
KW = 4
QH = 8
KVH = 2
HD = 128
PAGE = 32
LANES = 128
BLOCK = 16

EPSILON = 1e-05
FLOOR_SCORE = -1e30
FIRST_LIMIT = 60 * 1024 * 1024
VMEM_LIMIT = 57 * 1024 * 1024
LAST_LIMIT = 24 * 1024 * 1024

F32 = jnp.float32
BF16 = jnp.bfloat16
I32 = jnp.int32

SMEM_SPEC = pl.BlockSpec(memory_space=pltpu.SMEM)
BRIEF = pl.CostEstimate(flops=1, bytes_accessed=1, transcendentals=0)
VMEM_SPEC = pl.BlockSpec(memory_space=pltpu.VMEM)
ANY_SPEC = pl.BlockSpec(memory_space=pl.ANY)


def silu(v):
    return v / (1.0 + jnp.exp(-v))


def dot(a, b):
    return jnp.dot(a, b, preferred_element_type=F32)


def dot_t(a, b):
    return lax.dot_general(a, b, (((1,), (1,)), ((), ())), preferred_element_type=F32)


def row_iota(shape):
    return lax.broadcasted_iota(I32, shape, 0)


def lane_iota(shape):
    return lax.broadcasted_iota(I32, shape, 1)


class Columns:
    def __init__(self, inner):
        self.z = 0
        self.x = inner
        self.bc = 2 * inner
        self.q = self.bc + 2 * NS
        self.kv = self.q + QH * HD
        self.tail = self.kv + 2 * KVH * HD
        self.width = self.tail + 2 * LANES


class Plan:
    def __init__(self, slots, moves):
        self.length = 0
        self.slot = slots
        self.target = self.slot + moves
        self.away = self.target + moves
        self.source = self.away + moves
        self.from_away = self.source + moves
        self.arrived_length = self.from_away + moves
        self.stay = self.arrived_length + moves
        self.size = self.stay + slots - moves


class Note:
    mixed, key_value, drive, drive_low, mixing, conv_x, conv_bc = 0, 1, 2, 3, 4, 5, 8
    decay, decay_low = NS, NS + LANES


def project_kernel(
    row_ref, arrival, lengths, move_slot, move_target,
    tokens, gain, w_z, w_x, w_dt, w_bc, w_qkv,
    plan, mine, theirs,
    inverse, wide, picked, tail,
    *, slots,
):
    moves, row_count = move_slot.shape
    heads, depth = w_dt.shape
    inner = heads * HP
    cols, at = Columns(inner), Plan(slots, moves)
    me, half = row_ref[0], row_count // 2

    wide[...] = tokens[...].astype(F32)
    picked[...] = jnp.zeros_like(picked)

    def invert(t, carry):
        for s in range(slots):
            inverse[arrival[t * slots + s]] = t * slots + s
        return carry

    lax.fori_loop(0, row_count, invert, 0)

    def pick(b, carry):
        d = jnp.where(b < half, 2 * b, 2 * (b - half) + 1)
        first = lax.bitwise_xor(me, d) * slots
        for s in range(slots):
            picked[pl.ds(b * BLOCK + s, 1), :] = wide[pl.ds(inverse[first + s], 1), :]
        return carry

    lax.fori_loop(0, row_count, pick, 0)

    rows = picked[...]
    squares = jnp.sum(rows * rows, axis=1, keepdims=True)
    scaled = (rows * gain[...].astype(F32).reshape(1, depth)).astype(BF16)

    def put(start, value):
        span = slice(start, start + value.shape[1])
        mine[:, span] = value[: half * BLOCK].astype(F32)
        theirs[:, span] = value[half * BLOCK :].astype(BF16)

    put(cols.z, dot(scaled, w_z[...]))
    put(cols.x, dot(scaled, w_x[...]))
    put(cols.bc, dot(scaled, w_bc[...]))
    put(cols.q, dot(scaled, w_qkv[...]))
    tail[...] = jnp.zeros_like(tail)
    tail[:, :heads] = dot_t(scaled, w_dt[...])
    tail[:, heads : heads + 1] = squares
    high = tail[...].astype(BF16)
    put(cols.tail, high)
    put(cols.tail + LANES, tail[...] - high.astype(F32))

    stays = 0
    for s in range(slots):
        plan[at.length + s] = lengths[me * slots + s]
        leaves = move_slot[0, me] == s
        for m in range(1, moves):
            leaves = jnp.logical_or(leaves, move_slot[m, me] == s)

        @pl.when(jnp.logical_not(leaves))
        def _(s=s, stays=stays):
            plan[at.stay + stays] = s

        stays = stays + jnp.where(leaves, 0, 1)
    for m in range(moves):
        plan[at.slot + m] = move_slot[m, me]
        plan[at.target + m] = move_target[m, me]
        plan[at.away + m] = lax.bitwise_xor(move_target[m, me], me)

    def seek(i, turn):
        for m in range(moves):
            comes = move_target[m, i] == me

            @pl.when(comes)
            def _(m=m, turn=turn):
                plan[at.source + turn] = i
                plan[at.from_away + turn] = lax.bitwise_xor(i, me)
                plan[at.arrived_length + turn] = lengths[i * slots + move_slot[m, i]]

            turn = turn + jnp.where(comes, 1, 0)
        return turn

    lax.fori_loop(0, row_count, seek, I32(0))


def pack_kernel(plan, table, pool, state, *rest, moves, row_count):
    pages_here, slots = table.shape
    at = Plan(slots, moves)
    parcels = rest[: row_count - 1]
    packed, in_sems, out_sems = rest[row_count - 1 :]
    loads = []
    for m in range(moves):
        slot = plan[at.slot + m]
        loads.append([])
        for page in range(pages_here):
            loads[m].append(
                pltpu.make_async_copy(pool.at[table[page, slot]], packed.at[m, page], in_sems.at[m, page])
            )
        for part in range(2):
            loads[m].append(
                pltpu.make_async_copy(
                    state.at[slot, :, part * PAGE : (part + 1) * PAGE, :],
                    packed.at[m, pages_here:, :, part * NS : (part + 1) * NS],
                    in_sems.at[m, pages_here + part],
                )
            )
        for load in loads[m]:
            load.start()
    for m in range(moves):
        for load in loads[m]:
            load.wait()
        for d, parcel in enumerate(parcels, 1):

            @pl.when(plan[at.away + m] == d)
            def _(m=m, parcel=parcel):
                pltpu.make_async_copy(packed.at[m], parcel, out_sems.at[m]).start()

    for m in range(moves):
        pltpu.make_async_copy(packed.at[m], parcels[0], out_sems.at[m]).wait()


def pair_kernel(mine, theirs, own, *others):
    for j, out in enumerate((own,) + others):
        span = slice(j * BLOCK, (j + 1) * BLOCK)
        out[...] = (mine[span, :] + theirs[span, :].astype(F32)).astype(out.dtype)


def widen(per_head, inner):
    rows = per_head.shape[0]
    first = lane_iota((rows, 2 * HP)) < HP
    pieces = []
    for h in range(0, inner // HP, 2):
        pieces.append(jnp.where(first, per_head[:, h : h + 1], per_head[:, h + 1 : h + 2]))
    return pieces[0] if len(pieces) == 1 else jnp.concatenate(pieces, axis=1)


class Sums:
    def __init__(self, received, heads, width):
        self.received = received
        cols = Columns(heads * HP)
        tail = self.total(cols.tail, cols.tail + LANES) + self.total(cols.tail + LANES, cols.width)
        self.root = jnp.sqrt(tail[:, heads : heads + 1] / width + EPSILON)
        self.step_in = (tail[:, :heads] / self.root).astype(BF16).astype(F32)

    def total(self, start, stop):
        return sum(part[:, start:stop].astype(F32) for part in self.received)

    def projected(self, start, stop):
        return (self.total(start, stop) / self.root).astype(BF16).astype(F32)


def inserted(page, row, offset):
    return jnp.where(row_iota(page.shape) == offset, row, page.astype(F32)).astype(BF16)


def place_of(length, col_count):
    logical = lax.div(length, I32(PAGE))
    return lax.rem(logical, I32(col_count)), lax.div(logical, I32(col_count)), lax.rem(length, I32(PAGE))


def attend_kernel(
    col_ref, plan, table, pool, *rest, moves, heads, chip_count, col_count, width
):
    received, (pool_next, kv_new, send) = rest[:chip_count], rest[chip_count : chip_count + 3]
    pages, queries, scores, weighted, peaks, totals, in_sems, out_sems = rest[chip_count + 3 :]
    pages_here, slots = table.shape
    cols, at = Columns(heads * HP), Plan(slots, moves)
    col = col_ref[0]
    tokens_here = pages_here * PAGE
    kv_width = KVH * HD
    chunks = in_sems.shape[0]
    step = pool.shape[0] // chunks
    spans = [pl.ds(k * step, step) for k in range(chunks)]
    loads = [pltpu.make_async_copy(pool.at[span], pages.at[span], in_sems.at[k]) for k, span in enumerate(spans)]
    for load in loads:
        load.start()

    sums = Sums(received, heads, width)
    kv_new[...] = sums.projected(cols.kv, cols.tail)
    q_in = sums.projected(cols.q, cols.kv)
    for h in range(QH):
        queries[pl.ds(h, BLOCK, stride=QH), :] = q_in[:, h * HD : (h + 1) * HD]

    first_group = row_iota((QH, HD)) < QH // KVH
    lane = lane_iota((QH, tokens_here))
    position = (lax.shift_right_logical(lane, 5) * col_count + col) * PAGE + lax.bitwise_and(lane, PAGE - 1)
    for load in loads:
        load.wait()
    for s in range(slots):
        owner, local_page, offset = place_of(plan[at.length + s], col_count)
        page = table[local_page, s]
        pages[page] = inserted(pages[page], kv_new[s : s + 1, :], jnp.where(owner == col, offset, -1))
    stores = [
        pltpu.make_async_copy(pages.at[span], pool_next.at[span], out_sems.at[k]) for k, span in enumerate(spans)
    ]
    for store in stores:
        store.start()

    def cached(s, start):
        parts = [pages[table[page, s], :, start : start + kv_width] for page in range(pages_here)]
        return jnp.concatenate(parts, axis=0)

    for s in range(slots):
        query = queries[s * QH : (s + 1) * QH, :]
        query = jnp.concatenate(
            [jnp.where(first_group, query, 0.0), jnp.where(first_group, 0.0, query)], axis=1
        ).astype(BF16)
        score = dot_t(query, cached(s, 0)) * (HD ** -0.5)
        scores[s * QH : (s + 1) * QH, :] = jnp.where(position <= plan[at.length + s], score, FLOOR_SCORE)

    live_rows = slots * QH
    everything = scores[0:live_rows, :]
    peak = jnp.max(everything, axis=1, keepdims=True)
    weights = jnp.where(everything > 0.5 * FLOOR_SCORE, jnp.exp(everything - peak), 0.0)
    total = jnp.sum(weights, axis=1, keepdims=True)
    scores[0:live_rows, :] = weights
    for ref, value in ((weighted, None), (peaks, peak), (totals, total)):
        ref[live_rows:, :] = jnp.zeros((BLOCK * QH - live_rows, HD), F32)
        if value is not None:
            ref[0:live_rows, :] = jnp.broadcast_to(value, (live_rows, HD))
    for s in range(slots):
        weight = scores[s * QH : (s + 1) * QH, :]
        high = weight.astype(BF16).astype(F32)
        both = dot(jnp.concatenate([high, weight - high], axis=0).astype(BF16), cached(s, kv_width))
        joined = both[:QH] + both[QH:]
        weighted[s * QH : (s + 1) * QH, :] = jnp.where(first_group, joined[:, :HD], joined[:, HD:])

    share = QH * HD // col_count
    part = min(share, HD)
    lanes = lane_iota((BLOCK, LANES))
    for c in range(col_count):
        block = slice(c * BLOCK, (c + 1) * BLOCK)
        stats = jnp.zeros((BLOCK, LANES), F32)
        for j in range(share // part):
            head, begin = divmod(c * share + j * part, HD)
            rows = pl.ds(head, BLOCK, stride=QH)
            send[block, j * part : (j + 1) * part] = weighted[rows, :][:, begin : begin + part]
            stats = jnp.where(lanes == 2 * j, peaks[rows, :], stats)
            stats = jnp.where(lanes == 2 * j + 1, totals[rows, :], stats)
        send[block, share:] = stats
    for store in stores:
        store.wait()


def mix_kernel(
    plan, conv_x, conv_bc, cw_x, cw_bc, dt_bias, a_log, d_skip, state, *rest, moves, chip_count, width
):
    received = rest[:chip_count]
    conv_x_next, conv_bc_next, state_next, gated, driven_out, decay, b_out = rest[chip_count : chip_count + 7]
    readout, held, made, drive, b_twice, in_sems, out_sems = rest[chip_count + 7 :]
    slots, inner = conv_x.shape[1], conv_x.shape[2]
    heads = dt_bias.shape[0]
    cols, at = Columns(inner), Plan(slots, moves)
    loads = []
    for s in range(slots):
        loads.append(pltpu.make_async_copy(state.at[s], held.at[s], in_sems.at[s]))
        loads[-1].start()

    sums = Sums(received, heads, width)

    def convolved(past, taps, fresh, following):
        past_rows = [past[k].astype(F32) for k in range(KW - 1)]
        total = fresh[:slots] * taps[KW - 1 : KW, :].astype(F32)
        for k in range(KW - 1):
            total = total + past_rows[k] * taps[k : k + 1, :].astype(F32)
            following[k] = past_rows[k + 1] if k < KW - 2 else fresh[:slots]
        return jnp.concatenate([silu(total), jnp.zeros((BLOCK - slots, total.shape[1]), F32)], axis=0)

    value_act = convolved(conv_x, cw_x, sums.projected(cols.x, cols.bc), conv_x_next)
    bc_act = convolved(conv_bc, cw_bc, sums.projected(cols.bc, cols.q), conv_bc_next)
    bc_act = bc_act.astype(BF16).astype(F32)
    b_in, c_val = bc_act[:, :NS], bc_act[:, NS:]
    b_out[...] = b_in
    b_twice[...] = jnp.concatenate([b_in, b_in], axis=0)
    c_out = c_val.astype(BF16)

    shifted = sums.step_in + dt_bias[...].reshape(1, heads)
    step_size = jnp.maximum(shifted, 0.0) + jnp.log(1.0 + jnp.exp(-jnp.abs(shifted)))
    rate = jnp.exp(-jnp.exp(a_log[...].reshape(1, heads)) * step_size)
    decay[...] = rate
    driven = widen(step_size, inner) * value_act
    driven_out[...] = driven
    high = driven.astype(BF16).astype(F32)
    drive[...] = jnp.transpose(jnp.concatenate([high, driven - high], axis=0)).astype(BF16)

    readout[...] = jnp.zeros_like(readout)

    for s in range(slots):
        loads[s].wait()
        value = dot_t(c_out, held[s].reshape(inner, NS))
        readout[s : s + 1, :] = value[s : s + 1]

    stores = []
    for j in range(slots - moves):
        slot = plan[at.stay + j]
        advance_state(slot, held.at[slot], b_twice, drive, decay, made.at[j])
        stores.append(pltpu.make_async_copy(made.at[j], state_next.at[slot], out_sems.at[j]))
        stores[-1].start()

    gate = silu(sums.projected(cols.z, cols.x))
    b_dot_c = jnp.sum(b_in * c_val, axis=1, keepdims=True)
    skip = widen(jnp.broadcast_to(d_skip[...].reshape(1, heads), (BLOCK, heads)), inner)
    total = widen(rate, inner) * readout[...] + driven * b_dot_c + skip * value_act
    gated[...] = (total * gate).astype(BF16).astype(F32)
    for store in stores:
        store.wait()


def advance_state(slot, prior, b_twice, drive, decay, result):
    heads = result.shape[0]
    twice = b_twice[...]
    half = twice.shape[0] // 2
    row = row_iota(twice.shape)
    selected = jnp.where((row == slot) | (row == slot + half), twice, 0.0).astype(BF16)
    outer = dot(drive[...], selected).reshape(heads, HP, NS)
    for h in range(heads):
        rate = decay[pl.ds(slot, 1), h : h + 1]
        result[h] = (rate * prior[h].astype(F32) + outer[h]).astype(BF16)


def output_kernel(gated, w_ssm, w_attn, partials, send, *, slots, col_count):
    share = w_attn.shape[0]
    part = min(share, HD)
    blocks = [partials[c * BLOCK : (c + 1) * BLOCK, :] for c in range(col_count)]
    pieces = []
    for j in range(share // part):
        peaks = [b[:, share + 2 * j : share + 2 * j + 1] for b in blocks]
        joint = functools.reduce(jnp.maximum, peaks)
        factors = [jnp.exp(p - joint) for p in peaks]
        total = sum(f * b[:, share + 2 * j + 1 : share + 2 * j + 2] for f, b in zip(factors, blocks))
        value = sum(f * b[:, j * part : (j + 1) * part] for f, b in zip(factors, blocks))
        pieces.append(value / total)
    joined = pieces[0] if len(pieces) == 1 else jnp.concatenate(pieces, axis=1)
    right = jnp.where(row_iota(joined.shape) < slots, joined, 0.0).astype(BF16)
    left = gated[...].astype(BF16)
    columns = w_ssm.shape[1] // col_count
    for c in range(col_count):
        span = slice(c * columns, (c + 1) * columns)
        send[c * BLOCK : (c + 1) * BLOCK, :] = dot(left, w_ssm[:, span]) + dot(right, w_attn[:, span])


def total_kernel(
    plan, kv_new, driven, decay, b_in, conv_x, conv_bc, terms, mixed, send, block, *, moves, col_count
):
    at = Plan(conv_x.shape[1], moves)
    total = sum(terms[c * BLOCK : (c + 1) * BLOCK, :] for c in range(col_count))
    mixed[...] = total.astype(BF16).astype(F32)

    block[...] = jnp.zeros_like(block)
    for m in range(moves):
        row = pl.ds(plan[at.slot + m], 1)

        def put(index, value, start=0):
            block[index : index + 1, start : start + value.shape[1]] = value

        put(Note.mixed, mixed[row, :])
        put(Note.key_value, kv_new[row, :])
        for index, value, start, low_index, low_start in (
            (Note.drive, driven[row, :], 0, Note.drive_low, 0),
            (Note.mixing, decay[row, :], Note.decay, Note.mixing, Note.decay_low),
        ):
            high = value.astype(BF16).astype(F32)
            put(index, high, start)
            put(low_index, value - high, low_start)
        put(Note.mixing, b_in[row, :])
        for k in range(KW - 1):
            put(Note.conv_x + k, conv_x[k, row, :])
            put(Note.conv_bc + k, conv_bc[k, row, :])
        start = pl.multiple_of(plan[at.target + m] * BLOCK, BLOCK)
        send[pl.ds(start, BLOCK), :] = block[...].astype(BF16)


def arrive_kernel(
    col_ref, plan, table, mixed_home, conv_x, conv_bc, state_in, pool_in, notes, *rest,
    moves, row_count, col_count,
):
    del state_in, pool_in
    parcels, rest = rest[: row_count - 1], rest[row_count - 1 :]
    pages_here, slots = table.shape
    inner = conv_x.shape[2]
    heads = inner // HP
    at = Plan(slots, moves)
    mixed, conv_x_next, conv_bc_next, state_next, pool_next = rest[:5]
    packed, made, drive, decay, b_twice, window_x, window_bc, window_mixed, in_sems, out_sems = rest[5:]
    col = col_ref[0]
    for m in range(moves):
        for d, parcel in enumerate(parcels, 1):

            @pl.when(plan[at.from_away + m] == d)
            def _(m=m, parcel=parcel):
                pltpu.make_async_copy(parcel, packed.at[m], in_sems.at[m]).start()


    for k in range(KW - 1):
        window_x[k] = conv_x[k]
        window_bc[k] = conv_bc[k]
    window_mixed[...] = mixed_home[...]
    rows = []
    b_twice[...] = jnp.zeros_like(b_twice)
    half = b_twice.shape[0] // 2
    for m in range(moves):
        start = pl.multiple_of(plan[at.source + m] * BLOCK, BLOCK)
        note = notes[pl.ds(start, BLOCK), :].astype(F32)
        rows.append(note)
        row = pl.ds(plan[at.slot + m], 1)
        window_mixed[row, :] = note[Note.mixed : Note.mixed + 1, : window_mixed.shape[1]]
        for k in range(KW - 1):
            window_x[k, row, :] = note[Note.conv_x + k : Note.conv_x + k + 1, :inner]
            window_bc[k, row, :] = note[Note.conv_bc + k : Note.conv_bc + k + 1, : 2 * NS]
        mixing = note[Note.mixing : Note.mixing + 1, :]
        b_twice[m : m + 1, :] = mixing[:, :NS]
        b_twice[half + m : half + m + 1, :] = mixing[:, :NS]
        decay[m : m + 1, :] = (
            mixing[:, Note.decay : Note.decay + heads] + mixing[:, Note.decay_low : Note.decay_low + heads]
        )
    padding = [jnp.zeros((half - moves, inner), F32)]
    stacked = [note[Note.drive : Note.drive + 1, :inner] for note in rows] + padding
    stacked += [note[Note.drive_low : Note.drive_low + 1, :inner] for note in rows] + padding
    drive[...] = jnp.transpose(jnp.concatenate(stacked, axis=0)).astype(BF16)
    mixed[...] = window_mixed[0:slots, :].astype(BF16)
    for k in range(KW - 1):
        conv_x_next[k] = window_x[k].astype(BF16)
        conv_bc_next[k] = window_bc[k].astype(BF16)

    stores = []
    for m in range(moves):
        slot = plan[at.slot + m]
        pltpu.make_async_copy(parcels[0], packed.at[m], in_sems.at[m]).wait()
        owner, local_page, offset = place_of(plan[at.arrived_length + m], col_count)
        key_value = rows[m][Note.key_value : Note.key_value + 1, : 2 * KVH * HD]

        @pl.when(owner == col)
        def _(m=m, local_page=local_page, offset=offset, key_value=key_value):
            packed[m, local_page] = inserted(packed[m, local_page], key_value, offset)

        for page in range(pages_here):
            stores.append(
                pltpu.make_async_copy(
                    packed.at[m, page], pool_next.at[table[page, slot]], out_sems.at[m, page]
                )
            )
            stores[-1].start()
        prior = [
            jnp.concatenate([packed[m, pages_here + h, :, :NS], packed[m, pages_here + h, :, NS:]], axis=0)
            for h in range(heads)
        ]
        advance_state(m, prior, b_twice, drive, decay, made.at[m])
        stores.append(pltpu.make_async_copy(made.at[m], state_next.at[slot], out_sems.at[m, pages_here]))
        stores[-1].start()
    for store in stores:
        store.wait()


def shape(dims, dtype):
    return jax.ShapeDtypeStruct(tuple(dims), dtype)


def params(limit=VMEM_LIMIT):
    return pltpu.CompilerParams(vmem_limit_bytes=limit)


def exchange(value, axis):
    return lax.all_to_all(value, axis, split_axis=0, concat_axis=0, tiled=True)


def trade(block, axis, d):
    return lax.ppermute(block, axis, [(i, i ^ d) for i in range(lax.axis_size(axis))])


def ordered(value, first):
    return lax.optimization_barrier((value, first))[0]


def local(
    tokens, arrival, cache_lengths, move_slot, move_target, page_table, kv_pool, ssm_state,
    conv_x, conv_bc, norm_gain, weight_z, weight_x, weight_dt, weight_bc, weight_qkv,
    conv_weight_x, conv_weight_bc, dt_bias, a_log, d_skip, weight_ssm_out, weight_attn_out,
):
    row_count = lax.axis_size("rows")
    col_count = lax.axis_size("cols")
    row_index = lax.axis_index("rows").astype(I32).reshape(1)
    col_index = lax.axis_index("cols").astype(I32).reshape(1)
    slots, heads = ssm_state.shape[0], ssm_state.shape[1]
    total, depth = tokens.shape
    moves = move_slot.shape[1]
    pages_here, width = page_table.shape[3], kv_pool.shape[3]
    inner = heads * HP
    stays = slots - moves
    cols, at = Columns(inner), Plan(slots, moves)
    table = page_table[0, 0].T
    pool = kv_pool[:, 0]
    past_x, past_bc = conv_x.transpose(1, 0, 2), conv_bc.transpose(1, 0, 2)
    rows = row_count * BLOCK
    model = depth * row_count
    share = QH * HD // col_count
    parcel = (pages_here + heads, PAGE, width)
    parcels_here = pltpu.VMEM((moves,) + parcel, BF16)

    chip_count = row_count // 2
    plan, mine, theirs = pl.pallas_call(
        functools.partial(project_kernel, slots=slots),
        out_shape=[
            shape((at.size,), I32),
            shape((chip_count * BLOCK, cols.width), F32),
            shape((chip_count * BLOCK, cols.width), BF16),
        ],
        in_specs=[SMEM_SPEC] * 5 + [VMEM_SPEC] * 7,
        out_specs=[SMEM_SPEC] + [VMEM_SPEC] * 2,
        scratch_shapes=[
            pltpu.SMEM((total,), I32),
            pltpu.VMEM((total, depth), F32),
            pltpu.VMEM((rows, depth), F32),
            pltpu.VMEM((rows, LANES), F32),
        ],
        compiler_params=params(FIRST_LIMIT),
        cost_estimate=BRIEF,
        name="project",
    )(
        row_index, arrival, cache_lengths, move_slot.T, move_target.T,
        tokens, norm_gain, weight_z, weight_x, weight_dt.T, weight_bc, weight_qkv,
    )
    parcels = pl.pallas_call(
        functools.partial(pack_kernel, moves=moves, row_count=row_count),
        out_shape=[shape(parcel, BF16)] * (row_count - 1),
        in_specs=[SMEM_SPEC] * 2 + [ANY_SPEC] * 2,
        out_specs=[ANY_SPEC] * (row_count - 1),
        scratch_shapes=[
            parcels_here,
            pltpu.SemaphoreType.DMA((moves, pages_here + 2)),
            pltpu.SemaphoreType.DMA((moves,)),
        ],
        compiler_params=params(FIRST_LIMIT),
        cost_estimate=BRIEF,
        name="pack",
    )(plan, table, pool, ssm_state)

    sums = pl.pallas_call(
        pair_kernel,
        out_shape=[shape((BLOCK, cols.width), F32)] + [shape((BLOCK, cols.width), BF16)] * (chip_count - 1),
        in_specs=[VMEM_SPEC] * 2,
        out_specs=[VMEM_SPEC] * chip_count,
        compiler_params=params(FIRST_LIMIT),
        cost_estimate=BRIEF,
        name="pair",
    )(mine, trade(theirs, "rows", 1))
    received = [sums[0]] + [trade(block, "rows", 2 * j) for j, block in enumerate(sums[1:], 1)]

    order = [d for j in range(2) for d in range(2 + j, row_count, 2)] + [1]
    early = order[:-2]
    moving = {d: parcels[d - 1] for d in order}
    for d in early:
        moving[d] = ordered(moving[d], received)

    pool_next, kv_new, partials = pl.pallas_call(
        functools.partial(
            attend_kernel, moves=moves, heads=heads, chip_count=chip_count, col_count=col_count, width=model
        ),
        out_shape=[
            shape(pool.shape, BF16),
            shape((BLOCK, 2 * KVH * HD), F32),
            shape((col_count * BLOCK, share + LANES), F32),
        ],
        in_specs=[SMEM_SPEC] * 3 + [ANY_SPEC] + [VMEM_SPEC] * chip_count,
        out_specs=[ANY_SPEC] + [VMEM_SPEC] * 2,
        scratch_shapes=[
            pltpu.VMEM(pool.shape, BF16),
            pltpu.VMEM((BLOCK * QH, HD), F32),
            pltpu.VMEM((BLOCK * QH, pages_here * PAGE), F32),
            pltpu.VMEM((BLOCK * QH, HD), F32),
            pltpu.VMEM((BLOCK * QH, HD), F32),
            pltpu.VMEM((BLOCK * QH, HD), F32),
            pltpu.SemaphoreType.DMA((2 if pool.shape[0] % 4 else 4,)),
            pltpu.SemaphoreType.DMA((2 if pool.shape[0] % 4 else 4,)),
        ],
        compiler_params=params(),
        cost_estimate=BRIEF,
        name="attend",
    )(col_index, plan, table, pool, *received)
    received = ordered(received, partials)
    partials = exchange(partials, "cols")

    next_x, next_bc, state_next, gated, driven, decay, b_in = pl.pallas_call(
        functools.partial(mix_kernel, moves=moves, chip_count=chip_count, width=model),
        out_shape=(
            shape(past_x.shape, F32),
            shape(past_bc.shape, F32),
            shape(ssm_state.shape, BF16),
            shape((BLOCK, inner), F32),
            shape((BLOCK, inner), F32),
            shape((BLOCK, heads), F32),
            shape((BLOCK, NS), F32),
        ),
        in_specs=[SMEM_SPEC] + [VMEM_SPEC] * 7 + [ANY_SPEC] + [VMEM_SPEC] * chip_count,
        out_specs=(VMEM_SPEC, VMEM_SPEC, ANY_SPEC) + (VMEM_SPEC,) * 4,
        scratch_shapes=[
            pltpu.VMEM((BLOCK, inner), F32),
            pltpu.VMEM((slots, heads, HP, NS), BF16),
            pltpu.VMEM((stays, heads, HP, NS), BF16),
            pltpu.VMEM((inner, 2 * BLOCK), BF16),
            pltpu.VMEM((2 * BLOCK, NS), F32),
            pltpu.SemaphoreType.DMA((slots,)),
            pltpu.SemaphoreType.DMA((stays,)),
        ],
        compiler_params=params(),
        cost_estimate=BRIEF,
        name="mix",
    )(plan, past_x, past_bc, conv_weight_x, conv_weight_bc, dt_bias, a_log, d_skip, ssm_state, *received)

    columns = weight_ssm_out.shape[1] // col_count
    terms = pl.pallas_call(
        functools.partial(output_kernel, slots=slots, col_count=col_count),
        out_shape=shape((col_count * BLOCK, columns), F32),
        in_specs=[VMEM_SPEC] * 4,
        out_specs=VMEM_SPEC,
        compiler_params=params(),
        cost_estimate=BRIEF,
        name="output",
    )(gated, weight_ssm_out, weight_attn_out, partials)
    for d in order[-2:]:
        moving[d] = ordered(moving[d], terms)
    parcels = [trade(moving[d], "rows", d) for d in range(1, row_count)]
    terms = exchange(terms, "cols")

    note = (BLOCK, max(inner, 2 * NS, 2 * KVH * HD, columns))
    mixed_home, notes = pl.pallas_call(
        functools.partial(total_kernel, moves=moves, col_count=col_count),
        out_shape=[shape((BLOCK, columns), F32), shape((rows, note[1]), BF16)],
        in_specs=[SMEM_SPEC] + [VMEM_SPEC] * 7,
        out_specs=[VMEM_SPEC] * 2,
        scratch_shapes=[pltpu.VMEM(note, F32)],
        compiler_params=params(),
        cost_estimate=BRIEF,
        name="total",
    )(plan, kv_new, driven, decay, b_in, next_x, next_bc, terms)
    notes = exchange(notes, "rows")

    mixed, conv_x_next, conv_bc_next, state_next, pool_next = pl.pallas_call(
        functools.partial(arrive_kernel, moves=moves, row_count=row_count, col_count=col_count),
        out_shape=(
            shape((slots, columns), BF16),
            shape(past_x.shape, BF16),
            shape(past_bc.shape, BF16),
            shape(ssm_state.shape, BF16),
            shape(pool.shape, BF16),
        ),
        in_specs=[SMEM_SPEC] * 3 + [VMEM_SPEC] * 3 + [ANY_SPEC] * 2 + [VMEM_SPEC] + [ANY_SPEC] * (row_count - 1),
        out_specs=[VMEM_SPEC] * 3 + [ANY_SPEC] * 2,
        scratch_shapes=[
            parcels_here,
            pltpu.VMEM((moves, heads, HP, NS), BF16),
            pltpu.VMEM((inner, 2 * BLOCK), BF16),
            pltpu.VMEM((BLOCK, heads), F32),
            pltpu.VMEM((2 * BLOCK, NS), F32),
            pltpu.VMEM((KW - 1, slots, inner), F32),
            pltpu.VMEM((KW - 1, slots, 2 * NS), F32),
            pltpu.VMEM((BLOCK, columns), F32),
            pltpu.SemaphoreType.DMA((moves,)),
            pltpu.SemaphoreType.DMA((moves, pages_here + 1)),
        ],
        input_output_aliases={6: 3, 7: 4},
        compiler_params=params(LAST_LIMIT),
        cost_estimate=BRIEF,
        name="arrive",
    )(col_index, plan, table, mixed_home, next_x, next_bc, state_next, pool_next, notes, *parcels)
    return (
        mixed, state_next, conv_x_next.transpose(1, 0, 2), conv_bc_next.transpose(1, 0, 2), pool_next[:, None]
    )


def solution(mesh):
    in_specs = (
        P(None, "rows"),
        P(),
        P(),
        P(),
        P(),
        P("rows", "cols", None, None),
        P("rows", "cols", None, None),
        P("rows", "cols", None, None),
        P("rows", None, "cols"),
        P("rows", None, None),
        P("rows"),
        P("rows", "cols"),
        P("rows", "cols"),
        P("rows", "cols"),
        P("rows", None),
        P("rows", None),
        P(None, "cols"),
        P(),
        P("cols"),
        P("cols"),
        P("cols"),
        P("cols", None),
        P("cols", None),
    )
    out_specs = (
        P("rows", "cols"),
        P("rows", "cols", None, None),
        P("rows", None, "cols"),
        P("rows", None, None),
        P("rows", "cols", None, None),
    )
    return jax.shard_map(local, mesh=mesh, in_specs=in_specs, out_specs=out_specs, check_vma=False)
```

```python
import functools

import jax
import jax.numpy as jnp
from jax import lax
from jax.experimental import pallas as pl
from jax.experimental.pallas import tpu as pltpu
from jax.sharding import PartitionSpec as P

HP = 64
NS = 256
KW = 4
QH = 8
KVH = 2
HD = 128
PAGE = 32
LANES = 128
BLOCK = 16

EPSILON = 1e-05
FLOOR_SCORE = -1e30
FIRST_LIMIT = 60 * 1024 * 1024
VMEM_LIMIT = 57 * 1024 * 1024
LAST_LIMIT = 24 * 1024 * 1024

F32 = jnp.float32
BF16 = jnp.bfloat16
I32 = jnp.int32

SMEM_SPEC = pl.BlockSpec(memory_space=pltpu.SMEM)
BRIEF = pl.CostEstimate(flops=1, bytes_accessed=1, transcendentals=0)
VMEM_SPEC = pl.BlockSpec(memory_space=pltpu.VMEM)
ANY_SPEC = pl.BlockSpec(memory_space=pl.ANY)


def silu(v):
    return v / (1.0 + jnp.exp(-v))


def dot(a, b):
    return jnp.dot(a, b, preferred_element_type=F32)


def dot_t(a, b):
    return lax.dot_general(a, b, (((1,), (1,)), ((), ())), preferred_element_type=F32)


def row_iota(shape):
    return lax.broadcasted_iota(I32, shape, 0)


def lane_iota(shape):
    return lax.broadcasted_iota(I32, shape, 1)


class Columns:
    def __init__(self, inner):
        self.z = 0
        self.x = inner
        self.bc = 2 * inner
        self.q = self.bc + 2 * NS
        self.kv = self.q + QH * HD
        self.tail = self.kv + 2 * KVH * HD
        self.width = self.tail + 2 * LANES


class Plan:
    def __init__(self, slots, moves):
        self.length = 0
        self.slot = slots
        self.target = self.slot + moves
        self.away = self.target + moves
        self.source = self.away + moves
        self.from_away = self.source + moves
        self.arrived_length = self.from_away + moves
        self.stay = self.arrived_length + moves
        self.me = self.stay + slots - moves
        self.size = self.me + 1


def early_parts(row_count):
    return [d for d in (2, 4) if d < row_count]


def parcel_parts(refs, row_count, pages_here):
    refs, early = list(refs), early_parts(row_count)
    parts = []
    for d in range(1, row_count):
        if d in early:
            parts.append((refs.pop(0), refs.pop(0)))
        else:
            whole = refs.pop(0)
            parts.append((whole.at[:pages_here], whole.at[pages_here:]))
    return parts


class Note:
    mixed, key_value, drive, drive_low, mixing, conv_x, conv_bc = 0, 1, 2, 3, 4, 5, 8
    decay, decay_low = NS, NS + LANES


def project_kernel(
    row_ref, arrival, lengths, move_slot, move_target, table,
    tokens, gain, w_z, w_x, w_dt, w_bc, w_qkv, pool, state,
    plan, mine, theirs, *rest,
):
    inverse, wide, picked, tail, packed, in_sems, out_sems = rest[-7:]
    moves, row_count = move_slot.shape
    pages_here, slots = table.shape
    parcels = parcel_parts(rest[:-7], row_count, pages_here)
    heads, depth = w_dt.shape
    inner = heads * HP
    cols, at = Columns(inner), Plan(slots, moves)
    me, half = row_ref[0], row_count // 2

    loads = []
    for m in range(moves):
        slot = move_slot[m, me]
        for page in range(pages_here):
            loads.append(
                pltpu.make_async_copy(pool.at[table[page, slot]], packed.at[m, page], in_sems.at[m, page])
            )
        for part in range(2):
            loads.append(
                pltpu.make_async_copy(
                    state.at[slot, :, part * PAGE : (part + 1) * PAGE, :],
                    packed.at[m, pages_here:, :, part * NS : (part + 1) * NS],
                    in_sems.at[m, pages_here + part],
                )
            )
    for load in loads:
        load.start()

    wide[...] = tokens[...].astype(F32)
    picked[...] = jnp.zeros_like(picked)

    def invert(t, carry):
        for s in range(slots):
            inverse[arrival[t * slots + s]] = t * slots + s
        return carry

    lax.fori_loop(0, row_count, invert, 0)

    def pick(b, carry):
        d = jnp.where(b < half, 2 * b, 2 * (b - half) + 1)
        first = lax.bitwise_xor(me, d) * slots
        for s in range(slots):
            picked[pl.ds(b * BLOCK + s, 1), :] = wide[pl.ds(inverse[first + s], 1), :]
        return carry

    lax.fori_loop(0, row_count, pick, 0)

    for load in loads:
        load.wait()

    def sent(m, to):
        pages, states = to
        return (
            pltpu.make_async_copy(packed.at[m, :pages_here], pages, out_sems.at[m, 0]),
            pltpu.make_async_copy(packed.at[m, pages_here:], states, out_sems.at[m, 1]),
        )

    for m in range(moves):
        away = lax.bitwise_xor(move_target[m, me], me)
        for d, parcel in enumerate(parcels, 1):

            @pl.when(away == d)
            def _(m=m, parcel=parcel):
                for copy in sent(m, parcel):
                    copy.start()

    rows = picked[...]
    squares = jnp.sum(rows * rows, axis=1, keepdims=True)
    scaled = (rows * gain[...].astype(F32).reshape(1, depth)).astype(BF16)

    def put(start, value):
        span = slice(start, start + value.shape[1])
        mine[:, span] = value[: half * BLOCK].astype(F32)
        theirs[:, span] = value[half * BLOCK :].astype(BF16)

    put(cols.z, dot(scaled, w_z[...]))
    put(cols.x, dot(scaled, w_x[...]))
    put(cols.bc, dot(scaled, w_bc[...]))
    put(cols.q, dot(scaled, w_qkv[...]))
    tail[...] = jnp.zeros_like(tail)
    tail[:, :heads] = dot_t(scaled, w_dt[...])
    tail[:, heads : heads + 1] = squares
    high = tail[...].astype(BF16)
    put(cols.tail, high)
    put(cols.tail + LANES, tail[...] - high.astype(F32))

    stays = 0
    for s in range(slots):
        plan[at.length + s] = lengths[me * slots + s]
        leaves = move_slot[0, me] == s
        for m in range(1, moves):
            leaves = jnp.logical_or(leaves, move_slot[m, me] == s)

        @pl.when(jnp.logical_not(leaves))
        def _(s=s, stays=stays):
            plan[at.stay + stays] = s

        stays = stays + jnp.where(leaves, 0, 1)
    for m in range(moves):
        plan[at.slot + m] = move_slot[m, me]
        plan[at.target + m] = move_target[m, me]
        plan[at.away + m] = lax.bitwise_xor(move_target[m, me], me)

    def seek(i, turn):
        for m in range(moves):
            comes = move_target[m, i] == me

            @pl.when(comes)
            def _(m=m, turn=turn):
                plan[at.source + turn] = i
                plan[at.from_away + turn] = lax.bitwise_xor(i, me)
                plan[at.arrived_length + turn] = lengths[i * slots + move_slot[m, i]]

            turn = turn + jnp.where(comes, 1, 0)
        return turn

    lax.fori_loop(0, row_count, seek, I32(0))
    plan[at.me] = me
    for m in range(moves):
        for copy in sent(m, parcels[0]):
            copy.wait()


def pair_kernel(mine, theirs, own, *others):
    for j, out in enumerate((own,) + others):
        span = slice(j * BLOCK, (j + 1) * BLOCK)
        out[...] = (mine[span, :] + theirs[span, :].astype(F32)).astype(out.dtype)


def widen(per_head, inner):
    rows = per_head.shape[0]
    first = lane_iota((rows, 2 * HP)) < HP
    pieces = []
    for h in range(0, inner // HP, 2):
        pieces.append(jnp.where(first, per_head[:, h : h + 1], per_head[:, h + 1 : h + 2]))
    return pieces[0] if len(pieces) == 1 else jnp.concatenate(pieces, axis=1)


class Sums:
    def __init__(self, received, heads, width):
        self.received = received
        cols = Columns(heads * HP)
        tail = self.total(cols.tail, cols.tail + LANES) + self.total(cols.tail + LANES, cols.width)
        self.root = jnp.sqrt(tail[:, heads : heads + 1] / width + EPSILON)
        self.step_in = (tail[:, :heads] / self.root).astype(BF16).astype(F32)

    def total(self, start, stop):
        return sum(part[:, start:stop].astype(F32) for part in self.received)

    def projected(self, start, stop):
        return (self.total(start, stop) / self.root).astype(BF16).astype(F32)


def inserted(page, row, offset):
    return jnp.where(row_iota(page.shape) == offset, row, page.astype(F32)).astype(BF16)


def place_of(length, col_count):
    logical = lax.div(length, I32(PAGE))
    return lax.rem(logical, I32(col_count)), lax.div(logical, I32(col_count)), lax.rem(length, I32(PAGE))


def attend_kernel(
    col_ref, plan, table, pool, *rest, moves, heads, chip_count, col_count, width
):
    received, (pool_next, kv_new, send) = rest[:chip_count], rest[chip_count : chip_count + 3]
    pages, queries, scores, weighted, peaks, totals, in_sems, out_sems = rest[chip_count + 3 :]
    pages_here, slots = table.shape
    cols, at = Columns(heads * HP), Plan(slots, moves)
    col = col_ref[0]
    tokens_here = pages_here * PAGE
    kv_width = KVH * HD
    chunks = in_sems.shape[0]
    step = pool.shape[0] // chunks
    spans = [pl.ds(k * step, step) for k in range(chunks)]
    loads = [pltpu.make_async_copy(pool.at[span], pages.at[span], in_sems.at[k]) for k, span in enumerate(spans)]
    for load in loads:
        load.start()

    sums = Sums(received, heads, width)
    kv_new[...] = sums.projected(cols.kv, cols.tail)
    q_in = sums.projected(cols.q, cols.kv)
    for h in range(QH):
        queries[pl.ds(h, BLOCK, stride=QH), :] = q_in[:, h * HD : (h + 1) * HD]

    first_group = row_iota((QH, HD)) < QH // KVH
    lane = lane_iota((QH, tokens_here))
    position = (lax.shift_right_logical(lane, 5) * col_count + col) * PAGE + lax.bitwise_and(lane, PAGE - 1)
    for load in loads:
        load.wait()
    for s in range(slots):
        owner, local_page, offset = place_of(plan[at.length + s], col_count)
        page = table[local_page, s]
        pages[page] = inserted(pages[page], kv_new[s : s + 1, :], jnp.where(owner == col, offset, -1))
    stores = [
        pltpu.make_async_copy(pages.at[span], pool_next.at[span], out_sems.at[k]) for k, span in enumerate(spans)
    ]
    for store in stores:
        store.start()

    def cached(s, start):
        parts = [pages[table[page, s], :, start : start + kv_width] for page in range(pages_here)]
        return jnp.concatenate(parts, axis=0)

    for s in range(slots):
        query = queries[s * QH : (s + 1) * QH, :]
        query = jnp.concatenate(
            [jnp.where(first_group, query, 0.0), jnp.where(first_group, 0.0, query)], axis=1
        ).astype(BF16)
        score = dot_t(query, cached(s, 0)) * (HD ** -0.5)
        scores[s * QH : (s + 1) * QH, :] = jnp.where(position <= plan[at.length + s], score, FLOOR_SCORE)

    live_rows = slots * QH
    everything = scores[0:live_rows, :]
    peak = jnp.max(everything, axis=1, keepdims=True)
    weights = jnp.where(everything > 0.5 * FLOOR_SCORE, jnp.exp(everything - peak), 0.0)
    total = jnp.sum(weights, axis=1, keepdims=True)
    scores[0:live_rows, :] = weights
    for ref, value in ((weighted, None), (peaks, peak), (totals, total)):
        ref[live_rows:, :] = jnp.zeros((BLOCK * QH - live_rows, HD), F32)
        if value is not None:
            ref[0:live_rows, :] = jnp.broadcast_to(value, (live_rows, HD))
    for s in range(slots):
        weight = scores[s * QH : (s + 1) * QH, :]
        high = weight.astype(BF16).astype(F32)
        both = dot(jnp.concatenate([high, weight - high], axis=0).astype(BF16), cached(s, kv_width))
        joined = both[:QH] + both[QH:]
        weighted[s * QH : (s + 1) * QH, :] = jnp.where(first_group, joined[:, :HD], joined[:, HD:])

    share = QH * HD // col_count
    part = min(share, HD)
    lanes = lane_iota((BLOCK, LANES))
    for c in range(col_count):
        block = slice(c * BLOCK, (c + 1) * BLOCK)
        stats = jnp.zeros((BLOCK, LANES), F32)
        for j in range(share // part):
            head, begin = divmod(c * share + j * part, HD)
            rows = pl.ds(head, BLOCK, stride=QH)
            send[block, j * part : (j + 1) * part] = weighted[rows, :][:, begin : begin + part]
            stats = jnp.where(lanes == 2 * j, peaks[rows, :], stats)
            stats = jnp.where(lanes == 2 * j + 1, totals[rows, :], stats)
        send[block, share:] = stats
    for store in stores:
        store.wait()


def mix_kernel(
    plan, conv_x, conv_bc, cw_x, cw_bc, dt_bias, a_log, d_skip, state, *rest, moves, chip_count, width
):
    received = rest[:chip_count]
    conv_x_next, conv_bc_next, state_next, gated, driven_out, decay, b_out = rest[chip_count : chip_count + 7]
    readout, held, made, drive, b_twice, in_sems, out_sems = rest[chip_count + 7 :]
    slots, inner = conv_x.shape[1], conv_x.shape[2]
    heads = dt_bias.shape[0]
    cols, at = Columns(inner), Plan(slots, moves)
    loads = []
    for s in range(slots):
        loads.append(pltpu.make_async_copy(state.at[s], held.at[s], in_sems.at[s]))
        loads[-1].start()

    sums = Sums(received, heads, width)

    def convolved(past, taps, fresh, following):
        past_rows = [past[k].astype(F32) for k in range(KW - 1)]
        total = fresh[:slots] * taps[KW - 1 : KW, :].astype(F32)
        for k in range(KW - 1):
            total = total + past_rows[k] * taps[k : k + 1, :].astype(F32)
            following[k] = past_rows[k + 1] if k < KW - 2 else fresh[:slots]
        return jnp.concatenate([silu(total), jnp.zeros((BLOCK - slots, total.shape[1]), F32)], axis=0)

    value_act = convolved(conv_x, cw_x, sums.projected(cols.x, cols.bc), conv_x_next)
    bc_act = convolved(conv_bc, cw_bc, sums.projected(cols.bc, cols.q), conv_bc_next)
    bc_act = bc_act.astype(BF16).astype(F32)
    b_in, c_val = bc_act[:, :NS], bc_act[:, NS:]
    b_out[...] = b_in
    b_twice[...] = jnp.concatenate([b_in, b_in], axis=0)
    c_out = c_val.astype(BF16)

    shifted = sums.step_in + dt_bias[...].reshape(1, heads)
    step_size = jnp.maximum(shifted, 0.0) + jnp.log(1.0 + jnp.exp(-jnp.abs(shifted)))
    rate = jnp.exp(-jnp.exp(a_log[...].reshape(1, heads)) * step_size)
    decay[...] = rate
    driven = widen(step_size, inner) * value_act
    driven_out[...] = driven
    high = driven.astype(BF16).astype(F32)
    drive[...] = jnp.transpose(jnp.concatenate([high, driven - high], axis=0)).astype(BF16)

    readout[...] = jnp.zeros_like(readout)

    for s in range(slots):
        loads[s].wait()
        value = dot_t(c_out, held[s].reshape(inner, NS))
        readout[s : s + 1, :] = value[s : s + 1]

    stores = []
    for j in range(slots - moves):
        slot = plan[at.stay + j]
        advance_state(slot, held.at[slot], b_twice, drive, decay, made.at[j])
        stores.append(pltpu.make_async_copy(made.at[j], state_next.at[slot], out_sems.at[j]))
        stores[-1].start()

    gate = silu(sums.projected(cols.z, cols.x))
    b_dot_c = jnp.sum(b_in * c_val, axis=1, keepdims=True)
    skip = widen(jnp.broadcast_to(d_skip[...].reshape(1, heads), (BLOCK, heads)), inner)
    total = widen(rate, inner) * readout[...] + driven * b_dot_c + skip * value_act
    gated[...] = (total * gate).astype(BF16).astype(F32)
    for store in stores:
        store.wait()


def advance_state(slot, prior, b_twice, drive, decay, result):
    heads = result.shape[0]
    twice = b_twice[...]
    half = twice.shape[0] // 2
    row = row_iota(twice.shape)
    selected = jnp.where((row == slot) | (row == slot + half), twice, 0.0).astype(BF16)
    outer = dot(drive[...], selected).reshape(heads, HP, NS)
    for h in range(heads):
        rate = decay[pl.ds(slot, 1), h : h + 1]
        result[h] = (rate * prior[h].astype(F32) + outer[h]).astype(BF16)


def output_kernel(
    gated, w_ssm_all, w_attn_all, partials, send, w_ssm, w_attn, sems, *, slots, col_count
):
    columns = w_ssm.shape[1] // col_count
    spans = [slice(c * columns, (c + 1) * columns) for c in range(col_count)]
    loads = [
        [
            pltpu.make_async_copy(whole.at[:, span], held.at[:, span], sems.at[c, k])
            for k, (whole, held) in enumerate(((w_ssm_all, w_ssm), (w_attn_all, w_attn)))
        ]
        for c, span in enumerate(spans)
    ]
    for load in loads:
        load[0].start()
        load[1].start()
    share = w_attn.shape[0]
    part = min(share, HD)
    blocks = [partials[c * BLOCK : (c + 1) * BLOCK, :] for c in range(col_count)]
    pieces = []
    for j in range(share // part):
        peaks = [b[:, share + 2 * j : share + 2 * j + 1] for b in blocks]
        joint = functools.reduce(jnp.maximum, peaks)
        factors = [jnp.exp(p - joint) for p in peaks]
        total = sum(f * b[:, share + 2 * j + 1 : share + 2 * j + 2] for f, b in zip(factors, blocks))
        value = sum(f * b[:, j * part : (j + 1) * part] for f, b in zip(factors, blocks))
        pieces.append(value / total)
    joined = pieces[0] if len(pieces) == 1 else jnp.concatenate(pieces, axis=1)
    right = jnp.where(row_iota(joined.shape) < slots, joined, 0.0).astype(BF16)
    left = gated[...].astype(BF16)
    for c, span in enumerate(spans):
        loads[c][0].wait()
        loads[c][1].wait()
        terms = dot(left, w_ssm[:, span]) + dot(right, w_attn[:, span])
        send[c * BLOCK : (c + 1) * BLOCK, :] = terms.astype(BF16)


def total_kernel(
    plan, kv_new, driven, decay, b_in, conv_x, conv_bc, terms, send, mixed, block, *, moves, col_count
):
    at = Plan(conv_x.shape[1], moves)
    total = sum(terms[c * BLOCK : (c + 1) * BLOCK, :].astype(F32) for c in range(col_count))
    mixed[...] = total
    send[pl.ds(pl.multiple_of(plan[at.me] * BLOCK, BLOCK), BLOCK), : total.shape[1]] = total.astype(BF16)

    block[...] = jnp.zeros_like(block)
    for m in range(moves):
        row = pl.ds(plan[at.slot + m], 1)

        def put(index, value, start=0):
            block[index : index + 1, start : start + value.shape[1]] = value

        put(Note.mixed, mixed[row, :])
        put(Note.key_value, kv_new[row, :])
        for index, value, start, low_index, low_start in (
            (Note.drive, driven[row, :], 0, Note.drive_low, 0),
            (Note.mixing, decay[row, :], Note.decay, Note.mixing, Note.decay_low),
        ):
            high = value.astype(BF16).astype(F32)
            put(index, high, start)
            put(low_index, value - high, low_start)
        put(Note.mixing, b_in[row, :])
        for k in range(KW - 1):
            put(Note.conv_x + k, conv_x[k, row, :])
            put(Note.conv_bc + k, conv_bc[k, row, :])
        start = pl.multiple_of(plan[at.target + m] * BLOCK, BLOCK)
        send[pl.ds(start, BLOCK), :] = block[...].astype(BF16)


def arrive_kernel(
    col_ref, plan, table, conv_x, conv_bc, state_in, pool_in, notes, *rest,
    moves, row_count, col_count,
):
    del state_in, pool_in
    parcel_count = row_count - 1 + len(early_parts(row_count))
    parcels, rest = rest[:parcel_count], rest[parcel_count:]
    pages_here, slots = table.shape
    inner = conv_x.shape[2]
    heads = inner // HP
    at = Plan(slots, moves)
    mixed, conv_x_next, conv_bc_next, state_next, pool_next = rest[:5]
    packed, made, drive, decay, b_twice, window_x, window_bc, window_mixed, in_sems, out_sems = rest[5:]
    col = col_ref[0]
    parcels = parcel_parts(parcels, row_count, pages_here)

    def loaded(m, parcel):
        pages, states = parcel
        return (
            pltpu.make_async_copy(pages, packed.at[m, :pages_here], in_sems.at[m, 0]),
            pltpu.make_async_copy(states, packed.at[m, pages_here:], in_sems.at[m, 1]),
        )

    for m in range(moves):
        for d, parcel in enumerate(parcels, 1):

            @pl.when(plan[at.from_away + m] == d)
            def _(m=m, parcel=parcel):
                for copy in loaded(m, parcel):
                    copy.start()


    for k in range(KW - 1):
        window_x[k] = conv_x[k]
        window_bc[k] = conv_bc[k]
    home = pl.multiple_of(plan[at.me] * BLOCK, BLOCK)
    window_mixed[...] = notes[pl.ds(home, BLOCK), : window_mixed.shape[1]].astype(F32)
    rows = []
    b_twice[...] = jnp.zeros_like(b_twice)
    half = b_twice.shape[0] // 2
    for m in range(moves):
        start = pl.multiple_of(plan[at.source + m] * BLOCK, BLOCK)
        note = notes[pl.ds(start, BLOCK), :].astype(F32)
        rows.append(note)
        row = pl.ds(plan[at.slot + m], 1)
        window_mixed[row, :] = note[Note.mixed : Note.mixed + 1, : window_mixed.shape[1]]
        for k in range(KW - 1):
            window_x[k, row, :] = note[Note.conv_x + k : Note.conv_x + k + 1, :inner]
            window_bc[k, row, :] = note[Note.conv_bc + k : Note.conv_bc + k + 1, : 2 * NS]
        mixing = note[Note.mixing : Note.mixing + 1, :]
        b_twice[m : m + 1, :] = mixing[:, :NS]
        b_twice[half + m : half + m + 1, :] = mixing[:, :NS]
        decay[m : m + 1, :] = (
            mixing[:, Note.decay : Note.decay + heads] + mixing[:, Note.decay_low : Note.decay_low + heads]
        )
    padding = [jnp.zeros((half - moves, inner), F32)]
    stacked = [note[Note.drive : Note.drive + 1, :inner] for note in rows] + padding
    stacked += [note[Note.drive_low : Note.drive_low + 1, :inner] for note in rows] + padding
    drive[...] = jnp.transpose(jnp.concatenate(stacked, axis=0)).astype(BF16)
    mixed[...] = window_mixed[0:slots, :].astype(BF16)
    for k in range(KW - 1):
        conv_x_next[k] = window_x[k].astype(BF16)
        conv_bc_next[k] = window_bc[k].astype(BF16)

    stores = []
    for m in range(moves):
        slot = plan[at.slot + m]
        for copy in loaded(m, parcels[0]):
            copy.wait()
        owner, local_page, offset = place_of(plan[at.arrived_length + m], col_count)
        key_value = rows[m][Note.key_value : Note.key_value + 1, : 2 * KVH * HD]

        @pl.when(owner == col)
        def _(m=m, local_page=local_page, offset=offset, key_value=key_value):
            packed[m, local_page] = inserted(packed[m, local_page], key_value, offset)

        for page in range(pages_here):
            stores.append(
                pltpu.make_async_copy(
                    packed.at[m, page], pool_next.at[table[page, slot]], out_sems.at[m, page]
                )
            )
            stores[-1].start()
        prior = [
            jnp.concatenate([packed[m, pages_here + h, :, :NS], packed[m, pages_here + h, :, NS:]], axis=0)
            for h in range(heads)
        ]
        advance_state(m, prior, b_twice, drive, decay, made.at[m])
        stores.append(pltpu.make_async_copy(made.at[m], state_next.at[slot], out_sems.at[m, pages_here]))
        stores[-1].start()
    for store in stores:
        store.wait()


def shape(dims, dtype):
    return jax.ShapeDtypeStruct(tuple(dims), dtype)


def params(limit=VMEM_LIMIT):
    return pltpu.CompilerParams(vmem_limit_bytes=limit)


def exchange(value, axis):
    return lax.all_to_all(value, axis, split_axis=0, concat_axis=0, tiled=True)


def trade(block, axis, d):
    return lax.ppermute(block, axis, [(i, i ^ d) for i in range(lax.axis_size(axis))])


def ordered(value, first):
    return lax.optimization_barrier((value, first))[0]


def local(
    tokens, arrival, cache_lengths, move_slot, move_target, page_table, kv_pool, ssm_state,
    conv_x, conv_bc, norm_gain, weight_z, weight_x, weight_dt, weight_bc, weight_qkv,
    conv_weight_x, conv_weight_bc, dt_bias, a_log, d_skip, weight_ssm_out, weight_attn_out,
):
    row_count = lax.axis_size("rows")
    col_count = lax.axis_size("cols")
    row_index = lax.axis_index("rows").astype(I32).reshape(1)
    col_index = lax.axis_index("cols").astype(I32).reshape(1)
    slots, heads = ssm_state.shape[0], ssm_state.shape[1]
    total, depth = tokens.shape
    moves = move_slot.shape[1]
    pages_here, width = page_table.shape[3], kv_pool.shape[3]
    inner = heads * HP
    stays = slots - moves
    cols, at = Columns(inner), Plan(slots, moves)
    table = page_table[0, 0].T
    pool = kv_pool[:, 0]
    past_x, past_bc = conv_x.transpose(1, 0, 2), conv_bc.transpose(1, 0, 2)
    rows = row_count * BLOCK
    model = depth * row_count
    share = QH * HD // col_count
    parcel = (pages_here + heads, PAGE, width)
    parcels_here = pltpu.VMEM((moves,) + parcel, BF16)

    chip_count = row_count // 2
    early = early_parts(row_count)
    parcels_out = []
    for d in range(1, row_count):
        if d in early:
            parcels_out += [shape((pages_here,) + parcel[1:], BF16), shape((heads,) + parcel[1:], BF16)]
        else:
            parcels_out.append(shape(parcel, BF16))
    plan, mine, theirs, *parcels = pl.pallas_call(
        project_kernel,
        out_shape=[
            shape((at.size,), I32),
            shape((chip_count * BLOCK, cols.width), F32),
            shape((chip_count * BLOCK, cols.width), BF16),
        ]
        + parcels_out,
        in_specs=[SMEM_SPEC] * 6 + [VMEM_SPEC] * 7 + [ANY_SPEC] * 2,
        out_specs=[SMEM_SPEC] + [VMEM_SPEC] * 2 + [ANY_SPEC] * len(parcels_out),
        scratch_shapes=[
            pltpu.SMEM((total,), I32),
            pltpu.VMEM((total, depth), F32),
            pltpu.VMEM((rows, depth), F32),
            pltpu.VMEM((rows, LANES), F32),
            parcels_here,
            pltpu.SemaphoreType.DMA((moves, pages_here + 2)),
            pltpu.SemaphoreType.DMA((moves, 2)),
        ],
        compiler_params=params(FIRST_LIMIT),
        cost_estimate=BRIEF,
        name="project",
    )(
        row_index, arrival, cache_lengths, move_slot.T, move_target.T, table,
        tokens, norm_gain, weight_z, weight_x, weight_dt.T, weight_bc, weight_qkv, pool, ssm_state,
    )
    moving = {}
    for d in range(1, row_count):
        moving[d] = [parcels.pop(0) for _ in range(2 if d in early else 1)]
    ahead = []
    for d in early:
        moving[d][0] = trade(moving[d][0], "rows", d)
        ahead.append(moving[d][0])

    sums = pl.pallas_call(
        pair_kernel,
        out_shape=[shape((BLOCK, cols.width), F32)] + [shape((BLOCK, cols.width), BF16)] * (chip_count - 1),
        in_specs=[VMEM_SPEC] * 2,
        out_specs=[VMEM_SPEC] * chip_count,
        compiler_params=params(FIRST_LIMIT),
        cost_estimate=BRIEF,
        name="pair",
    )(mine, trade(theirs, "rows", 1))
    received = [sums[0]] + [trade(block, "rows", 2 * j) for j, block in enumerate(sums[1:], 1)]

    def migrate(parts, after):
        for d in parts:
            moving[d][-1] = trade(ordered(moving[d][-1], after), "rows", d)

    order = [d for j in range(2) for d in range(2 + j, row_count, 2)] + [1]
    received = ordered(received, ahead)
    migrate(order[:-2], received)

    pool_next, kv_new, partials = pl.pallas_call(
        functools.partial(
            attend_kernel, moves=moves, heads=heads, chip_count=chip_count, col_count=col_count, width=model
        ),
        out_shape=[
            shape(pool.shape, BF16),
            shape((BLOCK, 2 * KVH * HD), F32),
            shape((col_count * BLOCK, share + LANES), F32),
        ],
        in_specs=[SMEM_SPEC] * 3 + [ANY_SPEC] + [VMEM_SPEC] * chip_count,
        out_specs=[ANY_SPEC] + [VMEM_SPEC] * 2,
        scratch_shapes=[
            pltpu.VMEM(pool.shape, BF16),
            pltpu.VMEM((BLOCK * QH, HD), F32),
            pltpu.VMEM((BLOCK * QH, pages_here * PAGE), F32),
            pltpu.VMEM((BLOCK * QH, HD), F32),
            pltpu.VMEM((BLOCK * QH, HD), F32),
            pltpu.VMEM((BLOCK * QH, HD), F32),
            pltpu.SemaphoreType.DMA((2 if pool.shape[0] % 4 else 4,)),
            pltpu.SemaphoreType.DMA((2 if pool.shape[0] % 4 else 4,)),
        ],
        compiler_params=params(),
        cost_estimate=BRIEF,
        name="attend",
    )(col_index, plan, table, pool, *received)
    received = ordered(received, partials)
    partials = exchange(partials, "cols")

    next_x, next_bc, state_next, gated, driven, decay, b_in = pl.pallas_call(
        functools.partial(mix_kernel, moves=moves, chip_count=chip_count, width=model),
        out_shape=(
            shape(past_x.shape, F32),
            shape(past_bc.shape, F32),
            shape(ssm_state.shape, BF16),
            shape((BLOCK, inner), F32),
            shape((BLOCK, inner), F32),
            shape((BLOCK, heads), F32),
            shape((BLOCK, NS), F32),
        ),
        in_specs=[SMEM_SPEC] + [VMEM_SPEC] * 7 + [ANY_SPEC] + [VMEM_SPEC] * chip_count,
        out_specs=(VMEM_SPEC, VMEM_SPEC, ANY_SPEC) + (VMEM_SPEC,) * 4,
        scratch_shapes=[
            pltpu.VMEM((BLOCK, inner), F32),
            pltpu.VMEM((slots, heads, HP, NS), BF16),
            pltpu.VMEM((stays, heads, HP, NS), BF16),
            pltpu.VMEM((inner, 2 * BLOCK), BF16),
            pltpu.VMEM((2 * BLOCK, NS), F32),
            pltpu.SemaphoreType.DMA((slots,)),
            pltpu.SemaphoreType.DMA((stays,)),
        ],
        compiler_params=params(),
        cost_estimate=BRIEF,
        name="mix",
    )(plan, past_x, past_bc, conv_weight_x, conv_weight_bc, dt_bias, a_log, d_skip, ssm_state, *received)

    columns = weight_ssm_out.shape[1] // col_count
    terms = pl.pallas_call(
        functools.partial(output_kernel, slots=slots, col_count=col_count),
        out_shape=shape((col_count * BLOCK, columns), BF16),
        in_specs=[VMEM_SPEC] + [ANY_SPEC] * 2 + [VMEM_SPEC],
        out_specs=VMEM_SPEC,
        scratch_shapes=[
            pltpu.VMEM(weight_ssm_out.shape, BF16),
            pltpu.VMEM(weight_attn_out.shape, BF16),
            pltpu.SemaphoreType.DMA((col_count, 2)),
        ],
        compiler_params=params(FIRST_LIMIT),
        cost_estimate=BRIEF,
        name="output",
    )(gated, weight_ssm_out, weight_attn_out, partials)
    migrate(order[-2:], terms)
    terms = exchange(terms, "cols")

    note = (BLOCK, max(inner, 2 * NS, 2 * KVH * HD, columns))
    notes = pl.pallas_call(
        functools.partial(total_kernel, moves=moves, col_count=col_count),
        out_shape=shape((rows, note[1]), BF16),
        in_specs=[SMEM_SPEC] + [VMEM_SPEC] * 7,
        out_specs=VMEM_SPEC,
        scratch_shapes=[pltpu.VMEM((BLOCK, columns), F32), pltpu.VMEM(note, F32)],
        compiler_params=params(),
        cost_estimate=BRIEF,
        name="total",
    )(plan, kv_new, driven, decay, b_in, next_x, next_bc, terms)
    notes = exchange(notes, "rows")

    mixed, conv_x_next, conv_bc_next, state_next, pool_next = pl.pallas_call(
        functools.partial(arrive_kernel, moves=moves, row_count=row_count, col_count=col_count),
        out_shape=(
            shape((slots, columns), BF16),
            shape(past_x.shape, BF16),
            shape(past_bc.shape, BF16),
            shape(ssm_state.shape, BF16),
            shape(pool.shape, BF16),
        ),
        in_specs=[SMEM_SPEC] * 3 + [VMEM_SPEC] * 2 + [ANY_SPEC] * 2 + [VMEM_SPEC] + [ANY_SPEC] * len(parcels_out),
        out_specs=[VMEM_SPEC] * 3 + [ANY_SPEC] * 2,
        scratch_shapes=[
            parcels_here,
            pltpu.VMEM((moves, heads, HP, NS), BF16),
            pltpu.VMEM((inner, 2 * BLOCK), BF16),
            pltpu.VMEM((BLOCK, heads), F32),
            pltpu.VMEM((2 * BLOCK, NS), F32),
            pltpu.VMEM((KW - 1, slots, inner), F32),
            pltpu.VMEM((KW - 1, slots, 2 * NS), F32),
            pltpu.VMEM((BLOCK, columns), F32),
            pltpu.SemaphoreType.DMA((moves, 2)),
            pltpu.SemaphoreType.DMA((moves, pages_here + 1)),
        ],
        input_output_aliases={5: 3, 6: 4},
        compiler_params=params(LAST_LIMIT),
        cost_estimate=BRIEF,
        name="arrive",
    )(
        col_index, plan, table, next_x, next_bc, state_next, pool_next, notes,
        *(part for d in range(1, row_count) for part in moving[d]),
    )
    return (
        mixed, state_next, conv_x_next.transpose(1, 0, 2), conv_bc_next.transpose(1, 0, 2), pool_next[:, None]
    )


def solution(mesh):
    in_specs = (
        P(None, "rows"),
        P(),
        P(),
        P(),
        P(),
        P("rows", "cols", None, None),
        P("rows", "cols", None, None),
        P("rows", "cols", None, None),
        P("rows", None, "cols"),
        P("rows", None, None),
        P("rows"),
        P("rows", "cols"),
        P("rows", "cols"),
        P("rows", "cols"),
        P("rows", None),
        P("rows", None),
        P(None, "cols"),
        P(),
        P("cols"),
        P("cols"),
        P("cols"),
        P("cols", None),
        P("cols", None),
    )
    out_specs = (
        P("rows", "cols"),
        P("rows", "cols", None, None),
        P("rows", None, "cols"),
        P("rows", None, None),
        P("rows", "cols", None, None),
    )
    return jax.shard_map(local, mesh=mesh, in_specs=in_specs, out_specs=out_specs, check_vma=False)
```

```python
import functools

import jax
import jax.numpy as jnp
from jax import lax
from jax.experimental import pallas as pl
from jax.experimental.pallas import tpu as pltpu
from jax.sharding import PartitionSpec as P

HP = 64
NS = 256
KW = 4
QH = 8
KVH = 2
HD = 128
PAGE = 32
LANES = 128
BLOCK = 16

EPSILON = 1e-05
FLOOR_SCORE = -1e30
FIRST_LIMIT = 60 * 1024 * 1024
VMEM_LIMIT = 57 * 1024 * 1024
LAST_LIMIT = 24 * 1024 * 1024

F32 = jnp.float32
BF16 = jnp.bfloat16
I32 = jnp.int32

SMEM_SPEC = pl.BlockSpec(memory_space=pltpu.SMEM)
BRIEF = pl.CostEstimate(flops=1, bytes_accessed=1, transcendentals=0)
VMEM_SPEC = pl.BlockSpec(memory_space=pltpu.VMEM)
ANY_SPEC = pl.BlockSpec(memory_space=pl.ANY)


def silu(v):
    return v / (1.0 + jnp.exp(-v))


def dot(a, b):
    return jnp.dot(a, b, preferred_element_type=F32)


def dot_t(a, b):
    return lax.dot_general(a, b, (((1,), (1,)), ((), ())), preferred_element_type=F32)


def row_iota(shape):
    return lax.broadcasted_iota(I32, shape, 0)


def lane_iota(shape):
    return lax.broadcasted_iota(I32, shape, 1)


class Columns:
    def __init__(self, inner):
        self.z = 0
        self.x = inner
        self.bc = 2 * inner
        self.q = self.bc + 2 * NS
        self.kv = self.q + QH * HD
        self.tail = self.kv + 2 * KVH * HD
        self.width = self.tail + 2 * LANES


class Plan:
    def __init__(self, slots, moves):
        self.length = 0
        self.slot = slots
        self.target = self.slot + moves
        self.away = self.target + moves
        self.source = self.away + moves
        self.from_away = self.source + moves
        self.arrived_length = self.from_away + moves
        self.stay = self.arrived_length + moves
        self.me = self.stay + slots - moves
        self.size = self.me + 1


def early_parts(row_count):
    return [d for d in (2, 4) if d < row_count]


def parcel_parts(refs, row_count, pages_here):
    refs, early = list(refs), early_parts(row_count)
    parts = []
    for d in range(1, row_count):
        if d in early:
            parts.append((refs.pop(0), refs.pop(0)))
        else:
            whole = refs.pop(0)
            parts.append((whole.at[:pages_here], whole.at[pages_here:]))
    return parts


class Note:
    mixed, key_value, drive, drive_low, mixing, conv_x, conv_bc = 0, 1, 2, 3, 4, 5, 8
    decay, decay_low = NS, NS + LANES


def project_kernel(
    row_ref, arrival, lengths, move_slot, move_target, table,
    tokens, gain, w_z, w_x, w_dt, w_bc, w_qkv, pool, state,
    plan, mine, theirs, *rest,
):
    inverse, wide, picked, tail, packed, in_sems, out_sems = rest[-7:]
    moves, row_count = move_slot.shape
    pages_here, slots = table.shape
    parcels = parcel_parts(rest[:-7], row_count, pages_here)
    heads, depth = w_dt.shape
    inner = heads * HP
    cols, at = Columns(inner), Plan(slots, moves)
    me, half = row_ref[0], row_count // 2

    loads = []
    for m in range(moves):
        slot = move_slot[m, me]
        for page in range(pages_here):
            loads.append(
                pltpu.make_async_copy(pool.at[table[page, slot]], packed.at[m, page], in_sems.at[m])
            )
        for part in range(2):
            loads.append(
                pltpu.make_async_copy(
                    state.at[slot, :, part * PAGE : (part + 1) * PAGE, :],
                    packed.at[m, pages_here:, :, part * NS : (part + 1) * NS],
                    in_sems.at[m],
                )
            )
    for load in loads:
        load.start()

    wide[...] = tokens[...].astype(F32)
    picked[...] = jnp.zeros_like(picked)

    def invert(t, carry):
        for s in range(slots):
            inverse[arrival[t * slots + s]] = t * slots + s
        return carry

    lax.fori_loop(0, row_count, invert, 0)

    def pick(b, carry):
        d = jnp.where(b < half, 2 * b, 2 * (b - half) + 1)
        first = lax.bitwise_xor(me, d) * slots
        for s in range(slots):
            picked[pl.ds(b * BLOCK + s, 1), :] = wide[pl.ds(inverse[first + s], 1), :]
        return carry

    lax.fori_loop(0, row_count, pick, 0)

    for m in range(moves):
        pltpu.make_async_copy(pool.at[: pages_here + heads], packed.at[m], in_sems.at[m]).wait()

    def sent(m, to):
        pages, states = to
        return (
            pltpu.make_async_copy(packed.at[m, :pages_here], pages, out_sems.at[m, 0]),
            pltpu.make_async_copy(packed.at[m, pages_here:], states, out_sems.at[m, 1]),
        )

    for m in range(moves):
        away = lax.bitwise_xor(move_target[m, me], me)
        for d, parcel in enumerate(parcels, 1):

            @pl.when(away == d)
            def _(m=m, parcel=parcel):
                for copy in sent(m, parcel):
                    copy.start()

    rows = picked[...]
    squares = jnp.sum(rows * rows, axis=1, keepdims=True)
    scaled = (rows * gain[...].astype(F32).reshape(1, depth)).astype(BF16)

    def put(start, value):
        span = slice(start, start + value.shape[1])
        mine[:, span] = value[: half * BLOCK].astype(F32)
        theirs[:, span] = value[half * BLOCK :].astype(BF16)

    put(cols.z, dot(scaled, w_z[...]))
    put(cols.x, dot(scaled, w_x[...]))
    put(cols.bc, dot(scaled, w_bc[...]))
    put(cols.q, dot(scaled, w_qkv[...]))
    tail[...] = jnp.zeros_like(tail)
    tail[:, :heads] = dot_t(scaled, w_dt[...])
    tail[:, heads : heads + 1] = squares
    high = tail[...].astype(BF16)
    put(cols.tail, high)
    put(cols.tail + LANES, tail[...] - high.astype(F32))

    stays = 0
    for s in range(slots):
        plan[at.length + s] = lengths[me * slots + s]
        leaves = move_slot[0, me] == s
        for m in range(1, moves):
            leaves = jnp.logical_or(leaves, move_slot[m, me] == s)

        @pl.when(jnp.logical_not(leaves))
        def _(s=s, stays=stays):
            plan[at.stay + stays] = s

        stays = stays + jnp.where(leaves, 0, 1)
    for m in range(moves):
        plan[at.slot + m] = move_slot[m, me]
        plan[at.target + m] = move_target[m, me]
        plan[at.away + m] = lax.bitwise_xor(move_target[m, me], me)

    def seek(i, turn):
        for m in range(moves):
            comes = move_target[m, i] == me

            @pl.when(comes)
            def _(m=m, turn=turn):
                plan[at.source + turn] = i
                plan[at.from_away + turn] = lax.bitwise_xor(i, me)
                plan[at.arrived_length + turn] = lengths[i * slots + move_slot[m, i]]

            turn = turn + jnp.where(comes, 1, 0)
        return turn

    lax.fori_loop(0, row_count, seek, I32(0))
    plan[at.me] = me
    for m in range(moves):
        for copy in sent(m, parcels[0]):
            copy.wait()


def pair_kernel(mine, theirs, own, *others):
    for j, out in enumerate((own,) + others):
        span = slice(j * BLOCK, (j + 1) * BLOCK)
        out[...] = (mine[span, :] + theirs[span, :].astype(F32)).astype(out.dtype)


def widen(per_head, inner):
    rows = per_head.shape[0]
    first = lane_iota((rows, 2 * HP)) < HP
    pieces = []
    for h in range(0, inner // HP, 2):
        pieces.append(jnp.where(first, per_head[:, h : h + 1], per_head[:, h + 1 : h + 2]))
    return pieces[0] if len(pieces) == 1 else jnp.concatenate(pieces, axis=1)


class Sums:
    def __init__(self, received, heads, width):
        self.received = received
        cols = Columns(heads * HP)
        tail = self.total(cols.tail, cols.tail + LANES) + self.total(cols.tail + LANES, cols.width)
        self.root = jnp.sqrt(tail[:, heads : heads + 1] / width + EPSILON)
        self.step_in = (tail[:, :heads] / self.root).astype(BF16).astype(F32)

    def total(self, start, stop):
        return sum(part[:, start:stop].astype(F32) for part in self.received)

    def projected(self, start, stop):
        return (self.total(start, stop) / self.root).astype(BF16).astype(F32)


def inserted(page, row, offset):
    return jnp.where(row_iota(page.shape) == offset, row, page.astype(F32)).astype(BF16)


def place_of(length, col_count):
    logical = lax.div(length, I32(PAGE))
    return lax.rem(logical, I32(col_count)), lax.div(logical, I32(col_count)), lax.rem(length, I32(PAGE))


def attend_kernel(
    col_ref, plan, table, pool, *rest, moves, heads, chip_count, col_count, width
):
    received, (pool_next, kv_new, send) = rest[:chip_count], rest[chip_count : chip_count + 3]
    pages, queries, scores, weighted, peaks, totals, in_sems, out_sems = rest[chip_count + 3 :]
    pages_here, slots = table.shape
    cols, at = Columns(heads * HP), Plan(slots, moves)
    col = col_ref[0]
    tokens_here = pages_here * PAGE
    kv_width = KVH * HD
    chunks = in_sems.shape[0]
    step = pool.shape[0] // chunks
    spans = [pl.ds(k * step, step) for k in range(chunks)]
    loads = [pltpu.make_async_copy(pool.at[span], pages.at[span], in_sems.at[k]) for k, span in enumerate(spans)]
    for load in loads:
        load.start()

    sums = Sums(received, heads, width)
    kv_new[...] = sums.projected(cols.kv, cols.tail)
    q_in = sums.projected(cols.q, cols.kv)
    for h in range(QH):
        queries[pl.ds(h, BLOCK, stride=QH), :] = q_in[:, h * HD : (h + 1) * HD]

    first_group = row_iota((QH, HD)) < QH // KVH
    lane = lane_iota((QH, tokens_here))
    position = (lax.shift_right_logical(lane, 5) * col_count + col) * PAGE + lax.bitwise_and(lane, PAGE - 1)
    for load in loads:
        load.wait()
    for s in range(slots):
        owner, local_page, offset = place_of(plan[at.length + s], col_count)
        page = table[local_page, s]
        pages[page] = inserted(pages[page], kv_new[s : s + 1, :], jnp.where(owner == col, offset, -1))
    stores = [
        pltpu.make_async_copy(pages.at[span], pool_next.at[span], out_sems.at[k]) for k, span in enumerate(spans)
    ]
    for store in stores:
        store.start()

    def cached(s, start):
        parts = [pages[table[page, s], :, start : start + kv_width] for page in range(pages_here)]
        return jnp.concatenate(parts, axis=0)

    for s in range(slots):
        query = queries[s * QH : (s + 1) * QH, :]
        query = jnp.concatenate(
            [jnp.where(first_group, query, 0.0), jnp.where(first_group, 0.0, query)], axis=1
        ).astype(BF16)
        score = dot_t(query, cached(s, 0)) * (HD ** -0.5)
        scores[s * QH : (s + 1) * QH, :] = jnp.where(position <= plan[at.length + s], score, FLOOR_SCORE)

    live_rows = slots * QH
    everything = scores[0:live_rows, :]
    peak = jnp.max(everything, axis=1, keepdims=True)
    weights = jnp.where(everything > 0.5 * FLOOR_SCORE, jnp.exp(everything - peak), 0.0)
    total = jnp.sum(weights, axis=1, keepdims=True)
    scores[0:live_rows, :] = weights
    for ref, value in ((weighted, None), (peaks, peak), (totals, total)):
        ref[live_rows:, :] = jnp.zeros((BLOCK * QH - live_rows, HD), F32)
        if value is not None:
            ref[0:live_rows, :] = jnp.broadcast_to(value, (live_rows, HD))
    for s in range(slots):
        weight = scores[s * QH : (s + 1) * QH, :]
        high = weight.astype(BF16).astype(F32)
        both = dot(jnp.concatenate([high, weight - high], axis=0).astype(BF16), cached(s, kv_width))
        joined = both[:QH] + both[QH:]
        weighted[s * QH : (s + 1) * QH, :] = jnp.where(first_group, joined[:, :HD], joined[:, HD:])

    share = QH * HD // col_count
    part = min(share, HD)
    lanes = lane_iota((BLOCK, LANES))
    for c in range(col_count):
        block = slice(c * BLOCK, (c + 1) * BLOCK)
        stats = jnp.zeros((BLOCK, LANES), F32)
        for j in range(share // part):
            head, begin = divmod(c * share + j * part, HD)
            rows = pl.ds(head, BLOCK, stride=QH)
            send[block, j * part : (j + 1) * part] = weighted[rows, :][:, begin : begin + part]
            stats = jnp.where(lanes == 2 * j, peaks[rows, :], stats)
            stats = jnp.where(lanes == 2 * j + 1, totals[rows, :], stats)
        send[block, share:] = stats
    for store in stores:
        store.wait()


def mix_kernel(
    conv_x, conv_bc, cw_x, cw_bc, dt_bias, a_log, d_skip, state, *rest, chip_count, width
):
    received = rest[:chip_count]
    conv_x_next, conv_bc_next, gated, driven_out, decay, drive, b_twice = rest[chip_count : chip_count + 7]
    readout, held, in_sems = rest[chip_count + 7 :]
    slots, inner = conv_x.shape[1], conv_x.shape[2]
    heads = dt_bias.shape[0]
    cols = Columns(inner)
    loads = []
    for s in range(slots):
        loads.append(pltpu.make_async_copy(state.at[s], held.at[s], in_sems.at[s]))
        loads[-1].start()

    sums = Sums(received, heads, width)

    def convolved(past, taps, fresh, following):
        past_rows = [past[k].astype(F32) for k in range(KW - 1)]
        total = fresh[:slots] * taps[KW - 1 : KW, :].astype(F32)
        for k in range(KW - 1):
            total = total + past_rows[k] * taps[k : k + 1, :].astype(F32)
            following[k] = past_rows[k + 1] if k < KW - 2 else fresh[:slots]
        return jnp.concatenate([silu(total), jnp.zeros((BLOCK - slots, total.shape[1]), F32)], axis=0)

    value_act = convolved(conv_x, cw_x, sums.projected(cols.x, cols.bc), conv_x_next)
    bc_act = convolved(conv_bc, cw_bc, sums.projected(cols.bc, cols.q), conv_bc_next)
    bc_act = bc_act.astype(BF16).astype(F32)
    b_in, c_val = bc_act[:, :NS], bc_act[:, NS:]
    b_twice[...] = jnp.concatenate([b_in, b_in], axis=0)
    c_out = c_val.astype(BF16)

    shifted = sums.step_in + dt_bias[...].reshape(1, heads)
    step_size = jnp.maximum(shifted, 0.0) + jnp.log(1.0 + jnp.exp(-jnp.abs(shifted)))
    rate = jnp.exp(-jnp.exp(a_log[...].reshape(1, heads)) * step_size)
    decay[...] = rate
    driven = widen(step_size, inner) * value_act
    driven_out[...] = driven
    high = driven.astype(BF16).astype(F32)
    drive[...] = jnp.transpose(jnp.concatenate([high, driven - high], axis=0)).astype(BF16)

    readout[...] = jnp.zeros_like(readout)

    for s in range(slots):
        loads[s].wait()
        value = dot_t(c_out, held[s].reshape(inner, NS))
        readout[s : s + 1, :] = value[s : s + 1]

    gate = silu(sums.projected(cols.z, cols.x))
    b_dot_c = jnp.sum(b_in * c_val, axis=1, keepdims=True)
    skip = widen(jnp.broadcast_to(d_skip[...].reshape(1, heads), (BLOCK, heads)), inner)
    total = widen(rate, inner) * readout[...] + driven * b_dot_c + skip * value_act
    gated[...] = (total * gate).astype(BF16).astype(F32)


def stay_kernel(plan, drive, decay, b_twice, state, state_next, held, made, in_sems, out_sems, *, moves):
    stays = held.shape[0]
    at = Plan(state.shape[0], moves)
    loads = []
    for j in range(stays):
        loads.append(pltpu.make_async_copy(state.at[plan[at.stay + j]], held.at[j], in_sems.at[j]))
        loads[-1].start()
    stores = []
    for j in range(stays):
        slot = plan[at.stay + j]
        loads[j].wait()
        advance_state(slot, held.at[j], b_twice, drive, decay, made.at[j])
        stores.append(pltpu.make_async_copy(made.at[j], state_next.at[slot], out_sems.at[j]))
        stores[-1].start()
    for store in stores:
        store.wait()


def advance_state(slot, prior, b_twice, drive, decay, result):
    heads = result.shape[0]
    twice = b_twice[...]
    half = twice.shape[0] // 2
    row = row_iota(twice.shape)
    selected = jnp.where((row == slot) | (row == slot + half), twice, 0.0).astype(BF16)
    outer = dot(drive[...], selected).reshape(heads, HP, NS)
    for h in range(heads):
        rate = decay[pl.ds(slot, 1), h : h + 1]
        result[h] = (rate * prior[h].astype(F32) + outer[h]).astype(BF16)


def output_kernel(gated, w_ssm, w_attn, partials, send, *, slots, col_count):
    share = w_attn.shape[0]
    part = min(share, HD)
    blocks = [partials[c * BLOCK : (c + 1) * BLOCK, :] for c in range(col_count)]
    pieces = []
    for j in range(share // part):
        peaks = [b[:, share + 2 * j : share + 2 * j + 1] for b in blocks]
        joint = functools.reduce(jnp.maximum, peaks)
        factors = [jnp.exp(p - joint) for p in peaks]
        total = sum(f * b[:, share + 2 * j + 1 : share + 2 * j + 2] for f, b in zip(factors, blocks))
        value = sum(f * b[:, j * part : (j + 1) * part] for f, b in zip(factors, blocks))
        pieces.append(value / total)
    joined = pieces[0] if len(pieces) == 1 else jnp.concatenate(pieces, axis=1)
    right = jnp.where(row_iota(joined.shape) < slots, joined, 0.0).astype(BF16)
    left = gated[...].astype(BF16)
    columns = w_ssm.shape[1] // col_count
    for c in range(col_count):
        span = slice(c * columns, (c + 1) * columns)
        terms = dot(left, w_ssm[:, span]) + dot(right, w_attn[:, span])
        send[c * BLOCK : (c + 1) * BLOCK, :] = terms.astype(BF16)


def total_kernel(
    plan, kv_new, driven, decay, b_twice, conv_x, conv_bc, terms, send, mixed, block, *, moves, col_count
):
    at = Plan(conv_x.shape[1], moves)
    total = sum(terms[c * BLOCK : (c + 1) * BLOCK, :].astype(F32) for c in range(col_count))
    mixed[...] = total
    send[pl.ds(pl.multiple_of(plan[at.me] * BLOCK, BLOCK), BLOCK), : total.shape[1]] = total.astype(BF16)

    block[...] = jnp.zeros_like(block)
    for m in range(moves):
        row = pl.ds(plan[at.slot + m], 1)

        def put(index, value, start=0):
            block[index : index + 1, start : start + value.shape[1]] = value

        put(Note.mixed, mixed[row, :])
        put(Note.key_value, kv_new[row, :])
        for index, value, start, low_index, low_start in (
            (Note.drive, driven[row, :], 0, Note.drive_low, 0),
            (Note.mixing, decay[row, :], Note.decay, Note.mixing, Note.decay_low),
        ):
            high = value.astype(BF16).astype(F32)
            put(index, high, start)
            put(low_index, value - high, low_start)
        put(Note.mixing, b_twice[row, :])
        for k in range(KW - 1):
            put(Note.conv_x + k, conv_x[k, row, :])
            put(Note.conv_bc + k, conv_bc[k, row, :])
        start = pl.multiple_of(plan[at.target + m] * BLOCK, BLOCK)
        send[pl.ds(start, BLOCK), :] = block[...].astype(BF16)


def arrive_kernel(
    col_ref, plan, table, conv_x, conv_bc, state_in, pool_in, notes, *rest,
    moves, row_count, col_count,
):
    del state_in, pool_in
    parcel_count = row_count - 1 + len(early_parts(row_count))
    parcels, rest = rest[:parcel_count], rest[parcel_count:]
    pages_here, slots = table.shape
    inner = conv_x.shape[2]
    heads = inner // HP
    at = Plan(slots, moves)
    mixed, conv_x_next, conv_bc_next, state_next, pool_next = rest[:5]
    packed, made, drive, decay, b_twice, window_x, window_bc, window_mixed, in_sems, out_sems = rest[5:]
    col = col_ref[0]
    parcels = parcel_parts(parcels, row_count, pages_here)

    def loaded(m, parcel):
        pages, states = parcel
        return (
            pltpu.make_async_copy(pages, packed.at[m, :pages_here], in_sems.at[m, 0]),
            pltpu.make_async_copy(states, packed.at[m, pages_here:], in_sems.at[m, 1]),
        )

    for m in range(moves):
        for d, parcel in enumerate(parcels, 1):

            @pl.when(plan[at.from_away + m] == d)
            def _(m=m, parcel=parcel):
                for copy in loaded(m, parcel):
                    copy.start()


    for k in range(KW - 1):
        window_x[k] = conv_x[k]
        window_bc[k] = conv_bc[k]
    home = pl.multiple_of(plan[at.me] * BLOCK, BLOCK)
    window_mixed[...] = notes[pl.ds(home, BLOCK), : window_mixed.shape[1]].astype(F32)
    rows = []
    b_twice[...] = jnp.zeros_like(b_twice)
    half = b_twice.shape[0] // 2
    for m in range(moves):
        start = pl.multiple_of(plan[at.source + m] * BLOCK, BLOCK)
        note = notes[pl.ds(start, BLOCK), :].astype(F32)
        rows.append(note)
        row = pl.ds(plan[at.slot + m], 1)
        window_mixed[row, :] = note[Note.mixed : Note.mixed + 1, : window_mixed.shape[1]]
        for k in range(KW - 1):
            window_x[k, row, :] = note[Note.conv_x + k : Note.conv_x + k + 1, :inner]
            window_bc[k, row, :] = note[Note.conv_bc + k : Note.conv_bc + k + 1, : 2 * NS]
        mixing = note[Note.mixing : Note.mixing + 1, :]
        b_twice[m : m + 1, :] = mixing[:, :NS]
        b_twice[half + m : half + m + 1, :] = mixing[:, :NS]
        decay[m : m + 1, :] = (
            mixing[:, Note.decay : Note.decay + heads] + mixing[:, Note.decay_low : Note.decay_low + heads]
        )
    padding = [jnp.zeros((half - moves, inner), F32)]
    stacked = [note[Note.drive : Note.drive + 1, :inner] for note in rows] + padding
    stacked += [note[Note.drive_low : Note.drive_low + 1, :inner] for note in rows] + padding
    drive[...] = jnp.transpose(jnp.concatenate(stacked, axis=0)).astype(BF16)
    mixed[...] = window_mixed[0:slots, :].astype(BF16)
    for k in range(KW - 1):
        conv_x_next[k] = window_x[k].astype(BF16)
        conv_bc_next[k] = window_bc[k].astype(BF16)

    stores = []
    for m in range(moves):
        slot = plan[at.slot + m]
        for copy in loaded(m, parcels[0]):
            copy.wait()
        owner, local_page, offset = place_of(plan[at.arrived_length + m], col_count)
        key_value = rows[m][Note.key_value : Note.key_value + 1, : 2 * KVH * HD]

        @pl.when(owner == col)
        def _(m=m, local_page=local_page, offset=offset, key_value=key_value):
            packed[m, local_page] = inserted(packed[m, local_page], key_value, offset)

        for page in range(pages_here):
            stores.append(
                pltpu.make_async_copy(
                    packed.at[m, page], pool_next.at[table[page, slot]], out_sems.at[m, page]
                )
            )
            stores[-1].start()
        prior = [
            jnp.concatenate([packed[m, pages_here + h, :, :NS], packed[m, pages_here + h, :, NS:]], axis=0)
            for h in range(heads)
        ]
        advance_state(m, prior, b_twice, drive, decay, made.at[m])
        stores.append(pltpu.make_async_copy(made.at[m], state_next.at[slot], out_sems.at[m, pages_here]))
        stores[-1].start()
    for store in stores:
        store.wait()


def shape(dims, dtype):
    return jax.ShapeDtypeStruct(tuple(dims), dtype)


def params(limit=VMEM_LIMIT):
    return pltpu.CompilerParams(vmem_limit_bytes=limit)


def exchange(value, axis):
    return lax.all_to_all(value, axis, split_axis=0, concat_axis=0, tiled=True)


def trade(block, axis, d):
    return lax.ppermute(block, axis, [(i, i ^ d) for i in range(lax.axis_size(axis))])


def ordered(value, first):
    return lax.optimization_barrier((value, first))[0]


def local(
    tokens, arrival, cache_lengths, move_slot, move_target, page_table, kv_pool, ssm_state,
    conv_x, conv_bc, norm_gain, weight_z, weight_x, weight_dt, weight_bc, weight_qkv,
    conv_weight_x, conv_weight_bc, dt_bias, a_log, d_skip, weight_ssm_out, weight_attn_out,
):
    row_count = lax.axis_size("rows")
    col_count = lax.axis_size("cols")
    row_index = lax.axis_index("rows").astype(I32).reshape(1)
    col_index = lax.axis_index("cols").astype(I32).reshape(1)
    slots, heads = ssm_state.shape[0], ssm_state.shape[1]
    total, depth = tokens.shape
    moves = move_slot.shape[1]
    pages_here, width = page_table.shape[3], kv_pool.shape[3]
    inner = heads * HP
    stays = slots - moves
    cols, at = Columns(inner), Plan(slots, moves)
    table = page_table[0, 0].T
    pool = kv_pool[:, 0]
    past_x, past_bc = conv_x.transpose(1, 0, 2), conv_bc.transpose(1, 0, 2)
    rows = row_count * BLOCK
    model = depth * row_count
    share = QH * HD // col_count
    parcel = (pages_here + heads, PAGE, width)
    parcels_here = pltpu.VMEM((moves,) + parcel, BF16)

    chip_count = row_count // 2
    early = early_parts(row_count)
    parcels_out = []
    for d in range(1, row_count):
        if d in early:
            parcels_out += [shape((pages_here,) + parcel[1:], BF16), shape((heads,) + parcel[1:], BF16)]
        else:
            parcels_out.append(shape(parcel, BF16))
    plan, mine, theirs, *parcels = pl.pallas_call(
        project_kernel,
        out_shape=[
            shape((at.size,), I32),
            shape((chip_count * BLOCK, cols.width), F32),
            shape((chip_count * BLOCK, cols.width), BF16),
        ]
        + parcels_out,
        in_specs=[SMEM_SPEC] * 6 + [VMEM_SPEC] * 7 + [ANY_SPEC] * 2,
        out_specs=[SMEM_SPEC] + [VMEM_SPEC] * 2 + [ANY_SPEC] * len(parcels_out),
        scratch_shapes=[
            pltpu.SMEM((total,), I32),
            pltpu.VMEM((total, depth), F32),
            pltpu.VMEM((rows, depth), F32),
            pltpu.VMEM((rows, LANES), F32),
            parcels_here,
            pltpu.SemaphoreType.DMA((moves,)),
            pltpu.SemaphoreType.DMA((moves, 2)),
        ],
        compiler_params=params(FIRST_LIMIT),
        cost_estimate=BRIEF,
        name="project",
    )(
        row_index, arrival, cache_lengths, move_slot.T, move_target.T, table,
        tokens, norm_gain, weight_z, weight_x, weight_dt.T, weight_bc, weight_qkv, pool, ssm_state,
    )
    moving = {}
    for d in range(1, row_count):
        moving[d] = [parcels.pop(0) for _ in range(2 if d in early else 1)]
    ahead = []
    for d in early:
        moving[d][0] = trade(moving[d][0], "rows", d)
        ahead.append(moving[d][0])

    sums = pl.pallas_call(
        pair_kernel,
        out_shape=[shape((BLOCK, cols.width), F32)] + [shape((BLOCK, cols.width), BF16)] * (chip_count - 1),
        in_specs=[VMEM_SPEC] * 2,
        out_specs=[VMEM_SPEC] * chip_count,
        compiler_params=params(FIRST_LIMIT),
        cost_estimate=BRIEF,
        name="pair",
    )(mine, trade(theirs, "rows", 1))
    received = [sums[0]] + [trade(block, "rows", 2 * j) for j, block in enumerate(sums[1:], 1)]

    def migrate(parts, after):
        for d in parts:
            moving[d][-1] = trade(ordered(moving[d][-1], after), "rows", d)

    order = [d for j in range(2) for d in range(2 + j, row_count, 2)] + [1]
    received = ordered(received, ahead)
    migrate(order[:-2], received)

    pool_next, kv_new, partials = pl.pallas_call(
        functools.partial(
            attend_kernel, moves=moves, heads=heads, chip_count=chip_count, col_count=col_count, width=model
        ),
        out_shape=[
            shape(pool.shape, BF16),
            shape((BLOCK, 2 * KVH * HD), F32),
            shape((col_count * BLOCK, share + LANES), F32),
        ],
        in_specs=[SMEM_SPEC] * 3 + [ANY_SPEC] + [VMEM_SPEC] * chip_count,
        out_specs=[ANY_SPEC] + [VMEM_SPEC] * 2,
        scratch_shapes=[
            pltpu.VMEM(pool.shape, BF16),
            pltpu.VMEM((BLOCK * QH, HD), F32),
            pltpu.VMEM((BLOCK * QH, pages_here * PAGE), F32),
            pltpu.VMEM((BLOCK * QH, HD), F32),
            pltpu.VMEM((BLOCK * QH, HD), F32),
            pltpu.VMEM((BLOCK * QH, HD), F32),
            pltpu.SemaphoreType.DMA((2 if pool.shape[0] % 4 else 4,)),
            pltpu.SemaphoreType.DMA((2 if pool.shape[0] % 4 else 4,)),
        ],
        compiler_params=params(),
        cost_estimate=BRIEF,
        name="attend",
    )(col_index, plan, table, pool, *received)
    received = ordered(received, partials)
    partials = exchange(partials, "cols")

    next_x, next_bc, gated, driven, decay, drive, b_twice = pl.pallas_call(
        functools.partial(mix_kernel, chip_count=chip_count, width=model),
        out_shape=(
            shape(past_x.shape, F32),
            shape(past_bc.shape, F32),
            shape((BLOCK, inner), F32),
            shape((BLOCK, inner), F32),
            shape((BLOCK, heads), F32),
            shape((inner, 2 * BLOCK), BF16),
            shape((2 * BLOCK, NS), F32),
        ),
        in_specs=[VMEM_SPEC] * 7 + [ANY_SPEC] + [VMEM_SPEC] * chip_count,
        out_specs=(VMEM_SPEC,) * 7,
        scratch_shapes=[
            pltpu.VMEM((BLOCK, inner), F32),
            pltpu.VMEM((slots, heads, HP, NS), BF16),
            pltpu.SemaphoreType.DMA((slots,)),
        ],
        compiler_params=params(),
        cost_estimate=BRIEF,
        name="mix",
    )(past_x, past_bc, conv_weight_x, conv_weight_bc, dt_bias, a_log, d_skip, ssm_state, *received)

    columns = weight_ssm_out.shape[1] // col_count
    terms = pl.pallas_call(
        functools.partial(output_kernel, slots=slots, col_count=col_count),
        out_shape=shape((col_count * BLOCK, columns), BF16),
        in_specs=[VMEM_SPEC] * 4,
        out_specs=VMEM_SPEC,
        compiler_params=params(),
        cost_estimate=BRIEF,
        name="output",
    )(gated, weight_ssm_out, weight_attn_out, partials)
    migrate(order[-2:], terms)
    drive = ordered(drive, terms)
    terms = exchange(terms, "cols")
    state_next = pl.pallas_call(
        functools.partial(stay_kernel, moves=moves),
        out_shape=shape(ssm_state.shape, BF16),
        in_specs=[SMEM_SPEC] + [VMEM_SPEC] * 3 + [ANY_SPEC],
        out_specs=ANY_SPEC,
        scratch_shapes=[
            pltpu.VMEM((stays, heads, HP, NS), BF16),
            pltpu.VMEM((stays, heads, HP, NS), BF16),
            pltpu.SemaphoreType.DMA((stays,)),
            pltpu.SemaphoreType.DMA((stays,)),
        ],
        compiler_params=params(),
        cost_estimate=BRIEF,
        name="stay",
    )(plan, drive, decay, b_twice, ssm_state)

    note = (BLOCK, max(inner, 2 * NS, 2 * KVH * HD, columns))
    notes = pl.pallas_call(
        functools.partial(total_kernel, moves=moves, col_count=col_count),
        out_shape=shape((rows, note[1]), BF16),
        in_specs=[SMEM_SPEC] + [VMEM_SPEC] * 7,
        out_specs=VMEM_SPEC,
        scratch_shapes=[pltpu.VMEM((BLOCK, columns), F32), pltpu.VMEM(note, F32)],
        compiler_params=params(),
        cost_estimate=BRIEF,
        name="total",
    )(plan, kv_new, driven, decay, b_twice, next_x, next_bc, terms)
    notes = exchange(notes, "rows")

    mixed, conv_x_next, conv_bc_next, state_next, pool_next = pl.pallas_call(
        functools.partial(arrive_kernel, moves=moves, row_count=row_count, col_count=col_count),
        out_shape=(
            shape((slots, columns), BF16),
            shape(past_x.shape, BF16),
            shape(past_bc.shape, BF16),
            shape(ssm_state.shape, BF16),
            shape(pool.shape, BF16),
        ),
        in_specs=[SMEM_SPEC] * 3 + [VMEM_SPEC] * 2 + [ANY_SPEC] * 2 + [VMEM_SPEC] + [ANY_SPEC] * len(parcels_out),
        out_specs=[VMEM_SPEC] * 3 + [ANY_SPEC] * 2,
        scratch_shapes=[
            parcels_here,
            pltpu.VMEM((moves, heads, HP, NS), BF16),
            pltpu.VMEM((inner, 2 * BLOCK), BF16),
            pltpu.VMEM((BLOCK, heads), F32),
            pltpu.VMEM((2 * BLOCK, NS), F32),
            pltpu.VMEM((KW - 1, slots, inner), F32),
            pltpu.VMEM((KW - 1, slots, 2 * NS), F32),
            pltpu.VMEM((BLOCK, columns), F32),
            pltpu.SemaphoreType.DMA((moves, 2)),
            pltpu.SemaphoreType.DMA((moves, pages_here + 1)),
        ],
        input_output_aliases={5: 3, 6: 4},
        compiler_params=params(LAST_LIMIT),
        cost_estimate=BRIEF,
        name="arrive",
    )(
        col_index, plan, table, next_x, next_bc, state_next, pool_next, notes,
        *(part for d in range(1, row_count) for part in moving[d]),
    )
    return (
        mixed, state_next, conv_x_next.transpose(1, 0, 2), conv_bc_next.transpose(1, 0, 2), pool_next[:, None]
    )


def solution(mesh):
    in_specs = (
        P(None, "rows"),
        P(),
        P(),
        P(),
        P(),
        P("rows", "cols", None, None),
        P("rows", "cols", None, None),
        P("rows", "cols", None, None),
        P("rows", None, "cols"),
        P("rows", None, None),
        P("rows"),
        P("rows", "cols"),
        P("rows", "cols"),
        P("rows", "cols"),
        P("rows", None),
        P("rows", None),
        P(None, "cols"),
        P(),
        P("cols"),
        P("cols"),
        P("cols"),
        P("cols", None),
        P("cols", None),
    )
    out_specs = (
        P("rows", "cols"),
        P("rows", "cols", None, None),
        P("rows", None, "cols"),
        P("rows", None, None),
        P("rows", "cols", None, None),
    )
    return jax.shard_map(local, mesh=mesh, in_specs=in_specs, out_specs=out_specs, check_vma=False)
```

```python
import functools

import jax
import jax.numpy as jnp
from jax import lax
from jax.experimental import pallas as pl
from jax.experimental.pallas import tpu as pltpu
from jax.sharding import PartitionSpec as P

HP = 64
NS = 256
KW = 4
QH = 8
KVH = 2
HD = 128
PAGE = 32
LANES = 128
BLOCK = 16

EPSILON = 1e-05
FLOOR_SCORE = -1e30
FIRST_LIMIT = 60 * 1024 * 1024
VMEM_LIMIT = 55 * 1024 * 1024
LAST_LIMIT = 24 * 1024 * 1024

F32 = jnp.float32
BF16 = jnp.bfloat16
I32 = jnp.int32

SMEM_SPEC = pl.BlockSpec(memory_space=pltpu.SMEM)
BRIEF = pl.CostEstimate(flops=1, bytes_accessed=1, transcendentals=0)
VMEM_SPEC = pl.BlockSpec(memory_space=pltpu.VMEM)
ANY_SPEC = pl.BlockSpec(memory_space=pl.ANY)


def silu(v):
    return v / (1.0 + jnp.exp(-v))


def dot(a, b):
    return jnp.dot(a, b, preferred_element_type=F32)


def dot_t(a, b):
    return lax.dot_general(a, b, (((1,), (1,)), ((), ())), preferred_element_type=F32)


def row_iota(shape):
    return lax.broadcasted_iota(I32, shape, 0)


def lane_iota(shape):
    return lax.broadcasted_iota(I32, shape, 1)


class Columns:
    def __init__(self, inner):
        self.z = 0
        self.x = inner
        self.bc = 2 * inner
        self.q = self.bc + 2 * NS
        self.kv = self.q + QH * HD
        self.tail = self.kv + 2 * KVH * HD
        self.width = self.tail + 2 * LANES


class Plan:
    def __init__(self, slots, moves):
        self.length = 0
        self.slot = slots
        self.target = self.slot + moves
        self.away = self.target + moves
        self.source = self.away + moves
        self.from_away = self.source + moves
        self.arrived_length = self.from_away + moves
        self.stay = self.arrived_length + moves
        self.me = self.stay + slots - moves
        self.size = self.me + 1


class Note:
    mixed, key_value, drive, drive_low, mixing, conv_x, conv_bc = 0, 1, 2, 3, 4, 5, 8
    decay, decay_low = NS, NS + LANES


def project_kernel(
    row_ref, arrival, lengths, move_slot, move_target,
    tokens, gain, w_z, w_x, w_dt, w_bc, w_qkv,
    plan, mine, theirs,
    inverse, wide, picked, tail,
    *, slots,
):
    moves, row_count = move_slot.shape
    heads, depth = w_dt.shape
    inner = heads * HP
    cols, at = Columns(inner), Plan(slots, moves)
    me, half = row_ref[0], row_count // 2

    wide[...] = tokens[...].astype(F32)
    picked[...] = jnp.zeros_like(picked)

    def invert(t, carry):
        for s in range(slots):
            inverse[arrival[t * slots + s]] = t * slots + s
        return carry

    lax.fori_loop(0, row_count, invert, 0)

    def pick(b, carry):
        d = jnp.where(b < half, 2 * b, 2 * (b - half) + 1)
        first = lax.bitwise_xor(me, d) * slots
        for s in range(slots):
            picked[pl.ds(b * BLOCK + s, 1), :] = wide[pl.ds(inverse[first + s], 1), :]
        return carry

    lax.fori_loop(0, row_count, pick, 0)

    rows = picked[...]
    squares = jnp.sum(rows * rows, axis=1, keepdims=True)
    scaled = (rows * gain[...].astype(F32).reshape(1, depth)).astype(BF16)

    def put(start, value):
        span = slice(start, start + value.shape[1])
        mine[:, span] = value[: half * BLOCK].astype(F32)
        theirs[:, span] = value[half * BLOCK :].astype(BF16)

    put(cols.z, dot(scaled, w_z[...]))
    put(cols.x, dot(scaled, w_x[...]))
    put(cols.bc, dot(scaled, w_bc[...]))
    put(cols.q, dot(scaled, w_qkv[...]))
    tail[...] = jnp.zeros_like(tail)
    tail[:, :heads] = dot_t(scaled, w_dt[...])
    tail[:, heads : heads + 1] = squares
    high = tail[...].astype(BF16)
    put(cols.tail, high)
    put(cols.tail + LANES, tail[...] - high.astype(F32))

    stays = 0
    for s in range(slots):
        plan[at.length + s] = lengths[me * slots + s]
        leaves = move_slot[0, me] == s
        for m in range(1, moves):
            leaves = jnp.logical_or(leaves, move_slot[m, me] == s)

        @pl.when(jnp.logical_not(leaves))
        def _(s=s, stays=stays):
            plan[at.stay + stays] = s

        stays = stays + jnp.where(leaves, 0, 1)
    for m in range(moves):
        plan[at.slot + m] = move_slot[m, me]
        plan[at.target + m] = move_target[m, me]
        plan[at.away + m] = lax.bitwise_xor(move_target[m, me], me)

    def seek(i, turn):
        for m in range(moves):
            comes = move_target[m, i] == me

            @pl.when(comes)
            def _(m=m, turn=turn):
                plan[at.source + turn] = i
                plan[at.from_away + turn] = lax.bitwise_xor(i, me)
                plan[at.arrived_length + turn] = lengths[i * slots + move_slot[m, i]]

            turn = turn + jnp.where(comes, 1, 0)
        return turn

    lax.fori_loop(0, row_count, seek, I32(0))
    plan[at.me] = me


def pack_kernel(plan, table, pool, state, *rest, moves, row_count):
    pages_here, slots = table.shape
    at = Plan(slots, moves)
    parcels = rest[: row_count - 1]
    packed, in_sems, out_sems = rest[row_count - 1 :]
    loads = []
    for m in range(moves):
        slot = plan[at.slot + m]
        loads.append([])
        for page in range(pages_here):
            loads[m].append(
                pltpu.make_async_copy(pool.at[table[page, slot]], packed.at[m, page], in_sems.at[m, page])
            )
        for part in range(2):
            loads[m].append(
                pltpu.make_async_copy(
                    state.at[slot, :, part * PAGE : (part + 1) * PAGE, :],
                    packed.at[m, pages_here:, :, part * NS : (part + 1) * NS],
                    in_sems.at[m, pages_here + part],
                )
            )
        for load in loads[m]:
            load.start()
    for m in range(moves):
        for load in loads[m]:
            load.wait()
        for d, parcel in enumerate(parcels, 1):

            @pl.when(plan[at.away + m] == d)
            def _(m=m, parcel=parcel):
                pltpu.make_async_copy(packed.at[m], parcel, out_sems.at[m]).start()

    for m in range(moves):
        pltpu.make_async_copy(packed.at[m], parcels[0], out_sems.at[m]).wait()


def pair_kernel(mine, theirs, own, *others):
    for j, out in enumerate((own,) + others):
        span = slice(j * BLOCK, (j + 1) * BLOCK)
        out[...] = (mine[span, :] + theirs[span, :].astype(F32)).astype(out.dtype)


def widen(per_head, inner):
    rows = per_head.shape[0]
    first = lane_iota((rows, 2 * HP)) < HP
    pieces = []
    for h in range(0, inner // HP, 2):
        pieces.append(jnp.where(first, per_head[:, h : h + 1], per_head[:, h + 1 : h + 2]))
    return pieces[0] if len(pieces) == 1 else jnp.concatenate(pieces, axis=1)


class Sums:
    def __init__(self, received, heads, width):
        self.received = received
        cols = Columns(heads * HP)
        tail = self.total(cols.tail, cols.tail + LANES) + self.total(cols.tail + LANES, cols.width)
        self.root = jnp.sqrt(tail[:, heads : heads + 1] / width + EPSILON)
        self.step_in = (tail[:, :heads] / self.root).astype(BF16).astype(F32)

    def total(self, start, stop):
        return sum(part[:, start:stop].astype(F32) for part in self.received)

    def projected(self, start, stop):
        return (self.total(start, stop) / self.root).astype(BF16).astype(F32)


def inserted(page, row, offset):
    return jnp.where(row_iota(page.shape) == offset, row, page.astype(F32)).astype(BF16)


def place_of(length, col_count):
    logical = lax.div(length, I32(PAGE))
    return lax.rem(logical, I32(col_count)), lax.div(logical, I32(col_count)), lax.rem(length, I32(PAGE))


def attend_kernel(
    col_ref, plan, table, pool, *rest, moves, heads, chip_count, col_count, width
):
    received, (pool_next, kv_new, send) = rest[:chip_count], rest[chip_count : chip_count + 3]
    pages, queries, scores, weighted, peaks, totals, in_sems, out_sems = rest[chip_count + 3 :]
    pages_here, slots = table.shape
    cols, at = Columns(heads * HP), Plan(slots, moves)
    col = col_ref[0]
    tokens_here = pages_here * PAGE
    kv_width = KVH * HD
    chunks = in_sems.shape[0]
    step = pool.shape[0] // chunks
    spans = [pl.ds(k * step, step) for k in range(chunks)]
    loads = [pltpu.make_async_copy(pool.at[span], pages.at[span], in_sems.at[k]) for k, span in enumerate(spans)]
    for load in loads:
        load.start()

    sums = Sums(received, heads, width)
    kv_new[...] = sums.projected(cols.kv, cols.tail)
    q_in = sums.projected(cols.q, cols.kv)
    for h in range(QH):
        queries[pl.ds(h, BLOCK, stride=QH), :] = q_in[:, h * HD : (h + 1) * HD]

    first_group = row_iota((QH, HD)) < QH // KVH
    lane = lane_iota((QH, tokens_here))
    position = (lax.shift_right_logical(lane, 5) * col_count + col) * PAGE + lax.bitwise_and(lane, PAGE - 1)
    for load in loads:
        load.wait()
    for s in range(slots):
        owner, local_page, offset = place_of(plan[at.length + s], col_count)
        page = table[local_page, s]
        pages[page] = inserted(pages[page], kv_new[s : s + 1, :], jnp.where(owner == col, offset, -1))
    stores = [
        pltpu.make_async_copy(pages.at[span], pool_next.at[span], out_sems.at[k]) for k, span in enumerate(spans)
    ]
    for store in stores:
        store.start()

    def cached(s, start):
        parts = [pages[table[page, s], :, start : start + kv_width] for page in range(pages_here)]
        return jnp.concatenate(parts, axis=0)

    for s in range(slots):
        query = queries[s * QH : (s + 1) * QH, :]
        query = jnp.concatenate(
            [jnp.where(first_group, query, 0.0), jnp.where(first_group, 0.0, query)], axis=1
        ).astype(BF16)
        score = dot_t(query, cached(s, 0)) * (HD ** -0.5)
        scores[s * QH : (s + 1) * QH, :] = jnp.where(position <= plan[at.length + s], score, FLOOR_SCORE)

    live_rows = slots * QH
    everything = scores[0:live_rows, :]
    peak = jnp.max(everything, axis=1, keepdims=True)
    weights = jnp.where(everything > 0.5 * FLOOR_SCORE, jnp.exp(everything - peak), 0.0)
    total = jnp.sum(weights, axis=1, keepdims=True)
    scores[0:live_rows, :] = weights
    for ref, value in ((weighted, None), (peaks, peak), (totals, total)):
        ref[live_rows:, :] = jnp.zeros((BLOCK * QH - live_rows, HD), F32)
        if value is not None:
            ref[0:live_rows, :] = jnp.broadcast_to(value, (live_rows, HD))
    for s in range(slots):
        weight = scores[s * QH : (s + 1) * QH, :]
        high = weight.astype(BF16).astype(F32)
        both = dot(jnp.concatenate([high, weight - high], axis=0).astype(BF16), cached(s, kv_width))
        joined = both[:QH] + both[QH:]
        weighted[s * QH : (s + 1) * QH, :] = jnp.where(first_group, joined[:, :HD], joined[:, HD:])

    share = QH * HD // col_count
    part = min(share, HD)
    lanes = lane_iota((BLOCK, LANES))
    for c in range(col_count):
        block = slice(c * BLOCK, (c + 1) * BLOCK)
        stats = jnp.zeros((BLOCK, LANES), F32)
        for j in range(share // part):
            head, begin = divmod(c * share + j * part, HD)
            rows = pl.ds(head, BLOCK, stride=QH)
            send[block, j * part : (j + 1) * part] = weighted[rows, :][:, begin : begin + part]
            stats = jnp.where(lanes == 2 * j, peaks[rows, :], stats)
            stats = jnp.where(lanes == 2 * j + 1, totals[rows, :], stats)
        send[block, share:] = stats
    for store in stores:
        store.wait()


def mix_kernel(
    conv_x, conv_bc, cw_x, cw_bc, dt_bias, a_log, d_skip, state, *rest, chip_count, width
):
    received = rest[:chip_count]
    conv_x_next, conv_bc_next, gated, driven_out, decay, drive, b_twice = rest[chip_count : chip_count + 7]
    readout, held, in_sems = rest[chip_count + 7 :]
    slots, inner = conv_x.shape[1], conv_x.shape[2]
    heads = dt_bias.shape[0]
    cols = Columns(inner)
    loads = []
    for s in range(slots):
        loads.append(pltpu.make_async_copy(state.at[s], held.at[s], in_sems.at[s]))
        loads[-1].start()

    sums = Sums(received, heads, width)

    def convolved(past, taps, fresh, following):
        past_rows = [past[k].astype(F32) for k in range(KW - 1)]
        total = fresh[:slots] * taps[KW - 1 : KW, :].astype(F32)
        for k in range(KW - 1):
            total = total + past_rows[k] * taps[k : k + 1, :].astype(F32)
            following[k] = past_rows[k + 1] if k < KW - 2 else fresh[:slots]
        return jnp.concatenate([silu(total), jnp.zeros((BLOCK - slots, total.shape[1]), F32)], axis=0)

    value_act = convolved(conv_x, cw_x, sums.projected(cols.x, cols.bc), conv_x_next)
    bc_act = convolved(conv_bc, cw_bc, sums.projected(cols.bc, cols.q), conv_bc_next)
    bc_act = bc_act.astype(BF16).astype(F32)
    b_in, c_val = bc_act[:, :NS], bc_act[:, NS:]
    b_twice[...] = jnp.concatenate([b_in, b_in], axis=0)
    c_out = c_val.astype(BF16)

    shifted = sums.step_in + dt_bias[...].reshape(1, heads)
    step_size = jnp.maximum(shifted, 0.0) + jnp.log(1.0 + jnp.exp(-jnp.abs(shifted)))
    rate = jnp.exp(-jnp.exp(a_log[...].reshape(1, heads)) * step_size)
    decay[...] = rate
    driven = widen(step_size, inner) * value_act
    driven_out[...] = driven
    high = driven.astype(BF16).astype(F32)
    drive[...] = jnp.transpose(jnp.concatenate([high, driven - high], axis=0)).astype(BF16)

    readout[...] = jnp.zeros_like(readout)

    for s in range(slots):
        loads[s].wait()
        value = dot_t(c_out, held[s].reshape(inner, NS))
        readout[s : s + 1, :] = value[s : s + 1]

    gate = silu(sums.projected(cols.z, cols.x))
    b_dot_c = jnp.sum(b_in * c_val, axis=1, keepdims=True)
    skip = widen(jnp.broadcast_to(d_skip[...].reshape(1, heads), (BLOCK, heads)), inner)
    total = widen(rate, inner) * readout[...] + driven * b_dot_c + skip * value_act
    gated[...] = (total * gate).astype(BF16).astype(F32)


def stay_kernel(plan, drive, decay, b_twice, state, state_next, held, made, in_sems, out_sems, *, moves):
    stays = held.shape[0]
    at = Plan(state.shape[0], moves)
    loads = []
    for j in range(stays):
        loads.append(pltpu.make_async_copy(state.at[plan[at.stay + j]], held.at[j], in_sems.at[j]))
        loads[-1].start()
    stores = []
    for j in range(stays):
        slot = plan[at.stay + j]
        loads[j].wait()
        advance_state(slot, held.at[j], b_twice, drive, decay, made.at[j])
        stores.append(pltpu.make_async_copy(made.at[j], state_next.at[slot], out_sems.at[j]))
        stores[-1].start()
    for store in stores:
        store.wait()


def advance_state(slot, prior, b_twice, drive, decay, result):
    heads = result.shape[0]
    twice = b_twice[...]
    half = twice.shape[0] // 2
    row = row_iota(twice.shape)
    selected = jnp.where((row == slot) | (row == slot + half), twice, 0.0).astype(BF16)
    outer = dot(drive[...], selected).reshape(heads, HP, NS)
    for h in range(heads):
        rate = decay[pl.ds(slot, 1), h : h + 1]
        result[h] = (rate * prior[h].astype(F32) + outer[h]).astype(BF16)


def output_kernel(gated, w_ssm, w_attn, partials, send, *, slots, col_count):
    share = w_attn.shape[0]
    part = min(share, HD)
    blocks = [partials[c * BLOCK : (c + 1) * BLOCK, :] for c in range(col_count)]
    pieces = []
    for j in range(share // part):
        peaks = [b[:, share + 2 * j : share + 2 * j + 1] for b in blocks]
        joint = functools.reduce(jnp.maximum, peaks)
        factors = [jnp.exp(p - joint) for p in peaks]
        total = sum(f * b[:, share + 2 * j + 1 : share + 2 * j + 2] for f, b in zip(factors, blocks))
        value = sum(f * b[:, j * part : (j + 1) * part] for f, b in zip(factors, blocks))
        pieces.append(value / total)
    joined = pieces[0] if len(pieces) == 1 else jnp.concatenate(pieces, axis=1)
    right = jnp.where(row_iota(joined.shape) < slots, joined, 0.0).astype(BF16)
    left = gated[...].astype(BF16)
    columns = w_ssm.shape[1] // col_count
    for c in range(col_count):
        span = slice(c * columns, (c + 1) * columns)
        terms = dot(left, w_ssm[:, span]) + dot(right, w_attn[:, span])
        send[c * BLOCK : (c + 1) * BLOCK, :] = terms.astype(BF16)


def total_kernel(
    plan, kv_new, driven, decay, b_twice, conv_x, conv_bc, terms, send, mixed, block, *, moves, col_count
):
    at = Plan(conv_x.shape[1], moves)
    total = sum(terms[c * BLOCK : (c + 1) * BLOCK, :].astype(F32) for c in range(col_count))
    mixed[...] = total
    send[pl.ds(pl.multiple_of(plan[at.me] * BLOCK, BLOCK), BLOCK), : total.shape[1]] = total.astype(BF16)

    block[...] = jnp.zeros_like(block)
    for m in range(moves):
        row = pl.ds(plan[at.slot + m], 1)

        def put(index, value, start=0):
            block[index : index + 1, start : start + value.shape[1]] = value

        put(Note.mixed, mixed[row, :])
        put(Note.key_value, kv_new[row, :])
        for index, value, start, low_index, low_start in (
            (Note.drive, driven[row, :], 0, Note.drive_low, 0),
            (Note.mixing, decay[row, :], Note.decay, Note.mixing, Note.decay_low),
        ):
            high = value.astype(BF16).astype(F32)
            put(index, high, start)
            put(low_index, value - high, low_start)
        put(Note.mixing, b_twice[row, :])
        for k in range(KW - 1):
            put(Note.conv_x + k, conv_x[k, row, :])
            put(Note.conv_bc + k, conv_bc[k, row, :])
        start = pl.multiple_of(plan[at.target + m] * BLOCK, BLOCK)
        send[pl.ds(start, BLOCK), :] = block[...].astype(BF16)


def arrive_kernel(
    col_ref, plan, table, conv_x, conv_bc, state_in, pool_in, notes, *rest,
    moves, row_count, col_count,
):
    del state_in, pool_in
    parcels, rest = rest[: row_count - 1], rest[row_count - 1 :]
    pages_here, slots = table.shape
    inner = conv_x.shape[2]
    heads = inner // HP
    at = Plan(slots, moves)
    mixed, conv_x_next, conv_bc_next, state_next, pool_next = rest[:5]
    packed, made, drive, decay, b_twice, window_x, window_bc, window_mixed, in_sems, out_sems = rest[5:]
    col = col_ref[0]
    for m in range(moves):
        for d, parcel in enumerate(parcels, 1):

            @pl.when(plan[at.from_away + m] == d)
            def _(m=m, parcel=parcel):
                pltpu.make_async_copy(parcel, packed.at[m], in_sems.at[m]).start()


    for k in range(KW - 1):
        window_x[k] = conv_x[k]
        window_bc[k] = conv_bc[k]
    home = pl.multiple_of(plan[at.me] * BLOCK, BLOCK)
    window_mixed[...] = notes[pl.ds(home, BLOCK), : window_mixed.shape[1]].astype(F32)
    rows = []
    b_twice[...] = jnp.zeros_like(b_twice)
    half = b_twice.shape[0] // 2
    for m in range(moves):
        start = pl.multiple_of(plan[at.source + m] * BLOCK, BLOCK)
        note = notes[pl.ds(start, BLOCK), :].astype(F32)
        rows.append(note)
        row = pl.ds(plan[at.slot + m], 1)
        window_mixed[row, :] = note[Note.mixed : Note.mixed + 1, : window_mixed.shape[1]]
        for k in range(KW - 1):
            window_x[k, row, :] = note[Note.conv_x + k : Note.conv_x + k + 1, :inner]
            window_bc[k, row, :] = note[Note.conv_bc + k : Note.conv_bc + k + 1, : 2 * NS]
        mixing = note[Note.mixing : Note.mixing + 1, :]
        b_twice[m : m + 1, :] = mixing[:, :NS]
        b_twice[half + m : half + m + 1, :] = mixing[:, :NS]
        decay[m : m + 1, :] = (
            mixing[:, Note.decay : Note.decay + heads] + mixing[:, Note.decay_low : Note.decay_low + heads]
        )
    padding = [jnp.zeros((half - moves, inner), F32)]
    stacked = [note[Note.drive : Note.drive + 1, :inner] for note in rows] + padding
    stacked += [note[Note.drive_low : Note.drive_low + 1, :inner] for note in rows] + padding
    drive[...] = jnp.transpose(jnp.concatenate(stacked, axis=0)).astype(BF16)
    mixed[...] = window_mixed[0:slots, :].astype(BF16)
    for k in range(KW - 1):
        conv_x_next[k] = window_x[k].astype(BF16)
        conv_bc_next[k] = window_bc[k].astype(BF16)

    stores = []
    for m in range(moves):
        slot = plan[at.slot + m]
        pltpu.make_async_copy(parcels[0], packed.at[m], in_sems.at[m]).wait()
        owner, local_page, offset = place_of(plan[at.arrived_length + m], col_count)
        key_value = rows[m][Note.key_value : Note.key_value + 1, : 2 * KVH * HD]

        @pl.when(owner == col)
        def _(m=m, local_page=local_page, offset=offset, key_value=key_value):
            packed[m, local_page] = inserted(packed[m, local_page], key_value, offset)

        for page in range(pages_here):
            stores.append(
                pltpu.make_async_copy(
                    packed.at[m, page], pool_next.at[table[page, slot]], out_sems.at[m, page]
                )
            )
            stores[-1].start()
        prior = [
            jnp.concatenate([packed[m, pages_here + h, :, :NS], packed[m, pages_here + h, :, NS:]], axis=0)
            for h in range(heads)
        ]
        advance_state(m, prior, b_twice, drive, decay, made.at[m])
        stores.append(pltpu.make_async_copy(made.at[m], state_next.at[slot], out_sems.at[m, pages_here]))
        stores[-1].start()
    for store in stores:
        store.wait()


def shape(dims, dtype):
    return jax.ShapeDtypeStruct(tuple(dims), dtype)


def params(limit=VMEM_LIMIT):
    return pltpu.CompilerParams(vmem_limit_bytes=limit)


def exchange(value, axis):
    return lax.all_to_all(value, axis, split_axis=0, concat_axis=0, tiled=True)


def trade(block, axis, d):
    return lax.ppermute(block, axis, [(i, i ^ d) for i in range(lax.axis_size(axis))])


def ordered(value, first):
    return lax.optimization_barrier((value, first))[0]


def local(
    tokens, arrival, cache_lengths, move_slot, move_target, page_table, kv_pool, ssm_state,
    conv_x, conv_bc, norm_gain, weight_z, weight_x, weight_dt, weight_bc, weight_qkv,
    conv_weight_x, conv_weight_bc, dt_bias, a_log, d_skip, weight_ssm_out, weight_attn_out,
):
    row_count = lax.axis_size("rows")
    col_count = lax.axis_size("cols")
    row_index = lax.axis_index("rows").astype(I32).reshape(1)
    col_index = lax.axis_index("cols").astype(I32).reshape(1)
    slots, heads = ssm_state.shape[0], ssm_state.shape[1]
    total, depth = tokens.shape
    moves = move_slot.shape[1]
    pages_here, width = page_table.shape[3], kv_pool.shape[3]
    inner = heads * HP
    stays = slots - moves
    cols, at = Columns(inner), Plan(slots, moves)
    table = page_table[0, 0].T
    pool = kv_pool[:, 0]
    past_x, past_bc = conv_x.transpose(1, 0, 2), conv_bc.transpose(1, 0, 2)
    rows = row_count * BLOCK
    model = depth * row_count
    share = QH * HD // col_count
    parcel = (pages_here + heads, PAGE, width)
    parcels_here = pltpu.VMEM((moves,) + parcel, BF16)

    chip_count = row_count // 2
    plan, mine, theirs = pl.pallas_call(
        functools.partial(project_kernel, slots=slots),
        out_shape=[
            shape((at.size,), I32),
            shape((chip_count * BLOCK, cols.width), F32),
            shape((chip_count * BLOCK, cols.width), BF16),
        ],
        in_specs=[SMEM_SPEC] * 5 + [VMEM_SPEC] * 7,
        out_specs=[SMEM_SPEC] + [VMEM_SPEC] * 2,
        scratch_shapes=[
            pltpu.SMEM((total,), I32),
            pltpu.VMEM((total, depth), F32),
            pltpu.VMEM((rows, depth), F32),
            pltpu.VMEM((rows, LANES), F32),
        ],
        compiler_params=params(FIRST_LIMIT),
        cost_estimate=BRIEF,
        name="project",
    )(
        row_index, arrival, cache_lengths, move_slot.T, move_target.T,
        tokens, norm_gain, weight_z, weight_x, weight_dt.T, weight_bc, weight_qkv,
    )
    parcels = pl.pallas_call(
        functools.partial(pack_kernel, moves=moves, row_count=row_count),
        out_shape=[shape(parcel, BF16)] * (row_count - 1),
        in_specs=[SMEM_SPEC] * 2 + [ANY_SPEC] * 2,
        out_specs=[ANY_SPEC] * (row_count - 1),
        scratch_shapes=[
            parcels_here,
            pltpu.SemaphoreType.DMA((moves, pages_here + 2)),
            pltpu.SemaphoreType.DMA((moves,)),
        ],
        compiler_params=params(FIRST_LIMIT),
        cost_estimate=BRIEF,
        name="pack",
    )(plan, table, pool, ssm_state)

    sums = pl.pallas_call(
        pair_kernel,
        out_shape=[shape((BLOCK, cols.width), F32)] + [shape((BLOCK, cols.width), BF16)] * (chip_count - 1),
        in_specs=[VMEM_SPEC] * 2,
        out_specs=[VMEM_SPEC] * chip_count,
        compiler_params=params(FIRST_LIMIT),
        cost_estimate=BRIEF,
        name="pair",
    )(mine, trade(theirs, "rows", 1))
    received = [sums[0]] + [trade(block, "rows", 2 * j) for j, block in enumerate(sums[1:], 1)]

    moving = [None, *parcels]

    def migrate(parts, after):
        for d in parts:
            moving[d] = trade(ordered(moving[d], after), "rows", d)
        return [moving[d] for d in parts]

    evens, odds = list(range(2, row_count, 2)), list(range(3, row_count, 2))
    first = [evens[-1], odds[len(odds) // 2]]
    second = [odds[0], evens[len(evens) // 2]]
    last = [d for d in evens + odds if d not in first + second] + [1]
    first_moved = migrate(first, received)
    second_moved = migrate(second, received)

    pool_next, kv_new, partials = pl.pallas_call(
        functools.partial(
            attend_kernel, moves=moves, heads=heads, chip_count=chip_count, col_count=col_count, width=model
        ),
        out_shape=[
            shape(pool.shape, BF16),
            shape((BLOCK, 2 * KVH * HD), F32),
            shape((col_count * BLOCK, share + LANES), F32),
        ],
        in_specs=[SMEM_SPEC] * 3 + [ANY_SPEC] + [VMEM_SPEC] * chip_count,
        out_specs=[ANY_SPEC] + [VMEM_SPEC] * 2,
        scratch_shapes=[
            pltpu.VMEM(pool.shape, BF16),
            pltpu.VMEM((BLOCK * QH, HD), F32),
            pltpu.VMEM((BLOCK * QH, pages_here * PAGE), F32),
            pltpu.VMEM((BLOCK * QH, HD), F32),
            pltpu.VMEM((BLOCK * QH, HD), F32),
            pltpu.VMEM((BLOCK * QH, HD), F32),
            pltpu.SemaphoreType.DMA((2 if pool.shape[0] % 4 else 4,)),
            pltpu.SemaphoreType.DMA((2 if pool.shape[0] % 4 else 4,)),
        ],
        compiler_params=params(),
        cost_estimate=BRIEF,
        name="attend",
    )(col_index, plan, table, pool, *received)
    received = ordered(received, partials)
    partials = exchange(partials, "cols")

    next_x, next_bc, gated, driven, decay, drive, b_twice = pl.pallas_call(
        functools.partial(mix_kernel, chip_count=chip_count, width=model),
        out_shape=(
            shape(past_x.shape, F32),
            shape(past_bc.shape, F32),
            shape((BLOCK, inner), F32),
            shape((BLOCK, inner), F32),
            shape((BLOCK, heads), F32),
            shape((inner, 2 * BLOCK), BF16),
            shape((2 * BLOCK, NS), F32),
        ),
        in_specs=[VMEM_SPEC] * 7 + [ANY_SPEC] + [VMEM_SPEC] * chip_count,
        out_specs=(VMEM_SPEC,) * 7,
        scratch_shapes=[
            pltpu.VMEM((BLOCK, inner), F32),
            pltpu.VMEM((slots, heads, HP, NS), BF16),
            pltpu.SemaphoreType.DMA((slots,)),
        ],
        compiler_params=params(),
        cost_estimate=BRIEF,
        name="mix",
    )(past_x, past_bc, conv_weight_x, conv_weight_bc, dt_bias, a_log, d_skip, ssm_state, *received)

    columns = weight_ssm_out.shape[1] // col_count
    terms = pl.pallas_call(
        functools.partial(output_kernel, slots=slots, col_count=col_count),
        out_shape=shape((col_count * BLOCK, columns), BF16),
        in_specs=[VMEM_SPEC] * 4,
        out_specs=VMEM_SPEC,
        compiler_params=params(),
        cost_estimate=BRIEF,
        name="output",
    )(gated, weight_ssm_out, weight_attn_out, partials)
    migrate(last, (terms, first_moved))
    drive = ordered(drive, terms)
    terms = exchange(terms, "cols")
    state_next = pl.pallas_call(
        functools.partial(stay_kernel, moves=moves),
        out_shape=shape(ssm_state.shape, BF16),
        in_specs=[SMEM_SPEC] + [VMEM_SPEC] * 3 + [ANY_SPEC],
        out_specs=ANY_SPEC,
        scratch_shapes=[
            pltpu.VMEM((stays, heads, HP, NS), BF16),
            pltpu.VMEM((stays, heads, HP, NS), BF16),
            pltpu.SemaphoreType.DMA((stays,)),
            pltpu.SemaphoreType.DMA((stays,)),
        ],
        compiler_params=params(),
        cost_estimate=BRIEF,
        name="stay",
    )(plan, drive, decay, b_twice, ssm_state)

    terms = ordered(terms, second_moved)
    note = (BLOCK, max(inner, 2 * NS, 2 * KVH * HD, columns))
    notes = pl.pallas_call(
        functools.partial(total_kernel, moves=moves, col_count=col_count),
        out_shape=shape((rows, note[1]), BF16),
        in_specs=[SMEM_SPEC] + [VMEM_SPEC] * 7,
        out_specs=VMEM_SPEC,
        scratch_shapes=[pltpu.VMEM((BLOCK, columns), F32), pltpu.VMEM(note, F32)],
        compiler_params=params(),
        cost_estimate=BRIEF,
        name="total",
    )(plan, kv_new, driven, decay, b_twice, next_x, next_bc, terms)
    notes = exchange(notes, "rows")

    mixed, conv_x_next, conv_bc_next, state_next, pool_next = pl.pallas_call(
        functools.partial(arrive_kernel, moves=moves, row_count=row_count, col_count=col_count),
        out_shape=(
            shape((slots, columns), BF16),
            shape(past_x.shape, BF16),
            shape(past_bc.shape, BF16),
            shape(ssm_state.shape, BF16),
            shape(pool.shape, BF16),
        ),
        in_specs=[SMEM_SPEC] * 3 + [VMEM_SPEC] * 2 + [ANY_SPEC] * 2 + [VMEM_SPEC] + [ANY_SPEC] * (row_count - 1),
        out_specs=[VMEM_SPEC] * 3 + [ANY_SPEC] * 2,
        scratch_shapes=[
            parcels_here,
            pltpu.VMEM((moves, heads, HP, NS), BF16),
            pltpu.VMEM((inner, 2 * BLOCK), BF16),
            pltpu.VMEM((BLOCK, heads), F32),
            pltpu.VMEM((2 * BLOCK, NS), F32),
            pltpu.VMEM((KW - 1, slots, inner), F32),
            pltpu.VMEM((KW - 1, slots, 2 * NS), F32),
            pltpu.VMEM((BLOCK, columns), F32),
            pltpu.SemaphoreType.DMA((moves,)),
            pltpu.SemaphoreType.DMA((moves, pages_here + 1)),
        ],
        input_output_aliases={5: 3, 6: 4},
        compiler_params=params(LAST_LIMIT),
        cost_estimate=BRIEF,
        name="arrive",
    )(col_index, plan, table, next_x, next_bc, state_next, pool_next, notes, *moving[1:])
    return (
        mixed, state_next, conv_x_next.transpose(1, 0, 2), conv_bc_next.transpose(1, 0, 2), pool_next[:, None]
    )


def solution(mesh):
    in_specs = (
        P(None, "rows"),
        P(),
        P(),
        P(),
        P(),
        P("rows", "cols", None, None),
        P("rows", "cols", None, None),
        P("rows", "cols", None, None),
        P("rows", None, "cols"),
        P("rows", None, None),
        P("rows"),
        P("rows", "cols"),
        P("rows", "cols"),
        P("rows", "cols"),
        P("rows", None),
        P("rows", None),
        P(None, "cols"),
        P(),
        P("cols"),
        P("cols"),
        P("cols"),
        P("cols", None),
        P("cols", None),
    )
    out_specs = (
        P("rows", "cols"),
        P("rows", "cols", None, None),
        P("rows", None, "cols"),
        P("rows", None, None),
        P("rows", "cols", None, None),
    )
    return jax.shard_map(local, mesh=mesh, in_specs=in_specs, out_specs=out_specs, check_vma=False)
```

```python
import functools

import jax
import jax.numpy as jnp
from jax import lax
from jax.experimental import pallas as pl
from jax.experimental.pallas import tpu as pltpu
from jax.sharding import PartitionSpec as P

HP = 64
NS = 256
KW = 4
QH = 8
KVH = 2
HD = 128
PAGE = 32
LANES = 128
BLOCK = 16

EPSILON = 1e-05
FLOOR_SCORE = -1e30
FIRST_LIMIT = 60 * 1024 * 1024
VMEM_LIMIT = 55 * 1024 * 1024
LAST_LIMIT = 24 * 1024 * 1024

F32 = jnp.float32
BF16 = jnp.bfloat16
I32 = jnp.int32

SMEM_SPEC = pl.BlockSpec(memory_space=pltpu.SMEM)
BRIEF = pl.CostEstimate(flops=1, bytes_accessed=1, transcendentals=0)
VMEM_SPEC = pl.BlockSpec(memory_space=pltpu.VMEM)
ANY_SPEC = pl.BlockSpec(memory_space=pl.ANY)


def silu(v):
    return v / (1.0 + jnp.exp(-v))


def dot(a, b):
    return jnp.dot(a, b, preferred_element_type=F32)


def dot_t(a, b):
    return lax.dot_general(a, b, (((1,), (1,)), ((), ())), preferred_element_type=F32)


def row_iota(shape):
    return lax.broadcasted_iota(I32, shape, 0)


def lane_iota(shape):
    return lax.broadcasted_iota(I32, shape, 1)


class Columns:
    def __init__(self, inner):
        self.z = 0
        self.x = inner
        self.bc = 2 * inner
        self.q = self.bc + 2 * NS
        self.kv = self.q + QH * HD
        self.tail = self.kv + 2 * KVH * HD
        self.width = self.tail + 2 * LANES


class Plan:
    def __init__(self, slots, moves):
        self.length = 0
        self.slot = slots
        self.target = self.slot + moves
        self.away = self.target + moves
        self.source = self.away + moves
        self.from_away = self.source + moves
        self.arrived_length = self.from_away + moves
        self.stay = self.arrived_length + moves
        self.me = self.stay + slots - moves
        self.size = self.me + 1


def early_parts(row_count):
    return [d for d in (2, 4) if d < row_count]


def parcel_parts(refs, row_count, pages_here):
    refs, early = list(refs), early_parts(row_count)
    parts = []
    for d in range(1, row_count):
        if d in early:
            parts.append((refs.pop(0), refs.pop(0)))
        else:
            whole = refs.pop(0)
            parts.append((whole.at[:pages_here], whole.at[pages_here:]))
    return parts


class Note:
    mixed, key_value, drive, drive_low, mixing, conv_x, conv_bc = 0, 1, 2, 3, 4, 5, 8
    decay, decay_low = NS, NS + LANES


def project_kernel(
    row_ref, arrival, lengths, move_slot, move_target, table,
    tokens, gain, w_z, w_x, w_dt, w_bc, w_qkv, pool,
    plan, mine, theirs, *rest,
):
    ahead = rest[:-5]
    inverse, wide, picked, tail, sems = rest[-5:]
    moves, row_count = move_slot.shape
    pages_here, slots = table.shape
    heads, depth = w_dt.shape
    inner = heads * HP
    cols, at = Columns(inner), Plan(slots, moves)
    me, half = row_ref[0], row_count // 2

    def each_ahead(act):
        for m in range(moves):
            for d, pages in zip(early_parts(row_count), ahead):

                @pl.when(lax.bitwise_xor(move_target[m, me], me) == d)
                def _(m=m, pages=pages):
                    for page in range(pages_here):
                        source = pool.at[table[page, move_slot[m, me]]]
                        act(pltpu.make_async_copy(source, pages.at[page], sems.at[m, page]))

    each_ahead(lambda copy: copy.start())

    wide[...] = tokens[...].astype(F32)
    picked[...] = jnp.zeros_like(picked)

    def invert(t, carry):
        for s in range(slots):
            inverse[arrival[t * slots + s]] = t * slots + s
        return carry

    lax.fori_loop(0, row_count, invert, 0)

    def pick(b, carry):
        d = jnp.where(b < half, 2 * b, 2 * (b - half) + 1)
        first = lax.bitwise_xor(me, d) * slots
        for s in range(slots):
            picked[pl.ds(b * BLOCK + s, 1), :] = wide[pl.ds(inverse[first + s], 1), :]
        return carry

    lax.fori_loop(0, row_count, pick, 0)

    rows = picked[...]
    squares = jnp.sum(rows * rows, axis=1, keepdims=True)
    scaled = (rows * gain[...].astype(F32).reshape(1, depth)).astype(BF16)

    def put(start, value):
        span = slice(start, start + value.shape[1])
        mine[:, span] = value[: half * BLOCK].astype(F32)
        theirs[:, span] = value[half * BLOCK :].astype(BF16)

    put(cols.z, dot(scaled, w_z[...]))
    put(cols.x, dot(scaled, w_x[...]))
    put(cols.bc, dot(scaled, w_bc[...]))
    put(cols.q, dot(scaled, w_qkv[...]))
    tail[...] = jnp.zeros_like(tail)
    tail[:, :heads] = dot_t(scaled, w_dt[...])
    tail[:, heads : heads + 1] = squares
    high = tail[...].astype(BF16)
    put(cols.tail, high)
    put(cols.tail + LANES, tail[...] - high.astype(F32))

    stays = 0
    for s in range(slots):
        plan[at.length + s] = lengths[me * slots + s]
        leaves = move_slot[0, me] == s
        for m in range(1, moves):
            leaves = jnp.logical_or(leaves, move_slot[m, me] == s)

        @pl.when(jnp.logical_not(leaves))
        def _(s=s, stays=stays):
            plan[at.stay + stays] = s

        stays = stays + jnp.where(leaves, 0, 1)
    for m in range(moves):
        plan[at.slot + m] = move_slot[m, me]
        plan[at.target + m] = move_target[m, me]
        plan[at.away + m] = lax.bitwise_xor(move_target[m, me], me)

    def seek(i, turn):
        for m in range(moves):
            comes = move_target[m, i] == me

            @pl.when(comes)
            def _(m=m, turn=turn):
                plan[at.source + turn] = i
                plan[at.from_away + turn] = lax.bitwise_xor(i, me)
                plan[at.arrived_length + turn] = lengths[i * slots + move_slot[m, i]]

            turn = turn + jnp.where(comes, 1, 0)
        return turn

    lax.fori_loop(0, row_count, seek, I32(0))
    plan[at.me] = me
    each_ahead(lambda copy: copy.wait())


def pack_kernel(plan, table, pool, state, *rest, moves, row_count):
    pages_here, slots = table.shape
    at, early = Plan(slots, moves), early_parts(row_count)
    parcels = rest[: row_count - 1]
    packed, in_sems, out_sems = rest[row_count - 1 :]
    for m in range(moves):
        slot = plan[at.slot + m]
        for page in range(pages_here):
            pltpu.make_async_copy(pool.at[table[page, slot]], packed.at[m, page], in_sems.at[m]).start()
        for part in range(2):
            pltpu.make_async_copy(
                state.at[slot, :, part * PAGE : (part + 1) * PAGE, :],
                packed.at[m, pages_here:, :, part * NS : (part + 1) * NS],
                in_sems.at[m],
            ).start()

    def sent(m, d):
        source = packed.at[m, pages_here:] if d in early else packed.at[m]
        return pltpu.make_async_copy(source, parcels[d - 1], out_sems.at[m])

    def each(m, act):
        for d in range(1, row_count):

            @pl.when(plan[at.away + m] == d)
            def _(d=d):
                act(sent(m, d))

    for m in range(moves):
        pltpu.make_async_copy(pool.at[: packed.shape[1]], packed.at[m], in_sems.at[m]).wait()
        each(m, lambda copy: copy.start())
    for m in range(moves):
        each(m, lambda copy: copy.wait())


def pair_kernel(mine, theirs, own, *others):
    for j, out in enumerate((own,) + others):
        span = slice(j * BLOCK, (j + 1) * BLOCK)
        out[...] = (mine[span, :] + theirs[span, :].astype(F32)).astype(out.dtype)


def widen(per_head, inner):
    rows = per_head.shape[0]
    first = lane_iota((rows, 2 * HP)) < HP
    pieces = []
    for h in range(0, inner // HP, 2):
        pieces.append(jnp.where(first, per_head[:, h : h + 1], per_head[:, h + 1 : h + 2]))
    return pieces[0] if len(pieces) == 1 else jnp.concatenate(pieces, axis=1)


class Sums:
    def __init__(self, received, heads, width):
        self.received = received
        cols = Columns(heads * HP)
        tail = self.total(cols.tail, cols.tail + LANES) + self.total(cols.tail + LANES, cols.width)
        self.root = jnp.sqrt(tail[:, heads : heads + 1] / width + EPSILON)
        self.step_in = (tail[:, :heads] / self.root).astype(BF16).astype(F32)

    def total(self, start, stop):
        return sum(part[:, start:stop].astype(F32) for part in self.received)

    def projected(self, start, stop):
        return (self.total(start, stop) / self.root).astype(BF16).astype(F32)


def inserted(page, row, offset):
    return jnp.where(row_iota(page.shape) == offset, row, page.astype(F32)).astype(BF16)


def place_of(length, col_count):
    logical = lax.div(length, I32(PAGE))
    return lax.rem(logical, I32(col_count)), lax.div(logical, I32(col_count)), lax.rem(length, I32(PAGE))


def attend_kernel(
    col_ref, plan, table, pool, *rest, moves, heads, chip_count, col_count, width
):
    received, (pool_next, kv_new, send) = rest[:chip_count], rest[chip_count : chip_count + 3]
    pages, queries, scores, weighted, peaks, totals, in_sems, out_sems = rest[chip_count + 3 :]
    pages_here, slots = table.shape
    cols, at = Columns(heads * HP), Plan(slots, moves)
    col = col_ref[0]
    tokens_here = pages_here * PAGE
    kv_width = KVH * HD
    chunks = in_sems.shape[0]
    step = pool.shape[0] // chunks
    spans = [pl.ds(k * step, step) for k in range(chunks)]
    loads = [pltpu.make_async_copy(pool.at[span], pages.at[span], in_sems.at[k]) for k, span in enumerate(spans)]
    for load in loads:
        load.start()

    sums = Sums(received, heads, width)
    kv_new[...] = sums.projected(cols.kv, cols.tail)
    q_in = sums.projected(cols.q, cols.kv)
    for h in range(QH):
        queries[pl.ds(h, BLOCK, stride=QH), :] = q_in[:, h * HD : (h + 1) * HD]

    first_group = row_iota((QH, HD)) < QH // KVH
    lane = lane_iota((QH, tokens_here))
    position = (lax.shift_right_logical(lane, 5) * col_count + col) * PAGE + lax.bitwise_and(lane, PAGE - 1)
    for load in loads:
        load.wait()
    for s in range(slots):
        owner, local_page, offset = place_of(plan[at.length + s], col_count)
        page = table[local_page, s]
        pages[page] = inserted(pages[page], kv_new[s : s + 1, :], jnp.where(owner == col, offset, -1))
    stores = [
        pltpu.make_async_copy(pages.at[span], pool_next.at[span], out_sems.at[k]) for k, span in enumerate(spans)
    ]
    for store in stores:
        store.start()

    def cached(s, start):
        parts = [pages[table[page, s], :, start : start + kv_width] for page in range(pages_here)]
        return jnp.concatenate(parts, axis=0)

    for s in range(slots):
        query = queries[s * QH : (s + 1) * QH, :]
        query = jnp.concatenate(
            [jnp.where(first_group, query, 0.0), jnp.where(first_group, 0.0, query)], axis=1
        ).astype(BF16)
        score = dot_t(query, cached(s, 0)) * (HD ** -0.5)
        scores[s * QH : (s + 1) * QH, :] = jnp.where(position <= plan[at.length + s], score, FLOOR_SCORE)

    live_rows = slots * QH
    everything = scores[0:live_rows, :]
    peak = jnp.max(everything, axis=1, keepdims=True)
    weights = jnp.where(everything > 0.5 * FLOOR_SCORE, jnp.exp(everything - peak), 0.0)
    total = jnp.sum(weights, axis=1, keepdims=True)
    scores[0:live_rows, :] = weights
    for ref, value in ((weighted, None), (peaks, peak), (totals, total)):
        ref[live_rows:, :] = jnp.zeros((BLOCK * QH - live_rows, HD), F32)
        if value is not None:
            ref[0:live_rows, :] = jnp.broadcast_to(value, (live_rows, HD))
    for s in range(slots):
        weight = scores[s * QH : (s + 1) * QH, :]
        high = weight.astype(BF16).astype(F32)
        both = dot(jnp.concatenate([high, weight - high], axis=0).astype(BF16), cached(s, kv_width))
        joined = both[:QH] + both[QH:]
        weighted[s * QH : (s + 1) * QH, :] = jnp.where(first_group, joined[:, :HD], joined[:, HD:])

    share = QH * HD // col_count
    part = min(share, HD)
    lanes = lane_iota((BLOCK, LANES))
    for c in range(col_count):
        block = slice(c * BLOCK, (c + 1) * BLOCK)
        stats = jnp.zeros((BLOCK, LANES), F32)
        for j in range(share // part):
            head, begin = divmod(c * share + j * part, HD)
            rows = pl.ds(head, BLOCK, stride=QH)
            send[block, j * part : (j + 1) * part] = weighted[rows, :][:, begin : begin + part]
            stats = jnp.where(lanes == 2 * j, peaks[rows, :], stats)
            stats = jnp.where(lanes == 2 * j + 1, totals[rows, :], stats)
        send[block, share:] = stats
    for store in stores:
        store.wait()


def mix_kernel(
    conv_x, conv_bc, cw_x, cw_bc, dt_bias, a_log, d_skip, state, *rest, chip_count, width
):
    received = rest[:chip_count]
    conv_x_next, conv_bc_next, gated, driven_out, decay, drive, b_twice = rest[chip_count : chip_count + 7]
    readout, held, in_sems = rest[chip_count + 7 :]
    slots, inner = conv_x.shape[1], conv_x.shape[2]
    heads = dt_bias.shape[0]
    cols = Columns(inner)
    loads = []
    for s in range(slots):
        loads.append(pltpu.make_async_copy(state.at[s], held.at[s], in_sems.at[s]))
        loads[-1].start()

    sums = Sums(received, heads, width)

    def convolved(past, taps, fresh, following):
        past_rows = [past[k].astype(F32) for k in range(KW - 1)]
        total = fresh[:slots] * taps[KW - 1 : KW, :].astype(F32)
        for k in range(KW - 1):
            total = total + past_rows[k] * taps[k : k + 1, :].astype(F32)
            following[k] = past_rows[k + 1] if k < KW - 2 else fresh[:slots]
        return jnp.concatenate([silu(total), jnp.zeros((BLOCK - slots, total.shape[1]), F32)], axis=0)

    value_act = convolved(conv_x, cw_x, sums.projected(cols.x, cols.bc), conv_x_next)
    bc_act = convolved(conv_bc, cw_bc, sums.projected(cols.bc, cols.q), conv_bc_next)
    bc_act = bc_act.astype(BF16).astype(F32)
    b_in, c_val = bc_act[:, :NS], bc_act[:, NS:]
    b_twice[...] = jnp.concatenate([b_in, b_in], axis=0)
    c_out = c_val.astype(BF16)

    shifted = sums.step_in + dt_bias[...].reshape(1, heads)
    step_size = jnp.maximum(shifted, 0.0) + jnp.log(1.0 + jnp.exp(-jnp.abs(shifted)))
    rate = jnp.exp(-jnp.exp(a_log[...].reshape(1, heads)) * step_size)
    decay[...] = rate
    driven = widen(step_size, inner) * value_act
    driven_out[...] = driven
    high = driven.astype(BF16).astype(F32)
    drive[...] = jnp.transpose(jnp.concatenate([high, driven - high], axis=0)).astype(BF16)

    readout[...] = jnp.zeros_like(readout)

    for s in range(slots):
        loads[s].wait()
        value = dot_t(c_out, held[s].reshape(inner, NS))
        readout[s : s + 1, :] = value[s : s + 1]

    gate = silu(sums.projected(cols.z, cols.x))
    b_dot_c = jnp.sum(b_in * c_val, axis=1, keepdims=True)
    skip = widen(jnp.broadcast_to(d_skip[...].reshape(1, heads), (BLOCK, heads)), inner)
    total = widen(rate, inner) * readout[...] + driven * b_dot_c + skip * value_act
    gated[...] = (total * gate).astype(BF16).astype(F32)


def stay_kernel(plan, drive, decay, b_twice, state, state_next, held, made, in_sems, out_sems, *, moves):
    stays = held.shape[0]
    at = Plan(state.shape[0], moves)
    loads = []
    for j in range(stays):
        loads.append(pltpu.make_async_copy(state.at[plan[at.stay + j]], held.at[j], in_sems.at[j]))
        loads[-1].start()
    stores = []
    for j in range(stays):
        slot = plan[at.stay + j]
        loads[j].wait()
        advance_state(slot, held.at[j], b_twice, drive, decay, made.at[j])
        stores.append(pltpu.make_async_copy(made.at[j], state_next.at[slot], out_sems.at[j]))
        stores[-1].start()
    for store in stores:
        store.wait()


def advance_state(slot, prior, b_twice, drive, decay, result):
    heads = result.shape[0]
    twice = b_twice[...]
    half = twice.shape[0] // 2
    row = row_iota(twice.shape)
    selected = jnp.where((row == slot) | (row == slot + half), twice, 0.0).astype(BF16)
    outer = dot(drive[...], selected).reshape(heads, HP, NS)
    for h in range(heads):
        rate = decay[pl.ds(slot, 1), h : h + 1]
        result[h] = (rate * prior[h].astype(F32) + outer[h]).astype(BF16)


def output_kernel(gated, w_ssm, w_attn, partials, send, *, slots, col_count):
    share = w_attn.shape[0]
    part = min(share, HD)
    blocks = [partials[c * BLOCK : (c + 1) * BLOCK, :] for c in range(col_count)]
    pieces = []
    for j in range(share // part):
        peaks = [b[:, share + 2 * j : share + 2 * j + 1] for b in blocks]
        joint = functools.reduce(jnp.maximum, peaks)
        factors = [jnp.exp(p - joint) for p in peaks]
        total = sum(f * b[:, share + 2 * j + 1 : share + 2 * j + 2] for f, b in zip(factors, blocks))
        value = sum(f * b[:, j * part : (j + 1) * part] for f, b in zip(factors, blocks))
        pieces.append(value / total)
    joined = pieces[0] if len(pieces) == 1 else jnp.concatenate(pieces, axis=1)
    right = jnp.where(row_iota(joined.shape) < slots, joined, 0.0).astype(BF16)
    left = gated[...].astype(BF16)
    columns = w_ssm.shape[1] // col_count
    for c in range(col_count):
        span = slice(c * columns, (c + 1) * columns)
        terms = dot(left, w_ssm[:, span]) + dot(right, w_attn[:, span])
        send[c * BLOCK : (c + 1) * BLOCK, :] = terms.astype(BF16)


def total_kernel(
    plan, kv_new, driven, decay, b_twice, conv_x, conv_bc, terms, send, mixed, block, *, moves, col_count
):
    at = Plan(conv_x.shape[1], moves)
    total = sum(terms[c * BLOCK : (c + 1) * BLOCK, :].astype(F32) for c in range(col_count))
    mixed[...] = total
    send[pl.ds(pl.multiple_of(plan[at.me] * BLOCK, BLOCK), BLOCK), : total.shape[1]] = total.astype(BF16)

    block[...] = jnp.zeros_like(block)
    for m in range(moves):
        row = pl.ds(plan[at.slot + m], 1)

        def put(index, value, start=0):
            block[index : index + 1, start : start + value.shape[1]] = value

        put(Note.mixed, mixed[row, :])
        put(Note.key_value, kv_new[row, :])
        for index, value, start, low_index, low_start in (
            (Note.drive, driven[row, :], 0, Note.drive_low, 0),
            (Note.mixing, decay[row, :], Note.decay, Note.mixing, Note.decay_low),
        ):
            high = value.astype(BF16).astype(F32)
            put(index, high, start)
            put(low_index, value - high, low_start)
        put(Note.mixing, b_twice[row, :])
        for k in range(KW - 1):
            put(Note.conv_x + k, conv_x[k, row, :])
            put(Note.conv_bc + k, conv_bc[k, row, :])
        start = pl.multiple_of(plan[at.target + m] * BLOCK, BLOCK)
        send[pl.ds(start, BLOCK), :] = block[...].astype(BF16)


def arrive_kernel(
    col_ref, plan, table, conv_x, conv_bc, state_in, pool_in, notes, *rest,
    moves, row_count, col_count,
):
    del state_in, pool_in
    parcel_count = row_count - 1 + len(early_parts(row_count))
    parcels, rest = rest[:parcel_count], rest[parcel_count:]
    pages_here, slots = table.shape
    inner = conv_x.shape[2]
    heads = inner // HP
    at = Plan(slots, moves)
    mixed, conv_x_next, conv_bc_next, state_next, pool_next = rest[:5]
    packed, made, drive, decay, b_twice, window_x, window_bc, window_mixed, in_sems, out_sems = rest[5:]
    col = col_ref[0]
    parcels = parcel_parts(parcels, row_count, pages_here)

    def loaded(m, parcel):
        pages, states = parcel
        return (
            pltpu.make_async_copy(pages, packed.at[m, :pages_here], in_sems.at[m, 0]),
            pltpu.make_async_copy(states, packed.at[m, pages_here:], in_sems.at[m, 1]),
        )

    for m in range(moves):
        for d, parcel in enumerate(parcels, 1):

            @pl.when(plan[at.from_away + m] == d)
            def _(m=m, parcel=parcel):
                for copy in loaded(m, parcel):
                    copy.start()


    for k in range(KW - 1):
        window_x[k] = conv_x[k]
        window_bc[k] = conv_bc[k]
    home = pl.multiple_of(plan[at.me] * BLOCK, BLOCK)
    window_mixed[...] = notes[pl.ds(home, BLOCK), : window_mixed.shape[1]].astype(F32)
    rows = []
    b_twice[...] = jnp.zeros_like(b_twice)
    half = b_twice.shape[0] // 2
    for m in range(moves):
        start = pl.multiple_of(plan[at.source + m] * BLOCK, BLOCK)
        note = notes[pl.ds(start, BLOCK), :].astype(F32)
        rows.append(note)
        row = pl.ds(plan[at.slot + m], 1)
        window_mixed[row, :] = note[Note.mixed : Note.mixed + 1, : window_mixed.shape[1]]
        for k in range(KW - 1):
            window_x[k, row, :] = note[Note.conv_x + k : Note.conv_x + k + 1, :inner]
            window_bc[k, row, :] = note[Note.conv_bc + k : Note.conv_bc + k + 1, : 2 * NS]
        mixing = note[Note.mixing : Note.mixing + 1, :]
        b_twice[m : m + 1, :] = mixing[:, :NS]
        b_twice[half + m : half + m + 1, :] = mixing[:, :NS]
        decay[m : m + 1, :] = (
            mixing[:, Note.decay : Note.decay + heads] + mixing[:, Note.decay_low : Note.decay_low + heads]
        )
    padding = [jnp.zeros((half - moves, inner), F32)]
    stacked = [note[Note.drive : Note.drive + 1, :inner] for note in rows] + padding
    stacked += [note[Note.drive_low : Note.drive_low + 1, :inner] for note in rows] + padding
    drive[...] = jnp.transpose(jnp.concatenate(stacked, axis=0)).astype(BF16)
    mixed[...] = window_mixed[0:slots, :].astype(BF16)
    for k in range(KW - 1):
        conv_x_next[k] = window_x[k].astype(BF16)
        conv_bc_next[k] = window_bc[k].astype(BF16)

    stores = []
    for m in range(moves):
        slot = plan[at.slot + m]
        for copy in loaded(m, parcels[0]):
            copy.wait()
        owner, local_page, offset = place_of(plan[at.arrived_length + m], col_count)
        key_value = rows[m][Note.key_value : Note.key_value + 1, : 2 * KVH * HD]

        @pl.when(owner == col)
        def _(m=m, local_page=local_page, offset=offset, key_value=key_value):
            packed[m, local_page] = inserted(packed[m, local_page], key_value, offset)

        for page in range(pages_here):
            stores.append(
                pltpu.make_async_copy(
                    packed.at[m, page], pool_next.at[table[page, slot]], out_sems.at[m, page]
                )
            )
            stores[-1].start()
        prior = [
            jnp.concatenate([packed[m, pages_here + h, :, :NS], packed[m, pages_here + h, :, NS:]], axis=0)
            for h in range(heads)
        ]
        advance_state(m, prior, b_twice, drive, decay, made.at[m])
        stores.append(pltpu.make_async_copy(made.at[m], state_next.at[slot], out_sems.at[m, pages_here]))
        stores[-1].start()
    for store in stores:
        store.wait()


def shape(dims, dtype):
    return jax.ShapeDtypeStruct(tuple(dims), dtype)


def params(limit=VMEM_LIMIT):
    return pltpu.CompilerParams(vmem_limit_bytes=limit)


def exchange(value, axis):
    return lax.all_to_all(value, axis, split_axis=0, concat_axis=0, tiled=True)


def trade(block, axis, d):
    return lax.ppermute(block, axis, [(i, i ^ d) for i in range(lax.axis_size(axis))])


def ordered(value, first):
    return lax.optimization_barrier((value, first))[0]


def local(
    tokens, arrival, cache_lengths, move_slot, move_target, page_table, kv_pool, ssm_state,
    conv_x, conv_bc, norm_gain, weight_z, weight_x, weight_dt, weight_bc, weight_qkv,
    conv_weight_x, conv_weight_bc, dt_bias, a_log, d_skip, weight_ssm_out, weight_attn_out,
):
    row_count = lax.axis_size("rows")
    col_count = lax.axis_size("cols")
    row_index = lax.axis_index("rows").astype(I32).reshape(1)
    col_index = lax.axis_index("cols").astype(I32).reshape(1)
    slots, heads = ssm_state.shape[0], ssm_state.shape[1]
    total, depth = tokens.shape
    moves = move_slot.shape[1]
    pages_here, width = page_table.shape[3], kv_pool.shape[3]
    inner = heads * HP
    stays = slots - moves
    cols, at = Columns(inner), Plan(slots, moves)
    table = page_table[0, 0].T
    pool = kv_pool[:, 0]
    past_x, past_bc = conv_x.transpose(1, 0, 2), conv_bc.transpose(1, 0, 2)
    rows = row_count * BLOCK
    model = depth * row_count
    share = QH * HD // col_count
    parcel = (pages_here + heads, PAGE, width)
    parcels_here = pltpu.VMEM((moves,) + parcel, BF16)

    chip_count = row_count // 2
    early = early_parts(row_count)
    plan, mine, theirs, *ahead = pl.pallas_call(
        project_kernel,
        out_shape=[
            shape((at.size,), I32),
            shape((chip_count * BLOCK, cols.width), F32),
            shape((chip_count * BLOCK, cols.width), BF16),
        ]
        + [shape((pages_here,) + parcel[1:], BF16)] * len(early),
        in_specs=[SMEM_SPEC] * 6 + [VMEM_SPEC] * 7 + [ANY_SPEC],
        out_specs=[SMEM_SPEC] + [VMEM_SPEC] * 2 + [ANY_SPEC] * len(early),
        scratch_shapes=[
            pltpu.SMEM((total,), I32),
            pltpu.VMEM((total, depth), F32),
            pltpu.VMEM((rows, depth), F32),
            pltpu.VMEM((rows, LANES), F32),
            pltpu.SemaphoreType.DMA((moves, pages_here)),
        ],
        compiler_params=params(FIRST_LIMIT),
        cost_estimate=BRIEF,
        name="project",
    )(
        row_index, arrival, cache_lengths, move_slot.T, move_target.T, table,
        tokens, norm_gain, weight_z, weight_x, weight_dt.T, weight_bc, weight_qkv, pool,
    )
    ahead = [trade(pages, "rows", d) for d, pages in zip(early, ahead)]
    parcels = pl.pallas_call(
        functools.partial(pack_kernel, moves=moves, row_count=row_count),
        out_shape=[
            shape((heads,) + parcel[1:] if d in early else parcel, BF16) for d in range(1, row_count)
        ],
        in_specs=[SMEM_SPEC] * 2 + [ANY_SPEC] * 2,
        out_specs=[ANY_SPEC] * (row_count - 1),
        scratch_shapes=[
            parcels_here,
            pltpu.SemaphoreType.DMA((moves,)),
            pltpu.SemaphoreType.DMA((moves,)),
        ],
        compiler_params=params(FIRST_LIMIT),
        cost_estimate=BRIEF,
        name="pack",
    )(plan, table, pool, ssm_state)

    sums = pl.pallas_call(
        pair_kernel,
        out_shape=[shape((BLOCK, cols.width), F32)] + [shape((BLOCK, cols.width), BF16)] * (chip_count - 1),
        in_specs=[VMEM_SPEC] * 2,
        out_specs=[VMEM_SPEC] * chip_count,
        compiler_params=params(FIRST_LIMIT),
        cost_estimate=BRIEF,
        name="pair",
    )(mine, trade(theirs, "rows", 1))
    received = [sums[0]] + [trade(block, "rows", 2 * j) for j, block in enumerate(sums[1:], 1)]

    moving = [None, *parcels]

    def migrate(parts, after):
        for d in parts:
            moving[d] = trade(ordered(moving[d], after), "rows", d)
        return [moving[d] for d in parts]

    evens, odds = list(range(2, row_count, 2)), list(range(3, row_count, 2))
    first = [evens[-1], odds[len(odds) // 2]]
    second = [odds[0], 1]
    last = [d for d in odds + evens if d not in first + second]
    received = ordered(received, ahead)
    first_moved = migrate(first, received)
    second_moved = migrate(second, received)

    pool_next, kv_new, partials = pl.pallas_call(
        functools.partial(
            attend_kernel, moves=moves, heads=heads, chip_count=chip_count, col_count=col_count, width=model
        ),
        out_shape=[
            shape(pool.shape, BF16),
            shape((BLOCK, 2 * KVH * HD), F32),
            shape((col_count * BLOCK, share + LANES), F32),
        ],
        in_specs=[SMEM_SPEC] * 3 + [ANY_SPEC] + [VMEM_SPEC] * chip_count,
        out_specs=[ANY_SPEC] + [VMEM_SPEC] * 2,
        scratch_shapes=[
            pltpu.VMEM(pool.shape, BF16),
            pltpu.VMEM((BLOCK * QH, HD), F32),
            pltpu.VMEM((BLOCK * QH, pages_here * PAGE), F32),
            pltpu.VMEM((BLOCK * QH, HD), F32),
            pltpu.VMEM((BLOCK * QH, HD), F32),
            pltpu.VMEM((BLOCK * QH, HD), F32),
            pltpu.SemaphoreType.DMA((2 if pool.shape[0] % 4 else 4,)),
            pltpu.SemaphoreType.DMA((2 if pool.shape[0] % 4 else 4,)),
        ],
        compiler_params=params(),
        cost_estimate=BRIEF,
        name="attend",
    )(col_index, plan, table, pool, *received)
    received = ordered(received, partials)
    partials = exchange(partials, "cols")

    next_x, next_bc, gated, driven, decay, drive, b_twice = pl.pallas_call(
        functools.partial(mix_kernel, chip_count=chip_count, width=model),
        out_shape=(
            shape(past_x.shape, F32),
            shape(past_bc.shape, F32),
            shape((BLOCK, inner), F32),
            shape((BLOCK, inner), F32),
            shape((BLOCK, heads), F32),
            shape((inner, 2 * BLOCK), BF16),
            shape((2 * BLOCK, NS), F32),
        ),
        in_specs=[VMEM_SPEC] * 7 + [ANY_SPEC] + [VMEM_SPEC] * chip_count,
        out_specs=(VMEM_SPEC,) * 7,
        scratch_shapes=[
            pltpu.VMEM((BLOCK, inner), F32),
            pltpu.VMEM((slots, heads, HP, NS), BF16),
            pltpu.SemaphoreType.DMA((slots,)),
        ],
        compiler_params=params(),
        cost_estimate=BRIEF,
        name="mix",
    )(past_x, past_bc, conv_weight_x, conv_weight_bc, dt_bias, a_log, d_skip, ssm_state, *received)

    columns = weight_ssm_out.shape[1] // col_count
    terms = pl.pallas_call(
        functools.partial(output_kernel, slots=slots, col_count=col_count),
        out_shape=shape((col_count * BLOCK, columns), BF16),
        in_specs=[VMEM_SPEC] * 4,
        out_specs=VMEM_SPEC,
        compiler_params=params(),
        cost_estimate=BRIEF,
        name="output",
    )(gated, weight_ssm_out, weight_attn_out, partials)
    migrate(last, (terms, first_moved))
    drive = ordered(drive, terms)
    terms = exchange(terms, "cols")
    state_next = pl.pallas_call(
        functools.partial(stay_kernel, moves=moves),
        out_shape=shape(ssm_state.shape, BF16),
        in_specs=[SMEM_SPEC] + [VMEM_SPEC] * 3 + [ANY_SPEC],
        out_specs=ANY_SPEC,
        scratch_shapes=[
            pltpu.VMEM((stays, heads, HP, NS), BF16),
            pltpu.VMEM((stays, heads, HP, NS), BF16),
            pltpu.SemaphoreType.DMA((stays,)),
            pltpu.SemaphoreType.DMA((stays,)),
        ],
        compiler_params=params(),
        cost_estimate=BRIEF,
        name="stay",
    )(plan, drive, decay, b_twice, ssm_state)

    terms = ordered(terms, second_moved)
    note = (BLOCK, max(inner, 2 * NS, 2 * KVH * HD, columns))
    notes = pl.pallas_call(
        functools.partial(total_kernel, moves=moves, col_count=col_count),
        out_shape=shape((rows, note[1]), BF16),
        in_specs=[SMEM_SPEC] + [VMEM_SPEC] * 7,
        out_specs=VMEM_SPEC,
        scratch_shapes=[pltpu.VMEM((BLOCK, columns), F32), pltpu.VMEM(note, F32)],
        compiler_params=params(),
        cost_estimate=BRIEF,
        name="total",
    )(plan, kv_new, driven, decay, b_twice, next_x, next_bc, terms)
    notes = exchange(notes, "rows")

    parts = []
    for d in range(1, row_count):
        parts += [ahead[early.index(d)], moving[d]] if d in early else [moving[d]]
    mixed, conv_x_next, conv_bc_next, state_next, pool_next = pl.pallas_call(
        functools.partial(arrive_kernel, moves=moves, row_count=row_count, col_count=col_count),
        out_shape=(
            shape((slots, columns), BF16),
            shape(past_x.shape, BF16),
            shape(past_bc.shape, BF16),
            shape(ssm_state.shape, BF16),
            shape(pool.shape, BF16),
        ),
        in_specs=[SMEM_SPEC] * 3 + [VMEM_SPEC] * 2 + [ANY_SPEC] * 2 + [VMEM_SPEC] + [ANY_SPEC] * (row_count - 1 + len(early)),
        out_specs=[VMEM_SPEC] * 3 + [ANY_SPEC] * 2,
        scratch_shapes=[
            parcels_here,
            pltpu.VMEM((moves, heads, HP, NS), BF16),
            pltpu.VMEM((inner, 2 * BLOCK), BF16),
            pltpu.VMEM((BLOCK, heads), F32),
            pltpu.VMEM((2 * BLOCK, NS), F32),
            pltpu.VMEM((KW - 1, slots, inner), F32),
            pltpu.VMEM((KW - 1, slots, 2 * NS), F32),
            pltpu.VMEM((BLOCK, columns), F32),
            pltpu.SemaphoreType.DMA((moves, 2)),
            pltpu.SemaphoreType.DMA((moves, pages_here + 1)),
        ],
        input_output_aliases={5: 3, 6: 4},
        compiler_params=params(LAST_LIMIT),
        cost_estimate=BRIEF,
        name="arrive",
    )(col_index, plan, table, next_x, next_bc, state_next, pool_next, notes, *parts)
    return (
        mixed, state_next, conv_x_next.transpose(1, 0, 2), conv_bc_next.transpose(1, 0, 2), pool_next[:, None]
    )


def solution(mesh):
    in_specs = (
        P(None, "rows"),
        P(),
        P(),
        P(),
        P(),
        P("rows", "cols", None, None),
        P("rows", "cols", None, None),
        P("rows", "cols", None, None),
        P("rows", None, "cols"),
        P("rows", None, None),
        P("rows"),
        P("rows", "cols"),
        P("rows", "cols"),
        P("rows", "cols"),
        P("rows", None),
        P("rows", None),
        P(None, "cols"),
        P(),
        P("cols"),
        P("cols"),
        P("cols"),
        P("cols", None),
        P("cols", None),
    )
    out_specs = (
        P("rows", "cols"),
        P("rows", "cols", None, None),
        P("rows", None, "cols"),
        P("rows", None, None),
        P("rows", "cols", None, None),
    )
    return jax.shard_map(local, mesh=mesh, in_specs=in_specs, out_specs=out_specs, check_vma=False)
```

```python
import functools

import jax
import jax.numpy as jnp
from jax import lax
from jax.experimental import pallas as pl
from jax.experimental.pallas import tpu as pltpu
from jax.sharding import PartitionSpec as P

HP = 64
NS = 256
KW = 4
QH = 8
KVH = 2
HD = 128
PAGE = 32
LANES = 128
BLOCK = 16

EPSILON = 1e-05
FLOOR_SCORE = -1e30
FIRST_LIMIT = 60 * 1024 * 1024
VMEM_LIMIT = 55 * 1024 * 1024
LAST_LIMIT = 24 * 1024 * 1024

F32 = jnp.float32
BF16 = jnp.bfloat16
I32 = jnp.int32

SMEM_SPEC = pl.BlockSpec(memory_space=pltpu.SMEM)
BRIEF = pl.CostEstimate(flops=1, bytes_accessed=1, transcendentals=0)
VMEM_SPEC = pl.BlockSpec(memory_space=pltpu.VMEM)
ANY_SPEC = pl.BlockSpec(memory_space=pl.ANY)


def silu(v):
    return v / (1.0 + jnp.exp(-v))


def dot(a, b):
    return jnp.dot(a, b, preferred_element_type=F32)


def dot_t(a, b):
    return lax.dot_general(a, b, (((1,), (1,)), ((), ())), preferred_element_type=F32)


def row_iota(shape):
    return lax.broadcasted_iota(I32, shape, 0)


def lane_iota(shape):
    return lax.broadcasted_iota(I32, shape, 1)


class Columns:
    def __init__(self, inner):
        self.z = 0
        self.x = inner
        self.bc = 2 * inner
        self.q = self.bc + 2 * NS
        self.kv = self.q + QH * HD
        self.tail = self.kv + 2 * KVH * HD
        self.width = self.tail + 2 * LANES


class Plan:
    def __init__(self, slots, moves):
        self.length = 0
        self.slot = slots
        self.target = self.slot + moves
        self.away = self.target + moves
        self.source = self.away + moves
        self.from_away = self.source + moves
        self.arrived_length = self.from_away + moves
        self.stay = self.arrived_length + moves
        self.me = self.stay + slots - moves
        self.size = self.me + 1


def early_parts(row_count):
    return [d for d in (2, 4) if d < row_count]


def parcel_parts(refs, row_count, pages_here):
    refs, early = list(refs), early_parts(row_count)
    parts = []
    for d in range(1, row_count):
        if d in early:
            parts.append((refs.pop(0), refs.pop(0)))
        else:
            whole = refs.pop(0)
            parts.append((whole.at[:pages_here], whole.at[pages_here:]))
    return parts


class Note:
    mixed, key_value, drive, drive_low, mixing, conv_x, conv_bc = 0, 1, 2, 3, 4, 5, 8
    decay, decay_low = NS, NS + LANES


def project_kernel(
    row_ref, arrival, lengths, move_slot, move_target, table,
    tokens, gain, w_z, w_x, w_dt, w_bc, w_qkv, pool,
    plan, mine, theirs, *rest,
):
    ahead = rest[:-7]
    inverse, wide, picked, tail, staged, in_sems, out_sems = rest[-7:]
    moves, row_count = move_slot.shape
    pages_here, slots = table.shape
    heads, depth = w_dt.shape
    inner = heads * HP
    cols, at = Columns(inner), Plan(slots, moves)
    me, half = row_ref[0], row_count // 2

    loads, stores = [], []
    for e, (d, pages) in enumerate(zip(early_parts(row_count), ahead)):
        slot = move_slot[0, me]
        for m in range(1, moves):
            slot = jnp.where(lax.bitwise_xor(move_target[m, me], me) == d, move_slot[m, me], slot)
        for page in range(pages_here):
            pltpu.make_async_copy(pool.at[table[page, slot]], staged.at[e, page], in_sems.at[e]).start()
        loads.append(pltpu.make_async_copy(pool.at[:pages_here], staged.at[e], in_sems.at[e]))
        stores.append(pltpu.make_async_copy(staged.at[e], pages, out_sems.at[e]))

    wide[...] = tokens[...].astype(F32)
    picked[...] = jnp.zeros_like(picked)

    def invert(t, carry):
        for s in range(slots):
            inverse[arrival[t * slots + s]] = t * slots + s
        return carry

    lax.fori_loop(0, row_count, invert, 0)

    def pick(b, carry):
        d = jnp.where(b < half, 2 * b, 2 * (b - half) + 1)
        first = lax.bitwise_xor(me, d) * slots
        for s in range(slots):
            picked[pl.ds(b * BLOCK + s, 1), :] = wide[pl.ds(inverse[first + s], 1), :]
        return carry

    lax.fori_loop(0, row_count, pick, 0)

    for load, store in zip(loads, stores):
        load.wait()
        store.start()

    rows = picked[...]
    squares = jnp.sum(rows * rows, axis=1, keepdims=True)
    scaled = (rows * gain[...].astype(F32).reshape(1, depth)).astype(BF16)

    def put(start, value):
        span = slice(start, start + value.shape[1])
        mine[:, span] = value[: half * BLOCK].astype(F32)
        theirs[:, span] = value[half * BLOCK :].astype(BF16)

    put(cols.z, dot(scaled, w_z[...]))
    put(cols.x, dot(scaled, w_x[...]))
    put(cols.bc, dot(scaled, w_bc[...]))
    put(cols.q, dot(scaled, w_qkv[...]))
    tail[...] = jnp.zeros_like(tail)
    tail[:, :heads] = dot_t(scaled, w_dt[...])
    tail[:, heads : heads + 1] = squares
    high = tail[...].astype(BF16)
    put(cols.tail, high)
    put(cols.tail + LANES, tail[...] - high.astype(F32))

    stays = 0
    for s in range(slots):
        plan[at.length + s] = lengths[me * slots + s]
        leaves = move_slot[0, me] == s
        for m in range(1, moves):
            leaves = jnp.logical_or(leaves, move_slot[m, me] == s)

        @pl.when(jnp.logical_not(leaves))
        def _(s=s, stays=stays):
            plan[at.stay + stays] = s

        stays = stays + jnp.where(leaves, 0, 1)
    for m in range(moves):
        plan[at.slot + m] = move_slot[m, me]
        plan[at.target + m] = move_target[m, me]
        plan[at.away + m] = lax.bitwise_xor(move_target[m, me], me)

    def seek(i, turn):
        for m in range(moves):
            comes = move_target[m, i] == me

            @pl.when(comes)
            def _(m=m, turn=turn):
                plan[at.source + turn] = i
                plan[at.from_away + turn] = lax.bitwise_xor(i, me)
                plan[at.arrived_length + turn] = lengths[i * slots + move_slot[m, i]]

            turn = turn + jnp.where(comes, 1, 0)
        return turn

    lax.fori_loop(0, row_count, seek, I32(0))
    plan[at.me] = me
    for store in stores:
        store.wait()


def pack_kernel(plan, table, pool, state, *rest, moves, row_count):
    pages_here, slots = table.shape
    at, early = Plan(slots, moves), early_parts(row_count)
    parcels = rest[: row_count - 1]
    packed, in_sems, out_sems = rest[row_count - 1 :]
    for m in range(moves):
        slot = plan[at.slot + m]
        for page in range(pages_here):
            pltpu.make_async_copy(pool.at[table[page, slot]], packed.at[m, page], in_sems.at[m]).start()
        for part in range(2):
            pltpu.make_async_copy(
                state.at[slot, :, part * PAGE : (part + 1) * PAGE, :],
                packed.at[m, pages_here:, :, part * NS : (part + 1) * NS],
                in_sems.at[m],
            ).start()

    def sent(m, d):
        source = packed.at[m, pages_here:] if d in early else packed.at[m]
        return pltpu.make_async_copy(source, parcels[d - 1], out_sems.at[m])

    def each(m, act):
        for d in range(1, row_count):

            @pl.when(plan[at.away + m] == d)
            def _(d=d):
                act(sent(m, d))

    for m in range(moves):
        pltpu.make_async_copy(pool.at[: packed.shape[1]], packed.at[m], in_sems.at[m]).wait()
        each(m, lambda copy: copy.start())
    for m in range(moves):
        each(m, lambda copy: copy.wait())


def pair_kernel(mine, theirs, own, *others):
    for j, out in enumerate((own,) + others):
        span = slice(j * BLOCK, (j + 1) * BLOCK)
        out[...] = (mine[span, :] + theirs[span, :].astype(F32)).astype(out.dtype)


def widen(per_head, inner):
    rows = per_head.shape[0]
    first = lane_iota((rows, 2 * HP)) < HP
    pieces = []
    for h in range(0, inner // HP, 2):
        pieces.append(jnp.where(first, per_head[:, h : h + 1], per_head[:, h + 1 : h + 2]))
    return pieces[0] if len(pieces) == 1 else jnp.concatenate(pieces, axis=1)


class Sums:
    def __init__(self, received, heads, width):
        self.received = received
        cols = Columns(heads * HP)
        tail = self.total(cols.tail, cols.tail + LANES) + self.total(cols.tail + LANES, cols.width)
        self.root = jnp.sqrt(tail[:, heads : heads + 1] / width + EPSILON)
        self.step_in = (tail[:, :heads] / self.root).astype(BF16).astype(F32)

    def total(self, start, stop):
        return sum(part[:, start:stop].astype(F32) for part in self.received)

    def projected(self, start, stop):
        return (self.total(start, stop) / self.root).astype(BF16).astype(F32)


def inserted(page, row, offset):
    return jnp.where(row_iota(page.shape) == offset, row, page.astype(F32)).astype(BF16)


def place_of(length, col_count):
    logical = lax.div(length, I32(PAGE))
    return lax.rem(logical, I32(col_count)), lax.div(logical, I32(col_count)), lax.rem(length, I32(PAGE))


def attend_kernel(
    col_ref, plan, table, pool, *rest, moves, heads, chip_count, col_count, width
):
    received, (pool_next, kv_new, send) = rest[:chip_count], rest[chip_count : chip_count + 3]
    pages, queries, scores, weighted, peaks, totals, in_sems, out_sems = rest[chip_count + 3 :]
    pages_here, slots = table.shape
    cols, at = Columns(heads * HP), Plan(slots, moves)
    col = col_ref[0]
    tokens_here = pages_here * PAGE
    kv_width = KVH * HD
    chunks = in_sems.shape[0]
    step = pool.shape[0] // chunks
    spans = [pl.ds(k * step, step) for k in range(chunks)]
    loads = [pltpu.make_async_copy(pool.at[span], pages.at[span], in_sems.at[k]) for k, span in enumerate(spans)]
    for load in loads:
        load.start()

    sums = Sums(received, heads, width)
    kv_new[...] = sums.projected(cols.kv, cols.tail)
    q_in = sums.projected(cols.q, cols.kv)
    for h in range(QH):
        queries[pl.ds(h, BLOCK, stride=QH), :] = q_in[:, h * HD : (h + 1) * HD]

    first_group = row_iota((QH, HD)) < QH // KVH
    lane = lane_iota((QH, tokens_here))
    position = (lax.shift_right_logical(lane, 5) * col_count + col) * PAGE + lax.bitwise_and(lane, PAGE - 1)
    for load in loads:
        load.wait()
    for s in range(slots):
        owner, local_page, offset = place_of(plan[at.length + s], col_count)
        page = table[local_page, s]
        pages[page] = inserted(pages[page], kv_new[s : s + 1, :], jnp.where(owner == col, offset, -1))
    stores = [
        pltpu.make_async_copy(pages.at[span], pool_next.at[span], out_sems.at[k]) for k, span in enumerate(spans)
    ]
    for store in stores:
        store.start()

    def cached(s, start):
        parts = [pages[table[page, s], :, start : start + kv_width] for page in range(pages_here)]
        return jnp.concatenate(parts, axis=0)

    for s in range(slots):
        query = queries[s * QH : (s + 1) * QH, :]
        query = jnp.concatenate(
            [jnp.where(first_group, query, 0.0), jnp.where(first_group, 0.0, query)], axis=1
        ).astype(BF16)
        score = dot_t(query, cached(s, 0)) * (HD ** -0.5)
        scores[s * QH : (s + 1) * QH, :] = jnp.where(position <= plan[at.length + s], score, FLOOR_SCORE)

    live_rows = slots * QH
    everything = scores[0:live_rows, :]
    peak = jnp.max(everything, axis=1, keepdims=True)
    weights = jnp.where(everything > 0.5 * FLOOR_SCORE, jnp.exp(everything - peak), 0.0)
    total = jnp.sum(weights, axis=1, keepdims=True)
    scores[0:live_rows, :] = weights
    for ref, value in ((weighted, None), (peaks, peak), (totals, total)):
        ref[live_rows:, :] = jnp.zeros((BLOCK * QH - live_rows, HD), F32)
        if value is not None:
            ref[0:live_rows, :] = jnp.broadcast_to(value, (live_rows, HD))
    for s in range(slots):
        weight = scores[s * QH : (s + 1) * QH, :]
        high = weight.astype(BF16).astype(F32)
        both = dot(jnp.concatenate([high, weight - high], axis=0).astype(BF16), cached(s, kv_width))
        joined = both[:QH] + both[QH:]
        weighted[s * QH : (s + 1) * QH, :] = jnp.where(first_group, joined[:, :HD], joined[:, HD:])

    share = QH * HD // col_count
    part = min(share, HD)
    lanes = lane_iota((BLOCK, LANES))
    for c in range(col_count):
        block = slice(c * BLOCK, (c + 1) * BLOCK)
        stats = jnp.zeros((BLOCK, LANES), F32)
        for j in range(share // part):
            head, begin = divmod(c * share + j * part, HD)
            rows = pl.ds(head, BLOCK, stride=QH)
            send[block, j * part : (j + 1) * part] = weighted[rows, :][:, begin : begin + part]
            stats = jnp.where(lanes == 2 * j, peaks[rows, :], stats)
            stats = jnp.where(lanes == 2 * j + 1, totals[rows, :], stats)
        send[block, share:] = stats
    for store in stores:
        store.wait()


def mix_kernel(
    conv_x, conv_bc, cw_x, cw_bc, dt_bias, a_log, d_skip, state, *rest, chip_count, width
):
    received = rest[:chip_count]
    conv_x_next, conv_bc_next, gated, driven_out, decay, drive, b_twice = rest[chip_count : chip_count + 7]
    readout, held, in_sems = rest[chip_count + 7 :]
    slots, inner = conv_x.shape[1], conv_x.shape[2]
    heads = dt_bias.shape[0]
    cols = Columns(inner)
    loads = []
    for s in range(slots):
        loads.append(pltpu.make_async_copy(state.at[s], held.at[s], in_sems.at[s]))
        loads[-1].start()

    sums = Sums(received, heads, width)

    def convolved(past, taps, fresh, following):
        past_rows = [past[k].astype(F32) for k in range(KW - 1)]
        total = fresh[:slots] * taps[KW - 1 : KW, :].astype(F32)
        for k in range(KW - 1):
            total = total + past_rows[k] * taps[k : k + 1, :].astype(F32)
            following[k] = past_rows[k + 1] if k < KW - 2 else fresh[:slots]
        return jnp.concatenate([silu(total), jnp.zeros((BLOCK - slots, total.shape[1]), F32)], axis=0)

    value_act = convolved(conv_x, cw_x, sums.projected(cols.x, cols.bc), conv_x_next)
    bc_act = convolved(conv_bc, cw_bc, sums.projected(cols.bc, cols.q), conv_bc_next)
    bc_act = bc_act.astype(BF16).astype(F32)
    b_in, c_val = bc_act[:, :NS], bc_act[:, NS:]
    b_twice[...] = jnp.concatenate([b_in, b_in], axis=0)
    c_out = c_val.astype(BF16)

    shifted = sums.step_in + dt_bias[...].reshape(1, heads)
    step_size = jnp.maximum(shifted, 0.0) + jnp.log(1.0 + jnp.exp(-jnp.abs(shifted)))
    rate = jnp.exp(-jnp.exp(a_log[...].reshape(1, heads)) * step_size)
    decay[...] = rate
    driven = widen(step_size, inner) * value_act
    driven_out[...] = driven
    high = driven.astype(BF16).astype(F32)
    drive[...] = jnp.transpose(jnp.concatenate([high, driven - high], axis=0)).astype(BF16)

    readout[...] = jnp.zeros_like(readout)

    for s in range(slots):
        loads[s].wait()
        value = dot_t(c_out, held[s].reshape(inner, NS))
        readout[s : s + 1, :] = value[s : s + 1]

    gate = silu(sums.projected(cols.z, cols.x))
    b_dot_c = jnp.sum(b_in * c_val, axis=1, keepdims=True)
    skip = widen(jnp.broadcast_to(d_skip[...].reshape(1, heads), (BLOCK, heads)), inner)
    total = widen(rate, inner) * readout[...] + driven * b_dot_c + skip * value_act
    gated[...] = (total * gate).astype(BF16).astype(F32)


def stay_kernel(plan, drive, decay, b_twice, state, state_next, held, made, in_sems, out_sems, *, moves):
    stays = held.shape[0]
    at = Plan(state.shape[0], moves)
    loads = []
    for j in range(stays):
        loads.append(pltpu.make_async_copy(state.at[plan[at.stay + j]], held.at[j], in_sems.at[j]))
        loads[-1].start()
    stores = []
    for j in range(stays):
        slot = plan[at.stay + j]
        loads[j].wait()
        advance_state(slot, held.at[j], b_twice, drive, decay, made.at[j])
        stores.append(pltpu.make_async_copy(made.at[j], state_next.at[slot], out_sems.at[j]))
        stores[-1].start()
    for store in stores:
        store.wait()


def advance_state(slot, prior, b_twice, drive, decay, result):
    heads = result.shape[0]
    twice = b_twice[...]
    half = twice.shape[0] // 2
    row = row_iota(twice.shape)
    selected = jnp.where((row == slot) | (row == slot + half), twice, 0.0).astype(BF16)
    outer = dot(drive[...], selected).reshape(heads, HP, NS)
    for h in range(heads):
        rate = decay[pl.ds(slot, 1), h : h + 1]
        result[h] = (rate * prior[h].astype(F32) + outer[h]).astype(BF16)


def output_kernel(gated, w_ssm, w_attn, partials, send, *, slots, col_count):
    share = w_attn.shape[0]
    part = min(share, HD)
    blocks = [partials[c * BLOCK : (c + 1) * BLOCK, :] for c in range(col_count)]
    pieces = []
    for j in range(share // part):
        peaks = [b[:, share + 2 * j : share + 2 * j + 1] for b in blocks]
        joint = functools.reduce(jnp.maximum, peaks)
        factors = [jnp.exp(p - joint) for p in peaks]
        total = sum(f * b[:, share + 2 * j + 1 : share + 2 * j + 2] for f, b in zip(factors, blocks))
        value = sum(f * b[:, j * part : (j + 1) * part] for f, b in zip(factors, blocks))
        pieces.append(value / total)
    joined = pieces[0] if len(pieces) == 1 else jnp.concatenate(pieces, axis=1)
    right = jnp.where(row_iota(joined.shape) < slots, joined, 0.0).astype(BF16)
    left = gated[...].astype(BF16)
    columns = w_ssm.shape[1] // col_count
    for c in range(col_count):
        span = slice(c * columns, (c + 1) * columns)
        terms = dot(left, w_ssm[:, span]) + dot(right, w_attn[:, span])
        send[c * BLOCK : (c + 1) * BLOCK, :] = terms.astype(BF16)


def total_kernel(
    plan, kv_new, driven, decay, b_twice, conv_x, conv_bc, terms, send, mixed, block, *, moves, col_count
):
    at = Plan(conv_x.shape[1], moves)
    total = sum(terms[c * BLOCK : (c + 1) * BLOCK, :].astype(F32) for c in range(col_count))
    mixed[...] = total
    send[pl.ds(pl.multiple_of(plan[at.me] * BLOCK, BLOCK), BLOCK), : total.shape[1]] = total.astype(BF16)

    block[...] = jnp.zeros_like(block)
    for m in range(moves):
        row = pl.ds(plan[at.slot + m], 1)

        def put(index, value, start=0):
            block[index : index + 1, start : start + value.shape[1]] = value

        put(Note.mixed, mixed[row, :])
        put(Note.key_value, kv_new[row, :])
        for index, value, start, low_index, low_start in (
            (Note.drive, driven[row, :], 0, Note.drive_low, 0),
            (Note.mixing, decay[row, :], Note.decay, Note.mixing, Note.decay_low),
        ):
            high = value.astype(BF16).astype(F32)
            put(index, high, start)
            put(low_index, value - high, low_start)
        put(Note.mixing, b_twice[row, :])
        for k in range(KW - 1):
            put(Note.conv_x + k, conv_x[k, row, :])
            put(Note.conv_bc + k, conv_bc[k, row, :])
        start = pl.multiple_of(plan[at.target + m] * BLOCK, BLOCK)
        send[pl.ds(start, BLOCK), :] = block[...].astype(BF16)


def arrive_kernel(
    col_ref, plan, table, conv_x, conv_bc, state_in, pool_in, notes, *rest,
    moves, row_count, col_count,
):
    del state_in, pool_in
    parcel_count = row_count - 1 + len(early_parts(row_count))
    parcels, rest = rest[:parcel_count], rest[parcel_count:]
    pages_here, slots = table.shape
    inner = conv_x.shape[2]
    heads = inner // HP
    at = Plan(slots, moves)
    mixed, conv_x_next, conv_bc_next, state_next, pool_next = rest[:5]
    packed, made, drive, decay, b_twice, window_x, window_bc, window_mixed, in_sems, out_sems = rest[5:]
    col = col_ref[0]
    parcels = parcel_parts(parcels, row_count, pages_here)

    def loaded(m, parcel):
        pages, states = parcel
        return (
            pltpu.make_async_copy(pages, packed.at[m, :pages_here], in_sems.at[m, 0]),
            pltpu.make_async_copy(states, packed.at[m, pages_here:], in_sems.at[m, 1]),
        )

    for m in range(moves):
        for d, parcel in enumerate(parcels, 1):

            @pl.when(plan[at.from_away + m] == d)
            def _(m=m, parcel=parcel):
                for copy in loaded(m, parcel):
                    copy.start()


    for k in range(KW - 1):
        window_x[k] = conv_x[k]
        window_bc[k] = conv_bc[k]
    home = pl.multiple_of(plan[at.me] * BLOCK, BLOCK)
    window_mixed[...] = notes[pl.ds(home, BLOCK), : window_mixed.shape[1]].astype(F32)
    rows = []
    b_twice[...] = jnp.zeros_like(b_twice)
    half = b_twice.shape[0] // 2
    for m in range(moves):
        start = pl.multiple_of(plan[at.source + m] * BLOCK, BLOCK)
        note = notes[pl.ds(start, BLOCK), :].astype(F32)
        rows.append(note)
        row = pl.ds(plan[at.slot + m], 1)
        window_mixed[row, :] = note[Note.mixed : Note.mixed + 1, : window_mixed.shape[1]]
        for k in range(KW - 1):
            window_x[k, row, :] = note[Note.conv_x + k : Note.conv_x + k + 1, :inner]
            window_bc[k, row, :] = note[Note.conv_bc + k : Note.conv_bc + k + 1, : 2 * NS]
        mixing = note[Note.mixing : Note.mixing + 1, :]
        b_twice[m : m + 1, :] = mixing[:, :NS]
        b_twice[half + m : half + m + 1, :] = mixing[:, :NS]
        decay[m : m + 1, :] = (
            mixing[:, Note.decay : Note.decay + heads] + mixing[:, Note.decay_low : Note.decay_low + heads]
        )
    padding = [jnp.zeros((half - moves, inner), F32)]
    stacked = [note[Note.drive : Note.drive + 1, :inner] for note in rows] + padding
    stacked += [note[Note.drive_low : Note.drive_low + 1, :inner] for note in rows] + padding
    drive[...] = jnp.transpose(jnp.concatenate(stacked, axis=0)).astype(BF16)
    mixed[...] = window_mixed[0:slots, :].astype(BF16)
    for k in range(KW - 1):
        conv_x_next[k] = window_x[k].astype(BF16)
        conv_bc_next[k] = window_bc[k].astype(BF16)

    stores = []
    for m in range(moves):
        slot = plan[at.slot + m]
        for copy in loaded(m, parcels[0]):
            copy.wait()
        owner, local_page, offset = place_of(plan[at.arrived_length + m], col_count)
        key_value = rows[m][Note.key_value : Note.key_value + 1, : 2 * KVH * HD]

        @pl.when(owner == col)
        def _(m=m, local_page=local_page, offset=offset, key_value=key_value):
            packed[m, local_page] = inserted(packed[m, local_page], key_value, offset)

        for page in range(pages_here):
            stores.append(
                pltpu.make_async_copy(
                    packed.at[m, page], pool_next.at[table[page, slot]], out_sems.at[m, page]
                )
            )
            stores[-1].start()
        prior = [
            jnp.concatenate([packed[m, pages_here + h, :, :NS], packed[m, pages_here + h, :, NS:]], axis=0)
            for h in range(heads)
        ]
        advance_state(m, prior, b_twice, drive, decay, made.at[m])
        stores.append(pltpu.make_async_copy(made.at[m], state_next.at[slot], out_sems.at[m, pages_here]))
        stores[-1].start()
    for store in stores:
        store.wait()


def shape(dims, dtype):
    return jax.ShapeDtypeStruct(tuple(dims), dtype)


def params(limit=VMEM_LIMIT):
    return pltpu.CompilerParams(vmem_limit_bytes=limit)


def exchange(value, axis):
    return lax.all_to_all(value, axis, split_axis=0, concat_axis=0, tiled=True)


def trade(block, axis, d):
    return lax.ppermute(block, axis, [(i, i ^ d) for i in range(lax.axis_size(axis))])


def ordered(value, first):
    return lax.optimization_barrier((value, first))[0]


def local(
    tokens, arrival, cache_lengths, move_slot, move_target, page_table, kv_pool, ssm_state,
    conv_x, conv_bc, norm_gain, weight_z, weight_x, weight_dt, weight_bc, weight_qkv,
    conv_weight_x, conv_weight_bc, dt_bias, a_log, d_skip, weight_ssm_out, weight_attn_out,
):
    row_count = lax.axis_size("rows")
    col_count = lax.axis_size("cols")
    row_index = lax.axis_index("rows").astype(I32).reshape(1)
    col_index = lax.axis_index("cols").astype(I32).reshape(1)
    slots, heads = ssm_state.shape[0], ssm_state.shape[1]
    total, depth = tokens.shape
    moves = move_slot.shape[1]
    pages_here, width = page_table.shape[3], kv_pool.shape[3]
    inner = heads * HP
    stays = slots - moves
    cols, at = Columns(inner), Plan(slots, moves)
    table = page_table[0, 0].T
    pool = kv_pool[:, 0]
    past_x, past_bc = conv_x.transpose(1, 0, 2), conv_bc.transpose(1, 0, 2)
    rows = row_count * BLOCK
    model = depth * row_count
    share = QH * HD // col_count
    parcel = (pages_here + heads, PAGE, width)
    parcels_here = pltpu.VMEM((moves,) + parcel, BF16)

    chip_count = row_count // 2
    early = early_parts(row_count)
    plan, mine, theirs, *ahead = pl.pallas_call(
        project_kernel,
        out_shape=[
            shape((at.size,), I32),
            shape((chip_count * BLOCK, cols.width), F32),
            shape((chip_count * BLOCK, cols.width), BF16),
        ]
        + [shape((pages_here,) + parcel[1:], BF16)] * len(early),
        in_specs=[SMEM_SPEC] * 6 + [VMEM_SPEC] * 7 + [ANY_SPEC],
        out_specs=[SMEM_SPEC] + [VMEM_SPEC] * 2 + [ANY_SPEC] * len(early),
        scratch_shapes=[
            pltpu.SMEM((total,), I32),
            pltpu.VMEM((total, depth), F32),
            pltpu.VMEM((rows, depth), F32),
            pltpu.VMEM((rows, LANES), F32),
            pltpu.VMEM((len(early), pages_here, PAGE, width), BF16),
            pltpu.SemaphoreType.DMA((len(early),)),
            pltpu.SemaphoreType.DMA((len(early),)),
        ],
        compiler_params=params(FIRST_LIMIT),
        cost_estimate=BRIEF,
        name="project",
    )(
        row_index, arrival, cache_lengths, move_slot.T, move_target.T, table,
        tokens, norm_gain, weight_z, weight_x, weight_dt.T, weight_bc, weight_qkv, pool,
    )
    ahead = [trade(pages, "rows", d) for d, pages in zip(early, ahead)]
    parcels = pl.pallas_call(
        functools.partial(pack_kernel, moves=moves, row_count=row_count),
        out_shape=[
            shape((heads,) + parcel[1:] if d in early else parcel, BF16) for d in range(1, row_count)
        ],
        in_specs=[SMEM_SPEC] * 2 + [ANY_SPEC] * 2,
        out_specs=[ANY_SPEC] * (row_count - 1),
        scratch_shapes=[
            parcels_here,
            pltpu.SemaphoreType.DMA((moves,)),
            pltpu.SemaphoreType.DMA((moves,)),
        ],
        compiler_params=params(FIRST_LIMIT),
        cost_estimate=BRIEF,
        name="pack",
    )(plan, table, pool, ssm_state)

    sums = pl.pallas_call(
        pair_kernel,
        out_shape=[shape((BLOCK, cols.width), F32)] + [shape((BLOCK, cols.width), BF16)] * (chip_count - 1),
        in_specs=[VMEM_SPEC] * 2,
        out_specs=[VMEM_SPEC] * chip_count,
        compiler_params=params(FIRST_LIMIT),
        cost_estimate=BRIEF,
        name="pair",
    )(mine, trade(theirs, "rows", 1))
    received = [sums[0]] + [trade(block, "rows", 2 * j) for j, block in enumerate(sums[1:], 1)]

    moving = [None, *parcels]

    def migrate(parts, after):
        for d in parts:
            moving[d] = trade(ordered(moving[d], after), "rows", d)
        return [moving[d] for d in parts]

    evens, odds = list(range(2, row_count, 2)), list(range(3, row_count, 2))
    first = [odds[0], odds[len(odds) // 2]]
    second = [evens[-1], 1]
    last = [d for d in odds + evens if d not in first + second]
    received = ordered(received, ahead)
    first_moved = migrate(first, received)
    second_moved = migrate(second, received)

    pool_next, kv_new, partials = pl.pallas_call(
        functools.partial(
            attend_kernel, moves=moves, heads=heads, chip_count=chip_count, col_count=col_count, width=model
        ),
        out_shape=[
            shape(pool.shape, BF16),
            shape((BLOCK, 2 * KVH * HD), F32),
            shape((col_count * BLOCK, share + LANES), F32),
        ],
        in_specs=[SMEM_SPEC] * 3 + [ANY_SPEC] + [VMEM_SPEC] * chip_count,
        out_specs=[ANY_SPEC] + [VMEM_SPEC] * 2,
        scratch_shapes=[
            pltpu.VMEM(pool.shape, BF16),
            pltpu.VMEM((BLOCK * QH, HD), F32),
            pltpu.VMEM((BLOCK * QH, pages_here * PAGE), F32),
            pltpu.VMEM((BLOCK * QH, HD), F32),
            pltpu.VMEM((BLOCK * QH, HD), F32),
            pltpu.VMEM((BLOCK * QH, HD), F32),
            pltpu.SemaphoreType.DMA((2 if pool.shape[0] % 4 else 4,)),
            pltpu.SemaphoreType.DMA((2 if pool.shape[0] % 4 else 4,)),
        ],
        compiler_params=params(),
        cost_estimate=BRIEF,
        name="attend",
    )(col_index, plan, table, pool, *received)
    received = ordered(received, partials)
    partials = exchange(partials, "cols")

    next_x, next_bc, gated, driven, decay, drive, b_twice = pl.pallas_call(
        functools.partial(mix_kernel, chip_count=chip_count, width=model),
        out_shape=(
            shape(past_x.shape, F32),
            shape(past_bc.shape, F32),
            shape((BLOCK, inner), F32),
            shape((BLOCK, inner), F32),
            shape((BLOCK, heads), F32),
            shape((inner, 2 * BLOCK), BF16),
            shape((2 * BLOCK, NS), F32),
        ),
        in_specs=[VMEM_SPEC] * 7 + [ANY_SPEC] + [VMEM_SPEC] * chip_count,
        out_specs=(VMEM_SPEC,) * 7,
        scratch_shapes=[
            pltpu.VMEM((BLOCK, inner), F32),
            pltpu.VMEM((slots, heads, HP, NS), BF16),
            pltpu.SemaphoreType.DMA((slots,)),
        ],
        compiler_params=params(),
        cost_estimate=BRIEF,
        name="mix",
    )(past_x, past_bc, conv_weight_x, conv_weight_bc, dt_bias, a_log, d_skip, ssm_state, *received)

    columns = weight_ssm_out.shape[1] // col_count
    terms = pl.pallas_call(
        functools.partial(output_kernel, slots=slots, col_count=col_count),
        out_shape=shape((col_count * BLOCK, columns), BF16),
        in_specs=[VMEM_SPEC] * 4,
        out_specs=VMEM_SPEC,
        compiler_params=params(),
        cost_estimate=BRIEF,
        name="output",
    )(gated, weight_ssm_out, weight_attn_out, partials)
    migrate(last, (terms, first_moved))
    drive = ordered(drive, terms)
    terms = exchange(terms, "cols")
    state_next = pl.pallas_call(
        functools.partial(stay_kernel, moves=moves),
        out_shape=shape(ssm_state.shape, BF16),
        in_specs=[SMEM_SPEC] + [VMEM_SPEC] * 3 + [ANY_SPEC],
        out_specs=ANY_SPEC,
        scratch_shapes=[
            pltpu.VMEM((stays, heads, HP, NS), BF16),
            pltpu.VMEM((stays, heads, HP, NS), BF16),
            pltpu.SemaphoreType.DMA((stays,)),
            pltpu.SemaphoreType.DMA((stays,)),
        ],
        compiler_params=params(),
        cost_estimate=BRIEF,
        name="stay",
    )(plan, drive, decay, b_twice, ssm_state)

    terms = ordered(terms, second_moved)
    note = (BLOCK, max(inner, 2 * NS, 2 * KVH * HD, columns))
    notes = pl.pallas_call(
        functools.partial(total_kernel, moves=moves, col_count=col_count),
        out_shape=shape((rows, note[1]), BF16),
        in_specs=[SMEM_SPEC] + [VMEM_SPEC] * 7,
        out_specs=VMEM_SPEC,
        scratch_shapes=[pltpu.VMEM((BLOCK, columns), F32), pltpu.VMEM(note, F32)],
        compiler_params=params(),
        cost_estimate=BRIEF,
        name="total",
    )(plan, kv_new, driven, decay, b_twice, next_x, next_bc, terms)
    notes = exchange(notes, "rows")

    parts = []
    for d in range(1, row_count):
        parts += [ahead[early.index(d)], moving[d]] if d in early else [moving[d]]
    mixed, conv_x_next, conv_bc_next, state_next, pool_next = pl.pallas_call(
        functools.partial(arrive_kernel, moves=moves, row_count=row_count, col_count=col_count),
        out_shape=(
            shape((slots, columns), BF16),
            shape(past_x.shape, BF16),
            shape(past_bc.shape, BF16),
            shape(ssm_state.shape, BF16),
            shape(pool.shape, BF16),
        ),
        in_specs=[SMEM_SPEC] * 3 + [VMEM_SPEC] * 2 + [ANY_SPEC] * 2 + [VMEM_SPEC] + [ANY_SPEC] * (row_count - 1 + len(early)),
        out_specs=[VMEM_SPEC] * 3 + [ANY_SPEC] * 2,
        scratch_shapes=[
            parcels_here,
            pltpu.VMEM((moves, heads, HP, NS), BF16),
            pltpu.VMEM((inner, 2 * BLOCK), BF16),
            pltpu.VMEM((BLOCK, heads), F32),
            pltpu.VMEM((2 * BLOCK, NS), F32),
            pltpu.VMEM((KW - 1, slots, inner), F32),
            pltpu.VMEM((KW - 1, slots, 2 * NS), F32),
            pltpu.VMEM((BLOCK, columns), F32),
            pltpu.SemaphoreType.DMA((moves, 2)),
            pltpu.SemaphoreType.DMA((moves, pages_here + 1)),
        ],
        input_output_aliases={5: 3, 6: 4},
        compiler_params=params(LAST_LIMIT),
        cost_estimate=BRIEF,
        name="arrive",
    )(col_index, plan, table, next_x, next_bc, state_next, pool_next, notes, *parts)
    return (
        mixed, state_next, conv_x_next.transpose(1, 0, 2), conv_bc_next.transpose(1, 0, 2), pool_next[:, None]
    )


def solution(mesh):
    in_specs = (
        P(None, "rows"),
        P(),
        P(),
        P(),
        P(),
        P("rows", "cols", None, None),
        P("rows", "cols", None, None),
        P("rows", "cols", None, None),
        P("rows", None, "cols"),
        P("rows", None, None),
        P("rows"),
        P("rows", "cols"),
        P("rows", "cols"),
        P("rows", "cols"),
        P("rows", None),
        P("rows", None),
        P(None, "cols"),
        P(),
        P("cols"),
        P("cols"),
        P("cols"),
        P("cols", None),
        P("cols", None),
    )
    out_specs = (
        P("rows", "cols"),
        P("rows", "cols", None, None),
        P("rows", None, "cols"),
        P("rows", None, None),
        P("rows", "cols", None, None),
    )
    return jax.shard_map(local, mesh=mesh, in_specs=in_specs, out_specs=out_specs, check_vma=False)
```

```python
import functools

import jax
import jax.numpy as jnp
from jax import lax
from jax.experimental import pallas as pl
from jax.experimental.pallas import tpu as pltpu
from jax.sharding import PartitionSpec as P

HP = 64
NS = 256
KW = 4
QH = 8
KVH = 2
HD = 128
PAGE = 32
LANES = 128
BLOCK = 16

EPSILON = 1e-05
FLOOR_SCORE = -1e30
FIRST_LIMIT = 60 * 1024 * 1024
VMEM_LIMIT = 55 * 1024 * 1024
LAST_LIMIT = 24 * 1024 * 1024

F32 = jnp.float32
BF16 = jnp.bfloat16
I32 = jnp.int32

SMEM_SPEC = pl.BlockSpec(memory_space=pltpu.SMEM)
BRIEF = pl.CostEstimate(flops=1, bytes_accessed=1, transcendentals=0)
VMEM_SPEC = pl.BlockSpec(memory_space=pltpu.VMEM)
ANY_SPEC = pl.BlockSpec(memory_space=pl.ANY)


def silu(v):
    return v / (1.0 + jnp.exp(-v))


def dot(a, b):
    return jnp.dot(a, b, preferred_element_type=F32)


def dot_t(a, b):
    return lax.dot_general(a, b, (((1,), (1,)), ((), ())), preferred_element_type=F32)


def row_iota(shape):
    return lax.broadcasted_iota(I32, shape, 0)


def lane_iota(shape):
    return lax.broadcasted_iota(I32, shape, 1)


class Columns:
    def __init__(self, inner):
        self.z = 0
        self.x = inner
        self.bc = 2 * inner
        self.q = self.bc + 2 * NS
        self.kv = self.q + QH * HD
        self.tail = self.kv + 2 * KVH * HD
        self.width = self.tail + 2 * LANES


class Plan:
    def __init__(self, slots, moves):
        self.length = 0
        self.slot = slots
        self.target = self.slot + moves
        self.away = self.target + moves
        self.source = self.away + moves
        self.from_away = self.source + moves
        self.arrived_length = self.from_away + moves
        self.stay = self.arrived_length + moves
        self.me = self.stay + slots - moves
        self.size = self.me + 1


def early_parts(row_count):
    return [d for d in (2, 4) if d < row_count]


def parcel_parts(refs, row_count, pages_here):
    refs, early = list(refs), early_parts(row_count)
    parts = []
    for d in range(1, row_count):
        if d in early:
            parts.append((refs.pop(0), refs.pop(0)))
        else:
            whole = refs.pop(0)
            parts.append((whole.at[:pages_here], whole.at[pages_here:]))
    return parts


class Note:
    mixed, key_value, drive, drive_low, mixing, conv_x, conv_bc = 0, 1, 2, 3, 4, 5, 8
    decay, decay_low = NS, NS + LANES


def project_kernel(
    row_ref, arrival, lengths, move_slot, move_target, table,
    tokens, gain, w_z, w_x, w_dt, w_bc, w_qkv, pool,
    plan, mine, theirs, *rest,
):
    ahead = rest[:-7]
    inverse, wide, picked, tail, staged, in_sems, out_sems = rest[-7:]
    moves, row_count = move_slot.shape
    pages_here, slots = table.shape
    heads, depth = w_dt.shape
    inner = heads * HP
    cols, at = Columns(inner), Plan(slots, moves)
    me, half = row_ref[0], row_count // 2

    loads, stores = [], []
    for e, (d, pages) in enumerate(zip(early_parts(row_count), ahead)):
        slot = move_slot[0, me]
        for m in range(1, moves):
            slot = jnp.where(lax.bitwise_xor(move_target[m, me], me) == d, move_slot[m, me], slot)
        for page in range(pages_here):
            pltpu.make_async_copy(pool.at[table[page, slot]], staged.at[e, page], in_sems.at[e]).start()
        loads.append(pltpu.make_async_copy(pool.at[:pages_here], staged.at[e], in_sems.at[e]))
        stores.append(pltpu.make_async_copy(staged.at[e], pages, out_sems.at[e]))

    wide[...] = tokens[...].astype(F32)
    picked[...] = jnp.zeros_like(picked)

    def invert(t, carry):
        for s in range(slots):
            inverse[arrival[t * slots + s]] = t * slots + s
        return carry

    lax.fori_loop(0, row_count, invert, 0)

    def pick(b, carry):
        d = jnp.where(b < half, 2 * b, 2 * (b - half) + 1)
        first = lax.bitwise_xor(me, d) * slots
        for s in range(slots):
            picked[pl.ds(b * BLOCK + s, 1), :] = wide[pl.ds(inverse[first + s], 1), :]
        return carry

    lax.fori_loop(0, row_count, pick, 0)

    for load, store in zip(loads, stores):
        load.wait()
        store.start()

    rows = picked[...]
    squares = jnp.sum(rows * rows, axis=1, keepdims=True)
    scaled = (rows * gain[...].astype(F32).reshape(1, depth)).astype(BF16)

    def put(start, value):
        span = slice(start, start + value.shape[1])
        mine[:, span] = value[: half * BLOCK].astype(F32)
        theirs[:, span] = value[half * BLOCK :].astype(BF16)

    put(cols.z, dot(scaled, w_z[...]))
    put(cols.x, dot(scaled, w_x[...]))
    put(cols.bc, dot(scaled, w_bc[...]))
    put(cols.q, dot(scaled, w_qkv[...]))
    tail[...] = jnp.zeros_like(tail)
    tail[:, :heads] = dot_t(scaled, w_dt[...])
    tail[:, heads : heads + 1] = squares
    high = tail[...].astype(BF16)
    put(cols.tail, high)
    put(cols.tail + LANES, tail[...] - high.astype(F32))

    stays = 0
    for s in range(slots):
        plan[at.length + s] = lengths[me * slots + s]
        leaves = move_slot[0, me] == s
        for m in range(1, moves):
            leaves = jnp.logical_or(leaves, move_slot[m, me] == s)

        @pl.when(jnp.logical_not(leaves))
        def _(s=s, stays=stays):
            plan[at.stay + stays] = s

        stays = stays + jnp.where(leaves, 0, 1)
    for m in range(moves):
        plan[at.slot + m] = move_slot[m, me]
        plan[at.target + m] = move_target[m, me]
        plan[at.away + m] = lax.bitwise_xor(move_target[m, me], me)

    def seek(i, turn):
        for m in range(moves):
            comes = move_target[m, i] == me

            @pl.when(comes)
            def _(m=m, turn=turn):
                plan[at.source + turn] = i
                plan[at.from_away + turn] = lax.bitwise_xor(i, me)
                plan[at.arrived_length + turn] = lengths[i * slots + move_slot[m, i]]

            turn = turn + jnp.where(comes, 1, 0)
        return turn

    lax.fori_loop(0, row_count, seek, I32(0))
    plan[at.me] = me
    for store in stores:
        store.wait()


def pack_kernel(plan, table, pool, state, *rest, moves, row_count):
    pages_here, slots = table.shape
    at, early = Plan(slots, moves), early_parts(row_count)
    parcels = rest[: row_count - 1]
    packed, in_sems, out_sems = rest[row_count - 1 :]
    for m in range(moves):
        slot = plan[at.slot + m]
        for page in range(pages_here):
            pltpu.make_async_copy(pool.at[table[page, slot]], packed.at[m, page], in_sems.at[m]).start()
        for part in range(2):
            pltpu.make_async_copy(
                state.at[slot, :, part * PAGE : (part + 1) * PAGE, :],
                packed.at[m, pages_here:, :, part * NS : (part + 1) * NS],
                in_sems.at[m],
            ).start()

    def sent(m, d):
        source = packed.at[m, pages_here:] if d in early else packed.at[m]
        return pltpu.make_async_copy(source, parcels[d - 1], out_sems.at[m])

    def each(m, act):
        for d in range(1, row_count):

            @pl.when(plan[at.away + m] == d)
            def _(d=d):
                act(sent(m, d))

    for m in range(moves):
        pltpu.make_async_copy(pool.at[: packed.shape[1]], packed.at[m], in_sems.at[m]).wait()
        each(m, lambda copy: copy.start())
    for m in range(moves):
        each(m, lambda copy: copy.wait())


def pair_kernel(mine, theirs, own, *others):
    for j, out in enumerate((own,) + others):
        span = slice(j * BLOCK, (j + 1) * BLOCK)
        out[...] = (mine[span, :] + theirs[span, :].astype(F32)).astype(out.dtype)


def widen(per_head, inner):
    rows = per_head.shape[0]
    first = lane_iota((rows, 2 * HP)) < HP
    pieces = []
    for h in range(0, inner // HP, 2):
        pieces.append(jnp.where(first, per_head[:, h : h + 1], per_head[:, h + 1 : h + 2]))
    return pieces[0] if len(pieces) == 1 else jnp.concatenate(pieces, axis=1)


class Sums:
    def __init__(self, received, heads, width):
        self.received = received
        cols = Columns(heads * HP)
        tail = self.total(cols.tail, cols.tail + LANES) + self.total(cols.tail + LANES, cols.width)
        self.root = jnp.sqrt(tail[:, heads : heads + 1] / width + EPSILON)
        self.step_in = (tail[:, :heads] / self.root).astype(BF16).astype(F32)

    def total(self, start, stop):
        return sum(part[:, start:stop].astype(F32) for part in self.received)

    def projected(self, start, stop):
        return (self.total(start, stop) / self.root).astype(BF16).astype(F32)


def inserted(page, row, offset):
    return jnp.where(row_iota(page.shape) == offset, row, page.astype(F32)).astype(BF16)


def place_of(length, col_count):
    logical = lax.div(length, I32(PAGE))
    return lax.rem(logical, I32(col_count)), lax.div(logical, I32(col_count)), lax.rem(length, I32(PAGE))


def attend_kernel(
    col_ref, plan, table, pool, *rest, moves, heads, chip_count, col_count, width
):
    received, (pool_next, kv_new, send) = rest[:chip_count], rest[chip_count : chip_count + 3]
    pages, queries, by_token, scores, weighted, peaks, totals, in_sems, out_sems = rest[chip_count + 3 :]
    pages_here, slots = table.shape
    cols, at = Columns(heads * HP), Plan(slots, moves)
    col = col_ref[0]
    tokens_here = pages_here * PAGE
    kv_width = KVH * HD
    chunks = in_sems.shape[0]
    step = pool.shape[0] // chunks
    spans = [pl.ds(k * step, step) for k in range(chunks)]
    loads = [pltpu.make_async_copy(pool.at[span], pages.at[span], in_sems.at[k]) for k, span in enumerate(spans)]
    for load in loads:
        load.start()

    sums = Sums(received, heads, width)
    kv_new[...] = sums.projected(cols.kv, cols.tail)
    q_in = sums.projected(cols.q, cols.kv)
    for h in range(QH):
        queries[pl.ds(h, BLOCK, stride=QH), :] = q_in[:, h * HD : (h + 1) * HD]

    first_group = row_iota((QH, HD)) < QH // KVH
    stacked = queries[...]
    first_rows = lax.rem(row_iota(stacked.shape), I32(QH)) < QH // KVH
    query_columns = jnp.transpose(
        jnp.concatenate([jnp.where(first_rows, stacked, 0.0), jnp.where(first_rows, 0.0, stacked)], axis=1)
    ).astype(BF16)
    token = row_iota((tokens_here, BLOCK * QH))
    position = (lax.shift_right_logical(token, 5) * col_count + col) * PAGE + lax.bitwise_and(token, PAGE - 1)
    slot_of = lax.div(lane_iota((tokens_here, BLOCK * QH)), I32(QH))
    for load in loads:
        load.wait()
    for s in range(slots):
        owner, local_page, offset = place_of(plan[at.length + s], col_count)
        page = table[local_page, s]
        pages[page] = inserted(pages[page], kv_new[s : s + 1, :], jnp.where(owner == col, offset, -1))
    stores = [
        pltpu.make_async_copy(pages.at[span], pool_next.at[span], out_sems.at[k]) for k, span in enumerate(spans)
    ]
    for store in stores:
        store.start()

    def cached(s, start):
        parts = [pages[table[page, s], :, start : start + kv_width] for page in range(pages_here)]
        return jnp.concatenate(parts, axis=0)

    for s in range(slots):
        score = dot(cached(s, 0), query_columns) * (HD ** -0.5)
        score = jnp.where(position <= plan[at.length + s], score, FLOOR_SCORE)
        by_token[...] = jnp.where(slot_of == s, score, by_token[...] if s else FLOOR_SCORE)

    everything = jnp.transpose(by_token[...])
    peak = jnp.max(everything, axis=1, keepdims=True)
    weights = jnp.where(everything > 0.5 * FLOOR_SCORE, jnp.exp(everything - peak), 0.0)
    scores[...] = weights
    peaks[...] = jnp.broadcast_to(peak, peaks.shape)
    totals[...] = jnp.broadcast_to(jnp.sum(weights, axis=1, keepdims=True), totals.shape)
    weighted[slots * QH :, :] = jnp.zeros(((BLOCK - slots) * QH, HD), F32)
    for s in range(slots):
        weight = scores[s * QH : (s + 1) * QH, :]
        high = weight.astype(BF16).astype(F32)
        both = dot(jnp.concatenate([high, weight - high], axis=0).astype(BF16), cached(s, kv_width))
        joined = both[:QH] + both[QH:]
        weighted[s * QH : (s + 1) * QH, :] = jnp.where(first_group, joined[:, :HD], joined[:, HD:])

    share = QH * HD // col_count
    part = min(share, HD)
    lanes = lane_iota((BLOCK, LANES))
    for c in range(col_count):
        block = slice(c * BLOCK, (c + 1) * BLOCK)
        stats = jnp.zeros((BLOCK, LANES), F32)
        for j in range(share // part):
            head, begin = divmod(c * share + j * part, HD)
            rows = pl.ds(head, BLOCK, stride=QH)
            send[block, j * part : (j + 1) * part] = weighted[rows, :][:, begin : begin + part]
            stats = jnp.where(lanes == 2 * j, peaks[rows, :], stats)
            stats = jnp.where(lanes == 2 * j + 1, totals[rows, :], stats)
        send[block, share:] = stats
    for store in stores:
        store.wait()


def mix_kernel(
    conv_x, conv_bc, cw_x, cw_bc, dt_bias, a_log, d_skip, state, *rest, chip_count, width
):
    received = rest[:chip_count]
    conv_x_next, conv_bc_next, gated, driven_out, decay, drive, b_twice = rest[chip_count : chip_count + 7]
    by_value, held, in_sems = rest[chip_count + 7 :]
    slots, inner = conv_x.shape[1], conv_x.shape[2]
    heads = dt_bias.shape[0]
    cols = Columns(inner)
    loads = []
    for s in range(slots):
        loads.append(pltpu.make_async_copy(state.at[s], held.at[s], in_sems.at[s]))
        loads[-1].start()

    sums = Sums(received, heads, width)

    def convolved(past, taps, fresh, following):
        past_rows = [past[k].astype(F32) for k in range(KW - 1)]
        total = fresh[:slots] * taps[KW - 1 : KW, :].astype(F32)
        for k in range(KW - 1):
            total = total + past_rows[k] * taps[k : k + 1, :].astype(F32)
            following[k] = past_rows[k + 1] if k < KW - 2 else fresh[:slots]
        return jnp.concatenate([silu(total), jnp.zeros((BLOCK - slots, total.shape[1]), F32)], axis=0)

    value_act = convolved(conv_x, cw_x, sums.projected(cols.x, cols.bc), conv_x_next)
    bc_act = convolved(conv_bc, cw_bc, sums.projected(cols.bc, cols.q), conv_bc_next)
    bc_act = bc_act.astype(BF16).astype(F32)
    b_in, c_val = bc_act[:, :NS], bc_act[:, NS:]
    b_twice[...] = jnp.concatenate([b_in, b_in], axis=0)
    padding = jnp.zeros((LANES - BLOCK, NS), F32)
    c_columns = jnp.transpose(jnp.concatenate([c_val, padding], axis=0)).astype(BF16)

    shifted = sums.step_in + dt_bias[...].reshape(1, heads)
    step_size = jnp.maximum(shifted, 0.0) + jnp.log(1.0 + jnp.exp(-jnp.abs(shifted)))
    rate = jnp.exp(-jnp.exp(a_log[...].reshape(1, heads)) * step_size)
    decay[...] = rate
    driven = widen(step_size, inner) * value_act
    driven_out[...] = driven
    high = driven.astype(BF16).astype(F32)
    drive[...] = jnp.transpose(jnp.concatenate([high, driven - high], axis=0)).astype(BF16)

    own_lane = lane_iota(by_value.shape)
    for s in range(slots):
        loads[s].wait()
        value = dot(held[s].reshape(inner, NS), c_columns)
        by_value[...] = jnp.where(own_lane == s, value, by_value[...] if s else 0.0)
    readout = jnp.transpose(by_value[...])[:BLOCK]

    gate = silu(sums.projected(cols.z, cols.x))
    b_dot_c = jnp.sum(b_in * c_val, axis=1, keepdims=True)
    skip = widen(jnp.broadcast_to(d_skip[...].reshape(1, heads), (BLOCK, heads)), inner)
    total = widen(rate, inner) * readout + driven * b_dot_c + skip * value_act
    gated[...] = (total * gate).astype(BF16).astype(F32)


def stay_kernel(plan, drive, decay, b_twice, state, state_next, held, made, in_sems, out_sems, *, moves):
    stays = held.shape[0]
    at = Plan(state.shape[0], moves)
    loads = []
    for j in range(stays):
        loads.append(pltpu.make_async_copy(state.at[plan[at.stay + j]], held.at[j], in_sems.at[j]))
        loads[-1].start()
    stores = []
    for j in range(stays):
        slot = plan[at.stay + j]
        loads[j].wait()
        advance_state(slot, held.at[j], b_twice, drive, decay, made.at[j])
        stores.append(pltpu.make_async_copy(made.at[j], state_next.at[slot], out_sems.at[j]))
        stores[-1].start()
    for store in stores:
        store.wait()


def advance_state(slot, prior, b_twice, drive, decay, result):
    heads = result.shape[0]
    twice = b_twice[...]
    half = twice.shape[0] // 2
    row = row_iota(twice.shape)
    selected = jnp.where((row == slot) | (row == slot + half), twice, 0.0).astype(BF16)
    outer = dot(drive[...], selected).reshape(heads, HP, NS)
    for h in range(heads):
        rate = decay[pl.ds(slot, 1), h : h + 1]
        result[h] = (rate * prior[h].astype(F32) + outer[h]).astype(BF16)


def output_kernel(gated, w_ssm, w_attn, partials, send, *, slots, col_count):
    share = w_attn.shape[0]
    part = min(share, HD)
    blocks = [partials[c * BLOCK : (c + 1) * BLOCK, :] for c in range(col_count)]
    pieces = []
    for j in range(share // part):
        peaks = [b[:, share + 2 * j : share + 2 * j + 1] for b in blocks]
        joint = functools.reduce(jnp.maximum, peaks)
        factors = [jnp.exp(p - joint) for p in peaks]
        total = sum(f * b[:, share + 2 * j + 1 : share + 2 * j + 2] for f, b in zip(factors, blocks))
        value = sum(f * b[:, j * part : (j + 1) * part] for f, b in zip(factors, blocks))
        pieces.append(value / total)
    joined = pieces[0] if len(pieces) == 1 else jnp.concatenate(pieces, axis=1)
    right = jnp.where(row_iota(joined.shape) < slots, joined, 0.0).astype(BF16)
    left = gated[...].astype(BF16)
    columns = w_ssm.shape[1] // col_count
    for c in range(col_count):
        span = slice(c * columns, (c + 1) * columns)
        terms = dot(left, w_ssm[:, span]) + dot(right, w_attn[:, span])
        send[c * BLOCK : (c + 1) * BLOCK, :] = terms.astype(BF16)


def total_kernel(
    plan, kv_new, driven, decay, b_twice, conv_x, conv_bc, terms, send, mixed, block, *, moves, col_count
):
    at = Plan(conv_x.shape[1], moves)
    total = sum(terms[c * BLOCK : (c + 1) * BLOCK, :].astype(F32) for c in range(col_count))
    mixed[...] = total
    send[pl.ds(pl.multiple_of(plan[at.me] * BLOCK, BLOCK), BLOCK), : total.shape[1]] = total.astype(BF16)

    block[...] = jnp.zeros_like(block)
    for m in range(moves):
        row = pl.ds(plan[at.slot + m], 1)

        def put(index, value, start=0):
            block[index : index + 1, start : start + value.shape[1]] = value

        put(Note.mixed, mixed[row, :])
        put(Note.key_value, kv_new[row, :])
        for index, value, start, low_index, low_start in (
            (Note.drive, driven[row, :], 0, Note.drive_low, 0),
            (Note.mixing, decay[row, :], Note.decay, Note.mixing, Note.decay_low),
        ):
            high = value.astype(BF16).astype(F32)
            put(index, high, start)
            put(low_index, value - high, low_start)
        put(Note.mixing, b_twice[row, :])
        for k in range(KW - 1):
            put(Note.conv_x + k, conv_x[k, row, :])
            put(Note.conv_bc + k, conv_bc[k, row, :])
        start = pl.multiple_of(plan[at.target + m] * BLOCK, BLOCK)
        send[pl.ds(start, BLOCK), :] = block[...].astype(BF16)


def arrive_kernel(
    col_ref, plan, table, conv_x, conv_bc, state_in, pool_in, notes, *rest,
    moves, row_count, col_count,
):
    del state_in, pool_in
    parcel_count = row_count - 1 + len(early_parts(row_count))
    parcels, rest = rest[:parcel_count], rest[parcel_count:]
    pages_here, slots = table.shape
    inner = conv_x.shape[2]
    heads = inner // HP
    at = Plan(slots, moves)
    mixed, conv_x_next, conv_bc_next, state_next, pool_next = rest[:5]
    packed, made, drive, decay, b_twice, window_x, window_bc, window_mixed, in_sems, out_sems = rest[5:]
    col = col_ref[0]
    parcels = parcel_parts(parcels, row_count, pages_here)

    def loaded(m, parcel):
        pages, states = parcel
        return (
            pltpu.make_async_copy(pages, packed.at[m, :pages_here], in_sems.at[m, 0]),
            pltpu.make_async_copy(states, packed.at[m, pages_here:], in_sems.at[m, 1]),
        )

    for m in range(moves):
        for d, parcel in enumerate(parcels, 1):

            @pl.when(plan[at.from_away + m] == d)
            def _(m=m, parcel=parcel):
                for copy in loaded(m, parcel):
                    copy.start()


    for k in range(KW - 1):
        window_x[k] = conv_x[k]
        window_bc[k] = conv_bc[k]
    home = pl.multiple_of(plan[at.me] * BLOCK, BLOCK)
    window_mixed[...] = notes[pl.ds(home, BLOCK), : window_mixed.shape[1]].astype(F32)
    rows = []
    b_twice[...] = jnp.zeros_like(b_twice)
    half = b_twice.shape[0] // 2
    for m in range(moves):
        start = pl.multiple_of(plan[at.source + m] * BLOCK, BLOCK)
        note = notes[pl.ds(start, BLOCK), :].astype(F32)
        rows.append(note)
        row = pl.ds(plan[at.slot + m], 1)
        window_mixed[row, :] = note[Note.mixed : Note.mixed + 1, : window_mixed.shape[1]]
        for k in range(KW - 1):
            window_x[k, row, :] = note[Note.conv_x + k : Note.conv_x + k + 1, :inner]
            window_bc[k, row, :] = note[Note.conv_bc + k : Note.conv_bc + k + 1, : 2 * NS]
        mixing = note[Note.mixing : Note.mixing + 1, :]
        b_twice[m : m + 1, :] = mixing[:, :NS]
        b_twice[half + m : half + m + 1, :] = mixing[:, :NS]
        decay[m : m + 1, :] = (
            mixing[:, Note.decay : Note.decay + heads] + mixing[:, Note.decay_low : Note.decay_low + heads]
        )
    padding = [jnp.zeros((half - moves, inner), F32)]
    stacked = [note[Note.drive : Note.drive + 1, :inner] for note in rows] + padding
    stacked += [note[Note.drive_low : Note.drive_low + 1, :inner] for note in rows] + padding
    drive[...] = jnp.transpose(jnp.concatenate(stacked, axis=0)).astype(BF16)
    mixed[...] = window_mixed[0:slots, :].astype(BF16)
    for k in range(KW - 1):
        conv_x_next[k] = window_x[k].astype(BF16)
        conv_bc_next[k] = window_bc[k].astype(BF16)

    stores = []
    for m in range(moves):
        slot = plan[at.slot + m]
        for copy in loaded(m, parcels[0]):
            copy.wait()
        owner, local_page, offset = place_of(plan[at.arrived_length + m], col_count)
        key_value = rows[m][Note.key_value : Note.key_value + 1, : 2 * KVH * HD]

        @pl.when(owner == col)
        def _(m=m, local_page=local_page, offset=offset, key_value=key_value):
            packed[m, local_page] = inserted(packed[m, local_page], key_value, offset)

        for page in range(pages_here):
            stores.append(
                pltpu.make_async_copy(
                    packed.at[m, page], pool_next.at[table[page, slot]], out_sems.at[m, page]
                )
            )
            stores[-1].start()
        prior = [
            jnp.concatenate([packed[m, pages_here + h, :, :NS], packed[m, pages_here + h, :, NS:]], axis=0)
            for h in range(heads)
        ]
        advance_state(m, prior, b_twice, drive, decay, made.at[m])
        stores.append(pltpu.make_async_copy(made.at[m], state_next.at[slot], out_sems.at[m, pages_here]))
        stores[-1].start()
    for store in stores:
        store.wait()


def shape(dims, dtype):
    return jax.ShapeDtypeStruct(tuple(dims), dtype)


def params(limit=VMEM_LIMIT):
    return pltpu.CompilerParams(vmem_limit_bytes=limit)


def exchange(value, axis):
    return lax.all_to_all(value, axis, split_axis=0, concat_axis=0, tiled=True)


def trade(block, axis, d):
    return lax.ppermute(block, axis, [(i, i ^ d) for i in range(lax.axis_size(axis))])


def ordered(value, first):
    return lax.optimization_barrier((value, first))[0]


def local(
    tokens, arrival, cache_lengths, move_slot, move_target, page_table, kv_pool, ssm_state,
    conv_x, conv_bc, norm_gain, weight_z, weight_x, weight_dt, weight_bc, weight_qkv,
    conv_weight_x, conv_weight_bc, dt_bias, a_log, d_skip, weight_ssm_out, weight_attn_out,
):
    row_count = lax.axis_size("rows")
    col_count = lax.axis_size("cols")
    row_index = lax.axis_index("rows").astype(I32).reshape(1)
    col_index = lax.axis_index("cols").astype(I32).reshape(1)
    slots, heads = ssm_state.shape[0], ssm_state.shape[1]
    total, depth = tokens.shape
    moves = move_slot.shape[1]
    pages_here, width = page_table.shape[3], kv_pool.shape[3]
    inner = heads * HP
    stays = slots - moves
    cols, at = Columns(inner), Plan(slots, moves)
    table = page_table[0, 0].T
    pool = kv_pool[:, 0]
    past_x, past_bc = conv_x.transpose(1, 0, 2), conv_bc.transpose(1, 0, 2)
    rows = row_count * BLOCK
    model = depth * row_count
    share = QH * HD // col_count
    parcel = (pages_here + heads, PAGE, width)
    parcels_here = pltpu.VMEM((moves,) + parcel, BF16)

    chip_count = row_count // 2
    early = early_parts(row_count)
    plan, mine, theirs, *ahead = pl.pallas_call(
        project_kernel,
        out_shape=[
            shape((at.size,), I32),
            shape((chip_count * BLOCK, cols.width), F32),
            shape((chip_count * BLOCK, cols.width), BF16),
        ]
        + [shape((pages_here,) + parcel[1:], BF16)] * len(early),
        in_specs=[SMEM_SPEC] * 6 + [VMEM_SPEC] * 7 + [ANY_SPEC],
        out_specs=[SMEM_SPEC] + [VMEM_SPEC] * 2 + [ANY_SPEC] * len(early),
        scratch_shapes=[
            pltpu.SMEM((total,), I32),
            pltpu.VMEM((total, depth), F32),
            pltpu.VMEM((rows, depth), F32),
            pltpu.VMEM((rows, LANES), F32),
            pltpu.VMEM((len(early), pages_here, PAGE, width), BF16),
            pltpu.SemaphoreType.DMA((len(early),)),
            pltpu.SemaphoreType.DMA((len(early),)),
        ],
        compiler_params=params(FIRST_LIMIT),
        cost_estimate=BRIEF,
        name="project",
    )(
        row_index, arrival, cache_lengths, move_slot.T, move_target.T, table,
        tokens, norm_gain, weight_z, weight_x, weight_dt.T, weight_bc, weight_qkv, pool,
    )
    ahead = [trade(pages, "rows", d) for d, pages in zip(early, ahead)]
    parcels = pl.pallas_call(
        functools.partial(pack_kernel, moves=moves, row_count=row_count),
        out_shape=[
            shape((heads,) + parcel[1:] if d in early else parcel, BF16) for d in range(1, row_count)
        ],
        in_specs=[SMEM_SPEC] * 2 + [ANY_SPEC] * 2,
        out_specs=[ANY_SPEC] * (row_count - 1),
        scratch_shapes=[
            parcels_here,
            pltpu.SemaphoreType.DMA((moves,)),
            pltpu.SemaphoreType.DMA((moves,)),
        ],
        compiler_params=params(FIRST_LIMIT),
        cost_estimate=BRIEF,
        name="pack",
    )(plan, table, pool, ssm_state)

    sums = pl.pallas_call(
        pair_kernel,
        out_shape=[shape((BLOCK, cols.width), F32)] + [shape((BLOCK, cols.width), BF16)] * (chip_count - 1),
        in_specs=[VMEM_SPEC] * 2,
        out_specs=[VMEM_SPEC] * chip_count,
        compiler_params=params(FIRST_LIMIT),
        cost_estimate=BRIEF,
        name="pair",
    )(mine, trade(theirs, "rows", 1))
    received = [sums[0]] + [trade(block, "rows", 2 * j) for j, block in enumerate(sums[1:], 1)]

    moving = [None, *parcels]

    def migrate(parts, after):
        for d in parts:
            moving[d] = trade(ordered(moving[d], after), "rows", d)
        return [moving[d] for d in parts]

    evens, odds = list(range(2, row_count, 2)), list(range(3, row_count, 2))
    first = [odds[0], odds[len(odds) // 2]]
    second = [evens[-1], 1]
    last = [d for d in odds + evens if d not in first + second]
    received = ordered(received, ahead)
    first_moved = migrate(first, received)
    second_moved = migrate(second, received)

    pool_next, kv_new, partials = pl.pallas_call(
        functools.partial(
            attend_kernel, moves=moves, heads=heads, chip_count=chip_count, col_count=col_count, width=model
        ),
        out_shape=[
            shape(pool.shape, BF16),
            shape((BLOCK, 2 * KVH * HD), F32),
            shape((col_count * BLOCK, share + LANES), F32),
        ],
        in_specs=[SMEM_SPEC] * 3 + [ANY_SPEC] + [VMEM_SPEC] * chip_count,
        out_specs=[ANY_SPEC] + [VMEM_SPEC] * 2,
        scratch_shapes=[
            pltpu.VMEM(pool.shape, BF16),
            pltpu.VMEM((BLOCK * QH, HD), F32),
            pltpu.VMEM((pages_here * PAGE, BLOCK * QH), F32),
            pltpu.VMEM((BLOCK * QH, pages_here * PAGE), F32),
            pltpu.VMEM((BLOCK * QH, HD), F32),
            pltpu.VMEM((BLOCK * QH, HD), F32),
            pltpu.VMEM((BLOCK * QH, HD), F32),
            pltpu.SemaphoreType.DMA((2 if pool.shape[0] % 4 else 4,)),
            pltpu.SemaphoreType.DMA((2 if pool.shape[0] % 4 else 4,)),
        ],
        compiler_params=params(),
        cost_estimate=BRIEF,
        name="attend",
    )(col_index, plan, table, pool, *received)
    received = ordered(received, partials)
    partials = exchange(partials, "cols")

    next_x, next_bc, gated, driven, decay, drive, b_twice = pl.pallas_call(
        functools.partial(mix_kernel, chip_count=chip_count, width=model),
        out_shape=(
            shape(past_x.shape, F32),
            shape(past_bc.shape, F32),
            shape((BLOCK, inner), F32),
            shape((BLOCK, inner), F32),
            shape((BLOCK, heads), F32),
            shape((inner, 2 * BLOCK), BF16),
            shape((2 * BLOCK, NS), F32),
        ),
        in_specs=[VMEM_SPEC] * 7 + [ANY_SPEC] + [VMEM_SPEC] * chip_count,
        out_specs=(VMEM_SPEC,) * 7,
        scratch_shapes=[
            pltpu.VMEM((inner, LANES), F32),
            pltpu.VMEM((slots, heads, HP, NS), BF16),
            pltpu.SemaphoreType.DMA((slots,)),
        ],
        compiler_params=params(),
        cost_estimate=BRIEF,
        name="mix",
    )(past_x, past_bc, conv_weight_x, conv_weight_bc, dt_bias, a_log, d_skip, ssm_state, *received)

    columns = weight_ssm_out.shape[1] // col_count
    terms = pl.pallas_call(
        functools.partial(output_kernel, slots=slots, col_count=col_count),
        out_shape=shape((col_count * BLOCK, columns), BF16),
        in_specs=[VMEM_SPEC] * 4,
        out_specs=VMEM_SPEC,
        compiler_params=params(),
        cost_estimate=BRIEF,
        name="output",
    )(gated, weight_ssm_out, weight_attn_out, partials)
    migrate(last, (terms, first_moved))
    drive = ordered(drive, terms)
    terms = exchange(terms, "cols")
    state_next = pl.pallas_call(
        functools.partial(stay_kernel, moves=moves),
        out_shape=shape(ssm_state.shape, BF16),
        in_specs=[SMEM_SPEC] + [VMEM_SPEC] * 3 + [ANY_SPEC],
        out_specs=ANY_SPEC,
        scratch_shapes=[
            pltpu.VMEM((stays, heads, HP, NS), BF16),
            pltpu.VMEM((stays, heads, HP, NS), BF16),
            pltpu.SemaphoreType.DMA((stays,)),
            pltpu.SemaphoreType.DMA((stays,)),
        ],
        compiler_params=params(),
        cost_estimate=BRIEF,
        name="stay",
    )(plan, drive, decay, b_twice, ssm_state)

    terms = ordered(terms, second_moved)
    note = (BLOCK, max(inner, 2 * NS, 2 * KVH * HD, columns))
    notes = pl.pallas_call(
        functools.partial(total_kernel, moves=moves, col_count=col_count),
        out_shape=shape((rows, note[1]), BF16),
        in_specs=[SMEM_SPEC] + [VMEM_SPEC] * 7,
        out_specs=VMEM_SPEC,
        scratch_shapes=[pltpu.VMEM((BLOCK, columns), F32), pltpu.VMEM(note, F32)],
        compiler_params=params(),
        cost_estimate=BRIEF,
        name="total",
    )(plan, kv_new, driven, decay, b_twice, next_x, next_bc, terms)
    notes = exchange(notes, "rows")

    parts = []
    for d in range(1, row_count):
        parts += [ahead[early.index(d)], moving[d]] if d in early else [moving[d]]
    mixed, conv_x_next, conv_bc_next, state_next, pool_next = pl.pallas_call(
        functools.partial(arrive_kernel, moves=moves, row_count=row_count, col_count=col_count),
        out_shape=(
            shape((slots, columns), BF16),
            shape(past_x.shape, BF16),
            shape(past_bc.shape, BF16),
            shape(ssm_state.shape, BF16),
            shape(pool.shape, BF16),
        ),
        in_specs=[SMEM_SPEC] * 3 + [VMEM_SPEC] * 2 + [ANY_SPEC] * 2 + [VMEM_SPEC] + [ANY_SPEC] * (row_count - 1 + len(early)),
        out_specs=[VMEM_SPEC] * 3 + [ANY_SPEC] * 2,
        scratch_shapes=[
            parcels_here,
            pltpu.VMEM((moves, heads, HP, NS), BF16),
            pltpu.VMEM((inner, 2 * BLOCK), BF16),
            pltpu.VMEM((BLOCK, heads), F32),
            pltpu.VMEM((2 * BLOCK, NS), F32),
            pltpu.VMEM((KW - 1, slots, inner), F32),
            pltpu.VMEM((KW - 1, slots, 2 * NS), F32),
            pltpu.VMEM((BLOCK, columns), F32),
            pltpu.SemaphoreType.DMA((moves, 2)),
            pltpu.SemaphoreType.DMA((moves, pages_here + 1)),
        ],
        input_output_aliases={5: 3, 6: 4},
        compiler_params=params(LAST_LIMIT),
        cost_estimate=BRIEF,
        name="arrive",
    )(col_index, plan, table, next_x, next_bc, state_next, pool_next, notes, *parts)
    return (
        mixed, state_next, conv_x_next.transpose(1, 0, 2), conv_bc_next.transpose(1, 0, 2), pool_next[:, None]
    )


def solution(mesh):
    in_specs = (
        P(None, "rows"),
        P(),
        P(),
        P(),
        P(),
        P("rows", "cols", None, None),
        P("rows", "cols", None, None),
        P("rows", "cols", None, None),
        P("rows", None, "cols"),
        P("rows", None, None),
        P("rows"),
        P("rows", "cols"),
        P("rows", "cols"),
        P("rows", "cols"),
        P("rows", None),
        P("rows", None),
        P(None, "cols"),
        P(),
        P("cols"),
        P("cols"),
        P("cols"),
        P("cols", None),
        P("cols", None),
    )
    out_specs = (
        P("rows", "cols"),
        P("rows", "cols", None, None),
        P("rows", None, "cols"),
        P("rows", None, None),
        P("rows", "cols", None, None),
    )
    return jax.shard_map(local, mesh=mesh, in_specs=in_specs, out_specs=out_specs, check_vma=False)
```

```python
import functools

import jax
import jax.numpy as jnp
from jax import lax
from jax.experimental import pallas as pl
from jax.experimental.pallas import tpu as pltpu
from jax.sharding import PartitionSpec as P

HP = 64
NS = 256
KW = 4
QH = 8
KVH = 2
HD = 128
PAGE = 32
LANES = 128
BLOCK = 16

EPSILON = 1e-05
FLOOR_SCORE = -1e30
FIRST_LIMIT = 60 * 1024 * 1024
PAIR_LIMIT = 62_700_000
VMEM_LIMIT = 55 * 1024 * 1024
LAST_LIMIT = 24 * 1024 * 1024

F32 = jnp.float32
BF16 = jnp.bfloat16
I32 = jnp.int32

SMEM_SPEC = pl.BlockSpec(memory_space=pltpu.SMEM)
BRIEF = pl.CostEstimate(flops=1, bytes_accessed=1, transcendentals=0)
VMEM_SPEC = pl.BlockSpec(memory_space=pltpu.VMEM)
ANY_SPEC = pl.BlockSpec(memory_space=pl.ANY)


def silu(v):
    return v / (1.0 + jnp.exp(-v))


def dot(a, b):
    return jnp.dot(a, b, preferred_element_type=F32)


def dot_t(a, b):
    return lax.dot_general(a, b, (((1,), (1,)), ((), ())), preferred_element_type=F32)


def row_iota(shape):
    return lax.broadcasted_iota(I32, shape, 0)


def lane_iota(shape):
    return lax.broadcasted_iota(I32, shape, 1)


class Columns:
    def __init__(self, inner):
        self.z = 0
        self.x = inner
        self.bc = 2 * inner
        self.q = self.bc + 2 * NS
        self.kv = self.q + QH * HD
        self.tail = self.kv + 2 * KVH * HD
        self.width = self.tail + 2 * LANES


class Plan:
    def __init__(self, slots, moves):
        self.length = 0
        self.slot = slots
        self.target = self.slot + moves
        self.away = self.target + moves
        self.source = self.away + moves
        self.from_away = self.source + moves
        self.arrived_length = self.from_away + moves
        self.stay = self.arrived_length + moves
        self.me = self.stay + slots - moves
        self.size = self.me + 1


def early_parts(row_count):
    return [row_count - 2] if row_count > 2 else []


def parcel_parts(refs, row_count, pages_here):
    refs, early = list(refs), early_parts(row_count)
    parts = []
    for d in range(1, row_count):
        if d in early:
            parts.append((refs.pop(0), refs.pop(0)))
        else:
            whole = refs.pop(0)
            parts.append((whole.at[:pages_here], whole.at[pages_here:]))
    return parts


class Note:
    mixed, key_value, drive, drive_low, mixing, conv_x, conv_bc = 0, 1, 2, 3, 4, 5, 8
    decay, decay_low = NS, NS + LANES


def project_kernel(
    row_ref, arrival, lengths, move_slot, move_target, table,
    tokens, gain, w_z, w_x, w_dt, w_bc, w_qkv, pool,
    plan, mine, theirs, *rest,
):
    ahead = rest[:-7]
    inverse, wide, picked, tail, staged, in_sems, out_sems = rest[-7:]
    moves, row_count = move_slot.shape
    pages_here, slots = table.shape
    heads, depth = w_dt.shape
    inner = heads * HP
    cols, at = Columns(inner), Plan(slots, moves)
    me, half = row_ref[0], row_count // 2

    loads, stores = [], []
    for e, (d, pages) in enumerate(zip(early_parts(row_count), ahead)):
        slot = move_slot[0, me]
        for m in range(1, moves):
            slot = jnp.where(lax.bitwise_xor(move_target[m, me], me) == d, move_slot[m, me], slot)
        for page in range(pages_here):
            pltpu.make_async_copy(pool.at[table[page, slot]], staged.at[e, page], in_sems.at[e]).start()
        loads.append(pltpu.make_async_copy(pool.at[:pages_here], staged.at[e], in_sems.at[e]))
        stores.append(pltpu.make_async_copy(staged.at[e], pages, out_sems.at[e]))

    wide[...] = tokens[...].astype(F32)
    picked[...] = jnp.zeros_like(picked)

    def invert(t, carry):
        for s in range(slots):
            inverse[arrival[t * slots + s]] = t * slots + s
        return carry

    lax.fori_loop(0, row_count, invert, 0)

    def pick(b, carry):
        d = jnp.where(b < half, 2 * b, 2 * (b - half) + 1)
        first = lax.bitwise_xor(me, d) * slots
        for s in range(slots):
            picked[pl.ds(b * BLOCK + s, 1), :] = wide[pl.ds(inverse[first + s], 1), :]
        return carry

    lax.fori_loop(0, row_count, pick, 0)

    for load, store in zip(loads, stores):
        load.wait()
        store.start()

    rows = picked[...]
    squares = jnp.sum(rows * rows, axis=1, keepdims=True)
    scaled = (rows * gain[...].astype(F32).reshape(1, depth)).astype(BF16)

    def put(start, value):
        span = slice(start, start + value.shape[1])
        mine[:, span] = value[: half * BLOCK].astype(F32)
        theirs[:, span] = value[half * BLOCK :].astype(BF16)

    put(cols.z, dot(scaled, w_z[...]))
    put(cols.x, dot(scaled, w_x[...]))
    put(cols.bc, dot(scaled, w_bc[...]))
    put(cols.q, dot(scaled, w_qkv[...]))
    tail[...] = jnp.zeros_like(tail)
    tail[:, :heads] = dot_t(scaled, w_dt[...])
    tail[:, heads : heads + 1] = squares
    high = tail[...].astype(BF16)
    put(cols.tail, high)
    put(cols.tail + LANES, tail[...] - high.astype(F32))

    stays = 0
    for s in range(slots):
        plan[at.length + s] = lengths[me * slots + s]
        leaves = move_slot[0, me] == s
        for m in range(1, moves):
            leaves = jnp.logical_or(leaves, move_slot[m, me] == s)

        @pl.when(jnp.logical_not(leaves))
        def _(s=s, stays=stays):
            plan[at.stay + stays] = s

        stays = stays + jnp.where(leaves, 0, 1)
    for m in range(moves):
        plan[at.slot + m] = move_slot[m, me]
        plan[at.target + m] = move_target[m, me]
        plan[at.away + m] = lax.bitwise_xor(move_target[m, me], me)

    def seek(i, turn):
        for m in range(moves):
            comes = move_target[m, i] == me

            @pl.when(comes)
            def _(m=m, turn=turn):
                plan[at.source + turn] = i
                plan[at.from_away + turn] = lax.bitwise_xor(i, me)
                plan[at.arrived_length + turn] = lengths[i * slots + move_slot[m, i]]

            turn = turn + jnp.where(comes, 1, 0)
        return turn

    lax.fori_loop(0, row_count, seek, I32(0))
    plan[at.me] = me
    for store in stores:
        store.wait()


def pack_kernel(plan, table, pool, state, *rest, moves, row_count):
    pages_here, slots = table.shape
    at, early = Plan(slots, moves), early_parts(row_count)
    parcels = rest[: row_count - 1]
    packed, in_sems, out_sems = rest[row_count - 1 :]
    for m in range(moves):
        slot = plan[at.slot + m]
        for page in range(pages_here):
            pltpu.make_async_copy(pool.at[table[page, slot]], packed.at[m, page], in_sems.at[m]).start()
        for part in range(2):
            pltpu.make_async_copy(
                state.at[slot, :, part * PAGE : (part + 1) * PAGE, :],
                packed.at[m, pages_here:, :, part * NS : (part + 1) * NS],
                in_sems.at[m],
            ).start()

    def sent(m, d):
        source = packed.at[m, pages_here:] if d in early else packed.at[m]
        return pltpu.make_async_copy(source, parcels[d - 1], out_sems.at[m])

    def each(m, act):
        for d in range(1, row_count):

            @pl.when(plan[at.away + m] == d)
            def _(d=d):
                act(sent(m, d))

    for m in range(moves):
        pltpu.make_async_copy(pool.at[: packed.shape[1]], packed.at[m], in_sems.at[m]).wait()
        each(m, lambda copy: copy.start())
    for m in range(moves):
        each(m, lambda copy: copy.wait())


def pair_kernel(mine, theirs, own, *others):
    for j, out in enumerate((own,) + others):
        span = slice(j * BLOCK, (j + 1) * BLOCK)
        out[...] = (mine[span, :] + theirs[span, :].astype(F32)).astype(out.dtype)


def widen(per_head, inner):
    rows = per_head.shape[0]
    first = lane_iota((rows, 2 * HP)) < HP
    pieces = []
    for h in range(0, inner // HP, 2):
        pieces.append(jnp.where(first, per_head[:, h : h + 1], per_head[:, h + 1 : h + 2]))
    return pieces[0] if len(pieces) == 1 else jnp.concatenate(pieces, axis=1)


class Sums:
    def __init__(self, received, heads, width):
        self.received = received
        cols = Columns(heads * HP)
        tail = self.total(cols.tail, cols.tail + LANES) + self.total(cols.tail + LANES, cols.width)
        self.root = jnp.sqrt(tail[:, heads : heads + 1] / width + EPSILON)
        self.step_in = (tail[:, :heads] / self.root).astype(BF16).astype(F32)

    def total(self, start, stop):
        return sum(part[:, start:stop].astype(F32) for part in self.received)

    def projected(self, start, stop):
        return (self.total(start, stop) / self.root).astype(BF16).astype(F32)


def inserted(page, row, offset):
    return jnp.where(row_iota(page.shape) == offset, row, page.astype(F32)).astype(BF16)


def place_of(length, col_count):
    logical = lax.div(length, I32(PAGE))
    return lax.rem(logical, I32(col_count)), lax.div(logical, I32(col_count)), lax.rem(length, I32(PAGE))


def attend_kernel(
    col_ref, plan, table, pool, *rest, moves, heads, chip_count, col_count, width
):
    received, (pool_next, kv_new, send) = rest[:chip_count], rest[chip_count : chip_count + 3]
    pages, queries, scores, weighted, peaks, totals, in_sems, out_sems = rest[chip_count + 3 :]
    pages_here, slots = table.shape
    cols, at = Columns(heads * HP), Plan(slots, moves)
    col = col_ref[0]
    tokens_here = pages_here * PAGE
    kv_width = KVH * HD
    chunks = in_sems.shape[0]
    step = pool.shape[0] // chunks
    spans = [pl.ds(k * step, step) for k in range(chunks)]
    loads = [pltpu.make_async_copy(pool.at[span], pages.at[span], in_sems.at[k]) for k, span in enumerate(spans)]
    for load in loads:
        load.start()

    sums = Sums(received, heads, width)
    kv_new[...] = sums.projected(cols.kv, cols.tail)
    q_in = sums.projected(cols.q, cols.kv)
    for h in range(QH):
        queries[pl.ds(h, BLOCK, stride=QH), :] = q_in[:, h * HD : (h + 1) * HD]

    first_group = row_iota((QH, HD)) < QH // KVH
    lane = lane_iota((QH, tokens_here))
    position = (lax.shift_right_logical(lane, 5) * col_count + col) * PAGE + lax.bitwise_and(lane, PAGE - 1)
    for load in loads:
        load.wait()
    for s in range(slots):
        owner, local_page, offset = place_of(plan[at.length + s], col_count)
        page = table[local_page, s]
        pages[page] = inserted(pages[page], kv_new[s : s + 1, :], jnp.where(owner == col, offset, -1))
    stores = [
        pltpu.make_async_copy(pages.at[span], pool_next.at[span], out_sems.at[k]) for k, span in enumerate(spans)
    ]
    for store in stores:
        store.start()

    def cached(s, start):
        parts = [pages[table[page, s], :, start : start + kv_width] for page in range(pages_here)]
        return jnp.concatenate(parts, axis=0)

    for s in range(slots):
        query = queries[s * QH : (s + 1) * QH, :]
        query = jnp.concatenate(
            [jnp.where(first_group, query, 0.0), jnp.where(first_group, 0.0, query)], axis=1
        ).astype(BF16)
        score = dot_t(query, cached(s, 0)) * (HD ** -0.5)
        scores[s * QH : (s + 1) * QH, :] = jnp.where(position <= plan[at.length + s], score, FLOOR_SCORE)

    live_rows = slots * QH
    everything = scores[0:live_rows, :]
    peak = jnp.max(everything, axis=1, keepdims=True)
    weights = jnp.where(everything > 0.5 * FLOOR_SCORE, jnp.exp(everything - peak), 0.0)
    total = jnp.sum(weights, axis=1, keepdims=True)
    scores[0:live_rows, :] = weights
    for ref, value in ((weighted, None), (peaks, peak), (totals, total)):
        ref[live_rows:, :] = jnp.zeros((BLOCK * QH - live_rows, HD), F32)
        if value is not None:
            ref[0:live_rows, :] = jnp.broadcast_to(value, (live_rows, HD))
    for s in range(slots):
        weight = scores[s * QH : (s + 1) * QH, :]
        high = weight.astype(BF16).astype(F32)
        both = dot(jnp.concatenate([high, weight - high], axis=0).astype(BF16), cached(s, kv_width))
        joined = both[:QH] + both[QH:]
        weighted[s * QH : (s + 1) * QH, :] = jnp.where(first_group, joined[:, :HD], joined[:, HD:])

    share = QH * HD // col_count
    part = min(share, HD)
    lanes = lane_iota((BLOCK, LANES))
    for c in range(col_count):
        block = slice(c * BLOCK, (c + 1) * BLOCK)
        stats = jnp.zeros((BLOCK, LANES), F32)
        for j in range(share // part):
            head, begin = divmod(c * share + j * part, HD)
            rows = pl.ds(head, BLOCK, stride=QH)
            send[block, j * part : (j + 1) * part] = weighted[rows, :][:, begin : begin + part]
            stats = jnp.where(lanes == 2 * j, peaks[rows, :], stats)
            stats = jnp.where(lanes == 2 * j + 1, totals[rows, :], stats)
        send[block, share:] = stats
    for store in stores:
        store.wait()


def mix_kernel(
    conv_x, conv_bc, cw_x, cw_bc, dt_bias, a_log, d_skip, state, *rest, chip_count, width
):
    received = rest[:chip_count]
    conv_x_next, conv_bc_next, gated, driven_out, decay, drive, b_twice = rest[chip_count : chip_count + 7]
    readout, held, in_sems = rest[chip_count + 7 :]
    slots, inner = conv_x.shape[1], conv_x.shape[2]
    heads = dt_bias.shape[0]
    cols = Columns(inner)
    loads = []
    for s in range(slots):
        loads.append(pltpu.make_async_copy(state.at[s], held.at[s], in_sems.at[s]))
        loads[-1].start()

    sums = Sums(received, heads, width)

    def convolved(past, taps, fresh, following):
        past_rows = [past[k].astype(F32) for k in range(KW - 1)]
        total = fresh[:slots] * taps[KW - 1 : KW, :].astype(F32)
        for k in range(KW - 1):
            total = total + past_rows[k] * taps[k : k + 1, :].astype(F32)
            following[k] = past_rows[k + 1] if k < KW - 2 else fresh[:slots]
        return jnp.concatenate([silu(total), jnp.zeros((BLOCK - slots, total.shape[1]), F32)], axis=0)

    value_act = convolved(conv_x, cw_x, sums.projected(cols.x, cols.bc), conv_x_next)
    bc_act = convolved(conv_bc, cw_bc, sums.projected(cols.bc, cols.q), conv_bc_next)
    bc_act = bc_act.astype(BF16).astype(F32)
    b_in, c_val = bc_act[:, :NS], bc_act[:, NS:]
    b_twice[...] = jnp.concatenate([b_in, b_in], axis=0)
    c_out = c_val.astype(BF16)

    shifted = sums.step_in + dt_bias[...].reshape(1, heads)
    step_size = jnp.maximum(shifted, 0.0) + jnp.log(1.0 + jnp.exp(-jnp.abs(shifted)))
    rate = jnp.exp(-jnp.exp(a_log[...].reshape(1, heads)) * step_size)
    decay[...] = rate
    driven = widen(step_size, inner) * value_act
    driven_out[...] = driven
    high = driven.astype(BF16).astype(F32)
    drive[...] = jnp.transpose(jnp.concatenate([high, driven - high], axis=0)).astype(BF16)

    readout[...] = jnp.zeros_like(readout)

    for s in range(slots):
        loads[s].wait()
        value = dot_t(c_out, held[s].reshape(inner, NS))
        readout[s : s + 1, :] = value[s : s + 1]

    gate = silu(sums.projected(cols.z, cols.x))
    b_dot_c = jnp.sum(b_in * c_val, axis=1, keepdims=True)
    skip = widen(jnp.broadcast_to(d_skip[...].reshape(1, heads), (BLOCK, heads)), inner)
    total = widen(rate, inner) * readout[...] + driven * b_dot_c + skip * value_act
    gated[...] = (total * gate).astype(BF16).astype(F32)


def stay_kernel(plan, drive, decay, b_twice, state, state_next, held, made, in_sems, out_sems, *, moves):
    stays = held.shape[0]
    at = Plan(state.shape[0], moves)
    loads = []
    for j in range(stays):
        loads.append(pltpu.make_async_copy(state.at[plan[at.stay + j]], held.at[j], in_sems.at[j]))
        loads[-1].start()
    stores = []
    for j in range(stays):
        slot = plan[at.stay + j]
        loads[j].wait()
        advance_state(slot, held.at[j], b_twice, drive, decay, made.at[j])
        stores.append(pltpu.make_async_copy(made.at[j], state_next.at[slot], out_sems.at[j]))
        stores[-1].start()
    for store in stores:
        store.wait()


def advance_state(slot, prior, b_twice, drive, decay, result):
    heads = result.shape[0]
    twice = b_twice[...]
    half = twice.shape[0] // 2
    row = row_iota(twice.shape)
    selected = jnp.where((row == slot) | (row == slot + half), twice, 0.0).astype(BF16)
    outer = dot(drive[...], selected).reshape(heads, HP, NS)
    for h in range(heads):
        rate = decay[pl.ds(slot, 1), h : h + 1]
        result[h] = (rate * prior[h].astype(F32) + outer[h]).astype(BF16)


def output_kernel(gated, w_ssm, w_attn, partials, send, *, slots, col_count):
    share = w_attn.shape[0]
    part = min(share, HD)
    blocks = [partials[c * BLOCK : (c + 1) * BLOCK, :] for c in range(col_count)]
    pieces = []
    for j in range(share // part):
        peaks = [b[:, share + 2 * j : share + 2 * j + 1] for b in blocks]
        joint = functools.reduce(jnp.maximum, peaks)
        factors = [jnp.exp(p - joint) for p in peaks]
        total = sum(f * b[:, share + 2 * j + 1 : share + 2 * j + 2] for f, b in zip(factors, blocks))
        value = sum(f * b[:, j * part : (j + 1) * part] for f, b in zip(factors, blocks))
        pieces.append(value / total)
    joined = pieces[0] if len(pieces) == 1 else jnp.concatenate(pieces, axis=1)
    right = jnp.where(row_iota(joined.shape) < slots, joined, 0.0).astype(BF16)
    left = gated[...].astype(BF16)
    columns = w_ssm.shape[1] // col_count
    for c in range(col_count):
        span = slice(c * columns, (c + 1) * columns)
        terms = dot(left, w_ssm[:, span]) + dot(right, w_attn[:, span])
        send[c * BLOCK : (c + 1) * BLOCK, :] = terms.astype(BF16)


def total_kernel(
    plan, kv_new, driven, decay, b_twice, conv_x, conv_bc, terms, send, mixed, block, *, moves, col_count
):
    at = Plan(conv_x.shape[1], moves)
    total = sum(terms[c * BLOCK : (c + 1) * BLOCK, :].astype(F32) for c in range(col_count))
    mixed[...] = total
    send[pl.ds(pl.multiple_of(plan[at.me] * BLOCK, BLOCK), BLOCK), : total.shape[1]] = total.astype(BF16)

    block[...] = jnp.zeros_like(block)
    for m in range(moves):
        row = pl.ds(plan[at.slot + m], 1)

        def put(index, value, start=0):
            block[index : index + 1, start : start + value.shape[1]] = value

        put(Note.mixed, mixed[row, :])
        put(Note.key_value, kv_new[row, :])
        for index, value, start, low_index, low_start in (
            (Note.drive, driven[row, :], 0, Note.drive_low, 0),
            (Note.mixing, decay[row, :], Note.decay, Note.mixing, Note.decay_low),
        ):
            high = value.astype(BF16).astype(F32)
            put(index, high, start)
            put(low_index, value - high, low_start)
        put(Note.mixing, b_twice[row, :])
        for k in range(KW - 1):
            put(Note.conv_x + k, conv_x[k, row, :])
            put(Note.conv_bc + k, conv_bc[k, row, :])
        start = pl.multiple_of(plan[at.target + m] * BLOCK, BLOCK)
        send[pl.ds(start, BLOCK), :] = block[...].astype(BF16)


def arrive_kernel(
    col_ref, plan, table, conv_x, conv_bc, state_in, pool_in, notes, *rest,
    moves, row_count, col_count,
):
    del state_in, pool_in
    parcel_count = row_count - 1 + len(early_parts(row_count))
    parcels, rest = rest[:parcel_count], rest[parcel_count:]
    pages_here, slots = table.shape
    inner = conv_x.shape[2]
    heads = inner // HP
    at = Plan(slots, moves)
    mixed, conv_x_next, conv_bc_next, state_next, pool_next = rest[:5]
    packed, made, drive, decay, b_twice, window_x, window_bc, window_mixed, in_sems, out_sems = rest[5:]
    col = col_ref[0]
    parcels = parcel_parts(parcels, row_count, pages_here)

    def loaded(m, parcel):
        pages, states = parcel
        return (
            pltpu.make_async_copy(pages, packed.at[m, :pages_here], in_sems.at[m, 0]),
            pltpu.make_async_copy(states, packed.at[m, pages_here:], in_sems.at[m, 1]),
        )

    for m in range(moves):
        for d, parcel in enumerate(parcels, 1):

            @pl.when(plan[at.from_away + m] == d)
            def _(m=m, parcel=parcel):
                for copy in loaded(m, parcel):
                    copy.start()


    for k in range(KW - 1):
        window_x[k] = conv_x[k]
        window_bc[k] = conv_bc[k]
    home = pl.multiple_of(plan[at.me] * BLOCK, BLOCK)
    window_mixed[...] = notes[pl.ds(home, BLOCK), : window_mixed.shape[1]].astype(F32)
    rows = []
    b_twice[...] = jnp.zeros_like(b_twice)
    half = b_twice.shape[0] // 2
    for m in range(moves):
        start = pl.multiple_of(plan[at.source + m] * BLOCK, BLOCK)
        note = notes[pl.ds(start, BLOCK), :].astype(F32)
        rows.append(note)
        row = pl.ds(plan[at.slot + m], 1)
        window_mixed[row, :] = note[Note.mixed : Note.mixed + 1, : window_mixed.shape[1]]
        for k in range(KW - 1):
            window_x[k, row, :] = note[Note.conv_x + k : Note.conv_x + k + 1, :inner]
            window_bc[k, row, :] = note[Note.conv_bc + k : Note.conv_bc + k + 1, : 2 * NS]
        mixing = note[Note.mixing : Note.mixing + 1, :]
        b_twice[m : m + 1, :] = mixing[:, :NS]
        b_twice[half + m : half + m + 1, :] = mixing[:, :NS]
        decay[m : m + 1, :] = (
            mixing[:, Note.decay : Note.decay + heads] + mixing[:, Note.decay_low : Note.decay_low + heads]
        )
    padding = [jnp.zeros((half - moves, inner), F32)]
    stacked = [note[Note.drive : Note.drive + 1, :inner] for note in rows] + padding
    stacked += [note[Note.drive_low : Note.drive_low + 1, :inner] for note in rows] + padding
    drive[...] = jnp.transpose(jnp.concatenate(stacked, axis=0)).astype(BF16)
    mixed[...] = window_mixed[0:slots, :].astype(BF16)
    for k in range(KW - 1):
        conv_x_next[k] = window_x[k].astype(BF16)
        conv_bc_next[k] = window_bc[k].astype(BF16)

    stores = []
    for m in range(moves):
        slot = plan[at.slot + m]
        for copy in loaded(m, parcels[0]):
            copy.wait()
        owner, local_page, offset = place_of(plan[at.arrived_length + m], col_count)
        key_value = rows[m][Note.key_value : Note.key_value + 1, : 2 * KVH * HD]

        @pl.when(owner == col)
        def _(m=m, local_page=local_page, offset=offset, key_value=key_value):
            packed[m, local_page] = inserted(packed[m, local_page], key_value, offset)

        for page in range(pages_here):
            stores.append(
                pltpu.make_async_copy(
                    packed.at[m, page], pool_next.at[table[page, slot]], out_sems.at[m, page]
                )
            )
            stores[-1].start()
        prior = [
            jnp.concatenate([packed[m, pages_here + h, :, :NS], packed[m, pages_here + h, :, NS:]], axis=0)
            for h in range(heads)
        ]
        advance_state(m, prior, b_twice, drive, decay, made.at[m])
        stores.append(pltpu.make_async_copy(made.at[m], state_next.at[slot], out_sems.at[m, pages_here]))
        stores[-1].start()
    for store in stores:
        store.wait()


def shape(dims, dtype):
    return jax.ShapeDtypeStruct(tuple(dims), dtype)


def params(limit=VMEM_LIMIT):
    return pltpu.CompilerParams(vmem_limit_bytes=limit)


def exchange(value, axis):
    return lax.all_to_all(value, axis, split_axis=0, concat_axis=0, tiled=True)


def trade(block, axis, d):
    return lax.ppermute(block, axis, [(i, i ^ d) for i in range(lax.axis_size(axis))])


def ordered(value, first):
    return lax.optimization_barrier((value, first))[0]


def local(
    tokens, arrival, cache_lengths, move_slot, move_target, page_table, kv_pool, ssm_state,
    conv_x, conv_bc, norm_gain, weight_z, weight_x, weight_dt, weight_bc, weight_qkv,
    conv_weight_x, conv_weight_bc, dt_bias, a_log, d_skip, weight_ssm_out, weight_attn_out,
):
    row_count = lax.axis_size("rows")
    col_count = lax.axis_size("cols")
    row_index = lax.axis_index("rows").astype(I32).reshape(1)
    col_index = lax.axis_index("cols").astype(I32).reshape(1)
    slots, heads = ssm_state.shape[0], ssm_state.shape[1]
    total, depth = tokens.shape
    moves = move_slot.shape[1]
    pages_here, width = page_table.shape[3], kv_pool.shape[3]
    inner = heads * HP
    stays = slots - moves
    cols, at = Columns(inner), Plan(slots, moves)
    table = page_table[0, 0].T
    pool = kv_pool[:, 0]
    past_x, past_bc = conv_x.transpose(1, 0, 2), conv_bc.transpose(1, 0, 2)
    rows = row_count * BLOCK
    model = depth * row_count
    share = QH * HD // col_count
    parcel = (pages_here + heads, PAGE, width)
    parcels_here = pltpu.VMEM((moves,) + parcel, BF16)

    chip_count = row_count // 2
    early = early_parts(row_count)
    plan, mine, theirs, *ahead = pl.pallas_call(
        project_kernel,
        out_shape=[
            shape((at.size,), I32),
            shape((chip_count * BLOCK, cols.width), F32),
            shape((chip_count * BLOCK, cols.width), BF16),
        ]
        + [shape((pages_here,) + parcel[1:], BF16)] * len(early),
        in_specs=[SMEM_SPEC] * 6 + [VMEM_SPEC] * 7 + [ANY_SPEC],
        out_specs=[SMEM_SPEC] + [VMEM_SPEC] * 2 + [ANY_SPEC] * len(early),
        scratch_shapes=[
            pltpu.SMEM((total,), I32),
            pltpu.VMEM((total, depth), F32),
            pltpu.VMEM((rows, depth), F32),
            pltpu.VMEM((rows, LANES), F32),
            pltpu.VMEM((len(early), pages_here, PAGE, width), BF16),
            pltpu.SemaphoreType.DMA((len(early),)),
            pltpu.SemaphoreType.DMA((len(early),)),
        ],
        compiler_params=params(FIRST_LIMIT),
        cost_estimate=BRIEF,
        name="project",
    )(
        row_index, arrival, cache_lengths, move_slot.T, move_target.T, table,
        tokens, norm_gain, weight_z, weight_x, weight_dt.T, weight_bc, weight_qkv, pool,
    )
    ahead = [trade(pages, "rows", d) for d, pages in zip(early, ahead)]
    parcels = pl.pallas_call(
        functools.partial(pack_kernel, moves=moves, row_count=row_count),
        out_shape=[
            shape((heads,) + parcel[1:] if d in early else parcel, BF16) for d in range(1, row_count)
        ],
        in_specs=[SMEM_SPEC] * 2 + [ANY_SPEC] * 2,
        out_specs=[ANY_SPEC] * (row_count - 1),
        scratch_shapes=[
            parcels_here,
            pltpu.SemaphoreType.DMA((moves,)),
            pltpu.SemaphoreType.DMA((moves,)),
        ],
        compiler_params=params(FIRST_LIMIT),
        cost_estimate=BRIEF,
        name="pack",
    )(plan, table, pool, ssm_state)

    sums = pl.pallas_call(
        pair_kernel,
        out_shape=[shape((BLOCK, cols.width), F32)] + [shape((BLOCK, cols.width), BF16)] * (chip_count - 1),
        in_specs=[VMEM_SPEC] * 2,
        out_specs=[VMEM_SPEC] * chip_count,
        compiler_params=params(PAIR_LIMIT),
        cost_estimate=BRIEF,
        name="pair",
    )(mine, trade(theirs, "rows", 1))
    received = [sums[0]] + [trade(block, "rows", 2 * j) for j, block in enumerate(sums[1:], 1)]

    moving = [None, *parcels]

    def migrate(parts, after):
        for d in parts:
            moving[d] = trade(ordered(moving[d], after), "rows", d)
        return [moving[d] for d in parts]

    evens, odds = list(range(2, row_count, 2)), list(range(3, row_count, 2))
    first = [odds[0], odds[len(odds) // 2]]
    second = [d for d in evens if d not in early] + [1]
    last = [d for d in odds + evens if d not in first + second]
    received = ordered(received, ahead)
    first_moved = migrate(first, received)
    second_moved = migrate(second, received)

    pool_next, kv_new, partials = pl.pallas_call(
        functools.partial(
            attend_kernel, moves=moves, heads=heads, chip_count=chip_count, col_count=col_count, width=model
        ),
        out_shape=[
            shape(pool.shape, BF16),
            shape((BLOCK, 2 * KVH * HD), F32),
            shape((col_count * BLOCK, share + LANES), F32),
        ],
        in_specs=[SMEM_SPEC] * 3 + [ANY_SPEC] + [VMEM_SPEC] * chip_count,
        out_specs=[ANY_SPEC] + [VMEM_SPEC] * 2,
        scratch_shapes=[
            pltpu.VMEM(pool.shape, BF16),
            pltpu.VMEM((BLOCK * QH, HD), F32),
            pltpu.VMEM((BLOCK * QH, pages_here * PAGE), F32),
            pltpu.VMEM((BLOCK * QH, HD), F32),
            pltpu.VMEM((BLOCK * QH, HD), F32),
            pltpu.VMEM((BLOCK * QH, HD), F32),
            pltpu.SemaphoreType.DMA((2 if pool.shape[0] % 4 else 4,)),
            pltpu.SemaphoreType.DMA((2 if pool.shape[0] % 4 else 4,)),
        ],
        compiler_params=params(),
        cost_estimate=BRIEF,
        name="attend",
    )(col_index, plan, table, pool, *received)
    received = ordered(received, partials)
    partials = exchange(partials, "cols")

    next_x, next_bc, gated, driven, decay, drive, b_twice = pl.pallas_call(
        functools.partial(mix_kernel, chip_count=chip_count, width=model),
        out_shape=(
            shape(past_x.shape, F32),
            shape(past_bc.shape, F32),
            shape((BLOCK, inner), F32),
            shape((BLOCK, inner), F32),
            shape((BLOCK, heads), F32),
            shape((inner, 2 * BLOCK), BF16),
            shape((2 * BLOCK, NS), F32),
        ),
        in_specs=[VMEM_SPEC] * 7 + [ANY_SPEC] + [VMEM_SPEC] * chip_count,
        out_specs=(VMEM_SPEC,) * 7,
        scratch_shapes=[
            pltpu.VMEM((BLOCK, inner), F32),
            pltpu.VMEM((slots, heads, HP, NS), BF16),
            pltpu.SemaphoreType.DMA((slots,)),
        ],
        compiler_params=params(),
        cost_estimate=BRIEF,
        name="mix",
    )(past_x, past_bc, conv_weight_x, conv_weight_bc, dt_bias, a_log, d_skip, ssm_state, *received)

    columns = weight_ssm_out.shape[1] // col_count
    terms = pl.pallas_call(
        functools.partial(output_kernel, slots=slots, col_count=col_count),
        out_shape=shape((col_count * BLOCK, columns), BF16),
        in_specs=[VMEM_SPEC] * 4,
        out_specs=VMEM_SPEC,
        compiler_params=params(),
        cost_estimate=BRIEF,
        name="output",
    )(gated, weight_ssm_out, weight_attn_out, partials)
    migrate(last, (terms, first_moved))
    drive = ordered(drive, terms)
    terms = exchange(terms, "cols")
    state_next = pl.pallas_call(
        functools.partial(stay_kernel, moves=moves),
        out_shape=shape(ssm_state.shape, BF16),
        in_specs=[SMEM_SPEC] + [VMEM_SPEC] * 3 + [ANY_SPEC],
        out_specs=ANY_SPEC,
        scratch_shapes=[
            pltpu.VMEM((stays, heads, HP, NS), BF16),
            pltpu.VMEM((stays, heads, HP, NS), BF16),
            pltpu.SemaphoreType.DMA((stays,)),
            pltpu.SemaphoreType.DMA((stays,)),
        ],
        compiler_params=params(),
        cost_estimate=BRIEF,
        name="stay",
    )(plan, drive, decay, b_twice, ssm_state)

    terms = ordered(terms, second_moved)
    note = (BLOCK, max(inner, 2 * NS, 2 * KVH * HD, columns))
    notes = pl.pallas_call(
        functools.partial(total_kernel, moves=moves, col_count=col_count),
        out_shape=shape((rows, note[1]), BF16),
        in_specs=[SMEM_SPEC] + [VMEM_SPEC] * 7,
        out_specs=VMEM_SPEC,
        scratch_shapes=[pltpu.VMEM((BLOCK, columns), F32), pltpu.VMEM(note, F32)],
        compiler_params=params(),
        cost_estimate=BRIEF,
        name="total",
    )(plan, kv_new, driven, decay, b_twice, next_x, next_bc, terms)
    notes = exchange(notes, "rows")

    parts = []
    for d in range(1, row_count):
        parts += [ahead[early.index(d)], moving[d]] if d in early else [moving[d]]
    mixed, conv_x_next, conv_bc_next, state_next, pool_next = pl.pallas_call(
        functools.partial(arrive_kernel, moves=moves, row_count=row_count, col_count=col_count),
        out_shape=(
            shape((slots, columns), BF16),
            shape(past_x.shape, BF16),
            shape(past_bc.shape, BF16),
            shape(ssm_state.shape, BF16),
            shape(pool.shape, BF16),
        ),
        in_specs=[SMEM_SPEC] * 3 + [VMEM_SPEC] * 2 + [ANY_SPEC] * 2 + [VMEM_SPEC] + [ANY_SPEC] * (row_count - 1 + len(early)),
        out_specs=[VMEM_SPEC] * 3 + [ANY_SPEC] * 2,
        scratch_shapes=[
            parcels_here,
            pltpu.VMEM((moves, heads, HP, NS), BF16),
            pltpu.VMEM((inner, 2 * BLOCK), BF16),
            pltpu.VMEM((BLOCK, heads), F32),
            pltpu.VMEM((2 * BLOCK, NS), F32),
            pltpu.VMEM((KW - 1, slots, inner), F32),
            pltpu.VMEM((KW - 1, slots, 2 * NS), F32),
            pltpu.VMEM((BLOCK, columns), F32),
            pltpu.SemaphoreType.DMA((moves, 2)),
            pltpu.SemaphoreType.DMA((moves, pages_here + 1)),
        ],
        input_output_aliases={5: 3, 6: 4},
        compiler_params=params(LAST_LIMIT),
        cost_estimate=BRIEF,
        name="arrive",
    )(col_index, plan, table, next_x, next_bc, state_next, pool_next, notes, *parts)
    return (
        mixed, state_next, conv_x_next.transpose(1, 0, 2), conv_bc_next.transpose(1, 0, 2), pool_next[:, None]
    )


def solution(mesh):
    in_specs = (
        P(None, "rows"),
        P(),
        P(),
        P(),
        P(),
        P("rows", "cols", None, None),
        P("rows", "cols", None, None),
        P("rows", "cols", None, None),
        P("rows", None, "cols"),
        P("rows", None, None),
        P("rows"),
        P("rows", "cols"),
        P("rows", "cols"),
        P("rows", "cols"),
        P("rows", None),
        P("rows", None),
        P(None, "cols"),
        P(),
        P("cols"),
        P("cols"),
        P("cols"),
        P("cols", None),
        P("cols", None),
    )
    out_specs = (
        P("rows", "cols"),
        P("rows", "cols", None, None),
        P("rows", None, "cols"),
        P("rows", None, None),
        P("rows", "cols", None, None),
    )
    return jax.shard_map(local, mesh=mesh, in_specs=in_specs, out_specs=out_specs, check_vma=False)
```

```python
import functools

import jax
import jax.numpy as jnp
from jax import lax
from jax.experimental import pallas as pl
from jax.experimental.pallas import tpu as pltpu
from jax.sharding import PartitionSpec as P

HP = 64
NS = 256
KW = 4
QH = 8
KVH = 2
HD = 128
PAGE = 32
LANES = 128
BLOCK = 16

EPSILON = 1e-05
FLOOR_SCORE = -1e30
FIRST_LIMIT = 60 * 1024 * 1024
VMEM_LIMIT = 54 * 1024 * 1024
LAST_LIMIT = 24 * 1024 * 1024

F32 = jnp.float32
BF16 = jnp.bfloat16
I32 = jnp.int32

SMEM_SPEC = pl.BlockSpec(memory_space=pltpu.SMEM)
BRIEF = pl.CostEstimate(flops=1, bytes_accessed=1, transcendentals=0)
VMEM_SPEC = pl.BlockSpec(memory_space=pltpu.VMEM)
ANY_SPEC = pl.BlockSpec(memory_space=pl.ANY)


def silu(v):
    return v / (1.0 + jnp.exp(-v))


def dot(a, b):
    return jnp.dot(a, b, preferred_element_type=F32)


def dot_t(a, b):
    return lax.dot_general(a, b, (((1,), (1,)), ((), ())), preferred_element_type=F32)


def row_iota(shape):
    return lax.broadcasted_iota(I32, shape, 0)


def lane_iota(shape):
    return lax.broadcasted_iota(I32, shape, 1)


class Columns:
    def __init__(self, inner):
        self.z = 0
        self.x = inner
        self.bc = 2 * inner
        self.q = self.bc + 2 * NS
        self.kv = self.q + QH * HD
        self.tail = self.kv + 2 * KVH * HD
        self.width = self.tail + 2 * LANES


class Plan:
    def __init__(self, slots, moves):
        self.length = 0
        self.slot = slots
        self.target = self.slot + moves
        self.away = self.target + moves
        self.source = self.away + moves
        self.from_away = self.source + moves
        self.arrived_length = self.from_away + moves
        self.stay = self.arrived_length + moves
        self.me = self.stay + slots - moves
        self.size = self.me + 1


def early_parts(row_count):
    return [row_count - 2] if row_count > 2 else []


def parcel_parts(refs, row_count, pages_here):
    refs, early = list(refs), early_parts(row_count)
    parts = []
    for d in range(1, row_count):
        if d in early:
            parts.append((refs.pop(0), refs.pop(0)))
        else:
            whole = refs.pop(0)
            parts.append((whole.at[:pages_here], whole.at[pages_here:]))
    return parts


class Note:
    mixed, key_value, drive, drive_low, mixing, conv_x, conv_bc = 0, 1, 2, 3, 4, 5, 8
    decay, decay_low = NS, NS + LANES


def project_kernel(
    row_ref, arrival, lengths, move_slot, move_target, table,
    tokens, gain, w_z, w_x, w_dt, w_bc, w_qkv, pool,
    plan, mine, theirs, *rest,
):
    ahead = rest[:-7]
    inverse, wide, picked, tail, staged, in_sems, out_sems = rest[-7:]
    moves, row_count = move_slot.shape
    pages_here, slots = table.shape
    heads, depth = w_dt.shape
    inner = heads * HP
    cols, at = Columns(inner), Plan(slots, moves)
    me, half = row_ref[0], row_count // 2

    loads, stores = [], []
    for e, (d, pages) in enumerate(zip(early_parts(row_count), ahead)):
        slot = move_slot[0, me]
        for m in range(1, moves):
            slot = jnp.where(lax.bitwise_xor(move_target[m, me], me) == d, move_slot[m, me], slot)
        for page in range(pages_here):
            pltpu.make_async_copy(pool.at[table[page, slot]], staged.at[e, page], in_sems.at[e]).start()
        loads.append(pltpu.make_async_copy(pool.at[:pages_here], staged.at[e], in_sems.at[e]))
        stores.append(pltpu.make_async_copy(staged.at[e], pages, out_sems.at[e]))

    wide[...] = tokens[...].astype(F32)
    picked[...] = jnp.zeros_like(picked)

    def invert(t, carry):
        for s in range(slots):
            inverse[arrival[t * slots + s]] = t * slots + s
        return carry

    lax.fori_loop(0, row_count, invert, 0)

    def pick(b, carry):
        d = jnp.where(b < half, 2 * b, 2 * (b - half) + 1)
        first = lax.bitwise_xor(me, d) * slots
        for s in range(slots):
            picked[pl.ds(b * BLOCK + s, 1), :] = wide[pl.ds(inverse[first + s], 1), :]
        return carry

    lax.fori_loop(0, row_count, pick, 0)

    for load, store in zip(loads, stores):
        load.wait()
        store.start()

    rows = picked[...]
    squares = jnp.sum(rows * rows, axis=1, keepdims=True)
    scaled = (rows * gain[...].astype(F32).reshape(1, depth)).astype(BF16)

    def put(start, value):
        span = slice(start, start + value.shape[1])
        mine[:, span] = value[: half * BLOCK].astype(F32)
        theirs[:, span] = value[half * BLOCK :].astype(BF16)

    put(cols.z, dot(scaled, w_z[...]))
    put(cols.x, dot(scaled, w_x[...]))
    put(cols.bc, dot(scaled, w_bc[...]))
    put(cols.q, dot(scaled, w_qkv[...]))
    tail[...] = jnp.zeros_like(tail)
    tail[:, :heads] = dot_t(scaled, w_dt[...])
    tail[:, heads : heads + 1] = squares
    high = tail[...].astype(BF16)
    put(cols.tail, high)
    put(cols.tail + LANES, tail[...] - high.astype(F32))

    stays = 0
    for s in range(slots):
        plan[at.length + s] = lengths[me * slots + s]
        leaves = move_slot[0, me] == s
        for m in range(1, moves):
            leaves = jnp.logical_or(leaves, move_slot[m, me] == s)

        @pl.when(jnp.logical_not(leaves))
        def _(s=s, stays=stays):
            plan[at.stay + stays] = s

        stays = stays + jnp.where(leaves, 0, 1)
    for m in range(moves):
        plan[at.slot + m] = move_slot[m, me]
        plan[at.target + m] = move_target[m, me]
        plan[at.away + m] = lax.bitwise_xor(move_target[m, me], me)

    def seek(i, turn):
        for m in range(moves):
            comes = move_target[m, i] == me

            @pl.when(comes)
            def _(m=m, turn=turn):
                plan[at.source + turn] = i
                plan[at.from_away + turn] = lax.bitwise_xor(i, me)
                plan[at.arrived_length + turn] = lengths[i * slots + move_slot[m, i]]

            turn = turn + jnp.where(comes, 1, 0)
        return turn

    lax.fori_loop(0, row_count, seek, I32(0))
    plan[at.me] = me
    for store in stores:
        store.wait()


def pack_kernel(plan, table, pool, state, *rest, moves, row_count):
    pages_here, slots = table.shape
    at, early = Plan(slots, moves), early_parts(row_count)
    parcels = rest[: row_count - 1]
    packed, in_sems, out_sems = rest[row_count - 1 :]
    for m in range(moves):
        slot = plan[at.slot + m]
        for page in range(pages_here):
            pltpu.make_async_copy(pool.at[table[page, slot]], packed.at[m, page], in_sems.at[m]).start()
        for part in range(2):
            pltpu.make_async_copy(
                state.at[slot, :, part * PAGE : (part + 1) * PAGE, :],
                packed.at[m, pages_here:, :, part * NS : (part + 1) * NS],
                in_sems.at[m],
            ).start()

    def sent(m, d):
        source = packed.at[m, pages_here:] if d in early else packed.at[m]
        return pltpu.make_async_copy(source, parcels[d - 1], out_sems.at[m])

    def each(m, act):
        for d in range(1, row_count):

            @pl.when(plan[at.away + m] == d)
            def _(d=d):
                act(sent(m, d))

    for m in range(moves):
        pltpu.make_async_copy(pool.at[: packed.shape[1]], packed.at[m], in_sems.at[m]).wait()
        each(m, lambda copy: copy.start())
    for m in range(moves):
        each(m, lambda copy: copy.wait())


def pair_kernel(mine, theirs, own, *others):
    for j, out in enumerate((own,) + others):
        span = slice(j * BLOCK, (j + 1) * BLOCK)
        out[...] = (mine[span, :] + theirs[span, :].astype(F32)).astype(out.dtype)


def widen(per_head, inner):
    rows = per_head.shape[0]
    first = lane_iota((rows, 2 * HP)) < HP
    pieces = []
    for h in range(0, inner // HP, 2):
        pieces.append(jnp.where(first, per_head[:, h : h + 1], per_head[:, h + 1 : h + 2]))
    return pieces[0] if len(pieces) == 1 else jnp.concatenate(pieces, axis=1)


class Sums:
    def __init__(self, received, heads, width):
        self.received = received
        cols = Columns(heads * HP)
        tail = self.total(cols.tail, cols.tail + LANES) + self.total(cols.tail + LANES, cols.width)
        self.root = jnp.sqrt(tail[:, heads : heads + 1] / width + EPSILON)
        self.step_in = (tail[:, :heads] / self.root).astype(BF16).astype(F32)

    def total(self, start, stop):
        return sum(part[:, start:stop].astype(F32) for part in self.received)

    def projected(self, start, stop):
        return (self.total(start, stop) / self.root).astype(BF16).astype(F32)


def inserted(page, row, offset):
    return jnp.where(row_iota(page.shape) == offset, row, page.astype(F32)).astype(BF16)


def place_of(length, col_count):
    logical = lax.div(length, I32(PAGE))
    return lax.rem(logical, I32(col_count)), lax.div(logical, I32(col_count)), lax.rem(length, I32(PAGE))


def attend_kernel(
    col_ref, plan, table, pool, *rest, moves, heads, chip_count, col_count, width
):
    received, (pool_next, kv_new, send) = rest[:chip_count], rest[chip_count : chip_count + 3]
    pages, queries, scores, weighted, peaks, totals, in_sems, out_sems = rest[chip_count + 3 :]
    pages_here, slots = table.shape
    cols, at = Columns(heads * HP), Plan(slots, moves)
    col = col_ref[0]
    tokens_here = pages_here * PAGE
    kv_width = KVH * HD
    chunks = in_sems.shape[0]
    step = pool.shape[0] // chunks
    spans = [pl.ds(k * step, step) for k in range(chunks)]
    loads = [pltpu.make_async_copy(pool.at[span], pages.at[span], in_sems.at[k]) for k, span in enumerate(spans)]
    for load in loads:
        load.start()

    sums = Sums(received, heads, width)
    kv_new[...] = sums.projected(cols.kv, cols.tail)
    q_in = sums.projected(cols.q, cols.kv)
    for h in range(QH):
        queries[pl.ds(h, BLOCK, stride=QH), :] = q_in[:, h * HD : (h + 1) * HD]

    first_group = row_iota((QH, HD)) < QH // KVH
    lane = lane_iota((QH, tokens_here))
    position = (lax.shift_right_logical(lane, 5) * col_count + col) * PAGE + lax.bitwise_and(lane, PAGE - 1)
    for load in loads:
        load.wait()
    for s in range(slots):
        owner, local_page, offset = place_of(plan[at.length + s], col_count)
        page = table[local_page, s]
        pages[page] = inserted(pages[page], kv_new[s : s + 1, :], jnp.where(owner == col, offset, -1))
    stores = [
        pltpu.make_async_copy(pages.at[span], pool_next.at[span], out_sems.at[k]) for k, span in enumerate(spans)
    ]
    for store in stores:
        store.start()

    def cached(s, start):
        parts = [pages[table[page, s], :, start : start + kv_width] for page in range(pages_here)]
        return jnp.concatenate(parts, axis=0)

    for s in range(slots):
        query = queries[s * QH : (s + 1) * QH, :]
        query = jnp.concatenate(
            [jnp.where(first_group, query, 0.0), jnp.where(first_group, 0.0, query)], axis=1
        ).astype(BF16)
        score = dot_t(query, cached(s, 0)) * (HD ** -0.5)
        scores[s * QH : (s + 1) * QH, :] = jnp.where(position <= plan[at.length + s], score, FLOOR_SCORE)

    live_rows = slots * QH
    everything = scores[0:live_rows, :]
    peak = jnp.max(everything, axis=1, keepdims=True)
    weights = jnp.where(everything > 0.5 * FLOOR_SCORE, jnp.exp(everything - peak), 0.0)
    total = jnp.sum(weights, axis=1, keepdims=True)
    scores[0:live_rows, :] = weights
    for ref, value in ((weighted, None), (peaks, peak), (totals, total)):
        ref[live_rows:, :] = jnp.zeros((BLOCK * QH - live_rows, HD), F32)
        if value is not None:
            ref[0:live_rows, :] = jnp.broadcast_to(value, (live_rows, HD))
    for s in range(slots):
        weight = scores[s * QH : (s + 1) * QH, :]
        high = weight.astype(BF16).astype(F32)
        both = dot(jnp.concatenate([high, weight - high], axis=0).astype(BF16), cached(s, kv_width))
        joined = both[:QH] + both[QH:]
        weighted[s * QH : (s + 1) * QH, :] = jnp.where(first_group, joined[:, :HD], joined[:, HD:])

    share = QH * HD // col_count
    part = min(share, HD)
    lanes = lane_iota((BLOCK, LANES))
    for c in range(col_count):
        block = slice(c * BLOCK, (c + 1) * BLOCK)
        stats = jnp.zeros((BLOCK, LANES), F32)
        for j in range(share // part):
            head, begin = divmod(c * share + j * part, HD)
            rows = pl.ds(head, BLOCK, stride=QH)
            send[block, j * part : (j + 1) * part] = weighted[rows, :][:, begin : begin + part]
            stats = jnp.where(lanes == 2 * j, peaks[rows, :], stats)
            stats = jnp.where(lanes == 2 * j + 1, totals[rows, :], stats)
        send[block, share:] = stats
    for store in stores:
        store.wait()


def mix_kernel(
    conv_x, conv_bc, cw_x, cw_bc, dt_bias, a_log, d_skip, state, *rest, chip_count, width
):
    received = rest[:chip_count]
    conv_x_next, conv_bc_next, gated, driven_out, decay, drive, b_twice = rest[chip_count : chip_count + 7]
    readout, held, in_sems = rest[chip_count + 7 :]
    slots, inner = conv_x.shape[1], conv_x.shape[2]
    heads = dt_bias.shape[0]
    cols = Columns(inner)
    loads = []
    for s in range(slots):
        loads.append(pltpu.make_async_copy(state.at[s], held.at[s], in_sems.at[s]))
        loads[-1].start()

    sums = Sums(received, heads, width)

    def convolved(past, taps, fresh, following):
        past_rows = [past[k].astype(F32) for k in range(KW - 1)]
        total = fresh[:slots] * taps[KW - 1 : KW, :].astype(F32)
        for k in range(KW - 1):
            total = total + past_rows[k] * taps[k : k + 1, :].astype(F32)
            following[k] = past_rows[k + 1] if k < KW - 2 else fresh[:slots]
        return jnp.concatenate([silu(total), jnp.zeros((BLOCK - slots, total.shape[1]), F32)], axis=0)

    value_act = convolved(conv_x, cw_x, sums.projected(cols.x, cols.bc), conv_x_next)
    bc_act = convolved(conv_bc, cw_bc, sums.projected(cols.bc, cols.q), conv_bc_next)
    bc_act = bc_act.astype(BF16).astype(F32)
    b_in, c_val = bc_act[:, :NS], bc_act[:, NS:]
    b_twice[...] = jnp.concatenate([b_in, b_in], axis=0)
    c_out = c_val.astype(BF16)

    shifted = sums.step_in + dt_bias[...].reshape(1, heads)
    step_size = jnp.maximum(shifted, 0.0) + jnp.log(1.0 + jnp.exp(-jnp.abs(shifted)))
    rate = jnp.exp(-jnp.exp(a_log[...].reshape(1, heads)) * step_size)
    decay[...] = rate
    driven = widen(step_size, inner) * value_act
    driven_out[...] = driven
    high = driven.astype(BF16).astype(F32)
    drive[...] = jnp.transpose(jnp.concatenate([high, driven - high], axis=0)).astype(BF16)

    readout[...] = jnp.zeros_like(readout)

    for s in range(slots):
        loads[s].wait()
        value = dot_t(c_out, held[s].reshape(inner, NS))
        readout[s : s + 1, :] = value[s : s + 1]

    gate = silu(sums.projected(cols.z, cols.x))
    b_dot_c = jnp.sum(b_in * c_val, axis=1, keepdims=True)
    skip = widen(jnp.broadcast_to(d_skip[...].reshape(1, heads), (BLOCK, heads)), inner)
    total = widen(rate, inner) * readout[...] + driven * b_dot_c + skip * value_act
    gated[...] = (total * gate).astype(BF16).astype(F32)


def stay_kernel(plan, drive, decay, b_twice, state, state_next, held, made, in_sems, out_sems, *, moves):
    stays = held.shape[0]
    at = Plan(state.shape[0], moves)
    loads = []
    for j in range(stays):
        loads.append(pltpu.make_async_copy(state.at[plan[at.stay + j]], held.at[j], in_sems.at[j]))
        loads[-1].start()
    stores = []
    for j in range(stays):
        slot = plan[at.stay + j]
        loads[j].wait()
        advance_state(slot, held.at[j], b_twice, drive, decay, made.at[j])
        stores.append(pltpu.make_async_copy(made.at[j], state_next.at[slot], out_sems.at[j]))
        stores[-1].start()
    for store in stores:
        store.wait()


def advance_state(slot, prior, b_twice, drive, decay, result):
    heads = result.shape[0]
    twice = b_twice[...]
    half = twice.shape[0] // 2
    row = row_iota(twice.shape)
    selected = jnp.where((row == slot) | (row == slot + half), twice, 0.0).astype(BF16)
    outer = dot(drive[...], selected).reshape(heads, HP, NS)
    for h in range(heads):
        rate = decay[pl.ds(slot, 1), h : h + 1]
        result[h] = (rate * prior[h].astype(F32) + outer[h]).astype(BF16)


def output_kernel(gated, w_ssm, w_attn, partials, send, *, slots, col_count):
    share = w_attn.shape[0]
    part = min(share, HD)
    blocks = [partials[c * BLOCK : (c + 1) * BLOCK, :] for c in range(col_count)]
    pieces = []
    for j in range(share // part):
        peaks = [b[:, share + 2 * j : share + 2 * j + 1] for b in blocks]
        joint = functools.reduce(jnp.maximum, peaks)
        factors = [jnp.exp(p - joint) for p in peaks]
        total = sum(f * b[:, share + 2 * j + 1 : share + 2 * j + 2] for f, b in zip(factors, blocks))
        value = sum(f * b[:, j * part : (j + 1) * part] for f, b in zip(factors, blocks))
        pieces.append(value / total)
    joined = pieces[0] if len(pieces) == 1 else jnp.concatenate(pieces, axis=1)
    right = jnp.where(row_iota(joined.shape) < slots, joined, 0.0).astype(BF16)
    left = gated[...].astype(BF16)
    columns = w_ssm.shape[1] // col_count
    for c in range(col_count):
        span = slice(c * columns, (c + 1) * columns)
        terms = dot(left, w_ssm[:, span]) + dot(right, w_attn[:, span])
        send[c * BLOCK : (c + 1) * BLOCK, :] = terms.astype(BF16)


def total_kernel(
    plan, kv_new, driven, decay, b_twice, conv_x, conv_bc, terms, send, mixed, block, *, moves, col_count
):
    at = Plan(conv_x.shape[1], moves)
    total = sum(terms[c * BLOCK : (c + 1) * BLOCK, :].astype(F32) for c in range(col_count))
    mixed[...] = total
    send[pl.ds(pl.multiple_of(plan[at.me] * BLOCK, BLOCK), BLOCK), : total.shape[1]] = total.astype(BF16)

    block[...] = jnp.zeros_like(block)
    for m in range(moves):
        row = pl.ds(plan[at.slot + m], 1)

        def put(index, value, start=0):
            block[index : index + 1, start : start + value.shape[1]] = value

        put(Note.mixed, mixed[row, :])
        put(Note.key_value, kv_new[row, :])
        for index, value, start, low_index, low_start in (
            (Note.drive, driven[row, :], 0, Note.drive_low, 0),
            (Note.mixing, decay[row, :], Note.decay, Note.mixing, Note.decay_low),
        ):
            high = value.astype(BF16).astype(F32)
            put(index, high, start)
            put(low_index, value - high, low_start)
        put(Note.mixing, b_twice[row, :])
        for k in range(KW - 1):
            put(Note.conv_x + k, conv_x[k, row, :])
            put(Note.conv_bc + k, conv_bc[k, row, :])
        start = pl.multiple_of(plan[at.target + m] * BLOCK, BLOCK)
        send[pl.ds(start, BLOCK), :] = block[...].astype(BF16)


def arrive_kernel(
    col_ref, plan, table, conv_x, conv_bc, state_in, pool_in, notes, *rest,
    moves, row_count, col_count,
):
    del state_in, pool_in
    parcel_count = row_count - 1 + len(early_parts(row_count))
    parcels, rest = rest[:parcel_count], rest[parcel_count:]
    pages_here, slots = table.shape
    inner = conv_x.shape[2]
    heads = inner // HP
    at = Plan(slots, moves)
    mixed, conv_x_next, conv_bc_next, state_next, pool_next = rest[:5]
    packed, made, drive, decay, b_twice, window_x, window_bc, window_mixed, in_sems, out_sems = rest[5:]
    col = col_ref[0]
    parcels = parcel_parts(parcels, row_count, pages_here)

    def loaded(m, parcel):
        pages, states = parcel
        return (
            pltpu.make_async_copy(pages, packed.at[m, :pages_here], in_sems.at[m, 0]),
            pltpu.make_async_copy(states, packed.at[m, pages_here:], in_sems.at[m, 1]),
        )

    for m in range(moves):
        for d, parcel in enumerate(parcels, 1):

            @pl.when(plan[at.from_away + m] == d)
            def _(m=m, parcel=parcel):
                for copy in loaded(m, parcel):
                    copy.start()


    for k in range(KW - 1):
        window_x[k] = conv_x[k]
        window_bc[k] = conv_bc[k]
    home = pl.multiple_of(plan[at.me] * BLOCK, BLOCK)
    window_mixed[...] = notes[pl.ds(home, BLOCK), : window_mixed.shape[1]].astype(F32)
    rows = []
    b_twice[...] = jnp.zeros_like(b_twice)
    half = b_twice.shape[0] // 2
    for m in range(moves):
        start = pl.multiple_of(plan[at.source + m] * BLOCK, BLOCK)
        note = notes[pl.ds(start, BLOCK), :].astype(F32)
        rows.append(note)
        row = pl.ds(plan[at.slot + m], 1)
        window_mixed[row, :] = note[Note.mixed : Note.mixed + 1, : window_mixed.shape[1]]
        for k in range(KW - 1):
            window_x[k, row, :] = note[Note.conv_x + k : Note.conv_x + k + 1, :inner]
            window_bc[k, row, :] = note[Note.conv_bc + k : Note.conv_bc + k + 1, : 2 * NS]
        mixing = note[Note.mixing : Note.mixing + 1, :]
        b_twice[m : m + 1, :] = mixing[:, :NS]
        b_twice[half + m : half + m + 1, :] = mixing[:, :NS]
        decay[m : m + 1, :] = (
            mixing[:, Note.decay : Note.decay + heads] + mixing[:, Note.decay_low : Note.decay_low + heads]
        )
    padding = [jnp.zeros((half - moves, inner), F32)]
    stacked = [note[Note.drive : Note.drive + 1, :inner] for note in rows] + padding
    stacked += [note[Note.drive_low : Note.drive_low + 1, :inner] for note in rows] + padding
    drive[...] = jnp.transpose(jnp.concatenate(stacked, axis=0)).astype(BF16)
    mixed[...] = window_mixed[0:slots, :].astype(BF16)
    for k in range(KW - 1):
        conv_x_next[k] = window_x[k].astype(BF16)
        conv_bc_next[k] = window_bc[k].astype(BF16)

    stores = []
    for m in range(moves):
        slot = plan[at.slot + m]
        for copy in loaded(m, parcels[0]):
            copy.wait()
        owner, local_page, offset = place_of(plan[at.arrived_length + m], col_count)
        key_value = rows[m][Note.key_value : Note.key_value + 1, : 2 * KVH * HD]

        @pl.when(owner == col)
        def _(m=m, local_page=local_page, offset=offset, key_value=key_value):
            packed[m, local_page] = inserted(packed[m, local_page], key_value, offset)

        for page in range(pages_here):
            stores.append(
                pltpu.make_async_copy(
                    packed.at[m, page], pool_next.at[table[page, slot]], out_sems.at[m, page]
                )
            )
            stores[-1].start()
        prior = [
            jnp.concatenate([packed[m, pages_here + h, :, :NS], packed[m, pages_here + h, :, NS:]], axis=0)
            for h in range(heads)
        ]
        advance_state(m, prior, b_twice, drive, decay, made.at[m])
        stores.append(pltpu.make_async_copy(made.at[m], state_next.at[slot], out_sems.at[m, pages_here]))
        stores[-1].start()
    for store in stores:
        store.wait()


def shape(dims, dtype):
    return jax.ShapeDtypeStruct(tuple(dims), dtype)


def params(limit=VMEM_LIMIT):
    return pltpu.CompilerParams(vmem_limit_bytes=limit)


def exchange(value, axis):
    return lax.all_to_all(value, axis, split_axis=0, concat_axis=0, tiled=True)


def trade(block, axis, d):
    return lax.ppermute(block, axis, [(i, i ^ d) for i in range(lax.axis_size(axis))])


def ordered(value, first):
    return lax.optimization_barrier((value, first))[0]


def local(
    tokens, arrival, cache_lengths, move_slot, move_target, page_table, kv_pool, ssm_state,
    conv_x, conv_bc, norm_gain, weight_z, weight_x, weight_dt, weight_bc, weight_qkv,
    conv_weight_x, conv_weight_bc, dt_bias, a_log, d_skip, weight_ssm_out, weight_attn_out,
):
    row_count = lax.axis_size("rows")
    col_count = lax.axis_size("cols")
    row_index = lax.axis_index("rows").astype(I32).reshape(1)
    col_index = lax.axis_index("cols").astype(I32).reshape(1)
    slots, heads = ssm_state.shape[0], ssm_state.shape[1]
    total, depth = tokens.shape
    moves = move_slot.shape[1]
    pages_here, width = page_table.shape[3], kv_pool.shape[3]
    inner = heads * HP
    stays = slots - moves
    cols, at = Columns(inner), Plan(slots, moves)
    table = page_table[0, 0].T
    pool = kv_pool[:, 0]
    past_x, past_bc = conv_x.transpose(1, 0, 2), conv_bc.transpose(1, 0, 2)
    rows = row_count * BLOCK
    model = depth * row_count
    share = QH * HD // col_count
    parcel = (pages_here + heads, PAGE, width)
    parcels_here = pltpu.VMEM((moves,) + parcel, BF16)

    chip_count = row_count // 2
    early = early_parts(row_count)
    plan, mine, theirs, *ahead = pl.pallas_call(
        project_kernel,
        out_shape=[
            shape((at.size,), I32),
            shape((chip_count * BLOCK, cols.width), F32),
            shape((chip_count * BLOCK, cols.width), BF16),
        ]
        + [shape((pages_here,) + parcel[1:], BF16)] * len(early),
        in_specs=[SMEM_SPEC] * 6 + [VMEM_SPEC] * 7 + [ANY_SPEC],
        out_specs=[SMEM_SPEC] + [VMEM_SPEC] * 2 + [ANY_SPEC] * len(early),
        scratch_shapes=[
            pltpu.SMEM((total,), I32),
            pltpu.VMEM((total, depth), F32),
            pltpu.VMEM((rows, depth), F32),
            pltpu.VMEM((rows, LANES), F32),
            pltpu.VMEM((len(early), pages_here, PAGE, width), BF16),
            pltpu.SemaphoreType.DMA((len(early),)),
            pltpu.SemaphoreType.DMA((len(early),)),
        ],
        compiler_params=params(FIRST_LIMIT),
        cost_estimate=BRIEF,
        name="project",
    )(
        row_index, arrival, cache_lengths, move_slot.T, move_target.T, table,
        tokens, norm_gain, weight_z, weight_x, weight_dt.T, weight_bc, weight_qkv, pool,
    )
    ahead = [trade(pages, "rows", d) for d, pages in zip(early, ahead)]
    parcels = pl.pallas_call(
        functools.partial(pack_kernel, moves=moves, row_count=row_count),
        out_shape=[
            shape((heads,) + parcel[1:] if d in early else parcel, BF16) for d in range(1, row_count)
        ],
        in_specs=[SMEM_SPEC] * 2 + [ANY_SPEC] * 2,
        out_specs=[ANY_SPEC] * (row_count - 1),
        scratch_shapes=[
            parcels_here,
            pltpu.SemaphoreType.DMA((moves,)),
            pltpu.SemaphoreType.DMA((moves,)),
        ],
        compiler_params=params(FIRST_LIMIT),
        cost_estimate=BRIEF,
        name="pack",
    )(plan, table, pool, ssm_state)

    sums = pl.pallas_call(
        pair_kernel,
        out_shape=[shape((BLOCK, cols.width), F32)] + [shape((BLOCK, cols.width), BF16)] * (chip_count - 1),
        in_specs=[VMEM_SPEC] * 2,
        out_specs=[VMEM_SPEC] * chip_count,
        compiler_params=params(FIRST_LIMIT),
        cost_estimate=BRIEF,
        name="pair",
    )(mine, trade(theirs, "rows", 1))
    received = [sums[0]] + [trade(block, "rows", 2 * j) for j, block in enumerate(sums[1:], 1)]

    moving = [None, *parcels]

    def migrate(parts, after):
        for d in parts:
            moving[d] = trade(ordered(moving[d], after), "rows", d)
        return [moving[d] for d in parts]

    evens, odds = list(range(2, row_count, 2)), list(range(3, row_count, 2))
    first = [odds[0], odds[len(odds) // 2]]
    second = [d for d in evens if d not in early] + [1]
    last = [d for d in odds + evens if d not in first + second]
    received = ordered(received, ahead)
    first_moved = migrate(first, received)
    second_moved = migrate(second, received)

    pool_next, kv_new, partials = pl.pallas_call(
        functools.partial(
            attend_kernel, moves=moves, heads=heads, chip_count=chip_count, col_count=col_count, width=model
        ),
        out_shape=[
            shape(pool.shape, BF16),
            shape((BLOCK, 2 * KVH * HD), F32),
            shape((col_count * BLOCK, share + LANES), F32),
        ],
        in_specs=[SMEM_SPEC] * 3 + [ANY_SPEC] + [VMEM_SPEC] * chip_count,
        out_specs=[ANY_SPEC] + [VMEM_SPEC] * 2,
        scratch_shapes=[
            pltpu.VMEM(pool.shape, BF16),
            pltpu.VMEM((BLOCK * QH, HD), F32),
            pltpu.VMEM((BLOCK * QH, pages_here * PAGE), F32),
            pltpu.VMEM((BLOCK * QH, HD), F32),
            pltpu.VMEM((BLOCK * QH, HD), F32),
            pltpu.VMEM((BLOCK * QH, HD), F32),
            pltpu.SemaphoreType.DMA((2 if pool.shape[0] % 4 else 4,)),
            pltpu.SemaphoreType.DMA((2 if pool.shape[0] % 4 else 4,)),
        ],
        compiler_params=params(),
        cost_estimate=BRIEF,
        name="attend",
    )(col_index, plan, table, pool, *received)
    received = ordered(received, partials)
    partials = exchange(partials, "cols")

    next_x, next_bc, gated, driven, decay, drive, b_twice = pl.pallas_call(
        functools.partial(mix_kernel, chip_count=chip_count, width=model),
        out_shape=(
            shape(past_x.shape, F32),
            shape(past_bc.shape, F32),
            shape((BLOCK, inner), F32),
            shape((BLOCK, inner), F32),
            shape((BLOCK, heads), F32),
            shape((inner, 2 * BLOCK), BF16),
            shape((2 * BLOCK, NS), F32),
        ),
        in_specs=[VMEM_SPEC] * 7 + [ANY_SPEC] + [VMEM_SPEC] * chip_count,
        out_specs=(VMEM_SPEC,) * 7,
        scratch_shapes=[
            pltpu.VMEM((BLOCK, inner), F32),
            pltpu.VMEM((slots, heads, HP, NS), BF16),
            pltpu.SemaphoreType.DMA((slots,)),
        ],
        compiler_params=params(),
        cost_estimate=BRIEF,
        name="mix",
    )(past_x, past_bc, conv_weight_x, conv_weight_bc, dt_bias, a_log, d_skip, ssm_state, *received)

    columns = weight_ssm_out.shape[1] // col_count
    terms = pl.pallas_call(
        functools.partial(output_kernel, slots=slots, col_count=col_count),
        out_shape=shape((col_count * BLOCK, columns), BF16),
        in_specs=[VMEM_SPEC] * 4,
        out_specs=VMEM_SPEC,
        compiler_params=params(),
        cost_estimate=BRIEF,
        name="output",
    )(gated, weight_ssm_out, weight_attn_out, partials)
    migrate(last, (terms, first_moved))
    drive = ordered(drive, terms)
    terms = exchange(terms, "cols")
    state_next = pl.pallas_call(
        functools.partial(stay_kernel, moves=moves),
        out_shape=shape(ssm_state.shape, BF16),
        in_specs=[SMEM_SPEC] + [VMEM_SPEC] * 3 + [ANY_SPEC],
        out_specs=ANY_SPEC,
        scratch_shapes=[
            pltpu.VMEM((stays, heads, HP, NS), BF16),
            pltpu.VMEM((stays, heads, HP, NS), BF16),
            pltpu.SemaphoreType.DMA((stays,)),
            pltpu.SemaphoreType.DMA((stays,)),
        ],
        compiler_params=params(),
        cost_estimate=BRIEF,
        name="stay",
    )(plan, drive, decay, b_twice, ssm_state)

    terms = ordered(terms, second_moved)
    note = (BLOCK, max(inner, 2 * NS, 2 * KVH * HD, columns))
    notes = pl.pallas_call(
        functools.partial(total_kernel, moves=moves, col_count=col_count),
        out_shape=shape((rows, note[1]), BF16),
        in_specs=[SMEM_SPEC] + [VMEM_SPEC] * 7,
        out_specs=VMEM_SPEC,
        scratch_shapes=[pltpu.VMEM((BLOCK, columns), F32), pltpu.VMEM(note, F32)],
        compiler_params=params(),
        cost_estimate=BRIEF,
        name="total",
    )(plan, kv_new, driven, decay, b_twice, next_x, next_bc, terms)
    notes = exchange(notes, "rows")

    parts = []
    for d in range(1, row_count):
        parts += [ahead[early.index(d)], moving[d]] if d in early else [moving[d]]
    mixed, conv_x_next, conv_bc_next, state_next, pool_next = pl.pallas_call(
        functools.partial(arrive_kernel, moves=moves, row_count=row_count, col_count=col_count),
        out_shape=(
            shape((slots, columns), BF16),
            shape(past_x.shape, BF16),
            shape(past_bc.shape, BF16),
            shape(ssm_state.shape, BF16),
            shape(pool.shape, BF16),
        ),
        in_specs=[SMEM_SPEC] * 3 + [VMEM_SPEC] * 2 + [ANY_SPEC] * 2 + [VMEM_SPEC] + [ANY_SPEC] * (row_count - 1 + len(early)),
        out_specs=[VMEM_SPEC] * 3 + [ANY_SPEC] * 2,
        scratch_shapes=[
            parcels_here,
            pltpu.VMEM((moves, heads, HP, NS), BF16),
            pltpu.VMEM((inner, 2 * BLOCK), BF16),
            pltpu.VMEM((BLOCK, heads), F32),
            pltpu.VMEM((2 * BLOCK, NS), F32),
            pltpu.VMEM((KW - 1, slots, inner), F32),
            pltpu.VMEM((KW - 1, slots, 2 * NS), F32),
            pltpu.VMEM((BLOCK, columns), F32),
            pltpu.SemaphoreType.DMA((moves, 2)),
            pltpu.SemaphoreType.DMA((moves, pages_here + 1)),
        ],
        input_output_aliases={5: 3, 6: 4},
        compiler_params=params(LAST_LIMIT),
        cost_estimate=BRIEF,
        name="arrive",
    )(col_index, plan, table, next_x, next_bc, state_next, pool_next, notes, *parts)
    return (
        mixed, state_next, conv_x_next.transpose(1, 0, 2), conv_bc_next.transpose(1, 0, 2), pool_next[:, None]
    )


def solution(mesh):
    in_specs = (
        P(None, "rows"),
        P(),
        P(),
        P(),
        P(),
        P("rows", "cols", None, None),
        P("rows", "cols", None, None),
        P("rows", "cols", None, None),
        P("rows", None, "cols"),
        P("rows", None, None),
        P("rows"),
        P("rows", "cols"),
        P("rows", "cols"),
        P("rows", "cols"),
        P("rows", None),
        P("rows", None),
        P(None, "cols"),
        P(),
        P("cols"),
        P("cols"),
        P("cols"),
        P("cols", None),
        P("cols", None),
    )
    out_specs = (
        P("rows", "cols"),
        P("rows", "cols", None, None),
        P("rows", None, "cols"),
        P("rows", None, None),
        P("rows", "cols", None, None),
    )
    return jax.shard_map(local, mesh=mesh, in_specs=in_specs, out_specs=out_specs, check_vma=False)
```

```python
import functools

import jax
import jax.numpy as jnp
from jax import lax
from jax.experimental import pallas as pl
from jax.experimental.pallas import tpu as pltpu
from jax.sharding import PartitionSpec as P

HP = 64
NS = 256
KW = 4
QH = 8
KVH = 2
HD = 128
PAGE = 32
LANES = 128
BLOCK = 16

EPSILON = 1e-05
FLOOR_SCORE = -1e30
FIRST_LIMIT = 60 * 1024 * 1024
VMEM_LIMIT = 55 * 1024 * 1024
LAST_LIMIT = 24 * 1024 * 1024

F32 = jnp.float32
BF16 = jnp.bfloat16
I32 = jnp.int32

SMEM_SPEC = pl.BlockSpec(memory_space=pltpu.SMEM)
BRIEF = pl.CostEstimate(flops=1, bytes_accessed=1, transcendentals=0)
VMEM_SPEC = pl.BlockSpec(memory_space=pltpu.VMEM)
ANY_SPEC = pl.BlockSpec(memory_space=pl.ANY)


def silu(v):
    return v / (1.0 + jnp.exp(-v))


def dot(a, b):
    return jnp.dot(a, b, preferred_element_type=F32)


def dot_t(a, b):
    return lax.dot_general(a, b, (((1,), (1,)), ((), ())), preferred_element_type=F32)


def row_iota(shape):
    return lax.broadcasted_iota(I32, shape, 0)


def lane_iota(shape):
    return lax.broadcasted_iota(I32, shape, 1)


class Columns:
    def __init__(self, inner):
        self.z = 0
        self.x = inner
        self.bc = 2 * inner
        self.q = self.bc + 2 * NS
        self.kv = self.q + QH * HD
        self.tail = self.kv + 2 * KVH * HD
        self.width = self.tail + 2 * LANES


class Plan:
    def __init__(self, slots, moves):
        self.length = 0
        self.slot = slots
        self.target = self.slot + moves
        self.away = self.target + moves
        self.source = self.away + moves
        self.from_away = self.source + moves
        self.arrived_length = self.from_away + moves
        self.stay = self.arrived_length + moves
        self.me = self.stay + slots - moves
        self.size = self.me + 1


def early_parts(row_count):
    return [row_count - 2] if row_count > 2 else []


def parcel_parts(refs, row_count, pages_here):
    refs, early = list(refs), early_parts(row_count)
    parts = []
    for d in range(1, row_count):
        if d in early:
            parts.append((refs.pop(0), refs.pop(0)))
        else:
            whole = refs.pop(0)
            parts.append((whole.at[:pages_here], whole.at[pages_here:]))
    return parts


class Note:
    mixed, key_value, drive, drive_low, mixing, conv_x, conv_bc = 0, 1, 2, 3, 4, 5, 8
    decay, decay_low = NS, NS + LANES


def project_kernel(
    row_ref, arrival, lengths, move_slot, move_target, table,
    tokens, gain, w_z, w_x, w_dt, w_bc, w_qkv, pool,
    plan, mine, theirs, *rest,
):
    ahead = rest[:-7]
    inverse, wide, picked, tail, staged, in_sems, out_sems = rest[-7:]
    moves, row_count = move_slot.shape
    pages_here, slots = table.shape
    heads, depth = w_dt.shape
    inner = heads * HP
    cols, at = Columns(inner), Plan(slots, moves)
    me, half = row_ref[0], row_count // 2

    loads, stores = [], []
    for e, (d, pages) in enumerate(zip(early_parts(row_count), ahead)):
        slot = move_slot[0, me]
        for m in range(1, moves):
            slot = jnp.where(lax.bitwise_xor(move_target[m, me], me) == d, move_slot[m, me], slot)
        for page in range(pages_here):
            pltpu.make_async_copy(pool.at[table[page, slot]], staged.at[e, page], in_sems.at[e]).start()
        loads.append(pltpu.make_async_copy(pool.at[:pages_here], staged.at[e], in_sems.at[e]))
        stores.append(pltpu.make_async_copy(staged.at[e], pages, out_sems.at[e]))

    wide[...] = tokens[...].astype(F32)
    picked[...] = jnp.zeros_like(picked)

    def invert(t, carry):
        for s in range(slots):
            inverse[arrival[t * slots + s]] = t * slots + s
        return carry

    lax.fori_loop(0, row_count, invert, 0)

    def pick(b, carry):
        d = jnp.where(b < half, 2 * b, 2 * (b - half) + 1)
        first = lax.bitwise_xor(me, d) * slots
        for s in range(slots):
            picked[pl.ds(b * BLOCK + s, 1), :] = wide[pl.ds(inverse[first + s], 1), :]
        return carry

    lax.fori_loop(0, row_count, pick, 0)

    for load, store in zip(loads, stores):
        load.wait()
        store.start()

    rows = picked[...]
    squares = jnp.sum(rows * rows, axis=1, keepdims=True)
    scaled = (rows * gain[...].astype(F32).reshape(1, depth)).astype(BF16)

    def put(start, value):
        span = slice(start, start + value.shape[1])
        mine[:, span] = value[: half * BLOCK].astype(F32)
        theirs[:, span] = value[half * BLOCK :].astype(BF16)

    put(cols.z, dot(scaled, w_z[...]))
    put(cols.x, dot(scaled, w_x[...]))
    put(cols.bc, dot(scaled, w_bc[...]))
    put(cols.q, dot(scaled, w_qkv[...]))
    tail[...] = jnp.zeros_like(tail)
    tail[:, :heads] = dot_t(scaled, w_dt[...])
    tail[:, heads : heads + 1] = squares
    high = tail[...].astype(BF16)
    put(cols.tail, high)
    put(cols.tail + LANES, tail[...] - high.astype(F32))

    stays = 0
    for s in range(slots):
        plan[at.length + s] = lengths[me * slots + s]
        leaves = move_slot[0, me] == s
        for m in range(1, moves):
            leaves = jnp.logical_or(leaves, move_slot[m, me] == s)

        @pl.when(jnp.logical_not(leaves))
        def _(s=s, stays=stays):
            plan[at.stay + stays] = s

        stays = stays + jnp.where(leaves, 0, 1)
    for m in range(moves):
        plan[at.slot + m] = move_slot[m, me]
        plan[at.target + m] = move_target[m, me]
        plan[at.away + m] = lax.bitwise_xor(move_target[m, me], me)

    def seek(i, turn):
        for m in range(moves):
            comes = move_target[m, i] == me

            @pl.when(comes)
            def _(m=m, turn=turn):
                plan[at.source + turn] = i
                plan[at.from_away + turn] = lax.bitwise_xor(i, me)
                plan[at.arrived_length + turn] = lengths[i * slots + move_slot[m, i]]

            turn = turn + jnp.where(comes, 1, 0)
        return turn

    lax.fori_loop(0, row_count, seek, I32(0))
    plan[at.me] = me
    for store in stores:
        store.wait()


def pack_kernel(plan, table, pool, state, *rest, moves, row_count):
    pages_here, slots = table.shape
    at, early = Plan(slots, moves), early_parts(row_count)
    parcels = rest[: row_count - 1]
    packed, in_sems, out_sems = rest[row_count - 1 :]
    for m in range(moves):
        slot = plan[at.slot + m]
        for page in range(pages_here):
            pltpu.make_async_copy(pool.at[table[page, slot]], packed.at[m, page], in_sems.at[m]).start()
        for part in range(2):
            pltpu.make_async_copy(
                state.at[slot, :, part * PAGE : (part + 1) * PAGE, :],
                packed.at[m, pages_here:, :, part * NS : (part + 1) * NS],
                in_sems.at[m],
            ).start()

    def sent(m, d):
        source = packed.at[m, pages_here:] if d in early else packed.at[m]
        return pltpu.make_async_copy(source, parcels[d - 1], out_sems.at[m])

    def each(m, act):
        for d in range(1, row_count):

            @pl.when(plan[at.away + m] == d)
            def _(d=d):
                act(sent(m, d))

    for m in range(moves):
        pltpu.make_async_copy(pool.at[: packed.shape[1]], packed.at[m], in_sems.at[m]).wait()
        each(m, lambda copy: copy.start())
    for m in range(moves):
        each(m, lambda copy: copy.wait())


def pair_kernel(mine, theirs, own, *others):
    for j, out in enumerate((own,) + others):
        span = slice(j * BLOCK, (j + 1) * BLOCK)
        out[...] = (mine[span, :] + theirs[span, :].astype(F32)).astype(out.dtype)


def widen(per_head, inner):
    rows = per_head.shape[0]
    first = lane_iota((rows, 2 * HP)) < HP
    pieces = []
    for h in range(0, inner // HP, 2):
        pieces.append(jnp.where(first, per_head[:, h : h + 1], per_head[:, h + 1 : h + 2]))
    return pieces[0] if len(pieces) == 1 else jnp.concatenate(pieces, axis=1)


class Sums:
    def __init__(self, received, heads, width):
        self.received = received
        cols = Columns(heads * HP)
        tail = self.total(cols.tail, cols.tail + LANES) + self.total(cols.tail + LANES, cols.width)
        self.root = jnp.sqrt(tail[:, heads : heads + 1] / width + EPSILON)
        self.step_in = (tail[:, :heads] / self.root).astype(BF16).astype(F32)

    def total(self, start, stop):
        return sum(part[:, start:stop].astype(F32) for part in self.received)

    def projected(self, start, stop):
        return (self.total(start, stop) / self.root).astype(BF16).astype(F32)


def inserted(page, row, offset):
    return jnp.where(row_iota(page.shape) == offset, row, page.astype(F32)).astype(BF16)


def place_of(length, col_count):
    logical = lax.div(length, I32(PAGE))
    return lax.rem(logical, I32(col_count)), lax.div(logical, I32(col_count)), lax.rem(length, I32(PAGE))


def attend_kernel(
    col_ref, plan, table, pool, *rest, moves, heads, chip_count, col_count, width
):
    received, (pool_next, kv_new, send) = rest[:chip_count], rest[chip_count : chip_count + 3]
    pages, queries, scores, weighted, peaks, totals, in_sems, out_sems = rest[chip_count + 3 :]
    pages_here, slots = table.shape
    cols, at = Columns(heads * HP), Plan(slots, moves)
    col = col_ref[0]
    tokens_here = pages_here * PAGE
    kv_width = KVH * HD
    chunks = in_sems.shape[0]
    step = pool.shape[0] // chunks
    spans = [pl.ds(k * step, step) for k in range(chunks)]
    loads = [pltpu.make_async_copy(pool.at[span], pages.at[span], in_sems.at[k]) for k, span in enumerate(spans)]
    for load in loads:
        load.start()

    sums = Sums(received, heads, width)
    kv_new[...] = sums.projected(cols.kv, cols.tail)
    q_in = sums.projected(cols.q, cols.kv)
    for h in range(QH):
        queries[pl.ds(h, BLOCK, stride=QH), :] = q_in[:, h * HD : (h + 1) * HD]

    first_group = row_iota((QH, HD)) < QH // KVH
    lane = lane_iota((QH, tokens_here))
    position = (lax.shift_right_logical(lane, 5) * col_count + col) * PAGE + lax.bitwise_and(lane, PAGE - 1)
    for load in loads:
        load.wait()
    for s in range(slots):
        owner, local_page, offset = place_of(plan[at.length + s], col_count)
        page = table[local_page, s]
        pages[page] = inserted(pages[page], kv_new[s : s + 1, :], jnp.where(owner == col, offset, -1))
    stores = [
        pltpu.make_async_copy(pages.at[span], pool_next.at[span], out_sems.at[k]) for k, span in enumerate(spans)
    ]
    for store in stores:
        store.start()

    def cached(s, start):
        parts = [pages[table[page, s], :, start : start + kv_width] for page in range(pages_here)]
        return jnp.concatenate(parts, axis=0)

    for s in range(slots):
        query = queries[s * QH : (s + 1) * QH, :]
        query = jnp.concatenate(
            [jnp.where(first_group, query, 0.0), jnp.where(first_group, 0.0, query)], axis=1
        ).astype(BF16)
        score = dot_t(query, cached(s, 0)) * (HD ** -0.5)
        scores[s * QH : (s + 1) * QH, :] = jnp.where(position <= plan[at.length + s], score, FLOOR_SCORE)

    live_rows = slots * QH
    everything = scores[0:live_rows, :]
    peak = jnp.max(everything, axis=1, keepdims=True)
    weights = jnp.where(everything > 0.5 * FLOOR_SCORE, jnp.exp(everything - peak), 0.0)
    total = jnp.sum(weights, axis=1, keepdims=True)
    scores[0:live_rows, :] = weights
    for ref, value in ((weighted, None), (peaks, peak), (totals, total)):
        ref[live_rows:, :] = jnp.zeros((BLOCK * QH - live_rows, HD), F32)
        if value is not None:
            ref[0:live_rows, :] = jnp.broadcast_to(value, (live_rows, HD))
    for s in range(slots):
        weight = scores[s * QH : (s + 1) * QH, :]
        high = weight.astype(BF16).astype(F32)
        both = dot(jnp.concatenate([high, weight - high], axis=0).astype(BF16), cached(s, kv_width))
        joined = both[:QH] + both[QH:]
        weighted[s * QH : (s + 1) * QH, :] = jnp.where(first_group, joined[:, :HD], joined[:, HD:])

    share = QH * HD // col_count
    part = min(share, HD)
    lanes = lane_iota((BLOCK, LANES))
    for c in range(col_count):
        block = slice(c * BLOCK, (c + 1) * BLOCK)
        stats = jnp.zeros((BLOCK, LANES), F32)
        for j in range(share // part):
            head, begin = divmod(c * share + j * part, HD)
            rows = pl.ds(head, BLOCK, stride=QH)
            send[block, j * part : (j + 1) * part] = weighted[rows, :][:, begin : begin + part]
            stats = jnp.where(lanes == 2 * j, peaks[rows, :], stats)
            stats = jnp.where(lanes == 2 * j + 1, totals[rows, :], stats)
        send[block, share:] = stats
    for store in stores:
        store.wait()


def mix_kernel(
    conv_x, conv_bc, cw_x, cw_bc, dt_bias, a_log, d_skip, state, *rest, chip_count, width
):
    received = rest[:chip_count]
    conv_x_next, conv_bc_next, gated, driven_out, decay, drive, b_twice = rest[chip_count : chip_count + 7]
    readout, held, in_sems = rest[chip_count + 7 :]
    slots, inner = conv_x.shape[1], conv_x.shape[2]
    heads = dt_bias.shape[0]
    cols = Columns(inner)
    loads = []
    for s in range(slots):
        loads.append(pltpu.make_async_copy(state.at[s], held.at[s], in_sems.at[s]))
        loads[-1].start()

    sums = Sums(received, heads, width)

    def convolved(past, taps, fresh, following):
        past_rows = [past[k].astype(F32) for k in range(KW - 1)]
        total = fresh[:slots] * taps[KW - 1 : KW, :].astype(F32)
        for k in range(KW - 1):
            total = total + past_rows[k] * taps[k : k + 1, :].astype(F32)
            following[k] = past_rows[k + 1] if k < KW - 2 else fresh[:slots]
        return jnp.concatenate([silu(total), jnp.zeros((BLOCK - slots, total.shape[1]), F32)], axis=0)

    value_act = convolved(conv_x, cw_x, sums.projected(cols.x, cols.bc), conv_x_next)
    bc_act = convolved(conv_bc, cw_bc, sums.projected(cols.bc, cols.q), conv_bc_next)
    bc_act = bc_act.astype(BF16).astype(F32)
    b_in, c_val = bc_act[:, :NS], bc_act[:, NS:]
    b_twice[...] = jnp.concatenate([b_in, b_in], axis=0)
    c_out = c_val.astype(BF16)

    shifted = sums.step_in + dt_bias[...].reshape(1, heads)
    step_size = jnp.maximum(shifted, 0.0) + jnp.log(1.0 + jnp.exp(-jnp.abs(shifted)))
    rate = jnp.exp(-jnp.exp(a_log[...].reshape(1, heads)) * step_size)
    decay[...] = rate
    driven = widen(step_size, inner) * value_act
    driven_out[...] = driven
    high = driven.astype(BF16).astype(F32)
    drive[...] = jnp.transpose(jnp.concatenate([high, driven - high], axis=0)).astype(BF16)

    readout[...] = jnp.zeros_like(readout)

    for s in range(slots):
        loads[s].wait()
        value = dot_t(c_out, held[s].reshape(inner, NS))
        readout[s : s + 1, :] = value[s : s + 1]

    gate = silu(sums.projected(cols.z, cols.x))
    b_dot_c = jnp.sum(b_in * c_val, axis=1, keepdims=True)
    skip = widen(jnp.broadcast_to(d_skip[...].reshape(1, heads), (BLOCK, heads)), inner)
    total = widen(rate, inner) * readout[...] + driven * b_dot_c + skip * value_act
    gated[...] = (total * gate).astype(BF16).astype(F32)


def stay_kernel(plan, drive, decay, b_twice, state, state_next, held, made, in_sems, out_sems, *, moves):
    stays = held.shape[0]
    at = Plan(state.shape[0], moves)
    loads = []
    for j in range(stays):
        loads.append(pltpu.make_async_copy(state.at[plan[at.stay + j]], held.at[j], in_sems.at[j]))
        loads[-1].start()
    stores = []
    for j in range(stays):
        slot = plan[at.stay + j]
        loads[j].wait()
        advance_state(slot, held.at[j], b_twice, drive, decay, made.at[j])
        stores.append(pltpu.make_async_copy(made.at[j], state_next.at[slot], out_sems.at[j]))
        stores[-1].start()
    for store in stores:
        store.wait()


def advance_state(slot, prior, b_twice, drive, decay, result):
    heads = result.shape[0]
    twice = b_twice[...]
    half = twice.shape[0] // 2
    row = row_iota(twice.shape)
    selected = jnp.where((row == slot) | (row == slot + half), twice, 0.0).astype(BF16)
    outer = dot(drive[...], selected).reshape(heads, HP, NS)
    for h in range(heads):
        rate = decay[pl.ds(slot, 1), h : h + 1]
        result[h] = (rate * prior[h].astype(F32) + outer[h]).astype(BF16)


def output_kernel(gated, w_ssm, w_attn, partials, send, *, slots, col_count):
    share = w_attn.shape[0]
    part = min(share, HD)
    blocks = [partials[c * BLOCK : (c + 1) * BLOCK, :] for c in range(col_count)]
    pieces = []
    for j in range(share // part):
        peaks = [b[:, share + 2 * j : share + 2 * j + 1] for b in blocks]
        joint = functools.reduce(jnp.maximum, peaks)
        factors = [jnp.exp(p - joint) for p in peaks]
        total = sum(f * b[:, share + 2 * j + 1 : share + 2 * j + 2] for f, b in zip(factors, blocks))
        value = sum(f * b[:, j * part : (j + 1) * part] for f, b in zip(factors, blocks))
        pieces.append(value / total)
    joined = pieces[0] if len(pieces) == 1 else jnp.concatenate(pieces, axis=1)
    right = jnp.where(row_iota(joined.shape) < slots, joined, 0.0).astype(BF16)
    left = gated[...].astype(BF16)
    columns = w_ssm.shape[1] // col_count
    for c in range(col_count):
        span = slice(c * columns, (c + 1) * columns)
        terms = dot(left, w_ssm[:, span]) + dot(right, w_attn[:, span])
        send[c * BLOCK : (c + 1) * BLOCK, :] = terms.astype(BF16)


def total_kernel(
    plan, kv_new, driven, decay, b_twice, conv_x, conv_bc, terms, send, mixed, block, *, moves, col_count
):
    at = Plan(conv_x.shape[1], moves)
    total = sum(terms[c * BLOCK : (c + 1) * BLOCK, :].astype(F32) for c in range(col_count))
    mixed[...] = total
    send[pl.ds(pl.multiple_of(plan[at.me] * BLOCK, BLOCK), BLOCK), : total.shape[1]] = total.astype(BF16)

    block[...] = jnp.zeros_like(block)
    for m in range(moves):
        row = pl.ds(plan[at.slot + m], 1)

        def put(index, value, start=0):
            block[index : index + 1, start : start + value.shape[1]] = value

        put(Note.mixed, mixed[row, :])
        put(Note.key_value, kv_new[row, :])
        for index, value, start, low_index, low_start in (
            (Note.drive, driven[row, :], 0, Note.drive_low, 0),
            (Note.mixing, decay[row, :], Note.decay, Note.mixing, Note.decay_low),
        ):
            high = value.astype(BF16).astype(F32)
            put(index, high, start)
            put(low_index, value - high, low_start)
        put(Note.mixing, b_twice[row, :])
        for k in range(KW - 1):
            put(Note.conv_x + k, conv_x[k, row, :])
            put(Note.conv_bc + k, conv_bc[k, row, :])
        start = pl.multiple_of(plan[at.target + m] * BLOCK, BLOCK)
        send[pl.ds(start, BLOCK), :] = block[...].astype(BF16)


def arrive_kernel(
    col_ref, plan, table, conv_x, conv_bc, state_in, pool_in, notes, *rest,
    moves, row_count, col_count,
):
    del state_in, pool_in
    parcel_count = row_count - 1 + len(early_parts(row_count))
    parcels, rest = rest[:parcel_count], rest[parcel_count:]
    pages_here, slots = table.shape
    inner = conv_x.shape[2]
    heads = inner // HP
    at = Plan(slots, moves)
    mixed, conv_x_next, conv_bc_next, state_next, pool_next = rest[:5]
    packed, made, drive, decay, b_twice, window_x, window_bc, window_mixed, in_sems, out_sems = rest[5:]
    col = col_ref[0]
    parcels = parcel_parts(parcels, row_count, pages_here)

    def loaded(m, parcel):
        pages, states = parcel
        return (
            pltpu.make_async_copy(pages, packed.at[m, :pages_here], in_sems.at[m, 0]),
            pltpu.make_async_copy(states, packed.at[m, pages_here:], in_sems.at[m, 1]),
        )

    for m in range(moves):
        for d, parcel in enumerate(parcels, 1):

            @pl.when(plan[at.from_away + m] == d)
            def _(m=m, parcel=parcel):
                for copy in loaded(m, parcel):
                    copy.start()


    for k in range(KW - 1):
        window_x[k] = conv_x[k]
        window_bc[k] = conv_bc[k]
    home = pl.multiple_of(plan[at.me] * BLOCK, BLOCK)
    window_mixed[...] = notes[pl.ds(home, BLOCK), : window_mixed.shape[1]].astype(F32)
    rows = []
    b_twice[...] = jnp.zeros_like(b_twice)
    half = b_twice.shape[0] // 2
    for m in range(moves):
        start = pl.multiple_of(plan[at.source + m] * BLOCK, BLOCK)
        note = notes[pl.ds(start, BLOCK), :].astype(F32)
        rows.append(note)
        row = pl.ds(plan[at.slot + m], 1)
        window_mixed[row, :] = note[Note.mixed : Note.mixed + 1, : window_mixed.shape[1]]
        for k in range(KW - 1):
            window_x[k, row, :] = note[Note.conv_x + k : Note.conv_x + k + 1, :inner]
            window_bc[k, row, :] = note[Note.conv_bc + k : Note.conv_bc + k + 1, : 2 * NS]
        mixing = note[Note.mixing : Note.mixing + 1, :]
        b_twice[m : m + 1, :] = mixing[:, :NS]
        b_twice[half + m : half + m + 1, :] = mixing[:, :NS]
        decay[m : m + 1, :] = (
            mixing[:, Note.decay : Note.decay + heads] + mixing[:, Note.decay_low : Note.decay_low + heads]
        )
    padding = [jnp.zeros((half - moves, inner), F32)]
    stacked = [note[Note.drive : Note.drive + 1, :inner] for note in rows] + padding
    stacked += [note[Note.drive_low : Note.drive_low + 1, :inner] for note in rows] + padding
    drive[...] = jnp.transpose(jnp.concatenate(stacked, axis=0)).astype(BF16)
    mixed[...] = window_mixed[0:slots, :].astype(BF16)
    for k in range(KW - 1):
        conv_x_next[k] = window_x[k].astype(BF16)
        conv_bc_next[k] = window_bc[k].astype(BF16)

    stores = []
    for m in range(moves):
        slot = plan[at.slot + m]
        for copy in loaded(m, parcels[0]):
            copy.wait()
        owner, local_page, offset = place_of(plan[at.arrived_length + m], col_count)
        key_value = rows[m][Note.key_value : Note.key_value + 1, : 2 * KVH * HD]

        @pl.when(owner == col)
        def _(m=m, local_page=local_page, offset=offset, key_value=key_value):
            packed[m, local_page] = inserted(packed[m, local_page], key_value, offset)

        for page in range(pages_here):
            stores.append(
                pltpu.make_async_copy(
                    packed.at[m, page], pool_next.at[table[page, slot]], out_sems.at[m, page]
                )
            )
            stores[-1].start()
        prior = [
            jnp.concatenate([packed[m, pages_here + h, :, :NS], packed[m, pages_here + h, :, NS:]], axis=0)
            for h in range(heads)
        ]
        advance_state(m, prior, b_twice, drive, decay, made.at[m])
        stores.append(pltpu.make_async_copy(made.at[m], state_next.at[slot], out_sems.at[m, pages_here]))
        stores[-1].start()
    for store in stores:
        store.wait()


def shape(dims, dtype):
    return jax.ShapeDtypeStruct(tuple(dims), dtype)


def params(limit=VMEM_LIMIT):
    return pltpu.CompilerParams(vmem_limit_bytes=limit)


def exchange(value, axis):
    return lax.all_to_all(value, axis, split_axis=0, concat_axis=0, tiled=True)


def trade(block, axis, d):
    return lax.ppermute(block, axis, [(i, i ^ d) for i in range(lax.axis_size(axis))])


def ordered(value, first):
    return lax.optimization_barrier((value, first))[0]


def local(
    tokens, arrival, cache_lengths, move_slot, move_target, page_table, kv_pool, ssm_state,
    conv_x, conv_bc, norm_gain, weight_z, weight_x, weight_dt, weight_bc, weight_qkv,
    conv_weight_x, conv_weight_bc, dt_bias, a_log, d_skip, weight_ssm_out, weight_attn_out,
):
    row_count = lax.axis_size("rows")
    col_count = lax.axis_size("cols")
    row_index = lax.axis_index("rows").astype(I32).reshape(1)
    col_index = lax.axis_index("cols").astype(I32).reshape(1)
    slots, heads = ssm_state.shape[0], ssm_state.shape[1]
    total, depth = tokens.shape
    moves = move_slot.shape[1]
    pages_here, width = page_table.shape[3], kv_pool.shape[3]
    inner = heads * HP
    stays = slots - moves
    cols, at = Columns(inner), Plan(slots, moves)
    table = page_table[0, 0].T
    pool = kv_pool[:, 0]
    past_x, past_bc = conv_x.transpose(1, 0, 2), conv_bc.transpose(1, 0, 2)
    rows = row_count * BLOCK
    model = depth * row_count
    share = QH * HD // col_count
    parcel = (pages_here + heads, PAGE, width)
    parcels_here = pltpu.VMEM((moves,) + parcel, BF16)

    chip_count = row_count // 2
    early = early_parts(row_count)
    plan, mine, theirs, *ahead = pl.pallas_call(
        project_kernel,
        out_shape=[
            shape((at.size,), I32),
            shape((chip_count * BLOCK, cols.width), F32),
            shape((chip_count * BLOCK, cols.width), BF16),
        ]
        + [shape((pages_here,) + parcel[1:], BF16)] * len(early),
        in_specs=[SMEM_SPEC] * 6 + [VMEM_SPEC] * 7 + [ANY_SPEC],
        out_specs=[SMEM_SPEC] + [VMEM_SPEC] * 2 + [ANY_SPEC] * len(early),
        scratch_shapes=[
            pltpu.SMEM((total,), I32),
            pltpu.VMEM((total, depth), F32),
            pltpu.VMEM((rows, depth), F32),
            pltpu.VMEM((rows, LANES), F32),
            pltpu.VMEM((len(early), pages_here, PAGE, width), BF16),
            pltpu.SemaphoreType.DMA((len(early),)),
            pltpu.SemaphoreType.DMA((len(early),)),
        ],
        compiler_params=params(FIRST_LIMIT),
        cost_estimate=BRIEF,
        name="project",
    )(
        row_index, arrival, cache_lengths, move_slot.T, move_target.T, table,
        tokens, norm_gain, weight_z, weight_x, weight_dt.T, weight_bc, weight_qkv, pool,
    )
    ahead = [trade(pages, "rows", d) for d, pages in zip(early, ahead)]
    parcels = pl.pallas_call(
        functools.partial(pack_kernel, moves=moves, row_count=row_count),
        out_shape=[
            shape((heads,) + parcel[1:] if d in early else parcel, BF16) for d in range(1, row_count)
        ],
        in_specs=[SMEM_SPEC] * 2 + [ANY_SPEC] * 2,
        out_specs=[ANY_SPEC] * (row_count - 1),
        scratch_shapes=[
            parcels_here,
            pltpu.SemaphoreType.DMA((moves,)),
            pltpu.SemaphoreType.DMA((moves,)),
        ],
        compiler_params=params(FIRST_LIMIT),
        cost_estimate=BRIEF,
        name="pack",
    )(plan, table, pool, ssm_state)

    sums = pl.pallas_call(
        pair_kernel,
        out_shape=[shape((BLOCK, cols.width), F32)] + [shape((BLOCK, cols.width), BF16)] * (chip_count - 1),
        in_specs=[VMEM_SPEC] * 2,
        out_specs=[VMEM_SPEC] * chip_count,
        compiler_params=params(FIRST_LIMIT),
        cost_estimate=BRIEF,
        name="pair",
    )(mine, trade(theirs, "rows", 1))
    received = [sums[0]] + [trade(block, "rows", 2 * j) for j, block in enumerate(sums[1:], 1)]

    moving = [None, *parcels]

    def migrate(parts, after):
        for d in parts:
            moving[d] = trade(ordered(moving[d], after), "rows", d)
        return [moving[d] for d in parts]

    evens, odds = list(range(2, row_count, 2)), list(range(3, row_count, 2))
    first = [odds[0], odds[len(odds) // 2]]
    second = [d for d in evens if d not in early]
    last = [d for d in odds + evens if d not in first + second] + [1]
    received = ordered(received, ahead)
    first_moved = migrate(first, received)
    second_moved = migrate(second, received)

    pool_next, kv_new, partials = pl.pallas_call(
        functools.partial(
            attend_kernel, moves=moves, heads=heads, chip_count=chip_count, col_count=col_count, width=model
        ),
        out_shape=[
            shape(pool.shape, BF16),
            shape((BLOCK, 2 * KVH * HD), F32),
            shape((col_count * BLOCK, share + LANES), F32),
        ],
        in_specs=[SMEM_SPEC] * 3 + [ANY_SPEC] + [VMEM_SPEC] * chip_count,
        out_specs=[ANY_SPEC] + [VMEM_SPEC] * 2,
        scratch_shapes=[
            pltpu.VMEM(pool.shape, BF16),
            pltpu.VMEM((BLOCK * QH, HD), F32),
            pltpu.VMEM((BLOCK * QH, pages_here * PAGE), F32),
            pltpu.VMEM((BLOCK * QH, HD), F32),
            pltpu.VMEM((BLOCK * QH, HD), F32),
            pltpu.VMEM((BLOCK * QH, HD), F32),
            pltpu.SemaphoreType.DMA((2 if pool.shape[0] % 4 else 4,)),
            pltpu.SemaphoreType.DMA((2 if pool.shape[0] % 4 else 4,)),
        ],
        compiler_params=params(),
        cost_estimate=BRIEF,
        name="attend",
    )(col_index, plan, table, pool, *received)
    received = ordered(received, partials)
    partials = exchange(partials, "cols")

    next_x, next_bc, gated, driven, decay, drive, b_twice = pl.pallas_call(
        functools.partial(mix_kernel, chip_count=chip_count, width=model),
        out_shape=(
            shape(past_x.shape, F32),
            shape(past_bc.shape, F32),
            shape((BLOCK, inner), F32),
            shape((BLOCK, inner), F32),
            shape((BLOCK, heads), F32),
            shape((inner, 2 * BLOCK), BF16),
            shape((2 * BLOCK, NS), F32),
        ),
        in_specs=[VMEM_SPEC] * 7 + [ANY_SPEC] + [VMEM_SPEC] * chip_count,
        out_specs=(VMEM_SPEC,) * 7,
        scratch_shapes=[
            pltpu.VMEM((BLOCK, inner), F32),
            pltpu.VMEM((slots, heads, HP, NS), BF16),
            pltpu.SemaphoreType.DMA((slots,)),
        ],
        compiler_params=params(),
        cost_estimate=BRIEF,
        name="mix",
    )(past_x, past_bc, conv_weight_x, conv_weight_bc, dt_bias, a_log, d_skip, ssm_state, *received)

    columns = weight_ssm_out.shape[1] // col_count
    terms = pl.pallas_call(
        functools.partial(output_kernel, slots=slots, col_count=col_count),
        out_shape=shape((col_count * BLOCK, columns), BF16),
        in_specs=[VMEM_SPEC] * 4,
        out_specs=VMEM_SPEC,
        compiler_params=params(),
        cost_estimate=BRIEF,
        name="output",
    )(gated, weight_ssm_out, weight_attn_out, partials)
    migrate(last, (terms, first_moved))
    drive = ordered(drive, terms)
    terms = exchange(terms, "cols")
    state_next = pl.pallas_call(
        functools.partial(stay_kernel, moves=moves),
        out_shape=shape(ssm_state.shape, BF16),
        in_specs=[SMEM_SPEC] + [VMEM_SPEC] * 3 + [ANY_SPEC],
        out_specs=ANY_SPEC,
        scratch_shapes=[
            pltpu.VMEM((stays, heads, HP, NS), BF16),
            pltpu.VMEM((stays, heads, HP, NS), BF16),
            pltpu.SemaphoreType.DMA((stays,)),
            pltpu.SemaphoreType.DMA((stays,)),
        ],
        compiler_params=params(),
        cost_estimate=BRIEF,
        name="stay",
    )(plan, drive, decay, b_twice, ssm_state)

    terms = ordered(terms, second_moved)
    note = (BLOCK, max(inner, 2 * NS, 2 * KVH * HD, columns))
    notes = pl.pallas_call(
        functools.partial(total_kernel, moves=moves, col_count=col_count),
        out_shape=shape((rows, note[1]), BF16),
        in_specs=[SMEM_SPEC] + [VMEM_SPEC] * 7,
        out_specs=VMEM_SPEC,
        scratch_shapes=[pltpu.VMEM((BLOCK, columns), F32), pltpu.VMEM(note, F32)],
        compiler_params=params(),
        cost_estimate=BRIEF,
        name="total",
    )(plan, kv_new, driven, decay, b_twice, next_x, next_bc, terms)
    notes = exchange(notes, "rows")

    parts = []
    for d in range(1, row_count):
        parts += [ahead[early.index(d)], moving[d]] if d in early else [moving[d]]
    mixed, conv_x_next, conv_bc_next, state_next, pool_next = pl.pallas_call(
        functools.partial(arrive_kernel, moves=moves, row_count=row_count, col_count=col_count),
        out_shape=(
            shape((slots, columns), BF16),
            shape(past_x.shape, BF16),
            shape(past_bc.shape, BF16),
            shape(ssm_state.shape, BF16),
            shape(pool.shape, BF16),
        ),
        in_specs=[SMEM_SPEC] * 3 + [VMEM_SPEC] * 2 + [ANY_SPEC] * 2 + [VMEM_SPEC] + [ANY_SPEC] * (row_count - 1 + len(early)),
        out_specs=[VMEM_SPEC] * 3 + [ANY_SPEC] * 2,
        scratch_shapes=[
            parcels_here,
            pltpu.VMEM((moves, heads, HP, NS), BF16),
            pltpu.VMEM((inner, 2 * BLOCK), BF16),
            pltpu.VMEM((BLOCK, heads), F32),
            pltpu.VMEM((2 * BLOCK, NS), F32),
            pltpu.VMEM((KW - 1, slots, inner), F32),
            pltpu.VMEM((KW - 1, slots, 2 * NS), F32),
            pltpu.VMEM((BLOCK, columns), F32),
            pltpu.SemaphoreType.DMA((moves, 2)),
            pltpu.SemaphoreType.DMA((moves, pages_here + 1)),
        ],
        input_output_aliases={5: 3, 6: 4},
        compiler_params=params(LAST_LIMIT),
        cost_estimate=BRIEF,
        name="arrive",
    )(col_index, plan, table, next_x, next_bc, state_next, pool_next, notes, *parts)
    return (
        mixed, state_next, conv_x_next.transpose(1, 0, 2), conv_bc_next.transpose(1, 0, 2), pool_next[:, None]
    )


def solution(mesh):
    in_specs = (
        P(None, "rows"),
        P(),
        P(),
        P(),
        P(),
        P("rows", "cols", None, None),
        P("rows", "cols", None, None),
        P("rows", "cols", None, None),
        P("rows", None, "cols"),
        P("rows", None, None),
        P("rows"),
        P("rows", "cols"),
        P("rows", "cols"),
        P("rows", "cols"),
        P("rows", None),
        P("rows", None),
        P(None, "cols"),
        P(),
        P("cols"),
        P("cols"),
        P("cols"),
        P("cols", None),
        P("cols", None),
    )
    out_specs = (
        P("rows", "cols"),
        P("rows", "cols", None, None),
        P("rows", None, "cols"),
        P("rows", None, None),
        P("rows", "cols", None, None),
    )
    return jax.shard_map(local, mesh=mesh, in_specs=in_specs, out_specs=out_specs, check_vma=False)
```
